32 devices in a mesh: grp: 2 (over y), row: 4 (over z), col: 4 (over x, core).
Axes of the slice: x: 2, y: 2, z: 4, core: 2. Of those that a mesh axis runs over, the one named last changes fastest.
Arguments:
- frames: bfloat16 [16, 24576], P(None, ('grp', 'row', 'col')), parts along dimension 1, may hold values from -6 to 6
- vectors: bfloat16 [16, 24576], P(None, ('grp', 'row', 'col')), parts along dimension 1, may hold values from -8 to 8
- degrees: float32 [24576], P(('grp', 'row', 'col')), parts along dimension 0, may hold values from 1 to 10
- tile_table: int32 [16, 8, 2], replicated, may hold values from -1 to 15, as said below
Outputs:
- basis: float32 [16, 24576], P(None, ('grp', 'row', 'col')), parts along dimension 1
- ritz: float32 [32, 16], P('grp'), parts along dimension 0
The draws below stay inside these ranges and needn't reach their ends.
There are 2 independent parts, one for each index of `grp`. The reference program is written for one: setup_inputs(seed, part) draws one part's arguments, and reference() takes and returns one part's arrays. A program takes and returns all parts, laid end to end along the dimension named above; an argument that names none is the same for every part. Nothing has to cross between parts.
Inputs may be any that keep to these rules, and one draw needn't show every extreme that they name: `tile_table`: row d lists the tiles computed by device d of row+col (index row * 4 + col): pairs (I, J) of frame blocks with I <= J, filled from the front, the remaining slots -1 in both entries. Every pair (I, I) is listed once, every other pair at most once, 76 pairs in all. Some device has all 8 slots filled.
All inputs are finite; a program needn't handle non-finite values.
Results may differ from the reference program's by a relative error of at most 0.0047.
Values may be sent and summed in bfloat16 or wider, within the bound.
No kernel may reach another device: no remote copies, remote signals or barrier semaphores. Data moves between devices by JAX's collectives and lax.ppermute only.
A program may use at most 64 MiB of HBM per device.

```python
import math
import jax
import jax.numpy as jnp
import numpy as np
from jax import lax

NCV = 16
NVEC = 16
FR_DEV = 768
NB = 16
NF = 12288
NTILES = 76
TMAX = 8


def draw_vectors(key, part):
    key = jax.random.fold_in(key, 11)
    place = jnp.arange(NF, dtype=jnp.float32) / NF
    base = jax.random.normal(jax.random.fold_in(key, 1), (NVEC, NF), jnp.float32)
    rise = jnp.sqrt(1.0 + 2.0 * place)
    values = base * rise[None, :]
    return jnp.clip(values, -8.0, 8.0).astype(jnp.bfloat16)


def draw_tile_table(key, part):
    key = jax.random.fold_in(key, 23)
    upper = np.stack(np.triu_indices(NB, 1), axis=1).astype(np.int32)
    chosen = jax.random.permutation(jax.random.fold_in(key, 1), upper.shape[0])[:NTILES - NB]
    off_pairs = jnp.asarray(upper)[chosen]
    diag = jnp.arange(NB, dtype=jnp.int32)
    all_pairs = jnp.concatenate([jnp.stack([diag, diag], axis=1), off_pairs], axis=0)
    shuffle = jax.random.permutation(jax.random.fold_in(key, 2), NTILES)
    pairs = all_pairs[shuffle].astype(jnp.int32)
    quarter = NB // 4
    others = NB - quarter
    rest = NTILES - TMAX * quarter
    quota = np.full(NB, rest // others, np.int64)
    quota[quarter:quarter + rest % others] += 1
    quota[:quarter] = TMAX
    starts = np.concatenate([np.zeros(1, np.int64), np.cumsum(quota)[:-1]])
    slots = np.arange(TMAX)[None, :]
    by_rank = np.where(slots < quota[:, None], starts[:, None] + slots, -1).astype(np.int32)
    rank_of_device = jax.random.permutation(jax.random.fold_in(key, 3), NB)
    tiles = jnp.asarray(by_rank)[rank_of_device]
    picked = pairs[jnp.maximum(tiles, 0)]
    return jnp.where(tiles[:, :, None] >= 0, picked, -1).astype(jnp.int32)


def steps_of(own_key, dims, shards, low, top_value):
    gain = 1.0
    for dim, parts in shards:
        steps = jax.random.uniform(jax.random.fold_in(jax.random.fold_in(own_key, 6), dim), (parts,), jnp.float32, low / len(shards), top_value / len(shards))
        gain = gain * jnp.repeat(jnp.exp(steps), dims[dim] // parts).reshape((-1,) + (1,) * (len(dims) - 1 - dim))
    return gain


def bell_draw(own_key, extent, deviation, most, cuts=(), held_as=jnp.bfloat16):
    entries = deviation * jax.random.normal(own_key, extent, jnp.float32)
    if cuts:
        entries = entries * steps_of(own_key, extent, cuts, -0.22, 0.18)
    return jnp.clip(entries, -most, most).astype(held_as)


def setup_inputs(seed: int = 0, part: int = 0) -> dict:
    streams_of = jax.random.split(jax.random.key(seed), 5)
    part_splits = jax.random.split(jax.random.fold_in(streams_of[4], part), 5)
    return {
        "frames": bell_draw(part_splits[0], (NCV, NF), 1.0, 6.0, ((1, 16),)),
        "vectors": draw_vectors(jax.random.fold_in(jax.random.fold_in(streams_of[4], part), 71), part),
        "degrees": jnp.clip(jnp.exp(math.log(10.0) - 2.3025851 * jax.random.uniform(part_splits[2], (NF,), jnp.float32) ** steps_of(part_splits[2], (NF,), ((0, 16),), -0.2, 0.2)), 1.0, 10.0),
        "tile_table": draw_tile_table(jax.random.fold_in(streams_of[4], 71), part),
    }


kernel_width = 4.0

def tile_terms(frames_all, scaled_all, first, second, rows):
    left_x = lax.dynamic_slice_in_dim(frames_all, first * rows, rows, 1)
    right_x = lax.dynamic_slice_in_dim(frames_all, second * rows, rows, 1)
    left_v = lax.dynamic_slice_in_dim(scaled_all, first * rows, rows, 1)
    right_v = lax.dynamic_slice_in_dim(scaled_all, second * rows, rows, 1)
    left_sq = lax.optimization_barrier(jnp.sum(jnp.square(left_x.astype(jnp.float32)), axis=0))
    right_sq = lax.optimization_barrier(jnp.sum(jnp.square(right_x.astype(jnp.float32)), axis=0))
    cross = lax.dot_general(left_x.astype(jnp.float32), right_x.astype(jnp.float32), (((0,), (0,)), ((), ())), preferred_element_type=jnp.float32)
    dist = left_sq[:, None] + right_sq[None, :] - 2.0 * cross
    kern = jnp.exp(-dist / kernel_width).astype(jnp.bfloat16)
    to_left = lax.dot_general(right_v.astype(jnp.float32), kern.astype(jnp.float32), (((1,), (1,)), ((), ())), preferred_element_type=jnp.float32)
    to_right = lax.dot_general(left_v.astype(jnp.float32), kern.astype(jnp.float32), (((1,), (0,)), ((), ())), preferred_element_type=jnp.float32)
    return (to_left, to_right)

def add_block(image, term, start):
    old = lax.dynamic_slice_in_dim(image, start, term.shape[1], 1)
    return lax.dynamic_update_slice_in_dim(image, old + term, start, 1)

def reference(frames, vectors, degrees, tile_table):
    rows = FR_DEV
    scale_root = lax.rsqrt(degrees)
    scaled = (vectors.astype(jnp.float32) * scale_root[None, :]).astype(jnp.bfloat16)
    flat = tile_table.reshape(-1, 2)
    live = flat[:, 0] >= 0
    order = jnp.argsort(jnp.where(live, 0, 1).astype(jnp.int32), stable=True)
    listed = flat[order]
    count = jnp.sum(live.astype(jnp.int32))

    def visit(step, image):
        first = listed[step, 0].astype(jnp.int32)
        second = listed[step, 1].astype(jnp.int32)
        to_left, to_right = tile_terms(frames, scaled, first, second, rows)
        image = add_block(image, to_left, (first * rows).astype(jnp.int32))
        weight = (first != second).astype(jnp.float32)
        return add_block(image, to_right * weight, (second * rows).astype(jnp.int32))
    image = lax.fori_loop(0, count, visit, jnp.zeros((NVEC, NF), jnp.float32))
    applied = image * scale_root[None, :]
    image_gram = jnp.dot(applied, applied.T, precision=lax.Precision.HIGHEST)
    cross_gram = jnp.dot(vectors.astype(jnp.float32), applied.T, precision=lax.Precision.HIGHEST)
    vector_gram = jnp.dot(vectors.astype(jnp.float32), vectors.T.astype(jnp.float32), preferred_element_type=jnp.float32)
    image_factor = jnp.linalg.cholesky(image_gram)
    basis = jax.scipy.linalg.solve_triangular(image_factor, applied, lower=True) * math.sqrt(NF)
    vector_factor = jnp.linalg.cholesky(vector_gram)
    half = jax.scipy.linalg.solve_triangular(vector_factor, cross_gram, lower=True)
    ritz = jax.scipy.linalg.solve_triangular(vector_factor, half.T, lower=True).T
    return (basis, ritz)
```

```python
import functools
import math

import jax
import jax.numpy as jnp
from jax import lax
from jax.experimental import pallas as pl
from jax.experimental.pallas import tpu as pltpu
from jax.sharding import PartitionSpec as P

unit = -math.log2(math.e) / 4.0

NT = (((1,), (1,)), ((), ()))
TN = (((0,), (0,)), ((), ()))


def split3(x):
    high = x.astype(jnp.bfloat16).astype(jnp.float32)
    rest = x - high
    mid = rest.astype(jnp.bfloat16).astype(jnp.float32)
    low = (rest - mid).astype(jnp.bfloat16).astype(jnp.float32)
    return high, mid, low


def pack_kernel(frames_ref, vectors_ref, degrees_ref, out_ref):
    ncv = frames_ref.shape[0]
    root = lax.rsqrt(degrees_ref[...])
    out_ref[:ncv, :] = frames_ref[...]
    out_ref[ncv:, :] = (vectors_ref[...].astype(jnp.float32) * root).astype(jnp.bfloat16)


def edge_rows(square, ones_first):
    high, mid, low = split3(square * unit)
    shape = (16, square.shape[1])
    row = lax.broadcasted_iota(jnp.int32, shape, 0)
    base = 3 if ones_first else 0
    ones_at = 0 if ones_first else 3
    block = jnp.where((row >= ones_at) & (row < ones_at + 3), 1.0, 0.0)
    block = jnp.where(row == base, high, block)
    block = jnp.where(row == base + 1, mid, block)
    block = jnp.where(row == base + 2, low, block)
    return block.astype(jnp.bfloat16)


def image_kernel(
    list_ref, count_ref, all_ref, own_ref, vectors_ref, degrees_ref,
    applied_ref, gram_ref, left_ref, image_ref,
):
    ncv = own_ref.shape[0]
    own = own_ref[...].astype(jnp.float32)
    high, mid, low = split3(own * (-2.0 * unit))
    square = jnp.sum(own * own, axis=0, keepdims=True)
    edge = edge_rows(square, True).astype(jnp.float32)
    left = jnp.concatenate([high, mid, low, edge], axis=0)
    left_ref[...] = left.T.astype(jnp.bfloat16)
    image_ref[...] = jnp.zeros_like(image_ref)

    def visit(step, _):
        block = list_ref[step]
        x = all_ref[block, :ncv, :]
        v = all_ref[block, ncv:, :]
        wide = x.astype(jnp.float32)
        edge = edge_rows(jnp.sum(wide * wide, axis=0, keepdims=True), False)
        right = jnp.concatenate([x, x, x, edge], axis=0)
        power = jnp.dot(left_ref[...], right, preferred_element_type=jnp.float32)
        kern = jnp.exp2(power).astype(jnp.bfloat16)
        image_ref[...] += lax.dot_general(kern, v, NT, preferred_element_type=jnp.float32)
        return 0

    lax.fori_loop(0, count_ref[0], visit, 0)
    applied = image_ref[...].T * lax.rsqrt(degrees_ref[...])
    applied_ref[...] = applied
    both = jnp.concatenate([applied, vectors_ref[...].astype(jnp.float32)], axis=0)
    gram_ref[...] = lax.dot_general(
        both, both, NT, precision=lax.Precision.HIGHEST, preferred_element_type=jnp.float32
    )


def inverse_factor(gram):
    n = gram.shape[0]
    shape = (n, 2 * n)
    row = lax.broadcasted_iota(jnp.int32, shape, 0)
    lane = lax.broadcasted_iota(jnp.int32, shape, 1)
    work = jnp.concatenate([gram, (row == lane).astype(jnp.float32)[:, :n]], axis=1)
    for k in range(n - 1):
        column = jnp.broadcast_to(work[:, k : k + 1], shape)
        factor = jnp.where(row > k, column / column[k : k + 1, :], 0.0)
        work = work - factor * work[k : k + 1, :]
    pivot = jnp.sum(jnp.where(row == lane, work, 0.0), axis=1, keepdims=True)
    return work[:, n:] * lax.rsqrt(pivot)


def finish_kernel(total_frames, grams_ref, applied_ref, basis_ref, ritz_ref):
    gram = jnp.sum(grams_ref[...], axis=0)
    n = applied_ref.shape[0]
    exact = functools.partial(
        lax.dot_general, precision=lax.Precision.HIGHEST, preferred_element_type=jnp.float32
    )
    plain = (((1,), (0,)), ((), ()))
    image_inverse = inverse_factor(gram[:n, :n])
    vector_inverse = inverse_factor(gram[n:, n:])
    basis_ref[...] = exact(image_inverse * math.sqrt(total_frames), applied_ref[...], plain)
    half = exact(vector_inverse, gram[n:, :n], plain)
    ritz_ref[...] = exact(half, vector_inverse, NT)


def per_device(frames, vectors, degrees, tile_table):
    ncv, rows = frames.shape
    nvec = vectors.shape[0]
    axes = ("row", "col")
    devices = lax.axis_size("row") * lax.axis_size("col")
    me = lax.axis_index(axes)
    degrees = degrees[None, :]
    vmem = pl.BlockSpec(memory_space=pltpu.VMEM)
    smem = pl.BlockSpec(memory_space=pltpu.SMEM)
    params = pltpu.CompilerParams(vmem_limit_bytes=48 * 1024 * 1024)

    packed = pl.pallas_call(
        pack_kernel,
        out_shape=jax.ShapeDtypeStruct((ncv + nvec, rows), jnp.bfloat16),
        in_specs=[vmem] * 3,
        out_specs=vmem,
        name="pack",
    )(frames, vectors, degrees)
    everything = lax.all_gather(packed, axes, axis=0)

    first, second = tile_table[..., 0].reshape(-1), tile_table[..., 1].reshape(-1)
    blocks = jnp.arange(devices, dtype=jnp.int32)
    linked = jnp.any(
        ((first == me)[None, :] & (second[None, :] == blocks[:, None]))
        | ((second == me)[None, :] & (first[None, :] == blocks[:, None])),
        axis=1,
    ).astype(jnp.int32)
    place = jnp.sum(jnp.where(blocks[None, :] < blocks[:, None], linked[None, :], 0), axis=1)
    chosen = (place[None, :] == blocks[:, None]) & (linked[None, :] == 1)
    order = jnp.sum(jnp.where(chosen, blocks[None, :], 0), axis=1)
    count = jnp.sum(linked)[None]

    applied, gram = pl.pallas_call(
        image_kernel,
        out_shape=(
            jax.ShapeDtypeStruct((nvec, rows), jnp.float32),
            jax.ShapeDtypeStruct((2 * nvec, 2 * nvec), jnp.float32),
        ),
        in_specs=[smem, smem, vmem, vmem, vmem, vmem],
        out_specs=(vmem, vmem),
        scratch_shapes=[
            pltpu.VMEM((rows, 3 * ncv + 16), jnp.bfloat16),
            pltpu.VMEM((rows, nvec), jnp.float32),
        ],
        compiler_params=params,
        name="image",
    )(order, count, everything, frames, vectors, degrees)

    grams = lax.all_gather(gram, axes, axis=0)
    basis, ritz = pl.pallas_call(
        functools.partial(finish_kernel, rows * devices),
        out_shape=(
            jax.ShapeDtypeStruct((nvec, rows), jnp.float32),
            jax.ShapeDtypeStruct((nvec, nvec), jnp.float32),
        ),
        in_specs=[vmem, vmem],
        out_specs=(vmem, vmem),
        name="finish",
    )(grams, applied)
    return (basis, ritz)


def solution(mesh):
    split = P(None, ("grp", "row", "col"))
    return jax.shard_map(
        per_device,
        mesh=mesh,
        in_specs=(split, split, P(("grp", "row", "col")), P()),
        out_specs=(split, P("grp", None)),
        check_vma=False,
    )
```

```python
import functools
import math

import jax
import jax.numpy as jnp
from jax import lax
from jax.experimental import pallas as pl
from jax.experimental.pallas import tpu as pltpu
from jax.sharding import PartitionSpec as P

unit = -math.log2(math.e) / 4.0

NT = (((1,), (1,)), ((), ()))
TN = (((0,), (0,)), ((), ()))


def split3(x):
    high = x.astype(jnp.bfloat16).astype(jnp.float32)
    rest = x - high
    mid = rest.astype(jnp.bfloat16).astype(jnp.float32)
    low = (rest - mid).astype(jnp.bfloat16).astype(jnp.float32)
    return high, mid, low


def pack_kernel(frames_ref, vectors_ref, degrees_ref, out_ref):
    ncv = frames_ref.shape[0]
    root = lax.rsqrt(degrees_ref[...])
    out_ref[:ncv, :] = frames_ref[...]
    out_ref[ncv:, :] = (vectors_ref[...].astype(jnp.float32) * root).astype(jnp.bfloat16)


def edge_rows(square, ones_first):
    high, mid, low = split3(square * unit)
    shape = (16, square.shape[1])
    row = lax.broadcasted_iota(jnp.int32, shape, 0)
    base = 3 if ones_first else 0
    ones_at = 0 if ones_first else 3
    block = jnp.where((row >= ones_at) & (row < ones_at + 3), 1.0, 0.0)
    block = jnp.where(row == base, high, block)
    block = jnp.where(row == base + 1, mid, block)
    block = jnp.where(row == base + 2, low, block)
    return block.astype(jnp.bfloat16)


def image_kernel(
    linked_ref, near_ref, far_ref, own_ref, vectors_ref, degrees_ref,
    applied_ref, gram_ref, left_ref, image_ref,
):
    ncv = own_ref.shape[0]
    own = own_ref[...].astype(jnp.float32)
    high, mid, low = split3(own * (-2.0 * unit))
    square = jnp.sum(own * own, axis=0, keepdims=True)
    edge = edge_rows(square, True).astype(jnp.float32)
    left = jnp.concatenate([high, mid, low, edge], axis=0)
    left_ref[...] = left.T.astype(jnp.bfloat16)
    image_ref[...] = jnp.zeros_like(image_ref)

    def add_blocks(blocks_ref, offset):
        def visit(step, _):
            @pl.when(linked_ref[offset + step] > 0)
            def _():
                x = blocks_ref[step, :ncv, :]
                v = blocks_ref[step, ncv:, :]
                wide = x.astype(jnp.float32)
                edge = edge_rows(jnp.sum(wide * wide, axis=0, keepdims=True), False)
                right = jnp.concatenate([x, x, x, edge], axis=0)
                power = jnp.dot(left_ref[...], right, preferred_element_type=jnp.float32)
                kern = jnp.exp2(power).astype(jnp.bfloat16)
                image_ref[...] += lax.dot_general(
                    kern, v, NT, preferred_element_type=jnp.float32
                )

            return 0

        lax.fori_loop(0, blocks_ref.shape[0], visit, 0)

    add_blocks(near_ref, 0)
    add_blocks(far_ref, near_ref.shape[0])
    applied = image_ref[...].T * lax.rsqrt(degrees_ref[...])
    applied_ref[...] = applied
    both = jnp.concatenate([applied, vectors_ref[...].astype(jnp.float32)], axis=0)
    gram_ref[...] = lax.dot_general(
        both, both, NT, precision=lax.Precision.HIGHEST, preferred_element_type=jnp.float32
    )


def inverse_factor(gram):
    n = gram.shape[0]
    shape = (n, 2 * n)
    row = lax.broadcasted_iota(jnp.int32, shape, 0)
    lane = lax.broadcasted_iota(jnp.int32, shape, 1)
    work = jnp.concatenate([gram, (row == lane).astype(jnp.float32)[:, :n]], axis=1)
    for k in range(n - 1):
        column = jnp.broadcast_to(work[:, k : k + 1], shape)
        factor = jnp.where(row > k, column / column[k : k + 1, :], 0.0)
        work = work - factor * work[k : k + 1, :]
    pivot = jnp.sum(jnp.where(row == lane, work, 0.0), axis=1, keepdims=True)
    return work[:, n:] * lax.rsqrt(pivot)


def finish_kernel(total_frames, *refs):
    *grams_refs, applied_ref, basis_ref, ritz_ref = refs
    gram = sum(ref[...] for ref in grams_refs)
    n = applied_ref.shape[0]
    exact = functools.partial(
        lax.dot_general, precision=lax.Precision.HIGHEST, preferred_element_type=jnp.float32
    )
    plain = (((1,), (0,)), ((), ()))
    image_inverse = inverse_factor(gram[:n, :n])
    vector_inverse = inverse_factor(gram[n:, n:])
    basis_ref[...] = exact(image_inverse * math.sqrt(total_frames), applied_ref[...], plain)
    half = exact(vector_inverse, gram[n:, :n], plain)
    ritz_ref[...] = exact(half, vector_inverse, NT)


def shifted(x, axis, step):
    size = lax.axis_size(axis)
    return lax.ppermute(x, axis, [(i, (i + step) % size) for i in range(size)])


def swapped(x):
    return lax.ppermute(x, "col", [(i, i ^ 1) for i in range(lax.axis_size("col"))])


def per_device(frames, vectors, degrees, tile_table):
    ncv, rows = frames.shape
    nvec = vectors.shape[0]
    n_row, n_col = lax.axis_size("row"), lax.axis_size("col")
    devices = n_row * n_col
    my_row, my_col = lax.axis_index("row"), lax.axis_index("col")
    me = my_row * n_col + my_col
    degrees = degrees[None, :]
    vmem = pl.BlockSpec(memory_space=pltpu.VMEM)
    smem = pl.BlockSpec(memory_space=pltpu.SMEM)
    params = pltpu.CompilerParams(vmem_limit_bytes=48 * 1024 * 1024)

    packed = pl.pallas_call(
        pack_kernel,
        out_shape=jax.ShapeDtypeStruct((ncv + nvec, rows), jnp.bfloat16),
        in_specs=[vmem] * 3,
        out_specs=vmem,
        name="pack",
    )(frames, vectors, degrees)

    line = jnp.stack([packed] + [shifted(packed, "row", s) for s in range(1, n_row)])
    near = jnp.concatenate([line] + [shifted(line, "col", 2 * t) for t in range(1, n_col // 2)])
    far = swapped(near)

    packed, tile_table = lax.optimization_barrier((packed, tile_table))
    place = jnp.arange(devices // 2, dtype=jnp.int32)
    from_row = (my_row - place % n_row) % n_row
    from_col = jnp.concatenate(
        [(col - 2 * (place // n_row)) % n_col for col in (my_col, my_col ^ 1)]
    )
    block = jnp.concatenate([from_row, from_row]) * n_col + from_col
    first, second = tile_table[..., 0][None], tile_table[..., 1][None]
    block = block[:, None, None]
    hit = ((first == me) & (second == block)) | ((second == me) & (first == block))
    linked = jnp.max(hit.astype(jnp.int32), axis=(1, 2))

    applied, gram = pl.pallas_call(
        image_kernel,
        out_shape=(
            jax.ShapeDtypeStruct((nvec, rows), jnp.float32),
            jax.ShapeDtypeStruct((2 * nvec, 2 * nvec), jnp.float32),
        ),
        in_specs=[smem, vmem, vmem, vmem, vmem, vmem],
        out_specs=(vmem, vmem),
        scratch_shapes=[
            pltpu.VMEM((rows, 3 * ncv + 16), jnp.bfloat16),
            pltpu.VMEM((rows, nvec), jnp.float32),
        ],
        compiler_params=params,
        name="image",
    )(linked, near, far, frames, vectors, degrees)

    gram = gram + sum(shifted(gram, "row", s) for s in range(1, n_row))
    grams = [gram] + [shifted(gram, "col", s) for s in range(1, n_col)]
    basis, ritz = pl.pallas_call(
        functools.partial(finish_kernel, rows * devices),
        out_shape=(
            jax.ShapeDtypeStruct((nvec, rows), jnp.float32),
            jax.ShapeDtypeStruct((nvec, nvec), jnp.float32),
        ),
        in_specs=[vmem] * (n_col + 1),
        out_specs=(vmem, vmem),
        name="finish",
    )(*grams, applied)
    return (basis, ritz)


def solution(mesh):
    split = P(None, ("grp", "row", "col"))
    return jax.shard_map(
        per_device,
        mesh=mesh,
        in_specs=(split, split, P(("grp", "row", "col")), P()),
        out_specs=(split, P("grp", None)),
        check_vma=False,
    )
```

```python
import functools
import math

import jax
import jax.numpy as jnp
from jax import lax
from jax.experimental import pallas as pl
from jax.experimental.pallas import tpu as pltpu
from jax.sharding import PartitionSpec as P

unit = -math.log2(math.e) / 4.0

NT = (((1,), (1,)), ((), ()))
MIB = 1024 * 1024


def split3(x):
    high = x.astype(jnp.bfloat16).astype(jnp.float32)
    rest = x - high
    mid = rest.astype(jnp.bfloat16).astype(jnp.float32)
    low = (rest - mid).astype(jnp.bfloat16).astype(jnp.float32)
    return high, mid, low


def pack_kernel(frames_ref, vectors_ref, degrees_ref, out_ref):
    ncv = frames_ref.shape[0]
    root = lax.rsqrt(degrees_ref[...])[None, :]
    out_ref[:ncv, :] = frames_ref[...]
    out_ref[ncv:, :] = (vectors_ref[...].astype(jnp.float32) * root).astype(jnp.bfloat16)


def edge_rows(square, ones_first):
    high, mid, low = split3(square * unit)
    row = lax.broadcasted_iota(jnp.int32, (16, square.shape[1]), 0)
    base = 3 if ones_first else 0
    ones_at = 0 if ones_first else 3
    block = jnp.where((row >= ones_at) & (row < ones_at + 3), 1.0, 0.0)
    block = jnp.where(row == base, high, block)
    block = jnp.where(row == base + 1, mid, block)
    return jnp.where(row == base + 2, low, block)


def own_side(own):
    own = own.astype(jnp.float32)
    high, mid, low = split3(own * (-2.0 * unit))
    edge = edge_rows(jnp.sum(own * own, axis=0, keepdims=True), True)
    return jnp.concatenate([high, mid, low, edge], axis=0).T.astype(jnp.bfloat16)


def tile_image(left, x, v):
    wide = x.astype(jnp.float32)
    edge = edge_rows(jnp.sum(wide * wide, axis=0, keepdims=True), False).astype(jnp.bfloat16)
    right = jnp.concatenate([x, x, x, edge], axis=0)
    power = jnp.dot(left, right, preferred_element_type=jnp.float32)
    kern = jnp.exp2(power).astype(jnp.bfloat16)
    return lax.dot_general(kern, v, NT, preferred_element_type=jnp.float32)


def own_kernel(packed_ref, left_ref, image_ref):
    ncv = packed_ref.shape[0] // 2
    x = packed_ref[:ncv, :]
    left_ref[...] = own_side(x)
    image_ref[...] = tile_image(left_ref[...], x, packed_ref[ncv:, :])


def add_blocks(part, sizes, table_ref, left_ref, blocks_ref, image_ref):
    n_row, n_col = sizes
    ncv = blocks_ref.shape[1] // 2
    my_row, my_col = lax.axis_index("row"), lax.axis_index("col")
    me = my_row * n_col + my_col
    first, second = table_ref[:, 0, :], table_ref[:, 1, :]
    other = jnp.where(first == me, second, jnp.where(second == me, first, -1))
    words = []
    for start in range(0, n_row * n_col, 16):
        bit = jnp.zeros(other.shape, jnp.float32)
        for b in range(16):
            bit = jnp.where(other == start + b, float(1 << b), bit)
        words.append(jnp.sum(bit).astype(jnp.int32))
    lane_col = my_col ^ 1 if part in ("core", "far") else my_col

    def visit(step, _):
        shift = step // n_row + 1 if part in ("across", "far") else 0
        from_row = (my_row - step % n_row + n_row) % n_row
        from_col = (lane_col - 2 * shift + 2 * n_col) % n_col
        block = from_row * n_col + from_col
        word = words[0]
        for w in range(1, len(words)):
            word = jnp.where(block // 16 == w, words[w], word)

        @pl.when(((word >> (block % 16)) & 1) == 1)
        def _():
            image_ref[...] += tile_image(
                left_ref[...], blocks_ref[step, :ncv, :], blocks_ref[step, ncv:, :]
            )

        return 0

    lax.fori_loop(1 if part == "line" else 0, blocks_ref.shape[0], visit, 0)


def part_kernel(part, sizes, table_ref, left_ref, blocks_ref, before_ref, image_ref):
    image_ref[...] = before_ref[...]
    add_blocks(part, sizes, table_ref, left_ref, blocks_ref, image_ref)


def last_kernel(
    sizes, table_ref, left_ref, blocks_ref, before_ref, vectors_ref, degrees_ref,
    applied_ref, gram_ref, image_ref,
):
    image_ref[...] = before_ref[...]
    add_blocks("far", sizes, table_ref, left_ref, blocks_ref, image_ref)
    n = vectors_ref.shape[0]
    applied = image_ref[...].T * lax.rsqrt(degrees_ref[...])[None, :]
    applied_ref[...] = applied
    both = jnp.concatenate([applied, vectors_ref[...].astype(jnp.float32)], axis=0)
    gram = lax.dot_general(
        both, both, NT, precision=lax.Precision.HIGHEST, preferred_element_type=jnp.float32
    )
    wide = jnp.concatenate(
        [gram[:n, :n], gram[n:, :], jnp.zeros((n, n), jnp.float32)], axis=1
    )
    tile = jnp.concatenate([wide[: n // 2, :], wide[n // 2 :, :]], axis=1)
    for device in range(gram_ref.shape[0]):
        gram_ref[device] = tile


def inverse_factors(grams):
    n = grams[0].shape[0]
    half = 64
    tiles = range(n // 8)
    shape = (8, 2 * half)
    row = lax.broadcasted_iota(jnp.int32, shape, 0)
    lane = lax.broadcasted_iota(jnp.int32, shape, 1)
    columns = [
        [
            jnp.where(
                lane < half,
                jnp.broadcast_to(grams[0][8 * t : 8 * t + 8, j : j + 1], shape),
                jnp.broadcast_to(grams[1][8 * t : 8 * t + 8, j : j + 1], shape),
            )
            for t in tiles
        ]
        for j in range(n)
    ]
    right = [jnp.where(lane % half == row + 8 * t, 1.0, 0.0) for t in tiles]
    pivots = [jnp.ones(shape, jnp.float32) for t in tiles]
    for k in range(n):
        top, at = k // 8, k % 8
        pivot = columns[k][top][at : at + 1, :]
        pivots[top] = jnp.where(row == at, pivot, pivots[top])
        if k == n - 1:
            break
        scale = 1.0 / pivot
        factor = {t: columns[k][t] * scale for t in tiles if t >= top}
        factor[top] = jnp.where(row > at, factor[top], 0.0)
        for column in columns[k + 1 :] + [right]:
            line = column[top][at : at + 1, :]
            for t in factor:
                column[t] = column[t] - factor[t] * line
    result = jnp.concatenate([r * lax.rsqrt(p) for r, p in zip(right, pivots)], axis=0)
    return result[:, :n], result[:, half : half + n]


def finish_kernel(total_frames, grams_ref, applied_ref, basis_ref, ritz_ref):
    tile = grams_ref[0]
    for device in range(1, grams_ref.shape[0]):
        tile += grams_ref[device]
    n = applied_ref.shape[0]
    gram = jnp.concatenate([tile[:, : 4 * n], tile[:, 4 * n :]], axis=0)
    exact = functools.partial(
        lax.dot_general, precision=lax.Precision.HIGHEST, preferred_element_type=jnp.float32
    )
    plain = (((1,), (0,)), ((), ()))
    image_inverse, vector_inverse = inverse_factors([gram[:, :n], gram[:, 2 * n : 3 * n]])
    basis_ref[...] = exact(image_inverse * math.sqrt(total_frames), applied_ref[...], plain)
    half = exact(vector_inverse, gram[:, n : 2 * n], plain)
    ritz_ref[...] = exact(half, vector_inverse, NT)


def shifted(x, axis, step):
    size = lax.axis_size(axis)
    return lax.ppermute(x, axis, [(i, (i + step) % size) for i in range(size)])


def swapped(x):
    return lax.ppermute(x, "col", [(i, i ^ 1) for i in range(lax.axis_size("col"))])


def per_device(frames, vectors, degrees, tile_table):
    ncv, rows = frames.shape
    nvec = vectors.shape[0]
    n_row, n_col = lax.axis_size("row"), lax.axis_size("col")
    devices = n_row * n_col
    sizes = (n_row, n_col)
    vmem = pl.BlockSpec(memory_space=pltpu.VMEM)

    def call(kernel, name, outs, *args, limit=16, tiles=0, **keywords):
        shapes = [jax.ShapeDtypeStruct(*out) for out in outs]
        keywords["cost_estimate"] = pl.CostEstimate(
            flops=tiles * rows * rows * 2 * (4 * ncv + nvec),
            transcendentals=tiles * rows * rows,
            bytes_accessed=sum(a.size * a.dtype.itemsize for a in args),
        )
        return pl.pallas_call(
            kernel,
            out_shape=shapes,
            in_specs=[vmem] * len(args),
            out_specs=[vmem] * len(outs),
            compiler_params=pltpu.CompilerParams(vmem_limit_bytes=limit * MIB),
            name=name,
            **keywords,
        )(*args)

    table = tile_table.transpose(1, 2, 0)
    image_type = ((rows, nvec), jnp.float32)

    (packed,) = call(
        pack_kernel, "pack", [((ncv + nvec, rows), jnp.bfloat16)], frames, vectors, degrees
    )
    line = jnp.stack([packed] + [shifted(packed, "row", s) for s in range(1, n_row)])
    left, image = call(own_kernel, "own", [((rows, 3 * ncv + 16), jnp.bfloat16), image_type], packed, tiles=1)

    def add(part, blocks, image):
        (image,) = call(
            functools.partial(part_kernel, part, sizes),
            "add_" + part,
            [image_type],
            table,
            left,
            blocks,
            image,
            tiles=blocks.shape[0] // 2,
            input_output_aliases={3: 0},
        )
        return image

    line, image = lax.optimization_barrier((line, image))
    across = [shifted(line, "col", 2 * t) for t in range(1, n_col // 2)]
    across = across[0] if len(across) == 1 else jnp.concatenate(across)
    core = swapped(line)
    image = add("line", line, image)
    image = add("core", core, image)
    across, image = lax.optimization_barrier((across, image))
    far = swapped(across)
    image = add("across", across, image)
    applied, gram = call(
        functools.partial(last_kernel, sizes),
        "add_far",
        [((nvec, rows), jnp.float32), ((devices, nvec // 2, 8 * nvec), jnp.float32)],
        table,
        left,
        far,
        image,
        vectors,
        degrees,
        tiles=far.shape[0] // 2,
        scratch_shapes=[pltpu.VMEM(*image_type)],
    )
    grams = lax.all_to_all(gram, ("row", "col"), 0, 0)
    basis, ritz = call(
        functools.partial(finish_kernel, rows * devices),
        "finish",
        [((nvec, rows), jnp.float32), ((nvec, nvec), jnp.float32)],
        grams,
        applied,
    )
    return (basis, ritz)


def solution(mesh):
    split = P(None, ("grp", "row", "col"))
    return jax.shard_map(
        per_device,
        mesh=mesh,
        in_specs=(split, split, P(("grp", "row", "col")), P()),
        out_specs=(split, P("grp", None)),
        check_vma=False,
    )
```

```python
import functools
import math

import jax
import jax.numpy as jnp
from jax import lax
from jax.experimental import pallas as pl
from jax.experimental.pallas import tpu as pltpu
from jax.sharding import PartitionSpec as P

unit = -math.log2(math.e) / 4.0

NT = (((1,), (1,)), ((), ()))
MIB = 1024 * 1024


def split3(x):
    high = x.astype(jnp.bfloat16).astype(jnp.float32)
    rest = x - high
    mid = rest.astype(jnp.bfloat16).astype(jnp.float32)
    low = (rest - mid).astype(jnp.bfloat16).astype(jnp.float32)
    return high, mid, low


def pack_kernel(frames_ref, vectors_ref, degrees_ref, out_ref, raw_ref, degree_ref, sems):
    ncv = frames_ref.shape[0]
    copies = [
        pltpu.make_async_copy(vectors_ref, raw_ref, sems.at[0]),
        pltpu.make_async_copy(degrees_ref, degree_ref, sems.at[1]),
        pltpu.make_async_copy(frames_ref, out_ref.at[pl.ds(0, ncv)], sems.at[2]),
    ]
    for copy in copies:
        copy.start()
    copies[0].wait()
    copies[1].wait()
    root = lax.rsqrt(degree_ref[...])[None, :]
    out_ref[ncv:, :] = (raw_ref[...].astype(jnp.float32) * root).astype(jnp.bfloat16)
    copies[2].wait()


def edge_rows(square, ones_first):
    high, mid, low = split3(square * unit)
    row = lax.broadcasted_iota(jnp.int32, (16, square.shape[1]), 0)
    base = 3 if ones_first else 0
    ones_at = 0 if ones_first else 3
    block = jnp.where((row >= ones_at) & (row < ones_at + 3), 1.0, 0.0)
    block = jnp.where(row == base, high, block)
    block = jnp.where(row == base + 1, mid, block)
    return jnp.where(row == base + 2, low, block)


def own_side(own):
    own = own.astype(jnp.float32)
    high, mid, low = split3(own * (-2.0 * unit))
    edge = edge_rows(jnp.sum(own * own, axis=0, keepdims=True), True)
    return jnp.concatenate([high, mid, low, edge], axis=0).T.astype(jnp.bfloat16)


def tile_image(left_ref, x, v):
    wide = x.astype(jnp.float32)
    edge = edge_rows(jnp.sum(wide * wide, axis=0, keepdims=True), False).astype(jnp.bfloat16)
    right = jnp.concatenate([x, x, x, edge], axis=0)
    chunk = 256
    parts = []
    for start in range(0, x.shape[1], chunk):
        left = left_ref[start : start + chunk, :]
        power = jnp.dot(left, right, preferred_element_type=jnp.float32)
        kern = jnp.exp2(power).astype(jnp.bfloat16)
        parts.append(lax.dot_general(v, kern, NT, preferred_element_type=jnp.float32))
    return jnp.concatenate(parts, axis=1)


def own_kernel(packed_ref, left_ref, image_ref):
    ncv = packed_ref.shape[0] // 2
    x = packed_ref[:ncv, :]
    left_ref[...] = own_side(x)
    image_ref[...] = tile_image(left_ref, x, packed_ref[ncv:, :])


def add_blocks(part, sizes, table_ref, left_ref, blocks_ref, image_ref):
    n_row, n_col = sizes
    ncv = blocks_ref.shape[1] // 2
    my_row, my_col = lax.axis_index("row"), lax.axis_index("col")
    me = my_row * n_col + my_col
    first, second = table_ref[:, 0, :], table_ref[:, 1, :]
    other = jnp.where(first == me, second, jnp.where(second == me, first, -1))
    words = []
    for start in range(0, n_row * n_col, 16):
        bit = jnp.zeros(other.shape, jnp.float32)
        for b in range(16):
            bit = jnp.where(other == start + b, float(1 << b), bit)
        words.append(jnp.sum(bit).astype(jnp.int32))
    lane_col = my_col ^ 1 if part in ("core", "far") else my_col

    def visit(step, _):
        shift = step // n_row + 1 if part in ("across", "far") else 0
        from_row = (my_row - step % n_row + n_row) % n_row
        from_col = (lane_col - 2 * shift + 2 * n_col) % n_col
        block = from_row * n_col + from_col
        word = words[0]
        for w in range(1, len(words)):
            word = jnp.where(block // 16 == w, words[w], word)

        @pl.when(((word >> (block % 16)) & 1) == 1)
        def _():
            image_ref[...] += tile_image(
                left_ref, blocks_ref[step, :ncv, :], blocks_ref[step, ncv:, :]
            )

        return 0

    lax.fori_loop(1 if part == "line" else 0, blocks_ref.shape[0], visit, 0)


def part_kernel(part, sizes, table_ref, left_ref, blocks_ref, before_ref, image_ref):
    image_ref[...] = before_ref[...]
    add_blocks(part, sizes, table_ref, left_ref, blocks_ref, image_ref)


def last_kernel(
    sizes, table_ref, left_ref, blocks_ref, before_ref, vectors_ref, degrees_ref,
    applied_ref, gram_ref, image_ref,
):
    image_ref[...] = before_ref[...]
    add_blocks("far", sizes, table_ref, left_ref, blocks_ref, image_ref)
    n = vectors_ref.shape[0]
    applied = image_ref[...] * lax.rsqrt(degrees_ref[...])[None, :]
    applied_ref[...] = applied
    both = jnp.concatenate([applied, vectors_ref[...].astype(jnp.float32)], axis=0)
    gram = lax.dot_general(
        both, both, NT, precision=lax.Precision.HIGHEST, preferred_element_type=jnp.float32
    )
    wide = jnp.concatenate(
        [gram[:n, :n], gram[n:, :], jnp.zeros((n, n), jnp.float32)], axis=1
    )
    tile = jnp.concatenate([wide[: n // 2, :], wide[n // 2 :, :]], axis=1)
    for device in range(gram_ref.shape[0]):
        gram_ref[device] = tile


def inverse_factors(grams):
    n = grams[0].shape[0]
    half = 64
    tiles = range(n // 8)
    shape = (8, 2 * half)
    row = lax.broadcasted_iota(jnp.int32, shape, 0)
    lane = lax.broadcasted_iota(jnp.int32, shape, 1)
    columns = [
        [
            jnp.where(
                lane < half,
                jnp.broadcast_to(grams[0][8 * t : 8 * t + 8, j : j + 1], shape),
                jnp.broadcast_to(grams[1][8 * t : 8 * t + 8, j : j + 1], shape),
            )
            for t in tiles
        ]
        for j in range(n)
    ]
    right = [jnp.where(lane % half == row + 8 * t, 1.0, 0.0) for t in tiles]
    pivots = [jnp.ones(shape, jnp.float32) for t in tiles]
    for k in range(n):
        top, at = k // 8, k % 8
        pivot = columns[k][top][at : at + 1, :]
        pivots[top] = jnp.where(row == at, pivot, pivots[top])
        if k == n - 1:
            break
        scale = 1.0 / pivot
        factor = {t: columns[k][t] * scale for t in tiles if t >= top}
        factor[top] = jnp.where(row > at, factor[top], 0.0)
        for column in columns[k + 1 :] + [right]:
            line = column[top][at : at + 1, :]
            for t in factor:
                column[t] = column[t] - factor[t] * line
    result = jnp.concatenate([r * lax.rsqrt(p) for r, p in zip(right, pivots)], axis=0)
    return result[:, :n], result[:, half : half + n]


def finish_kernel(total_frames, grams_ref, applied_ref, basis_ref, ritz_ref):
    tile = grams_ref[0]
    for device in range(1, grams_ref.shape[0]):
        tile += grams_ref[device]
    n = applied_ref.shape[0]
    gram = jnp.concatenate([tile[:, : 4 * n], tile[:, 4 * n :]], axis=0)
    exact = functools.partial(
        lax.dot_general, precision=lax.Precision.HIGHEST, preferred_element_type=jnp.float32
    )
    plain = (((1,), (0,)), ((), ()))
    image_inverse, vector_inverse = inverse_factors([gram[:, :n], gram[:, 2 * n : 3 * n]])
    basis_ref[...] = exact(image_inverse * math.sqrt(total_frames), applied_ref[...], plain)
    half = exact(vector_inverse, gram[:, n : 2 * n], plain)
    ritz_ref[...] = exact(half, vector_inverse, NT)


def shifted(x, axis, step):
    size = lax.axis_size(axis)
    return lax.ppermute(x, axis, [(i, (i + step) % size) for i in range(size)])


def swapped(x):
    return lax.ppermute(x, "col", [(i, i ^ 1) for i in range(lax.axis_size("col"))])


def per_device(frames, vectors, degrees, tile_table):
    ncv, rows = frames.shape
    nvec = vectors.shape[0]
    n_row, n_col = lax.axis_size("row"), lax.axis_size("col")
    devices = n_row * n_col
    sizes = (n_row, n_col)
    vmem = pl.BlockSpec(memory_space=pltpu.VMEM)

    def call(kernel, name, outs, *args, limit=16, tiles=0, where=vmem, **keywords):
        shapes = [jax.ShapeDtypeStruct(*out) for out in outs]
        keywords["cost_estimate"] = pl.CostEstimate(
            flops=tiles * rows * rows * 2 * (4 * ncv + nvec),
            transcendentals=tiles * rows * rows,
            bytes_accessed=sum(a.size * a.dtype.itemsize for a in args),
        )
        return pl.pallas_call(
            kernel,
            out_shape=shapes,
            in_specs=[where] * len(args),
            out_specs=[vmem] * len(outs),
            compiler_params=pltpu.CompilerParams(vmem_limit_bytes=limit * MIB),
            name=name,
            **keywords,
        )(*args)

    table = tile_table.transpose(1, 2, 0)
    image_type = ((nvec, rows), jnp.float32)

    (packed,) = call(
        pack_kernel,
        "pack",
        [((ncv + nvec, rows), jnp.bfloat16)],
        *(pltpu.with_memory_space_constraint(x, pltpu.HBM) for x in (frames, vectors, degrees)),
        where=pl.BlockSpec(memory_space=pltpu.HBM),
        scratch_shapes=[
            pltpu.VMEM(vectors.shape, vectors.dtype),
            pltpu.VMEM(degrees.shape, degrees.dtype),
            pltpu.SemaphoreType.DMA((3,)),
        ],
    )
    line = jnp.stack([packed] + [shifted(packed, "row", s) for s in range(1, n_row)])
    left, image = call(own_kernel, "own", [((rows, 3 * ncv + 16), jnp.bfloat16), image_type], packed, tiles=1)

    def add(part, blocks, image):
        (image,) = call(
            functools.partial(part_kernel, part, sizes),
            "add_" + part,
            [image_type],
            table,
            left,
            blocks,
            image,
            tiles=blocks.shape[0] // 2,
            input_output_aliases={3: 0},
        )
        return image

    line, image = lax.optimization_barrier((line, image))
    across = [shifted(line, "col", 2 * t) for t in range(1, n_col // 2)]
    across = across[0] if len(across) == 1 else jnp.concatenate(across)
    core = swapped(line)
    image = add("line", line, image)
    image = add("core", core, image)
    across, image = lax.optimization_barrier((across, image))
    far = swapped(across)
    image = add("across", across, image)
    applied, gram = call(
        functools.partial(last_kernel, sizes),
        "add_far",
        [((nvec, rows), jnp.float32), ((n_row, nvec // 2, 8 * nvec), jnp.float32)],
        table,
        left,
        far,
        image,
        vectors,
        degrees,
        tiles=far.shape[0] // 2,
        scratch_shapes=[pltpu.VMEM(*image_type)],
    )
    grams = lax.all_to_all(gram, "row", 0, 0)
    gram = jnp.broadcast_to(jnp.sum(grams, axis=0), (n_col, nvec // 2, 8 * nvec))
    grams = lax.all_to_all(gram, "col", 0, 0)
    basis, ritz = call(
        functools.partial(finish_kernel, rows * devices),
        "finish",
        [((nvec, rows), jnp.float32), ((nvec, nvec), jnp.float32)],
        grams,
        applied,
    )
    return (basis, ritz)


def solution(mesh):
    split = P(None, ("grp", "row", "col"))
    return jax.shard_map(
        per_device,
        mesh=mesh,
        in_specs=(split, split, P(("grp", "row", "col")), P()),
        out_specs=(split, P("grp", None)),
        check_vma=False,
    )
```

```python
import functools
import math

import jax
import jax.numpy as jnp
from jax import lax
from jax.experimental import pallas as pl
from jax.experimental.pallas import tpu as pltpu
from jax.sharding import PartitionSpec as P

unit = -math.log2(math.e) / 4.0

NT = (((1,), (1,)), ((), ()))
MIB = 1024 * 1024


def split3(x):
    high = x.astype(jnp.bfloat16).astype(jnp.float32)
    rest = x - high
    mid = rest.astype(jnp.bfloat16).astype(jnp.float32)
    low = (rest - mid).astype(jnp.bfloat16).astype(jnp.float32)
    return high, mid, low


def pack_kernel(frames_ref, vectors_ref, degrees_ref, out_ref, raw_ref, degree_ref, sems):
    ncv = frames_ref.shape[0]
    copies = [
        pltpu.make_async_copy(vectors_ref, raw_ref, sems.at[0]),
        pltpu.make_async_copy(degrees_ref, degree_ref, sems.at[1]),
        pltpu.make_async_copy(frames_ref, out_ref.at[pl.ds(0, ncv)], sems.at[2]),
    ]
    for copy in copies:
        copy.start()
    copies[0].wait()
    copies[1].wait()
    root = lax.rsqrt(degree_ref[...])[None, :]
    out_ref[ncv:, :] = (raw_ref[...].astype(jnp.float32) * root).astype(jnp.bfloat16)
    copies[2].wait()


def edge_rows(square, ones_first):
    high, mid, low = split3(square * unit)
    row = lax.broadcasted_iota(jnp.int32, (16, square.shape[1]), 0)
    base = 3 if ones_first else 0
    ones_at = 0 if ones_first else 3
    block = jnp.where((row >= ones_at) & (row < ones_at + 3), 1.0, 0.0)
    block = jnp.where(row == base, high, block)
    block = jnp.where(row == base + 1, mid, block)
    return jnp.where(row == base + 2, low, block)


def own_side(own):
    own = own.astype(jnp.float32)
    high, mid, low = split3(own * (-2.0 * unit))
    edge = edge_rows(jnp.sum(own * own, axis=0, keepdims=True), True)
    return jnp.concatenate([high, mid, low, edge], axis=0).T.astype(jnp.bfloat16)


def tile_image(left_ref, x, v):
    wide = x.astype(jnp.float32)
    edge = edge_rows(jnp.sum(wide * wide, axis=0, keepdims=True), False).astype(jnp.bfloat16)
    right = jnp.concatenate([x, x, x, edge], axis=0)
    chunk = 256
    parts = []
    for start in range(0, x.shape[1], chunk):
        left = left_ref[start : start + chunk, :]
        power = jnp.dot(left, right, preferred_element_type=jnp.float32)
        kern = jnp.exp2(power).astype(jnp.bfloat16)
        parts.append(lax.dot_general(kern, v, NT, preferred_element_type=jnp.float32))
    return jnp.concatenate(parts, axis=0)


def own_kernel(packed_ref, left_ref, image_ref):
    ncv = packed_ref.shape[0] // 2
    x = packed_ref[:ncv, :]
    left_ref[...] = own_side(x)
    image_ref[...] = tile_image(left_ref, x, packed_ref[ncv:, :])


def add_blocks(part, sizes, table_ref, left_ref, blocks_ref, image_ref):
    n_row, n_col = sizes
    ncv = blocks_ref.shape[1] // 2
    my_row, my_col = lax.axis_index("row"), lax.axis_index("col")
    me = my_row * n_col + my_col
    first, second = table_ref[:, 0, :], table_ref[:, 1, :]
    other = jnp.where(first == me, second, jnp.where(second == me, first, -1))
    words = []
    for start in range(0, n_row * n_col, 16):
        bit = jnp.zeros(other.shape, jnp.float32)
        for b in range(16):
            bit = jnp.where(other == start + b, float(1 << b), bit)
        words.append(jnp.sum(bit).astype(jnp.int32))
    lane_col = my_col ^ 1 if part in ("core", "far") else my_col

    def visit(step, _):
        shift = step // n_row + 1 if part in ("across", "far") else 0
        from_row = (my_row - step % n_row + n_row) % n_row
        from_col = (lane_col - 2 * shift + 2 * n_col) % n_col
        block = from_row * n_col + from_col
        word = words[0]
        for w in range(1, len(words)):
            word = jnp.where(block // 16 == w, words[w], word)

        @pl.when(((word >> (block % 16)) & 1) == 1)
        def _():
            image_ref[...] += tile_image(
                left_ref, blocks_ref[step, :ncv, :], blocks_ref[step, ncv:, :]
            )

        return 0

    lax.fori_loop(1 if part == "line" else 0, blocks_ref.shape[0], visit, 0)


def part_kernel(part, sizes, table_ref, left_ref, blocks_ref, before_ref, image_ref):
    image_ref[...] = before_ref[...]
    add_blocks(part, sizes, table_ref, left_ref, blocks_ref, image_ref)


def last_kernel(
    sizes, table_ref, left_ref, blocks_ref, before_ref, vectors_ref, degrees_ref,
    applied_ref, gram_ref, image_ref,
):
    image_ref[...] = before_ref[...]
    add_blocks("far", sizes, table_ref, left_ref, blocks_ref, image_ref)
    n = vectors_ref.shape[0]
    applied = image_ref[...].T * lax.rsqrt(degrees_ref[...])[None, :]
    applied_ref[...] = applied
    both = jnp.concatenate([applied, vectors_ref[...].astype(jnp.float32)], axis=0)
    gram = lax.dot_general(
        both, both, NT, precision=lax.Precision.HIGHEST, preferred_element_type=jnp.float32
    )
    wide = jnp.concatenate(
        [gram[:n, :n], gram[n:, :], jnp.zeros((n, n), jnp.float32)], axis=1
    )
    gram_ref[...] = jnp.concatenate([wide[: n // 2, :], wide[n // 2 :, :]], axis=1)


def inverse_factors(grams):
    n = grams[0].shape[0]
    half = 64
    tiles = range(n // 8)
    shape = (8, 2 * half)
    row = lax.broadcasted_iota(jnp.int32, shape, 0)
    lane = lax.broadcasted_iota(jnp.int32, shape, 1)
    columns = [
        [
            jnp.where(
                lane < half,
                jnp.broadcast_to(grams[0][8 * t : 8 * t + 8, j : j + 1], shape),
                jnp.broadcast_to(grams[1][8 * t : 8 * t + 8, j : j + 1], shape),
            )
            for t in tiles
        ]
        for j in range(n)
    ]
    right = [jnp.where(lane % half == row + 8 * t, 1.0, 0.0) for t in tiles]
    pivots = [jnp.ones(shape, jnp.float32) for t in tiles]
    for k in range(n):
        top, at = k // 8, k % 8
        pivot = columns[k][top][at : at + 1, :]
        pivots[top] = jnp.where(row == at, pivot, pivots[top])
        if k == n - 1:
            break
        scale = 1.0 / pivot
        factor = {t: columns[k][t] * scale for t in tiles if t >= top}
        factor[top] = jnp.where(row > at, factor[top], 0.0)
        for column in columns[k + 1 :] + [right]:
            line = column[top][at : at + 1, :]
            for t in factor:
                column[t] = column[t] - factor[t] * line
    result = jnp.concatenate([r * lax.rsqrt(p) for r, p in zip(right, pivots)], axis=0)
    return result[:, :n], result[:, half : half + n]


def finish_kernel(total_frames, gram_ref, applied_ref, basis_ref, ritz_ref):
    tile = gram_ref[...]
    n = applied_ref.shape[0]
    gram = jnp.concatenate([tile[:, : 4 * n], tile[:, 4 * n :]], axis=0)
    exact = functools.partial(
        lax.dot_general, precision=lax.Precision.HIGHEST, preferred_element_type=jnp.float32
    )
    plain = (((1,), (0,)), ((), ()))
    image_inverse, vector_inverse = inverse_factors([gram[:, :n], gram[:, 2 * n : 3 * n]])
    basis_ref[...] = exact(image_inverse * math.sqrt(total_frames), applied_ref[...], plain)
    half = exact(vector_inverse, gram[:, n : 2 * n], plain)
    ritz_ref[...] = exact(half, vector_inverse, NT)


def shifted(x, axis, step):
    size = lax.axis_size(axis)
    return lax.ppermute(x, axis, [(i, (i + step) % size) for i in range(size)])


def paired(x, axis, bit):
    return lax.ppermute(x, axis, [(i, i ^ bit) for i in range(lax.axis_size(axis))])


def summed(x, axis):
    bit = 1
    while bit < lax.axis_size(axis):
        x = x + paired(x, axis, bit)
        bit *= 2
    return x


def per_device(frames, vectors, degrees, tile_table):
    ncv, rows = frames.shape
    nvec = vectors.shape[0]
    n_row, n_col = lax.axis_size("row"), lax.axis_size("col")
    devices = n_row * n_col
    sizes = (n_row, n_col)
    vmem = pl.BlockSpec(memory_space=pltpu.VMEM)

    def call(kernel, name, outs, *args, limit=16, tiles=0, where=vmem, **keywords):
        shapes = [jax.ShapeDtypeStruct(*out) for out in outs]
        keywords["cost_estimate"] = pl.CostEstimate(
            flops=tiles * rows * rows * 2 * (4 * ncv + nvec),
            transcendentals=tiles * rows * rows,
            bytes_accessed=sum(a.size * a.dtype.itemsize for a in args),
        )
        return pl.pallas_call(
            kernel,
            out_shape=shapes,
            in_specs=[where] * len(args),
            out_specs=[vmem] * len(outs),
            compiler_params=pltpu.CompilerParams(vmem_limit_bytes=limit * MIB),
            name=name,
            **keywords,
        )(*args)

    table = tile_table.transpose(1, 2, 0)
    image_type = ((rows, nvec), jnp.float32)

    (packed,) = call(
        pack_kernel,
        "pack",
        [((ncv + nvec, rows), jnp.bfloat16)],
        *(pltpu.with_memory_space_constraint(x, pltpu.HBM) for x in (frames, vectors, degrees)),
        where=pl.BlockSpec(memory_space=pltpu.HBM),
        scratch_shapes=[
            pltpu.VMEM(vectors.shape, vectors.dtype),
            pltpu.VMEM(degrees.shape, degrees.dtype),
            pltpu.SemaphoreType.DMA((3,)),
        ],
    )
    line = jnp.stack([packed] + [shifted(packed, "row", s) for s in range(1, n_row)])
    left, image = call(own_kernel, "own", [((rows, 3 * ncv + 16), jnp.bfloat16), image_type], packed, tiles=1)

    def add(part, blocks, image):
        (image,) = call(
            functools.partial(part_kernel, part, sizes),
            "add_" + part,
            [image_type],
            table,
            left,
            blocks,
            image,
            tiles=blocks.shape[0] // 2,
            input_output_aliases={3: 0},
        )
        return image

    line, image = lax.optimization_barrier((line, image))
    across = [shifted(line, "col", 2 * t) for t in range(1, n_col // 2)]
    across = across[0] if len(across) == 1 else jnp.concatenate(across)
    core = paired(line, "col", 1)
    image = add("line", line, image)
    image = add("core", core, image)
    across, image = lax.optimization_barrier((across, image))
    far = paired(across, "col", 1)
    image = add("across", across, image)
    applied, gram = call(
        functools.partial(last_kernel, sizes),
        "add_far",
        [((nvec, rows), jnp.float32), ((nvec // 2, 8 * nvec), jnp.float32)],
        table,
        left,
        far,
        image,
        vectors,
        degrees,
        tiles=far.shape[0] // 2,
        scratch_shapes=[pltpu.VMEM(*image_type)],
    )
    gram = summed(summed(gram, "col"), "row")
    basis, ritz = call(
        functools.partial(finish_kernel, rows * devices),
        "finish",
        [((nvec, rows), jnp.float32), ((nvec, nvec), jnp.float32)],
        gram,
        applied,
    )
    return (basis, ritz)


def solution(mesh):
    split = P(None, ("grp", "row", "col"))
    return jax.shard_map(
        per_device,
        mesh=mesh,
        in_specs=(split, split, P(("grp", "row", "col")), P()),
        out_specs=(split, P("grp", None)),
        check_vma=False,
    )
```

```python
import functools
import math

import jax
import jax.numpy as jnp
from jax import lax
from jax.experimental import pallas as pl
from jax.experimental.pallas import tpu as pltpu
from jax.sharding import PartitionSpec as P

unit = -math.log2(math.e) / 4.0

NT = (((1,), (1,)), ((), ()))
MIB = 1024 * 1024


def split3(x):
    high = x.astype(jnp.bfloat16).astype(jnp.float32)
    rest = x - high
    mid = rest.astype(jnp.bfloat16).astype(jnp.float32)
    low = (rest - mid).astype(jnp.bfloat16).astype(jnp.float32)
    return high, mid, low


def pack_kernel(frames_ref, vectors_ref, degrees_ref, out_ref, raw_ref, degree_ref, sems):
    ncv = frames_ref.shape[0]
    copies = [
        pltpu.make_async_copy(vectors_ref, raw_ref, sems.at[0]),
        pltpu.make_async_copy(degrees_ref, degree_ref, sems.at[1]),
        pltpu.make_async_copy(frames_ref, out_ref.at[pl.ds(0, ncv)], sems.at[2]),
    ]
    for copy in copies:
        copy.start()
    copies[0].wait()
    copies[1].wait()
    root = lax.rsqrt(degree_ref[...])[None, :]
    out_ref[ncv:, :] = (raw_ref[...].astype(jnp.float32) * root).astype(jnp.bfloat16)
    copies[2].wait()


def edge_rows(square, ones_first):
    high, mid, low = split3(square * unit)
    row = lax.broadcasted_iota(jnp.int32, (16, square.shape[1]), 0)
    base = 3 if ones_first else 0
    ones_at = 0 if ones_first else 3
    block = jnp.where((row >= ones_at) & (row < ones_at + 3), 1.0, 0.0)
    block = jnp.where(row == base, high, block)
    block = jnp.where(row == base + 1, mid, block)
    return jnp.where(row == base + 2, low, block)


def own_side(own):
    own = own.astype(jnp.float32)
    high, mid, low = split3(own * (-2.0 * unit))
    edge = edge_rows(jnp.sum(own * own, axis=0, keepdims=True), True)
    return jnp.concatenate([high, mid, low, edge], axis=0).T.astype(jnp.bfloat16)


def tile_image(left_ref, blocks):
    both = blocks[0] if len(blocks) == 1 else jnp.concatenate(blocks, axis=1)
    ncv = both.shape[0] // 2
    x, v = both[:ncv, :], both[ncv:, :]
    wide = x.astype(jnp.float32)
    edge = edge_rows(jnp.sum(wide * wide, axis=0, keepdims=True), False).astype(jnp.bfloat16)
    right = jnp.concatenate([x, x, x, edge], axis=0)
    power = jnp.dot(left_ref[...], right, preferred_element_type=jnp.float32)
    kern = jnp.exp2(power).astype(jnp.bfloat16)
    return lax.dot_general(kern, v, NT, preferred_element_type=jnp.float32)


def own_kernel(packed_ref, left_ref, image_ref):
    left_ref[...] = own_side(packed_ref[: packed_ref.shape[0] // 2, :])
    image_ref[...] = tile_image(left_ref, [packed_ref[...]])


def add_blocks(places, sizes, table_ref, left_ref, blocks_ref, image_ref, list_ref):
    n_row, n_col = sizes
    my_row, my_col = lax.axis_index("row"), lax.axis_index("col")
    me = my_row * n_col + my_col
    first, second = table_ref[:, 0, :], table_ref[:, 1, :]
    other = jnp.where(first == me, second, jnp.where(second == me, first, -1))
    words = []
    for start in range(0, n_row * n_col, 16):
        bit = jnp.zeros(other.shape, jnp.float32)
        for b in range(16):
            bit = jnp.where(other == start + b, float(1 << b), bit)
        words.append(jnp.sum(bit).astype(jnp.int32))

    count = jnp.int32(0)
    for step, (rows_back, chips_back, swap) in enumerate(places):
        from_row = (my_row + n_row - rows_back) % n_row
        from_col = ((my_col ^ swap) + n_col - 2 * chips_back) % n_col
        block = from_row * n_col + from_col
        word = words[0]
        for w in range(1, len(words)):
            word = jnp.where(block // 16 == w, words[w], word)
        list_ref[count] = step
        count += (word >> (block % 16)) & 1

    def visit(pair, _):
        blocks = [blocks_ref[list_ref[2 * pair]], blocks_ref[list_ref[2 * pair + 1]]]
        image_ref[...] += tile_image(left_ref, blocks)
        return 0

    lax.fori_loop(0, count // 2, visit, 0)

    @pl.when(count % 2 == 1)
    def _():
        image_ref[...] += tile_image(left_ref, [blocks_ref[list_ref[count - 1]]])


def part_kernel(places, sizes, table_ref, left_ref, blocks_ref, before_ref, image_ref, list_ref):
    image_ref[...] = before_ref[...]
    add_blocks(places, sizes, table_ref, left_ref, blocks_ref, image_ref, list_ref)


def last_kernel(
    places, sizes, table_ref, left_ref, blocks_ref, before_ref, vectors_ref, degrees_ref,
    applied_ref, gram_ref, image_ref, list_ref,
):
    image_ref[...] = before_ref[...]
    add_blocks(places, sizes, table_ref, left_ref, blocks_ref, image_ref, list_ref)
    n = vectors_ref.shape[0]
    applied = image_ref[...].T * lax.rsqrt(degrees_ref[...])[None, :]
    applied_ref[...] = applied
    both = jnp.concatenate([applied, vectors_ref[...].astype(jnp.float32)], axis=0)
    gram = lax.dot_general(
        both, both, NT, precision=lax.Precision.HIGHEST, preferred_element_type=jnp.float32
    )
    wide = jnp.concatenate(
        [gram[:n, :n], gram[n:, :], jnp.zeros((n, n), jnp.float32)], axis=1
    )
    tile = jnp.concatenate([wide[: n // 2, :], wide[n // 2 :, :]], axis=1)
    for device in range(gram_ref.shape[0]):
        gram_ref[device] = tile


def inverse_factors(grams):
    n = grams[0].shape[0]
    half = 64
    tiles = range(n // 8)
    shape = (8, 2 * half)
    row = lax.broadcasted_iota(jnp.int32, shape, 0)
    lane = lax.broadcasted_iota(jnp.int32, shape, 1)
    columns = [
        [
            jnp.where(
                lane < half,
                jnp.broadcast_to(grams[0][8 * t : 8 * t + 8, j : j + 1], shape),
                jnp.broadcast_to(grams[1][8 * t : 8 * t + 8, j : j + 1], shape),
            )
            for t in tiles
        ]
        for j in range(n)
    ]
    right = [jnp.where(lane % half == row + 8 * t, 1.0, 0.0) for t in tiles]
    pivots = [jnp.ones(shape, jnp.float32) for t in tiles]
    for k in range(n):
        top, at = k // 8, k % 8
        pivot = columns[k][top][at : at + 1, :]
        pivots[top] = jnp.where(row == at, pivot, pivots[top])
        if k == n - 1:
            break
        scale = 1.0 / pivot
        factor = {t: columns[k][t] * scale for t in tiles if t >= top}
        factor[top] = jnp.where(row > at, factor[top], 0.0)
        for column in columns[k + 1 :] + [right]:
            line = column[top][at : at + 1, :]
            for t in factor:
                column[t] = column[t] - factor[t] * line
    result = jnp.concatenate([r * lax.rsqrt(p) for r, p in zip(right, pivots)], axis=0)
    return result[:, :n], result[:, half : half + n]


def finish_kernel(total_frames, grams_ref, applied_ref, basis_ref, ritz_ref):
    tile = grams_ref[0]
    for device in range(1, grams_ref.shape[0]):
        tile += grams_ref[device]
    n = applied_ref.shape[0]
    gram = jnp.concatenate([tile[:, : 4 * n], tile[:, 4 * n :]], axis=0)
    exact = functools.partial(
        lax.dot_general, precision=lax.Precision.HIGHEST, preferred_element_type=jnp.float32
    )
    plain = (((1,), (0,)), ((), ()))
    image_inverse, vector_inverse = inverse_factors([gram[:, :n], gram[:, 2 * n : 3 * n]])
    basis_ref[...] = exact(image_inverse * math.sqrt(total_frames), applied_ref[...], plain)
    half = exact(vector_inverse, gram[:, n : 2 * n], plain)
    ritz_ref[...] = exact(half, vector_inverse, NT)


def shifted(x, axis, step):
    size = lax.axis_size(axis)
    return lax.ppermute(x, axis, [(i, (i + step) % size) for i in range(size)])


def swapped(x):
    return lax.ppermute(x, "col", [(i, i ^ 1) for i in range(lax.axis_size("col"))])


def per_device(frames, vectors, degrees, tile_table):
    ncv, rows = frames.shape
    nvec = vectors.shape[0]
    n_row, n_col = lax.axis_size("row"), lax.axis_size("col")
    devices = n_row * n_col
    sizes = (n_row, n_col)
    vmem = pl.BlockSpec(memory_space=pltpu.VMEM)

    def call(kernel, name, outs, *args, limit=16, tiles=0, where=vmem, **keywords):
        shapes = [jax.ShapeDtypeStruct(*out) for out in outs]
        keywords["cost_estimate"] = pl.CostEstimate(
            flops=tiles * rows * rows * 2 * (4 * ncv + nvec),
            transcendentals=tiles * rows * rows,
            bytes_accessed=sum(a.size * a.dtype.itemsize for a in args),
        )
        return pl.pallas_call(
            kernel,
            out_shape=shapes,
            in_specs=[where] * len(args),
            out_specs=[vmem] * len(outs),
            compiler_params=pltpu.CompilerParams(vmem_limit_bytes=limit * MIB),
            name=name,
            **keywords,
        )(*args)

    table = tile_table.transpose(1, 2, 0)
    image_type = ((rows, nvec), jnp.float32)

    (packed,) = call(
        pack_kernel,
        "pack",
        [((ncv + nvec, rows), jnp.bfloat16)],
        *(pltpu.with_memory_space_constraint(x, pltpu.HBM) for x in (frames, vectors, degrees)),
        where=pl.BlockSpec(memory_space=pltpu.HBM),
        scratch_shapes=[
            pltpu.VMEM(vectors.shape, vectors.dtype),
            pltpu.VMEM(degrees.shape, degrees.dtype),
            pltpu.SemaphoreType.DMA((3,)),
        ],
    )
    row_blocks = [shifted(packed, "row", s) for s in range(1, n_row)]
    chip_blocks = [shifted(packed, "col", 2 * t) for t in range(1, n_col // 2)]
    left, image = call(own_kernel, "own", [((rows, 3 * ncv + 16), jnp.bfloat16), image_type], packed, tiles=1)

    def add(name, places, blocks, image):
        (image,) = call(
            functools.partial(part_kernel, places, sizes),
            name,
            [image_type],
            table,
            left,
            blocks,
            image,
            tiles=len(places) // 2,
            input_output_aliases={3: 0},
            scratch_shapes=[pltpu.SMEM((len(places) + 1,), jnp.int32)],
        )
        return image

    near = jnp.stack(row_blocks + chip_blocks + [packed])
    near, image = lax.optimization_barrier((near, image))
    across = [shifted(near[: n_row - 1], "col", 2 * t) for t in range(1, n_col // 2)]
    across = across[0] if len(across) == 1 else jnp.concatenate(across)
    near_places = [(s, 0, 0) for s in range(1, n_row)] + [(0, t, 0) for t in range(1, n_col // 2)]
    across_places = [(s, t, 0) for t in range(1, n_col // 2) for s in range(1, n_row)]
    image = add("add_near", near_places, near, image)
    core = swapped(near)
    image = add("add_core", [(s, t, 1) for s, t, _ in near_places + [(0, 0, 0)]], core, image)
    across, image = lax.optimization_barrier((across, image))
    far = swapped(across)
    image = add("add_across", across_places, across, image)
    applied, gram = call(
        functools.partial(last_kernel, [(s, t, 1) for s, t, _ in across_places], sizes),
        "add_far",
        [((nvec, rows), jnp.float32), ((devices, nvec // 2, 8 * nvec), jnp.float32)],
        table,
        left,
        far,
        image,
        vectors,
        degrees,
        tiles=len(across_places) // 2,
        scratch_shapes=[
            pltpu.VMEM(*image_type),
            pltpu.SMEM((len(across_places) + 1,), jnp.int32),
        ],
    )
    grams = lax.all_to_all(gram, ("row", "col"), 0, 0)
    basis, ritz = call(
        functools.partial(finish_kernel, rows * devices),
        "finish",
        [((nvec, rows), jnp.float32), ((nvec, nvec), jnp.float32)],
        grams,
        applied,
    )
    return (basis, ritz)


def solution(mesh):
    split = P(None, ("grp", "row", "col"))
    return jax.shard_map(
        per_device,
        mesh=mesh,
        in_specs=(split, split, P(("grp", "row", "col")), P()),
        out_specs=(split, P("grp", None)),
        check_vma=False,
    )
```

```python
import functools
import math

import jax
import jax.numpy as jnp
from jax import lax
from jax.experimental import pallas as pl
from jax.experimental.pallas import tpu as pltpu
from jax.sharding import PartitionSpec as P

unit = -math.log2(math.e) / 4.0

NT = (((1,), (1,)), ((), ()))
MIB = 1024 * 1024


def split3(x):
    high = x.astype(jnp.bfloat16).astype(jnp.float32)
    rest = x - high
    mid = rest.astype(jnp.bfloat16).astype(jnp.float32)
    low = (rest - mid).astype(jnp.bfloat16).astype(jnp.float32)
    return high, mid, low


def pack_kernel(frames_ref, vectors_ref, degrees_ref, out_ref, raw_ref, degree_ref, sems):
    ncv = frames_ref.shape[0]
    copies = [
        pltpu.make_async_copy(vectors_ref, raw_ref, sems.at[0]),
        pltpu.make_async_copy(degrees_ref, degree_ref, sems.at[1]),
        pltpu.make_async_copy(frames_ref, out_ref.at[pl.ds(0, ncv)], sems.at[2]),
    ]
    for copy in copies:
        copy.start()
    copies[0].wait()
    copies[1].wait()
    root = lax.rsqrt(degree_ref[...])[None, :]
    out_ref[ncv:, :] = (raw_ref[...].astype(jnp.float32) * root).astype(jnp.bfloat16)
    copies[2].wait()


def edge_rows(square, ones_first):
    high, mid, low = split3(square * unit)
    row = lax.broadcasted_iota(jnp.int32, (16, square.shape[1]), 0)
    base = 3 if ones_first else 0
    ones_at = 0 if ones_first else 3
    block = jnp.where((row >= ones_at) & (row < ones_at + 3), 1.0, 0.0)
    block = jnp.where(row == base, high, block)
    block = jnp.where(row == base + 1, mid, block)
    return jnp.where(row == base + 2, low, block)


def own_side(own):
    own = own.astype(jnp.float32)
    high, mid, low = split3(own * (-2.0 * unit))
    edge = edge_rows(jnp.sum(own * own, axis=0, keepdims=True), True)
    return jnp.concatenate([high, mid, low, edge], axis=0).T.astype(jnp.bfloat16)


def tile_image(left_ref, blocks):
    both = blocks[0] if len(blocks) == 1 else jnp.concatenate(blocks, axis=1)
    ncv = both.shape[0] // 2
    x, v = both[:ncv, :], both[ncv:, :]
    wide = x.astype(jnp.float32)
    edge = edge_rows(jnp.sum(wide * wide, axis=0, keepdims=True), False).astype(jnp.bfloat16)
    right = jnp.concatenate([x, x, x, edge], axis=0)
    power = jnp.dot(left_ref[...], right, preferred_element_type=jnp.float32)
    kern = jnp.exp2(power).astype(jnp.bfloat16)
    return lax.dot_general(kern, v, NT, preferred_element_type=jnp.float32)


def own_kernel(packed_ref, left_ref, image_ref):
    left_ref[...] = own_side(packed_ref[: packed_ref.shape[0] // 2, :])
    image_ref[...] = tile_image(left_ref, [packed_ref[...]])


def add_blocks(swap, places, sizes, table_ref, left_ref, blocks_ref, image_ref, list_ref):
    n_row, n_col = sizes
    my_row, my_col = lax.axis_index("row"), lax.axis_index("col")
    me = my_row * n_col + my_col
    first, second = table_ref[:, 0, :], table_ref[:, 1, :]
    other = jnp.where(first == me, second, jnp.where(second == me, first, -1))
    words = []
    for start in range(0, n_row * n_col, 16):
        bit = jnp.zeros(other.shape, jnp.float32)
        for b in range(16):
            bit = jnp.where(other == start + b, float(1 << b), bit)
        words.append(jnp.sum(bit).astype(jnp.int32))

    count = jnp.int32(0)
    for step, (row_bits, chip_bits) in enumerate(places):
        block = (my_row ^ row_bits) * n_col + (my_col ^ (2 * chip_bits + swap))
        word = words[0]
        for w in range(1, len(words)):
            word = jnp.where(block // 16 == w, words[w], word)
        list_ref[count] = step
        count += (word >> (block % 16)) & 1

    def visit(pair, _):
        blocks = [blocks_ref[list_ref[2 * pair]], blocks_ref[list_ref[2 * pair + 1]]]
        image_ref[...] += tile_image(left_ref, blocks)
        return 0

    lax.fori_loop(0, count // 2, visit, 0)

    @pl.when(count % 2 == 1)
    def _():
        image_ref[...] += tile_image(left_ref, [blocks_ref[list_ref[count - 1]]])


def part_kernel(
    swap, places, sizes, table_ref, left_ref, blocks_ref, before_ref, image_ref, list_ref
):
    image_ref[...] = before_ref[...]
    add_blocks(swap, places, sizes, table_ref, left_ref, blocks_ref, image_ref, list_ref)


def last_kernel(
    swap, places, sizes, table_ref, left_ref, blocks_ref, before_ref, vectors_ref, degrees_ref,
    applied_ref, gram_ref, image_ref, list_ref,
):
    image_ref[...] = before_ref[...]
    add_blocks(swap, places, sizes, table_ref, left_ref, blocks_ref, image_ref, list_ref)
    n = vectors_ref.shape[0]
    applied = image_ref[...].T * lax.rsqrt(degrees_ref[...])[None, :]
    applied_ref[...] = applied
    both = jnp.concatenate([applied, vectors_ref[...].astype(jnp.float32)], axis=0)
    gram = lax.dot_general(
        both, both, NT, precision=lax.Precision.HIGHEST, preferred_element_type=jnp.float32
    )
    wide = jnp.concatenate(
        [gram[:n, :n], gram[n:, :], jnp.zeros((n, n), jnp.float32)], axis=1
    )
    tile = jnp.concatenate([wide[: n // 2, :], wide[n // 2 :, :]], axis=1)
    for device in range(gram_ref.shape[0]):
        gram_ref[device] = tile


def inverse_factors(grams):
    n = grams[0].shape[0]
    half = 64
    tiles = range(n // 8)
    shape = (8, 2 * half)
    row = lax.broadcasted_iota(jnp.int32, shape, 0)
    lane = lax.broadcasted_iota(jnp.int32, shape, 1)
    columns = [
        [
            jnp.where(
                lane < half,
                jnp.broadcast_to(grams[0][8 * t : 8 * t + 8, j : j + 1], shape),
                jnp.broadcast_to(grams[1][8 * t : 8 * t + 8, j : j + 1], shape),
            )
            for t in tiles
        ]
        for j in range(n)
    ]
    right = [jnp.where(lane % half == row + 8 * t, 1.0, 0.0) for t in tiles]
    pivots = [jnp.ones(shape, jnp.float32) for t in tiles]
    for k in range(n):
        top, at = k // 8, k % 8
        pivot = columns[k][top][at : at + 1, :]
        pivots[top] = jnp.where(row == at, pivot, pivots[top])
        if k == n - 1:
            break
        scale = 1.0 / pivot
        factor = {t: columns[k][t] * scale for t in tiles if t >= top}
        factor[top] = jnp.where(row > at, factor[top], 0.0)
        for column in columns[k + 1 :] + [right]:
            line = column[top][at : at + 1, :]
            for t in factor:
                column[t] = column[t] - factor[t] * line
    result = jnp.concatenate([r * lax.rsqrt(p) for r, p in zip(right, pivots)], axis=0)
    return result[:, :n], result[:, half : half + n]


def finish_kernel(total_frames, grams_ref, applied_ref, basis_ref, ritz_ref):
    tile = grams_ref[0]
    for device in range(1, grams_ref.shape[0]):
        tile += grams_ref[device]
    n = applied_ref.shape[0]
    gram = jnp.concatenate([tile[:, : 4 * n], tile[:, 4 * n :]], axis=0)
    exact = functools.partial(
        lax.dot_general, precision=lax.Precision.HIGHEST, preferred_element_type=jnp.float32
    )
    plain = (((1,), (0,)), ((), ()))
    image_inverse, vector_inverse = inverse_factors([gram[:, :n], gram[:, 2 * n : 3 * n]])
    basis_ref[...] = exact(image_inverse * math.sqrt(total_frames), applied_ref[...], plain)
    half = exact(vector_inverse, gram[:, n : 2 * n], plain)
    ritz_ref[...] = exact(half, vector_inverse, NT)


def sent(x, offset):
    rows, chips = offset
    axis, bits = ("row", rows) if rows else ("col", 2 * chips)
    return lax.ppermute(x, axis, [(i, i ^ bits) for i in range(lax.axis_size(axis))])


def exchange_plan(n_row, n_chip):
    if (n_row, n_chip) == (4, 2):
        direct = [(2, 0), (1, 0), (0, 1)]
        return direct, [((0, 1), [(1, 0), (2, 0)]), ((3, 0), [(0, 1)]), ((1, 0), [(2, 0)])]
    lines = [(r, 0) for r in range(1, n_row)]
    chips = [(0, c) for c in range(1, n_chip)]
    return lines + chips, [(chip, lines) for chip in chips]


def swapped(x):
    return lax.ppermute(x, "col", [(i, i ^ 1) for i in range(lax.axis_size("col"))])


def per_device(frames, vectors, degrees, tile_table):
    ncv, rows = frames.shape
    nvec = vectors.shape[0]
    n_row, n_col = lax.axis_size("row"), lax.axis_size("col")
    devices = n_row * n_col
    sizes = (n_row, n_col)
    vmem = pl.BlockSpec(memory_space=pltpu.VMEM)

    def call(kernel, name, outs, *args, limit=16, tiles=0, where=vmem, **keywords):
        shapes = [jax.ShapeDtypeStruct(*out) for out in outs]
        keywords["cost_estimate"] = pl.CostEstimate(
            flops=tiles * rows * rows * 2 * (4 * ncv + nvec),
            transcendentals=tiles * rows * rows,
            bytes_accessed=sum(a.size * a.dtype.itemsize for a in args),
        )
        return pl.pallas_call(
            kernel,
            out_shape=shapes,
            in_specs=[where] * len(args),
            out_specs=[vmem] * len(outs),
            compiler_params=pltpu.CompilerParams(vmem_limit_bytes=limit * MIB),
            name=name,
            **keywords,
        )(*args)

    table = tile_table.transpose(1, 2, 0)
    image_type = ((rows, nvec), jnp.float32)

    (packed,) = call(
        pack_kernel,
        "pack",
        [((ncv + nvec, rows), jnp.bfloat16)],
        *(pltpu.with_memory_space_constraint(x, pltpu.HBM) for x in (frames, vectors, degrees)),
        where=pl.BlockSpec(memory_space=pltpu.HBM),
        scratch_shapes=[
            pltpu.VMEM(vectors.shape, vectors.dtype),
            pltpu.VMEM(degrees.shape, degrees.dtype),
            pltpu.SemaphoreType.DMA((3,)),
        ],
    )
    direct, forwards = exchange_plan(n_row, n_col // 2)
    held = {offset: sent(packed, offset) for offset in direct}
    left, image = call(
        own_kernel, "own", [((rows, 3 * ncv + 16), jnp.bfloat16), image_type], packed, tiles=1
    )

    def add(name, swap, places, blocks, image):
        (image,) = call(
            functools.partial(part_kernel, swap, places, sizes),
            name,
            [image_type],
            table,
            left,
            blocks,
            image,
            tiles=len(places) // 2,
            input_output_aliases={3: 0},
            scratch_shapes=[pltpu.SMEM((len(places) + 1,), jnp.int32)],
        )
        return image

    near_places = direct + [(0, 0)]
    near = jnp.stack([held[offset] for offset in direct] + [packed])
    near, image, held = lax.optimization_barrier((near, image, held))
    across_places = []
    across = []
    for hop, offsets in forwards:
        across.append(sent(jnp.stack([held[offset] for offset in offsets]), hop))
        across_places += [(r ^ hop[0], c ^ hop[1]) for r, c in offsets]
    core = swapped(near)
    image = add("add_near", 0, direct, near, image)
    image = add("add_core", 1, near_places, core, image)
    across, image = lax.optimization_barrier((across, image))
    across = jnp.concatenate(across)
    far = swapped(across)
    image = add("add_across", 0, across_places, across, image)
    applied, gram = call(
        functools.partial(last_kernel, 1, across_places, sizes),
        "add_far",
        [((nvec, rows), jnp.float32), ((devices, nvec // 2, 8 * nvec), jnp.float32)],
        table,
        left,
        far,
        image,
        vectors,
        degrees,
        tiles=len(across_places) // 2,
        scratch_shapes=[
            pltpu.VMEM(*image_type),
            pltpu.SMEM((len(across_places) + 1,), jnp.int32),
        ],
    )
    grams = lax.all_to_all(gram, ("row", "col"), 0, 0)
    basis, ritz = call(
        functools.partial(finish_kernel, rows * devices),
        "finish",
        [((nvec, rows), jnp.float32), ((nvec, nvec), jnp.float32)],
        grams,
        applied,
    )
    return (basis, ritz)


def solution(mesh):
    split = P(None, ("grp", "row", "col"))
    return jax.shard_map(
        per_device,
        mesh=mesh,
        in_specs=(split, split, P(("grp", "row", "col")), P()),
        out_specs=(split, P("grp", None)),
        check_vma=False,
    )
```

```python
import functools
import math

import jax
import jax.numpy as jnp
from jax import lax
from jax.experimental import pallas as pl
from jax.experimental.pallas import tpu as pltpu
from jax.sharding import PartitionSpec as P

unit = -math.log2(math.e) / 4.0

NT = (((1,), (1,)), ((), ()))
MIB = 1024 * 1024


def split3(x):
    high = x.astype(jnp.bfloat16).astype(jnp.float32)
    rest = x - high
    mid = rest.astype(jnp.bfloat16).astype(jnp.float32)
    low = (rest - mid).astype(jnp.bfloat16).astype(jnp.float32)
    return high, mid, low


def pack_kernel(frames_ref, vectors_ref, degrees_ref, out_ref, raw_ref, degree_ref, sems):
    ncv = frames_ref.shape[0]
    copies = [
        pltpu.make_async_copy(vectors_ref, raw_ref, sems.at[0]),
        pltpu.make_async_copy(degrees_ref, degree_ref, sems.at[1]),
        pltpu.make_async_copy(frames_ref, out_ref.at[pl.ds(0, ncv)], sems.at[2]),
    ]
    for copy in copies:
        copy.start()
    copies[0].wait()
    copies[1].wait()
    root = lax.rsqrt(degree_ref[...])[None, :]
    out_ref[ncv:, :] = (raw_ref[...].astype(jnp.float32) * root).astype(jnp.bfloat16)
    copies[2].wait()


def edge_rows(square, ones_first):
    high, mid, low = split3(square * unit)
    row = lax.broadcasted_iota(jnp.int32, (16, square.shape[1]), 0)
    base = 3 if ones_first else 0
    ones_at = 0 if ones_first else 3
    block = jnp.where((row >= ones_at) & (row < ones_at + 3), 1.0, 0.0)
    block = jnp.where(row == base, high, block)
    block = jnp.where(row == base + 1, mid, block)
    return jnp.where(row == base + 2, low, block)


def own_side(own):
    own = own.astype(jnp.float32)
    high, mid, low = split3(own * (-2.0 * unit))
    edge = edge_rows(jnp.sum(own * own, axis=0, keepdims=True), True)
    return jnp.concatenate([high, mid, low, edge], axis=0).T.astype(jnp.bfloat16)


def tile_image(left_ref, blocks):
    both = blocks[0] if len(blocks) == 1 else jnp.concatenate(blocks, axis=1)
    ncv = both.shape[0] // 2
    x, v = both[:ncv, :], both[ncv:, :]
    wide = x.astype(jnp.float32)
    edge = edge_rows(jnp.sum(wide * wide, axis=0, keepdims=True), False).astype(jnp.bfloat16)
    right = jnp.concatenate([x, x, x, edge], axis=0)
    power = jnp.dot(left_ref[...], right, preferred_element_type=jnp.float32)
    kern = jnp.exp2(power).astype(jnp.bfloat16)
    return lax.dot_general(kern, v, NT, preferred_element_type=jnp.float32)


def own_kernel(packed_ref, left_ref, image_ref):
    left_ref[...] = own_side(packed_ref[: packed_ref.shape[0] // 2, :])
    image_ref[...] = tile_image(left_ref, [packed_ref[...]])


def add_blocks(places, sizes, table_ref, left_ref, blocks_ref, image_ref, list_ref):
    n_row, n_col = sizes
    my_row, my_col = lax.axis_index("row"), lax.axis_index("col")
    me = my_row * n_col + my_col
    first, second = table_ref[:, 0, :], table_ref[:, 1, :]
    other = jnp.where(first == me, second, jnp.where(second == me, first, -1))
    words = []
    for start in range(0, n_row * n_col, 16):
        bit = jnp.zeros(other.shape, jnp.float32)
        for b in range(16):
            bit = jnp.where(other == start + b, float(1 << b), bit)
        words.append(jnp.sum(bit).astype(jnp.int32))

    count = jnp.int32(0)
    for step, ((row_bits, chip_bits), swap) in enumerate(places):
        block = (my_row ^ row_bits) * n_col + (my_col ^ (2 * chip_bits + swap))
        word = words[0]
        for w in range(1, len(words)):
            word = jnp.where(block // 16 == w, words[w], word)
        list_ref[count] = step
        count += (word >> (block % 16)) & 1

    def visit(pair, _):
        blocks = [blocks_ref[list_ref[2 * pair]], blocks_ref[list_ref[2 * pair + 1]]]
        image_ref[...] += tile_image(left_ref, blocks)
        return 0

    lax.fori_loop(0, count // 2, visit, 0)

    @pl.when(count % 2 == 1)
    def _():
        image_ref[...] += tile_image(left_ref, [blocks_ref[list_ref[count - 1]]])


def part_kernel(places, sizes, table_ref, left_ref, blocks_ref, before_ref, image_ref, list_ref):
    image_ref[...] = before_ref[...]
    add_blocks(places, sizes, table_ref, left_ref, blocks_ref, image_ref, list_ref)


def last_kernel(
    places, sizes, table_ref, left_ref, blocks_ref, before_ref, vectors_ref, degrees_ref,
    applied_ref, gram_ref, image_ref, list_ref,
):
    image_ref[...] = before_ref[...]
    add_blocks(places, sizes, table_ref, left_ref, blocks_ref, image_ref, list_ref)
    n = vectors_ref.shape[0]
    applied = image_ref[...].T * lax.rsqrt(degrees_ref[...])[None, :]
    applied_ref[...] = applied
    both = jnp.concatenate([applied, vectors_ref[...].astype(jnp.float32)], axis=0)
    gram = lax.dot_general(
        both, both, NT, precision=lax.Precision.HIGHEST, preferred_element_type=jnp.float32
    )
    wide = jnp.concatenate(
        [gram[:n, :n], gram[n:, :], jnp.zeros((n, n), jnp.float32)], axis=1
    )
    tile = jnp.concatenate([wide[: n // 2, :], wide[n // 2 :, :]], axis=1)
    for device in range(gram_ref.shape[0]):
        gram_ref[device] = tile


def inverse_factors(grams):
    n = grams[0].shape[0]
    half = 64
    tiles = range(n // 8)
    shape = (8, 2 * half)
    row = lax.broadcasted_iota(jnp.int32, shape, 0)
    lane = lax.broadcasted_iota(jnp.int32, shape, 1)
    columns = [
        [
            jnp.where(
                lane < half,
                jnp.broadcast_to(grams[0][8 * t : 8 * t + 8, j : j + 1], shape),
                jnp.broadcast_to(grams[1][8 * t : 8 * t + 8, j : j + 1], shape),
            )
            for t in tiles
        ]
        for j in range(n)
    ]
    right = [jnp.where(lane % half == row + 8 * t, 1.0, 0.0) for t in tiles]
    pivots = [jnp.ones(shape, jnp.float32) for t in tiles]
    for k in range(n):
        top, at = k // 8, k % 8
        pivot = columns[k][top][at : at + 1, :]
        pivots[top] = jnp.where(row == at, pivot, pivots[top])
        if k == n - 1:
            break
        scale = 1.0 / pivot
        factor = {t: columns[k][t] * scale for t in tiles if t >= top}
        factor[top] = jnp.where(row > at, factor[top], 0.0)
        for column in columns[k + 1 :] + [right]:
            line = column[top][at : at + 1, :]
            for t in factor:
                column[t] = column[t] - factor[t] * line
    result = jnp.concatenate([r * lax.rsqrt(p) for r, p in zip(right, pivots)], axis=0)
    return result[:, :n], result[:, half : half + n]


def finish_kernel(total_frames, grams_ref, applied_ref, basis_ref, ritz_ref):
    tile = grams_ref[0]
    for device in range(1, grams_ref.shape[0]):
        tile += grams_ref[device]
    n = applied_ref.shape[0]
    gram = jnp.concatenate([tile[:, : 4 * n], tile[:, 4 * n :]], axis=0)
    exact = functools.partial(
        lax.dot_general, precision=lax.Precision.HIGHEST, preferred_element_type=jnp.float32
    )
    plain = (((1,), (0,)), ((), ()))
    image_inverse, vector_inverse = inverse_factors([gram[:, :n], gram[:, 2 * n : 3 * n]])
    basis_ref[...] = exact(image_inverse * math.sqrt(total_frames), applied_ref[...], plain)
    half = exact(vector_inverse, gram[:, n : 2 * n], plain)
    ritz_ref[...] = exact(half, vector_inverse, NT)


def sent(x, offset):
    rows, chips = offset
    axis, bits = ("row", rows) if rows else ("col", 2 * chips)
    return lax.ppermute(x, axis, [(i, i ^ bits) for i in range(lax.axis_size(axis))])


def swapped(x):
    return lax.ppermute(x, "col", [(i, i ^ 1) for i in range(lax.axis_size("col"))])


def per_device(frames, vectors, degrees, tile_table):
    ncv, rows = frames.shape
    nvec = vectors.shape[0]
    n_row, n_col = lax.axis_size("row"), lax.axis_size("col")
    devices = n_row * n_col
    sizes = (n_row, n_col)
    vmem = pl.BlockSpec(memory_space=pltpu.VMEM)

    def call(kernel, name, outs, *args, limit=16, where=vmem, **keywords):
        shapes = [jax.ShapeDtypeStruct(*out) for out in outs]
        return pl.pallas_call(
            kernel,
            out_shape=shapes,
            in_specs=[where] * len(args),
            out_specs=[vmem] * len(outs),
            compiler_params=pltpu.CompilerParams(vmem_limit_bytes=limit * MIB),
            name=name,
            **keywords,
        )(*args)

    table = tile_table.transpose(1, 2, 0)
    image_type = ((rows, nvec), jnp.float32)

    (packed,) = call(
        pack_kernel,
        "pack",
        [((ncv + nvec, rows), jnp.bfloat16)],
        *(pltpu.with_memory_space_constraint(x, pltpu.HBM) for x in (frames, vectors, degrees)),
        where=pl.BlockSpec(memory_space=pltpu.HBM),
        scratch_shapes=[
            pltpu.VMEM(vectors.shape, vectors.dtype),
            pltpu.VMEM(degrees.shape, degrees.dtype),
            pltpu.SemaphoreType.DMA((3,)),
        ],
    )
    def start_image(packed):
        return call(
            own_kernel, "own", [((rows, 3 * ncv + 16), jnp.bfloat16), image_type], packed
        )

    def add(name, offsets, swap, blocks, image):
        places = [(offset, swap) for offset in offsets]
        (image,) = call(
            functools.partial(part_kernel, places, sizes),
            name,
            [image_type],
            table,
            left,
            blocks,
            image,
            input_output_aliases={3: 0},
            scratch_shapes=[pltpu.SMEM((len(places) + 1,), jnp.int32)],
        )
        return image

    n_chip = n_col // 2
    own, row_1, row_2, row_3, chip = (0, 0), (1, 0), (2, 0), (3, 0), (0, 1)
    if (n_row, n_chip) == (4, 2):
        from_row_2, from_row_1, from_chip = sent(packed, row_2), sent(packed, row_1), sent(packed, chip)
        left, image = start_image(packed)
        (from_row_1, from_chip), image = lax.optimization_barrier(((from_row_1, from_chip), image))
        chip_row_1 = sent(from_row_1, chip)
        image = add("add_near", [row_1, chip], 0, jnp.stack([from_row_1, from_chip]), image)
        from_row_2, image = lax.optimization_barrier((from_row_2, image))
        chip_row_2 = sent(from_row_2, chip)
        from_row_3 = sent(from_row_2, row_1)
        core = swapped(jnp.stack([packed, from_row_1, from_chip, from_row_2, chip_row_1]))
        image = add("add_next", [row_2, (1, 1)], 0, jnp.stack([from_row_2, chip_row_1]), image)
        chip_row_2, image = lax.optimization_barrier((chip_row_2, image))
        chip_row_3 = sent(chip_row_2, row_1)
        image = add("add_core", [own, row_1, chip, row_2, (1, 1)], 1, core, image)
        last = [from_row_3, chip_row_2, chip_row_3]
        last, image = lax.optimization_barrier((last, image))
        last, last_offsets = jnp.stack(last), [row_3, (2, 1), (3, 1)]
    else:
        rows_on = [(r, 0) for r in range(1, n_row)]
        chips_on = [(0, c) for c in range(1, n_chip)]
        near = jnp.stack([sent(packed, offset) for offset in rows_on + chips_on] + [packed])
        left, image = start_image(packed)
        near, image = lax.optimization_barrier((near, image))
        last = [sent(near[: n_row - 1], offset) for offset in chips_on]
        core = swapped(near)
        image = add("add_near", rows_on + chips_on, 0, near, image)
        image = add("add_core", rows_on + chips_on + [own], 1, core, image)
        last, image = lax.optimization_barrier((last, image))
        last = jnp.concatenate(last)
        last_offsets = [(r, c) for _, c in chips_on for r, _ in rows_on]
    far = swapped(last)
    image = add("add_last", last_offsets, 0, last, image)
    applied, gram = call(
        functools.partial(last_kernel, [(offset, 1) for offset in last_offsets], sizes),
        "add_far",
        [((nvec, rows), jnp.float32), ((devices, nvec // 2, 8 * nvec), jnp.float32)],
        table,
        left,
        far,
        image,
        vectors,
        degrees,
        scratch_shapes=[
            pltpu.VMEM(*image_type),
            pltpu.SMEM((len(last_offsets) + 1,), jnp.int32),
        ],
    )
    grams = lax.all_to_all(gram, ("row", "col"), 0, 0)
    basis, ritz = call(
        functools.partial(finish_kernel, rows * devices),
        "finish",
        [((nvec, rows), jnp.float32), ((nvec, nvec), jnp.float32)],
        grams,
        applied,
    )
    return (basis, ritz)


def solution(mesh):
    split = P(None, ("grp", "row", "col"))
    return jax.shard_map(
        per_device,
        mesh=mesh,
        in_specs=(split, split, P(("grp", "row", "col")), P()),
        out_specs=(split, P("grp", None)),
        check_vma=False,
    )
```

```python
import functools
import math

import jax
import jax.numpy as jnp
from jax import lax
from jax.experimental import pallas as pl
from jax.experimental.pallas import tpu as pltpu
from jax.sharding import PartitionSpec as P

unit = -math.log2(math.e) / 4.0

NT = (((1,), (1,)), ((), ()))
MIB = 1024 * 1024


def split3(x):
    high = x.astype(jnp.bfloat16).astype(jnp.float32)
    rest = x - high
    mid = rest.astype(jnp.bfloat16).astype(jnp.float32)
    low = (rest - mid).astype(jnp.bfloat16).astype(jnp.float32)
    return high, mid, low


def pack_kernel(frames_ref, vectors_ref, degrees_ref, out_ref, raw_ref, degree_ref, sems):
    ncv = frames_ref.shape[0]
    copies = [
        pltpu.make_async_copy(vectors_ref, raw_ref, sems.at[0]),
        pltpu.make_async_copy(degrees_ref, degree_ref, sems.at[1]),
        pltpu.make_async_copy(frames_ref, out_ref.at[pl.ds(0, ncv)], sems.at[2]),
    ]
    for copy in copies:
        copy.start()
    copies[0].wait()
    copies[1].wait()
    root = lax.rsqrt(degree_ref[...])[None, :]
    out_ref[ncv:, :] = (raw_ref[...].astype(jnp.float32) * root).astype(jnp.bfloat16)
    copies[2].wait()


def edge_rows(square, ones_first):
    high, mid, low = split3(square * unit)
    row = lax.broadcasted_iota(jnp.int32, (16, square.shape[1]), 0)
    base = 3 if ones_first else 0
    ones_at = 0 if ones_first else 3
    block = jnp.where((row >= ones_at) & (row < ones_at + 3), 1.0, 0.0)
    block = jnp.where(row == base, high, block)
    block = jnp.where(row == base + 1, mid, block)
    return jnp.where(row == base + 2, low, block)


def own_side(own):
    own = own.astype(jnp.float32)
    high, mid, low = split3(own * (-2.0 * unit))
    edge = edge_rows(jnp.sum(own * own, axis=0, keepdims=True), True)
    return jnp.concatenate([high, mid, low, edge], axis=0).T.astype(jnp.bfloat16)


def tile_image(left_ref, blocks):
    both = blocks[0] if len(blocks) == 1 else jnp.concatenate(blocks, axis=1)
    ncv = both.shape[0] // 2
    x, v = both[:ncv, :], both[ncv:, :]
    wide = x.astype(jnp.float32)
    edge = edge_rows(jnp.sum(wide * wide, axis=0, keepdims=True), False).astype(jnp.bfloat16)
    right = jnp.concatenate([x, x, x, edge], axis=0)
    power = jnp.dot(left_ref[...], right, preferred_element_type=jnp.float32)
    kern = jnp.exp2(power).astype(jnp.bfloat16)
    return lax.dot_general(kern, v, NT, preferred_element_type=jnp.float32)


def own_kernel(packed_ref, left_ref, image_ref):
    left_ref[...] = own_side(packed_ref[: packed_ref.shape[0] // 2, :])
    image_ref[...] = tile_image(left_ref, [packed_ref[...]])


def add_blocks(places, sizes, table_ref, left_ref, blocks_ref, image_ref, list_ref):
    n_row, n_col = sizes
    my_row, my_col = lax.axis_index("row"), lax.axis_index("col")
    me = my_row * n_col + my_col
    first, second = table_ref[:, 0, :], table_ref[:, 1, :]
    other = jnp.where(first == me, second, jnp.where(second == me, first, -1))
    words = []
    for start in range(0, n_row * n_col, 16):
        bit = jnp.zeros(other.shape, jnp.float32)
        for b in range(16):
            bit = jnp.where(other == start + b, float(1 << b), bit)
        words.append(jnp.sum(bit).astype(jnp.int32))

    count = jnp.int32(0)
    for step, ((row_bits, chip_bits), swap) in enumerate(places):
        block = (my_row ^ row_bits) * n_col + (my_col ^ (2 * chip_bits + swap))
        word = words[0]
        for w in range(1, len(words)):
            word = jnp.where(block // 16 == w, words[w], word)
        list_ref[count] = step
        count += (word >> (block % 16)) & 1

    def visit(pair, _):
        blocks = [blocks_ref[list_ref[2 * pair]], blocks_ref[list_ref[2 * pair + 1]]]
        image_ref[...] += tile_image(left_ref, blocks)
        return 0

    lax.fori_loop(0, count // 2, visit, 0)

    @pl.when(count % 2 == 1)
    def _():
        image_ref[...] += tile_image(left_ref, [blocks_ref[list_ref[count - 1]]])


def part_kernel(places, sizes, table_ref, left_ref, blocks_ref, before_ref, image_ref, list_ref):
    image_ref[...] = before_ref[...]
    add_blocks(places, sizes, table_ref, left_ref, blocks_ref, image_ref, list_ref)


def last_kernel(
    places, sizes, table_ref, left_ref, blocks_ref, before_ref, vectors_ref, degrees_ref,
    applied_ref, gram_ref, image_ref, list_ref,
):
    image_ref[...] = before_ref[...]
    add_blocks(places, sizes, table_ref, left_ref, blocks_ref, image_ref, list_ref)
    n = vectors_ref.shape[0]
    applied = image_ref[...].T * lax.rsqrt(degrees_ref[...])[None, :]
    applied_ref[...] = applied
    both = jnp.concatenate([applied, vectors_ref[...].astype(jnp.float32)], axis=0)
    gram = lax.dot_general(
        both, both, NT, precision=lax.Precision.HIGHEST, preferred_element_type=jnp.float32
    )
    wide = jnp.concatenate(
        [gram[:n, :n], gram[n:, :], jnp.zeros((n, n), jnp.float32)], axis=1
    )
    tile = jnp.concatenate([wide[: n // 2, :], wide[n // 2 :, :]], axis=1)
    for device in range(gram_ref.shape[0]):
        gram_ref[device] = tile


def inverse_factors(grams):
    n = grams[0].shape[0]
    half = 64
    tiles = range(n // 8)
    shape = (8, 2 * half)
    row = lax.broadcasted_iota(jnp.int32, shape, 0)
    lane = lax.broadcasted_iota(jnp.int32, shape, 1)
    columns = [
        [
            jnp.where(
                lane < half,
                jnp.broadcast_to(grams[0][8 * t : 8 * t + 8, j : j + 1], shape),
                jnp.broadcast_to(grams[1][8 * t : 8 * t + 8, j : j + 1], shape),
            )
            for t in tiles
        ]
        for j in range(n)
    ]
    right = [jnp.where(lane % half == row + 8 * t, 1.0, 0.0) for t in tiles]
    pivots = [jnp.ones(shape, jnp.float32) for t in tiles]
    for k in range(n):
        top, at = k // 8, k % 8
        pivot = columns[k][top][at : at + 1, :]
        pivots[top] = jnp.where(row == at, pivot, pivots[top])
        if k == n - 1:
            break
        scale = 1.0 / pivot
        factor = {t: columns[k][t] * scale for t in tiles if t >= top}
        factor[top] = jnp.where(row > at, factor[top], 0.0)
        for column in columns[k + 1 :] + [right]:
            line = column[top][at : at + 1, :]
            for t in factor:
                column[t] = column[t] - factor[t] * line
    result = jnp.concatenate([r * lax.rsqrt(p) for r, p in zip(right, pivots)], axis=0)
    return result[:, :n], result[:, half : half + n]


def finish_kernel(total_frames, grams_ref, applied_ref, basis_ref, ritz_ref):
    tile = grams_ref[0]
    for device in range(1, grams_ref.shape[0]):
        tile += grams_ref[device]
    n = applied_ref.shape[0]
    gram = jnp.concatenate([tile[:, : 4 * n], tile[:, 4 * n :]], axis=0)
    exact = functools.partial(
        lax.dot_general, precision=lax.Precision.HIGHEST, preferred_element_type=jnp.float32
    )
    plain = (((1,), (0,)), ((), ()))
    image_inverse, vector_inverse = inverse_factors([gram[:, :n], gram[:, 2 * n : 3 * n]])
    basis_ref[...] = exact(image_inverse * math.sqrt(total_frames), applied_ref[...], plain)
    half = exact(vector_inverse, gram[:, n : 2 * n], plain)
    ritz_ref[...] = exact(half, vector_inverse, NT)


def sent(x, offset):
    rows, chips = offset
    axis, bits = ("row", rows) if rows else ("col", 2 * chips)
    return lax.ppermute(x, axis, [(i, i ^ bits) for i in range(lax.axis_size(axis))])


def swapped(x):
    return lax.ppermute(x, "col", [(i, i ^ 1) for i in range(lax.axis_size("col"))])


def per_device(frames, vectors, degrees, tile_table):
    ncv, rows = frames.shape
    nvec = vectors.shape[0]
    n_row, n_col = lax.axis_size("row"), lax.axis_size("col")
    devices = n_row * n_col
    sizes = (n_row, n_col)
    vmem = pl.BlockSpec(memory_space=pltpu.VMEM)

    def call(kernel, name, outs, *args, limit=16, where=vmem, **keywords):
        shapes = [jax.ShapeDtypeStruct(*out) for out in outs]
        return pl.pallas_call(
            kernel,
            out_shape=shapes,
            in_specs=[where] * len(args),
            out_specs=[vmem] * len(outs),
            compiler_params=pltpu.CompilerParams(vmem_limit_bytes=limit * MIB),
            name=name,
            **keywords,
        )(*args)

    table = tile_table.transpose(1, 2, 0)
    image_type = ((rows, nvec), jnp.float32)

    (packed,) = call(
        pack_kernel,
        "pack",
        [((ncv + nvec, rows), jnp.bfloat16)],
        *(pltpu.with_memory_space_constraint(x, pltpu.HBM) for x in (frames, vectors, degrees)),
        where=pl.BlockSpec(memory_space=pltpu.HBM),
        scratch_shapes=[
            pltpu.VMEM(vectors.shape, vectors.dtype),
            pltpu.VMEM(degrees.shape, degrees.dtype),
            pltpu.SemaphoreType.DMA((3,)),
        ],
    )
    def start_image(packed):
        return call(
            own_kernel, "own", [((rows, 3 * ncv + 16), jnp.bfloat16), image_type], packed
        )

    def add(name, offsets, swap, blocks, image):
        places = [(offset, swap) for offset in offsets]
        (image,) = call(
            functools.partial(part_kernel, places, sizes),
            name,
            [image_type],
            table,
            left,
            blocks,
            image,
            input_output_aliases={3: 0},
            scratch_shapes=[pltpu.SMEM((len(places) + 1,), jnp.int32)],
        )
        return image

    n_chip = n_col // 2
    own, row_1, row_2, row_3, chip = (0, 0), (1, 0), (2, 0), (3, 0), (0, 1)
    if (n_row, n_chip) == (4, 2):
        near = [sent(packed, chip), sent(packed, row_1), sent(packed, row_2)]
        core_own = swapped(packed)
        left, image = start_image(packed)
        core_own, image = lax.optimization_barrier((core_own, image))
        image = add("add_own", [own], 1, core_own[None], image)
        near, image = lax.optimization_barrier((near, image))
        across = sent(jnp.stack(near[1:]), chip)
        from_row_3 = sent(near[2], row_1)
        near = jnp.stack(near)
        core = swapped(near)
        image = add("add_near", [chip, row_1, row_2], 0, near, image)
        image = add("add_core", [chip, row_1, row_2], 1, core, image)
        from_row_3, image = lax.optimization_barrier((from_row_3, image))
        last = sent(from_row_3, chip)
        across = jnp.concatenate([from_row_3[None], across])
        core = swapped(across)
        image = add("add_across", [row_3, (1, 1), (2, 1)], 0, across, image)
        image = add("add_far", [row_3, (1, 1), (2, 1)], 1, core, image)
        last, image = lax.optimization_barrier((last, image))
        last, last_offsets = last[None], [(3, 1)]
    else:
        rows_on = [(r, 0) for r in range(1, n_row)]
        chips_on = [(0, c) for c in range(1, n_chip)]
        near = jnp.stack([sent(packed, offset) for offset in rows_on + chips_on] + [packed])
        left, image = start_image(packed)
        near, image = lax.optimization_barrier((near, image))
        last = [sent(near[: n_row - 1], offset) for offset in chips_on]
        core = swapped(near)
        image = add("add_near", rows_on + chips_on, 0, near, image)
        image = add("add_core", rows_on + chips_on + [own], 1, core, image)
        last, image = lax.optimization_barrier((last, image))
        last = jnp.concatenate(last)
        last_offsets = [(r, c) for _, c in chips_on for r, _ in rows_on]
    places = [(offset, 0) for offset in last_offsets] + [(offset, 1) for offset in last_offsets]
    last = jnp.concatenate([last, swapped(last)])
    applied, gram = call(
        functools.partial(last_kernel, places, sizes),
        "add_last",
        [((nvec, rows), jnp.float32), ((devices, nvec // 2, 8 * nvec), jnp.float32)],
        table,
        left,
        last,
        image,
        vectors,
        degrees,
        scratch_shapes=[
            pltpu.VMEM(*image_type),
            pltpu.SMEM((len(places) + 1,), jnp.int32),
        ],
    )
    grams = lax.all_to_all(gram, ("row", "col"), 0, 0)
    basis, ritz = call(
        functools.partial(finish_kernel, rows * devices),
        "finish",
        [((nvec, rows), jnp.float32), ((nvec, nvec), jnp.float32)],
        grams,
        applied,
    )
    return (basis, ritz)


def solution(mesh):
    split = P(None, ("grp", "row", "col"))
    return jax.shard_map(
        per_device,
        mesh=mesh,
        in_specs=(split, split, P(("grp", "row", "col")), P()),
        out_specs=(split, P("grp", None)),
        check_vma=False,
    )
```

```python
import functools
import math

import jax
import jax.numpy as jnp
from jax import lax
from jax.experimental import pallas as pl
from jax.experimental.pallas import tpu as pltpu
from jax.sharding import PartitionSpec as P

unit = -math.log2(math.e) / 4.0

NT = (((1,), (1,)), ((), ()))
MIB = 1024 * 1024


def split3(x):
    high = x.astype(jnp.bfloat16).astype(jnp.float32)
    rest = x - high
    mid = rest.astype(jnp.bfloat16).astype(jnp.float32)
    low = (rest - mid).astype(jnp.bfloat16).astype(jnp.float32)
    return high, mid, low


def pack_kernel(frames_ref, vectors_ref, degrees_ref, out_ref, raw_ref, degree_ref, sems):
    ncv = frames_ref.shape[0]
    copies = [
        pltpu.make_async_copy(vectors_ref, raw_ref, sems.at[0]),
        pltpu.make_async_copy(degrees_ref, degree_ref, sems.at[1]),
        pltpu.make_async_copy(frames_ref, out_ref.at[pl.ds(0, ncv)], sems.at[2]),
    ]
    for copy in copies:
        copy.start()
    copies[0].wait()
    copies[1].wait()
    root = lax.rsqrt(degree_ref[...])[None, :]
    out_ref[ncv:, :] = (raw_ref[...].astype(jnp.float32) * root).astype(jnp.bfloat16)
    copies[2].wait()


def edge_rows(square, ones_first):
    high, mid, low = split3(square * unit)
    row = lax.broadcasted_iota(jnp.int32, (16, square.shape[1]), 0)
    base = 3 if ones_first else 0
    ones_at = 0 if ones_first else 3
    block = jnp.where((row >= ones_at) & (row < ones_at + 3), 1.0, 0.0)
    block = jnp.where(row == base, high, block)
    block = jnp.where(row == base + 1, mid, block)
    return jnp.where(row == base + 2, low, block)


def own_side(own):
    own = own.astype(jnp.float32)
    high, mid, low = split3(own * (-2.0 * unit))
    edge = edge_rows(jnp.sum(own * own, axis=0, keepdims=True), True)
    return jnp.concatenate([high, mid, low, edge], axis=0).T.astype(jnp.bfloat16)


def tile_image(left_ref, blocks):
    both = blocks[0] if len(blocks) == 1 else jnp.concatenate(blocks, axis=1)
    ncv = both.shape[0] // 2
    x, v = both[:ncv, :], both[ncv:, :]
    wide = x.astype(jnp.float32)
    edge = edge_rows(jnp.sum(wide * wide, axis=0, keepdims=True), False).astype(jnp.bfloat16)
    right = jnp.concatenate([x, x, x, edge], axis=0)
    power = jnp.dot(left_ref[...], right, preferred_element_type=jnp.float32)
    kern = jnp.exp2(power).astype(jnp.bfloat16)
    return lax.dot_general(kern, v, NT, preferred_element_type=jnp.float32)


def linked_words(sizes, table_ref):
    n_row, n_col = sizes
    me = lax.axis_index("row") * n_col + lax.axis_index("col")
    first, second = table_ref[:, 0, :], table_ref[:, 1, :]
    other = jnp.where(first == me, second, jnp.where(second == me, first, -1))
    words = []
    for start in range(0, n_row * n_col, 16):
        bit = jnp.zeros(other.shape, jnp.float32)
        for b in range(16):
            bit = jnp.where(other == start + b, float(1 << b), bit)
        words.append(jnp.sum(bit).astype(jnp.int32))
    return words


def is_linked(words, block):
    word = words[0]
    for w in range(1, len(words)):
        word = jnp.where(block // 16 == w, words[w], word)
    return (word >> (block % 16)) & 1


def own_kernel(sizes, table_ref, chip_ref, left_ref, image_ref):
    left_ref[...] = own_side(chip_ref[0, : chip_ref.shape[1] // 2, :])
    other = (lax.axis_index("row") * sizes[1] + lax.axis_index("col")) ^ 1
    linked = is_linked(linked_words(sizes, table_ref), other)

    @pl.when(linked == 1)
    def _():
        image_ref[...] = tile_image(left_ref, [chip_ref[0], chip_ref[1]])

    @pl.when(linked == 0)
    def _():
        image_ref[...] = tile_image(left_ref, [chip_ref[0]])


def add_blocks(places, sizes, table_ref, left_ref, odd_ref, even_ref, image_ref, list_ref):
    my_row, my_col = lax.axis_index("row"), lax.axis_index("col")
    odd = my_col % 2 == 1
    words = linked_words(sizes, table_ref)
    count = jnp.int32(0)
    for step, ((row_bits, chip_bits), even) in enumerate(places):
        owner_col = ((my_col ^ (2 * chip_bits)) | 1) ^ even
        list_ref[count] = step
        count += is_linked(words, (my_row ^ row_bits) * sizes[1] + owner_col)

    def block(at):
        return jnp.where(odd, odd_ref[list_ref[at]], even_ref[list_ref[at]])

    def visit(pair, _):
        image_ref[...] += tile_image(left_ref, [block(2 * pair), block(2 * pair + 1)])
        return 0

    lax.fori_loop(0, count // 2, visit, 0)

    @pl.when(count % 2 == 1)
    def _():
        image_ref[...] += tile_image(left_ref, [block(count - 1)])


def part_kernel(
    places, sizes, table_ref, left_ref, odd_ref, even_ref, before_ref, image_ref, list_ref
):
    image_ref[...] = before_ref[...]
    add_blocks(places, sizes, table_ref, left_ref, odd_ref, even_ref, image_ref, list_ref)


def last_kernel(
    places, sizes, table_ref, left_ref, odd_ref, even_ref, before_ref, vectors_ref, degrees_ref,
    applied_ref, gram_ref, image_ref, list_ref,
):
    image_ref[...] = before_ref[...]
    add_blocks(places, sizes, table_ref, left_ref, odd_ref, even_ref, image_ref, list_ref)
    n = vectors_ref.shape[0]
    applied = image_ref[...].T * lax.rsqrt(degrees_ref[...])[None, :]
    applied_ref[...] = applied
    both = jnp.concatenate([applied, vectors_ref[...].astype(jnp.float32)], axis=0)
    gram = lax.dot_general(
        both, both, NT, precision=lax.Precision.HIGHEST, preferred_element_type=jnp.float32
    )
    wide = jnp.concatenate(
        [gram[:n, :n], gram[n:, :], jnp.zeros((n, n), jnp.float32)], axis=1
    )
    tile = jnp.concatenate([wide[: n // 2, :], wide[n // 2 :, :]], axis=1)
    for device in range(gram_ref.shape[0]):
        gram_ref[device] = tile


def inverse_factors(grams):
    n = grams[0].shape[0]
    half = 64
    tiles = range(n // 8)
    shape = (8, 2 * half)
    row = lax.broadcasted_iota(jnp.int32, shape, 0)
    lane = lax.broadcasted_iota(jnp.int32, shape, 1)
    columns = [
        [
            jnp.where(
                lane < half,
                jnp.broadcast_to(grams[0][8 * t : 8 * t + 8, j : j + 1], shape),
                jnp.broadcast_to(grams[1][8 * t : 8 * t + 8, j : j + 1], shape),
            )
            for t in tiles
        ]
        for j in range(n)
    ]
    right = [jnp.where(lane % half == row + 8 * t, 1.0, 0.0) for t in tiles]
    pivots = [jnp.ones(shape, jnp.float32) for t in tiles]
    for k in range(n):
        top, at = k // 8, k % 8
        pivot = columns[k][top][at : at + 1, :]
        pivots[top] = jnp.where(row == at, pivot, pivots[top])
        if k == n - 1:
            break
        scale = 1.0 / pivot
        factor = {t: columns[k][t] * scale for t in tiles if t >= top}
        factor[top] = jnp.where(row > at, factor[top], 0.0)
        for column in columns[k + 1 :] + [right]:
            line = column[top][at : at + 1, :]
            for t in factor:
                column[t] = column[t] - factor[t] * line
    result = jnp.concatenate([r * lax.rsqrt(p) for r, p in zip(right, pivots)], axis=0)
    return result[:, :n], result[:, half : half + n]


def finish_kernel(total_frames, grams_ref, applied_ref, basis_ref, ritz_ref):
    tile = grams_ref[0]
    for device in range(1, grams_ref.shape[0]):
        tile += grams_ref[device]
    n = applied_ref.shape[0]
    gram = jnp.concatenate([tile[:, : 4 * n], tile[:, 4 * n :]], axis=0)
    exact = functools.partial(
        lax.dot_general, precision=lax.Precision.HIGHEST, preferred_element_type=jnp.float32
    )
    plain = (((1,), (0,)), ((), ()))
    image_inverse, vector_inverse = inverse_factors([gram[:, :n], gram[:, 2 * n : 3 * n]])
    basis_ref[...] = exact(image_inverse * math.sqrt(total_frames), applied_ref[...], plain)
    half = exact(vector_inverse, gram[:, n : 2 * n], plain)
    ritz_ref[...] = exact(half, vector_inverse, NT)


def sent(x, offset):
    rows, chips = offset
    n_row, n_col = lax.axis_size("row"), lax.axis_size("col")
    pairs = [
        (r * n_col + c, (r ^ rows) * n_col + (c ^ (2 * chips)))
        for r in range(n_row)
        for c in range(1, n_col, 2)
    ]
    return lax.ppermute(x, ("row", "col"), pairs)


def swapped(x):
    return lax.ppermute(x, "col", [(i, i ^ 1) for i in range(lax.axis_size("col"))])


def passed_down(x):
    return lax.ppermute(x, "col", [(i, i ^ 1) for i in range(1, lax.axis_size("col"), 2)])


def per_device(frames, vectors, degrees, tile_table):
    ncv, rows = frames.shape
    nvec = vectors.shape[0]
    n_row, n_col = lax.axis_size("row"), lax.axis_size("col")
    devices = n_row * n_col
    sizes = (n_row, n_col)
    vmem = pl.BlockSpec(memory_space=pltpu.VMEM)

    def call(kernel, name, outs, *args, limit=16, where=vmem, **keywords):
        shapes = [jax.ShapeDtypeStruct(*out) for out in outs]
        return pl.pallas_call(
            kernel,
            out_shape=shapes,
            in_specs=[where] * len(args),
            out_specs=[vmem] * len(outs),
            compiler_params=pltpu.CompilerParams(vmem_limit_bytes=limit * MIB),
            name=name,
            **keywords,
        )(*args)

    table = tile_table.transpose(1, 2, 0)
    image_type = ((rows, nvec), jnp.float32)

    (packed,) = call(
        pack_kernel,
        "pack",
        [((ncv + nvec, rows), jnp.bfloat16)],
        *(pltpu.with_memory_space_constraint(x, pltpu.HBM) for x in (frames, vectors, degrees)),
        where=pl.BlockSpec(memory_space=pltpu.HBM),
        scratch_shapes=[
            pltpu.VMEM(vectors.shape, vectors.dtype),
            pltpu.VMEM(degrees.shape, degrees.dtype),
            pltpu.SemaphoreType.DMA((3,)),
        ],
    )
    def add(name, offsets, blocks, image):
        places = [(offset, even) for offset in offsets for even in (0, 1)]
        (image,) = call(
            functools.partial(part_kernel, places, sizes),
            name,
            [image_type],
            table,
            left,
            blocks,
            passed_down(blocks),
            image,
            input_output_aliases={4: 0},
            scratch_shapes=[pltpu.SMEM((len(places) + 1,), jnp.int32)],
        )
        return image

    n_chip = n_col // 2
    pair = jnp.stack([packed, swapped(packed)])
    row_hops = [(r, 0) for r in range(1, n_row)]
    chip_hops = [(0, c) for c in range(1, n_chip)]
    if (n_row, n_chip) == (4, 2):
        near_offsets = [(2, 0), (1, 0), (0, 1)]
    else:
        near_offsets = chip_hops + row_hops
    near = [sent(pair, offset) for offset in near_offsets]
    left, image = call(
        functools.partial(own_kernel, sizes),
        "own",
        [((rows, 3 * ncv + 16), jnp.bfloat16), image_type],
        table,
        pair,
    )
    near, image = lax.optimization_barrier((near, image))
    if (n_row, n_chip) == (4, 2):
        from_chip = sent(jnp.concatenate(near[:2]), (0, 1))
        from_row_3 = sent(near[0], (1, 0))
        image = add("add_near", near_offsets, jnp.concatenate(near), image)
        from_row_3, image = lax.optimization_barrier((from_row_3, image))
        last = sent(from_row_3, (0, 1))
        image = add(
            "add_next", [(3, 0), (2, 1), (1, 1)], jnp.concatenate([from_row_3, from_chip]), image
        )
        last, image = lax.optimization_barrier((last, image))
        last_offsets = [(3, 1)]
    else:
        lines = jnp.concatenate(near[len(chip_hops) :])
        last = jnp.concatenate([sent(lines, hop) for hop in chip_hops])
        image = add("add_near", near_offsets, jnp.concatenate(near), image)
        last, image = lax.optimization_barrier((last, image))
        last_offsets = [(r, c) for _, c in chip_hops for r, _ in row_hops]
    places = [(offset, even) for offset in last_offsets for even in (0, 1)]
    applied, gram = call(
        functools.partial(last_kernel, places, sizes),
        "add_last",
        [((nvec, rows), jnp.float32), ((devices, nvec // 2, 8 * nvec), jnp.float32)],
        table,
        left,
        last,
        passed_down(last),
        image,
        vectors,
        degrees,
        scratch_shapes=[
            pltpu.VMEM(*image_type),
            pltpu.SMEM((len(places) + 1,), jnp.int32),
        ],
    )
    grams = lax.all_to_all(gram, ("row", "col"), 0, 0)
    basis, ritz = call(
        functools.partial(finish_kernel, rows * devices),
        "finish",
        [((nvec, rows), jnp.float32), ((nvec, nvec), jnp.float32)],
        grams,
        applied,
    )
    return (basis, ritz)


def solution(mesh):
    split = P(None, ("grp", "row", "col"))
    return jax.shard_map(
        per_device,
        mesh=mesh,
        in_specs=(split, split, P(("grp", "row", "col")), P()),
        out_specs=(split, P("grp", None)),
        check_vma=False,
    )
```

```python
import functools
import math

import jax
import jax.numpy as jnp
from jax import lax
from jax.experimental import pallas as pl
from jax.experimental.pallas import tpu as pltpu
from jax.sharding import PartitionSpec as P

unit = -math.log2(math.e) / 4.0

NT = (((1,), (1,)), ((), ()))
MIB = 1024 * 1024


def split3(x):
    high = x.astype(jnp.bfloat16).astype(jnp.float32)
    rest = x - high
    mid = rest.astype(jnp.bfloat16).astype(jnp.float32)
    low = (rest - mid).astype(jnp.bfloat16).astype(jnp.float32)
    return high, mid, low


def pack_kernel(frames_ref, vectors_ref, degrees_ref, out_ref, raw_ref, degree_ref, sems):
    ncv = frames_ref.shape[0]
    copies = [
        pltpu.make_async_copy(vectors_ref, raw_ref, sems.at[0]),
        pltpu.make_async_copy(degrees_ref, degree_ref, sems.at[1]),
        pltpu.make_async_copy(frames_ref, out_ref.at[pl.ds(0, ncv)], sems.at[2]),
    ]
    for copy in copies:
        copy.start()
    copies[0].wait()
    copies[1].wait()
    root = lax.rsqrt(degree_ref[...])[None, :]
    out_ref[ncv:, :] = (raw_ref[...].astype(jnp.float32) * root).astype(jnp.bfloat16)
    copies[2].wait()


def edge_rows(square, ones_first):
    high, mid, low = split3(square * unit)
    row = lax.broadcasted_iota(jnp.int32, (16, square.shape[1]), 0)
    base = 3 if ones_first else 0
    ones_at = 0 if ones_first else 3
    block = jnp.where((row >= ones_at) & (row < ones_at + 3), 1.0, 0.0)
    block = jnp.where(row == base, high, block)
    block = jnp.where(row == base + 1, mid, block)
    return jnp.where(row == base + 2, low, block)


def own_side(own):
    own = own.astype(jnp.float32)
    high, mid, low = split3(own * (-2.0 * unit))
    edge = edge_rows(jnp.sum(own * own, axis=0, keepdims=True), True)
    return jnp.concatenate([high, mid, low, edge], axis=0).T.astype(jnp.bfloat16)


def tile_image(left_ref, blocks):
    both = blocks[0] if len(blocks) == 1 else jnp.concatenate(blocks, axis=1)
    ncv = both.shape[0] // 2
    x, v = both[:ncv, :], both[ncv:, :]
    wide = x.astype(jnp.float32)
    edge = edge_rows(jnp.sum(wide * wide, axis=0, keepdims=True), False).astype(jnp.bfloat16)
    right = jnp.concatenate([x, x, x, edge], axis=0)
    power = jnp.dot(left_ref[...], right, preferred_element_type=jnp.float32)
    kern = jnp.exp2(power).astype(jnp.bfloat16)
    return lax.dot_general(kern, v, NT, preferred_element_type=jnp.float32)


def own_kernel(packed_ref, left_ref, image_ref):
    left_ref[...] = own_side(packed_ref[: packed_ref.shape[0] // 2, :])
    image_ref[...] = tile_image(left_ref, [packed_ref[...]])


def add_blocks(places, sizes, table_ref, left_ref, blocks_ref, image_ref, list_ref):
    n_row, n_col = sizes
    my_row, my_col = lax.axis_index("row"), lax.axis_index("col")
    me = my_row * n_col + my_col
    first, second = table_ref[:, 0, :], table_ref[:, 1, :]
    other = jnp.where(first == me, second, jnp.where(second == me, first, -1))
    words = []
    for start in range(0, n_row * n_col, 16):
        bit = jnp.zeros(other.shape, jnp.float32)
        for b in range(16):
            bit = jnp.where(other == start + b, float(1 << b), bit)
        words.append(jnp.sum(bit).astype(jnp.int32))

    count = jnp.int32(0)
    for step, (row_bits, col_bits) in enumerate(places):
        block = (my_row ^ row_bits) * n_col + (my_col ^ col_bits)
        word = words[0]
        for w in range(1, len(words)):
            word = jnp.where(block // 16 == w, words[w], word)
        list_ref[count] = step
        count += (word >> (block % 16)) & 1

    def visit(pair, _):
        blocks = [blocks_ref[list_ref[2 * pair]], blocks_ref[list_ref[2 * pair + 1]]]
        image_ref[...] += tile_image(left_ref, blocks)
        return 0

    lax.fori_loop(0, count // 2, visit, 0)

    @pl.when(count % 2 == 1)
    def _():
        image_ref[...] += tile_image(left_ref, [blocks_ref[list_ref[count - 1]]])


def part_kernel(places, sizes, table_ref, left_ref, blocks_ref, before_ref, image_ref, list_ref):
    image_ref[...] = before_ref[...]
    add_blocks(places, sizes, table_ref, left_ref, blocks_ref, image_ref, list_ref)


def last_kernel(
    places, sizes, table_ref, left_ref, blocks_ref, before_ref, vectors_ref, degrees_ref,
    applied_ref, gram_ref, image_ref, list_ref,
):
    image_ref[...] = before_ref[...]
    add_blocks(places, sizes, table_ref, left_ref, blocks_ref, image_ref, list_ref)
    n = vectors_ref.shape[0]
    applied = image_ref[...].T * lax.rsqrt(degrees_ref[...])[None, :]
    applied_ref[...] = applied
    both = jnp.concatenate([applied, vectors_ref[...].astype(jnp.float32)], axis=0)
    gram = lax.dot_general(
        both, both, NT, precision=lax.Precision.HIGHEST, preferred_element_type=jnp.float32
    )
    wide = jnp.concatenate(
        [gram[:n, :n], gram[n:, :], jnp.zeros((n, n), jnp.float32)], axis=1
    )
    tile = jnp.concatenate([wide[: n // 2, :], wide[n // 2 :, :]], axis=1)
    for device in range(gram_ref.shape[0]):
        gram_ref[device] = tile


def inverse_factors(grams):
    n = grams[0].shape[0]
    half = 64
    tiles = range(n // 8)
    shape = (8, 2 * half)
    row = lax.broadcasted_iota(jnp.int32, shape, 0)
    lane = lax.broadcasted_iota(jnp.int32, shape, 1)
    columns = [
        [
            jnp.where(
                lane < half,
                jnp.broadcast_to(grams[0][8 * t : 8 * t + 8, j : j + 1], shape),
                jnp.broadcast_to(grams[1][8 * t : 8 * t + 8, j : j + 1], shape),
            )
            for t in tiles
        ]
        for j in range(n)
    ]
    right = [jnp.where(lane % half == row + 8 * t, 1.0, 0.0) for t in tiles]
    pivots = [jnp.ones(shape, jnp.float32) for t in tiles]
    for k in range(n):
        top, at = k // 8, k % 8
        pivot = columns[k][top][at : at + 1, :]
        pivots[top] = jnp.where(row == at, pivot, pivots[top])
        if k == n - 1:
            break
        scale = 1.0 / pivot
        factor = {t: columns[k][t] * scale for t in tiles if t >= top}
        factor[top] = jnp.where(row > at, factor[top], 0.0)
        for column in columns[k + 1 :] + [right]:
            line = column[top][at : at + 1, :]
            for t in factor:
                column[t] = column[t] - factor[t] * line
    result = jnp.concatenate([r * lax.rsqrt(p) for r, p in zip(right, pivots)], axis=0)
    return result[:, :n], result[:, half : half + n]


def finish_kernel(total_frames, grams_ref, applied_ref, basis_ref, ritz_ref):
    tile = grams_ref[0]
    for device in range(1, grams_ref.shape[0]):
        tile += grams_ref[device]
    n = applied_ref.shape[0]
    gram = jnp.concatenate([tile[:, : 4 * n], tile[:, 4 * n :]], axis=0)
    exact = functools.partial(
        lax.dot_general, precision=lax.Precision.HIGHEST, preferred_element_type=jnp.float32
    )
    plain = (((1,), (0,)), ((), ()))
    image_inverse, vector_inverse = inverse_factors([gram[:, :n], gram[:, 2 * n : 3 * n]])
    basis_ref[...] = exact(image_inverse * math.sqrt(total_frames), applied_ref[...], plain)
    half = exact(vector_inverse, gram[:, n : 2 * n], plain)
    ritz_ref[...] = exact(half, vector_inverse, NT)


def sent(x, hop):
    n_row, n_col = lax.axis_size("row"), lax.axis_size("col")
    pairs = [
        (r * n_col + c, (r ^ hop[0]) * n_col + (c ^ hop[1]))
        for r in range(n_row)
        for c in range(n_col)
    ]
    return lax.ppermute(x, ("row", "col"), pairs)


def beyond(offsets, hop):
    return [(r ^ hop[0], c ^ hop[1]) for r, c in offsets]


def exchange_plan(n_row, n_col):
    if (n_row, n_col) == (4, 4):
        direct = [(2, 1), (1, 1), (0, 3)]
        return direct, [((0, 3), [(1, 1), (2, 1)]), ((3, 1), [(0, 3)]), ((1, 1), [(2, 1)])]
    lines = [(r, 1) for r in range(1, n_row)]
    chips = [(0, c) for c in range(3, n_col, 2)]
    return lines + chips, [(chip, lines) for chip in chips]


def per_device(frames, vectors, degrees, tile_table):
    ncv, rows = frames.shape
    nvec = vectors.shape[0]
    n_row, n_col = lax.axis_size("row"), lax.axis_size("col")
    devices = n_row * n_col
    sizes = (n_row, n_col)
    vmem = pl.BlockSpec(memory_space=pltpu.VMEM)

    def call(kernel, name, outs, *args, limit=16, where=vmem, **keywords):
        shapes = [jax.ShapeDtypeStruct(*out) for out in outs]
        return pl.pallas_call(
            kernel,
            out_shape=shapes,
            in_specs=[where] * len(args),
            out_specs=[vmem] * len(outs),
            compiler_params=pltpu.CompilerParams(vmem_limit_bytes=limit * MIB),
            name=name,
            **keywords,
        )(*args)

    table = tile_table.transpose(1, 2, 0)
    image_type = ((rows, nvec), jnp.float32)

    (packed,) = call(
        pack_kernel,
        "pack",
        [((ncv + nvec, rows), jnp.bfloat16)],
        *(pltpu.with_memory_space_constraint(x, pltpu.HBM) for x in (frames, vectors, degrees)),
        where=pl.BlockSpec(memory_space=pltpu.HBM),
        scratch_shapes=[
            pltpu.VMEM(vectors.shape, vectors.dtype),
            pltpu.VMEM(degrees.shape, degrees.dtype),
            pltpu.SemaphoreType.DMA((3,)),
        ],
    )
    core = (0, 1)
    direct, forwards = exchange_plan(n_row, n_col)
    held = {offset: sent(packed, offset) for offset in direct}
    left, image = call(
        own_kernel, "own", [((rows, 3 * ncv + 16), jnp.bfloat16), image_type], packed
    )

    def add(name, places, blocks, image):
        (image,) = call(
            functools.partial(part_kernel, places, sizes),
            name,
            [image_type],
            table,
            left,
            blocks,
            image,
            input_output_aliases={3: 0},
            scratch_shapes=[pltpu.SMEM((len(places) + 1,), jnp.int32)],
        )
        return image

    near = jnp.stack([held[offset] for offset in direct] + [packed])
    near, image, held = lax.optimization_barrier((near, image, held))
    across_places = []
    across = []
    for hop, offsets in forwards:
        across.append(sent(jnp.stack([held[offset] for offset in offsets]), hop))
        across_places += beyond(offsets, hop)
    other_near = sent(near, core)
    image = add("add_near", direct, near, image)
    image = add("add_core", beyond(direct + [(0, 0)], core), other_near, image)
    across, image = lax.optimization_barrier((across, image))
    across = jnp.concatenate(across)
    far = sent(across, core)
    image = add("add_across", across_places, across, image)
    far_places = beyond(across_places, core)
    applied, gram = call(
        functools.partial(last_kernel, far_places, sizes),
        "add_far",
        [((nvec, rows), jnp.float32), ((devices, nvec // 2, 8 * nvec), jnp.float32)],
        table,
        left,
        far,
        image,
        vectors,
        degrees,
        scratch_shapes=[
            pltpu.VMEM(*image_type),
            pltpu.SMEM((len(far_places) + 1,), jnp.int32),
        ],
    )
    grams = lax.all_to_all(gram, ("row", "col"), 0, 0)
    basis, ritz = call(
        functools.partial(finish_kernel, rows * devices),
        "finish",
        [((nvec, rows), jnp.float32), ((nvec, nvec), jnp.float32)],
        grams,
        applied,
    )
    return (basis, ritz)


def solution(mesh):
    split = P(None, ("grp", "row", "col"))
    return jax.shard_map(
        per_device,
        mesh=mesh,
        in_specs=(split, split, P(("grp", "row", "col")), P()),
        out_specs=(split, P("grp", None)),
        check_vma=False,
    )
```

```python
import functools
import math

import jax
import jax.numpy as jnp
from jax import lax
from jax.experimental import pallas as pl
from jax.experimental.pallas import tpu as pltpu
from jax.sharding import PartitionSpec as P

unit = -math.log2(math.e) / 4.0

NT = (((1,), (1,)), ((), ()))
MIB = 1024 * 1024


def split3(x):
    high = x.astype(jnp.bfloat16).astype(jnp.float32)
    rest = x - high
    mid = rest.astype(jnp.bfloat16).astype(jnp.float32)
    low = (rest - mid).astype(jnp.bfloat16).astype(jnp.float32)
    return high, mid, low


def pack_kernel(frames_ref, vectors_ref, degrees_ref, out_ref, raw_ref, degree_ref, sems):
    ncv = frames_ref.shape[0]
    copies = [
        pltpu.make_async_copy(vectors_ref, raw_ref, sems.at[0]),
        pltpu.make_async_copy(degrees_ref, degree_ref, sems.at[1]),
        pltpu.make_async_copy(frames_ref, out_ref.at[pl.ds(0, ncv)], sems.at[2]),
    ]
    for copy in copies:
        copy.start()
    copies[0].wait()
    copies[1].wait()
    root = lax.rsqrt(degree_ref[...])[None, :]
    out_ref[ncv:, :] = (raw_ref[...].astype(jnp.float32) * root).astype(jnp.bfloat16)
    copies[2].wait()


def edge_rows(square, ones_first):
    high, mid, low = split3(square * unit)
    row = lax.broadcasted_iota(jnp.int32, (16, square.shape[1]), 0)
    base = 3 if ones_first else 0
    ones_at = 0 if ones_first else 3
    block = jnp.where((row >= ones_at) & (row < ones_at + 3), 1.0, 0.0)
    block = jnp.where(row == base, high, block)
    block = jnp.where(row == base + 1, mid, block)
    return jnp.where(row == base + 2, low, block)


def own_side(own):
    own = own.astype(jnp.float32)
    high, mid, low = split3(own * (-2.0 * unit))
    edge = edge_rows(jnp.sum(own * own, axis=0, keepdims=True), True)
    return jnp.concatenate([high, mid, low, edge], axis=0).T.astype(jnp.bfloat16)


def tile_image(left_ref, blocks):
    both = blocks[0] if len(blocks) == 1 else jnp.concatenate(blocks, axis=1)
    ncv = both.shape[0] // 2
    x, v = both[:ncv, :], both[ncv:, :]
    wide = x.astype(jnp.float32)
    edge = edge_rows(jnp.sum(wide * wide, axis=0, keepdims=True), False).astype(jnp.bfloat16)
    right = jnp.concatenate([x, x, x, edge], axis=0)
    power = jnp.dot(left_ref[...], right, preferred_element_type=jnp.float32)
    kern = jnp.exp2(power).astype(jnp.bfloat16)
    return lax.dot_general(kern, v, NT, preferred_element_type=jnp.float32)


def own_kernel(packed_ref, left_ref, image_ref):
    left_ref[...] = own_side(packed_ref[: packed_ref.shape[0] // 2, :])
    image_ref[...] = tile_image(left_ref, [packed_ref[...]])


def add_blocks(places, sizes, table_ref, left_ref, blocks_ref, image_ref, list_ref):
    n_row, n_col = sizes
    my_row, my_col = lax.axis_index("row"), lax.axis_index("col")
    me = my_row * n_col + my_col
    first, second = table_ref[:, 0, :], table_ref[:, 1, :]
    other = jnp.where(first == me, second, jnp.where(second == me, first, -1))
    words = []
    for start in range(0, n_row * n_col, 16):
        bit = jnp.zeros(other.shape, jnp.float32)
        for b in range(16):
            bit = jnp.where(other == start + b, float(1 << b), bit)
        words.append(jnp.sum(bit).astype(jnp.int32))

    count = jnp.int32(0)
    for step, (row_bits, col_bits) in enumerate(places):
        block = (my_row ^ row_bits) * n_col + (my_col ^ col_bits)
        word = words[0]
        for w in range(1, len(words)):
            word = jnp.where(block // 16 == w, words[w], word)
        list_ref[count] = step
        count += (word >> (block % 16)) & 1

    def visit(pair, _):
        blocks = [blocks_ref[list_ref[2 * pair]], blocks_ref[list_ref[2 * pair + 1]]]
        image_ref[...] += tile_image(left_ref, blocks)
        return 0

    lax.fori_loop(0, count // 2, visit, 0)

    @pl.when(count % 2 == 1)
    def _():
        image_ref[...] += tile_image(left_ref, [blocks_ref[list_ref[count - 1]]])


def part_kernel(places, sizes, table_ref, left_ref, blocks_ref, before_ref, image_ref, list_ref):
    image_ref[...] = before_ref[...]
    add_blocks(places, sizes, table_ref, left_ref, blocks_ref, image_ref, list_ref)


def last_kernel(
    places, sizes, table_ref, left_ref, blocks_ref, before_ref, vectors_ref, degrees_ref,
    applied_ref, gram_ref, image_ref, list_ref,
):
    image_ref[...] = before_ref[...]
    add_blocks(places, sizes, table_ref, left_ref, blocks_ref, image_ref, list_ref)
    n = vectors_ref.shape[0]
    applied = image_ref[...].T * lax.rsqrt(degrees_ref[...])[None, :]
    applied_ref[...] = applied
    both = jnp.concatenate([applied, vectors_ref[...].astype(jnp.float32)], axis=0)
    gram = lax.dot_general(
        both, both, NT, precision=lax.Precision.HIGHEST, preferred_element_type=jnp.float32
    )
    wide = jnp.concatenate(
        [gram[:n, :n], gram[n:, :], jnp.zeros((n, n), jnp.float32)], axis=1
    )
    tile = jnp.concatenate([wide[: n // 2, :], wide[n // 2 :, :]], axis=1)
    for device in range(gram_ref.shape[0]):
        gram_ref[device] = tile


def inverse_factors(grams):
    n = grams[0].shape[0]
    half = 64
    tiles = range(n // 8)
    shape = (8, 2 * half)
    row = lax.broadcasted_iota(jnp.int32, shape, 0)
    lane = lax.broadcasted_iota(jnp.int32, shape, 1)
    columns = [
        [
            jnp.where(
                lane < half,
                jnp.broadcast_to(grams[0][8 * t : 8 * t + 8, j : j + 1], shape),
                jnp.broadcast_to(grams[1][8 * t : 8 * t + 8, j : j + 1], shape),
            )
            for t in tiles
        ]
        for j in range(n)
    ]
    right = [jnp.where(lane % half == row + 8 * t, 1.0, 0.0) for t in tiles]
    pivots = [jnp.ones(shape, jnp.float32) for t in tiles]
    for k in range(n):
        top, at = k // 8, k % 8
        pivot = columns[k][top][at : at + 1, :]
        pivots[top] = jnp.where(row == at, pivot, pivots[top])
        if k == n - 1:
            break
        scale = 1.0 / pivot
        factor = {t: columns[k][t] * scale for t in tiles if t >= top}
        factor[top] = jnp.where(row > at, factor[top], 0.0)
        for column in columns[k + 1 :] + [right]:
            line = column[top][at : at + 1, :]
            for t in factor:
                column[t] = column[t] - factor[t] * line
    result = jnp.concatenate([r * lax.rsqrt(p) for r, p in zip(right, pivots)], axis=0)
    return result[:, :n], result[:, half : half + n]


def finish_kernel(total_frames, grams_ref, applied_ref, basis_ref, ritz_ref):
    tile = grams_ref[0]
    for device in range(1, grams_ref.shape[0]):
        tile += grams_ref[device]
    n = applied_ref.shape[0]
    gram = jnp.concatenate([tile[:, : 4 * n], tile[:, 4 * n :]], axis=0)
    exact = functools.partial(
        lax.dot_general, precision=lax.Precision.HIGHEST, preferred_element_type=jnp.float32
    )
    plain = (((1,), (0,)), ((), ()))
    image_inverse, vector_inverse = inverse_factors([gram[:, :n], gram[:, 2 * n : 3 * n]])
    basis_ref[...] = exact(image_inverse * math.sqrt(total_frames), applied_ref[...], plain)
    half = exact(vector_inverse, gram[:, n : 2 * n], plain)
    ritz_ref[...] = exact(half, vector_inverse, NT)


def sent(x, hop):
    n_row, n_col = lax.axis_size("row"), lax.axis_size("col")
    pairs = [
        (r * n_col + c, (r ^ hop[0]) * n_col + (c ^ hop[1]))
        for r in range(n_row)
        for c in range(n_col)
    ]
    return lax.ppermute(x, ("row", "col"), pairs)


def beyond(offsets, hop):
    return [(r ^ hop[0], c ^ hop[1]) for r, c in offsets]


def exchange_plan(n_row, n_col):
    if (n_row, n_col) == (4, 4):
        direct = [(2, 1), (1, 1), (0, 3)]
        return direct, [((0, 3), [(2, 1)]), ((1, 1), [(2, 1), (0, 3)]), ((1, 3), [(2, 1)])]
    lines = [(r, 1) for r in range(1, n_row)]
    chips = [(0, c) for c in range(3, n_col, 2)]
    return lines + chips, [(chip, lines) for chip in chips]


def per_device(frames, vectors, degrees, tile_table):
    ncv, rows = frames.shape
    nvec = vectors.shape[0]
    n_row, n_col = lax.axis_size("row"), lax.axis_size("col")
    devices = n_row * n_col
    sizes = (n_row, n_col)
    vmem = pl.BlockSpec(memory_space=pltpu.VMEM)

    def call(kernel, name, outs, *args, limit=16, where=vmem, **keywords):
        shapes = [jax.ShapeDtypeStruct(*out) for out in outs]
        return pl.pallas_call(
            kernel,
            out_shape=shapes,
            in_specs=[where] * len(args),
            out_specs=[vmem] * len(outs),
            compiler_params=pltpu.CompilerParams(vmem_limit_bytes=limit * MIB),
            name=name,
            **keywords,
        )(*args)

    table = tile_table.transpose(1, 2, 0)
    image_type = ((rows, nvec), jnp.float32)

    (packed,) = call(
        pack_kernel,
        "pack",
        [((ncv + nvec, rows), jnp.bfloat16)],
        *(pltpu.with_memory_space_constraint(x, pltpu.HBM) for x in (frames, vectors, degrees)),
        where=pl.BlockSpec(memory_space=pltpu.HBM),
        scratch_shapes=[
            pltpu.VMEM(vectors.shape, vectors.dtype),
            pltpu.VMEM(degrees.shape, degrees.dtype),
            pltpu.SemaphoreType.DMA((3,)),
        ],
    )
    core = (0, 1)
    direct, forwards = exchange_plan(n_row, n_col)
    held = {offset: sent(packed, offset) for offset in direct}
    left, image = call(
        own_kernel, "own", [((rows, 3 * ncv + 16), jnp.bfloat16), image_type], packed
    )

    def add(name, places, blocks, image):
        (image,) = call(
            functools.partial(part_kernel, places, sizes),
            name,
            [image_type],
            table,
            left,
            blocks,
            image,
            input_output_aliases={3: 0},
            scratch_shapes=[pltpu.SMEM((len(places) + 1,), jnp.int32)],
        )
        return image

    near = jnp.stack([held[offset] for offset in direct] + [packed])
    near, image, held = lax.optimization_barrier((near, image, held))
    across_places = []
    across = []
    for hop, offsets in forwards:
        across.append(sent(jnp.stack([held[offset] for offset in offsets]), hop))
        across_places += beyond(offsets, hop)
    other_near = sent(near, core)
    near = jnp.concatenate([near[:-1], other_near])
    image = add("add_near", direct + beyond(direct + [(0, 0)], core), near, image)
    across, image = lax.optimization_barrier((across, image))
    across = jnp.concatenate(across)
    far = sent(across, core)
    image = add("add_across", across_places, across, image)
    far_places = beyond(across_places, core)
    applied, gram = call(
        functools.partial(last_kernel, far_places, sizes),
        "add_far",
        [((nvec, rows), jnp.float32), ((devices, nvec // 2, 8 * nvec), jnp.float32)],
        table,
        left,
        far,
        image,
        vectors,
        degrees,
        scratch_shapes=[
            pltpu.VMEM(*image_type),
            pltpu.SMEM((len(far_places) + 1,), jnp.int32),
        ],
    )
    grams = lax.all_to_all(gram, ("row", "col"), 0, 0)
    basis, ritz = call(
        functools.partial(finish_kernel, rows * devices),
        "finish",
        [((nvec, rows), jnp.float32), ((nvec, nvec), jnp.float32)],
        grams,
        applied,
    )
    return (basis, ritz)


def solution(mesh):
    split = P(None, ("grp", "row", "col"))
    return jax.shard_map(
        per_device,
        mesh=mesh,
        in_specs=(split, split, P(("grp", "row", "col")), P()),
        out_specs=(split, P("grp", None)),
        check_vma=False,
    )
```

```python
import functools
import math

import jax
import jax.numpy as jnp
from jax import lax
from jax.experimental import pallas as pl
from jax.experimental.pallas import tpu as pltpu
from jax.sharding import PartitionSpec as P

unit = -math.log2(math.e) / 4.0

NT = (((1,), (1,)), ((), ()))
MIB = 1024 * 1024


def split3(x):
    high = x.astype(jnp.bfloat16).astype(jnp.float32)
    rest = x - high
    mid = rest.astype(jnp.bfloat16).astype(jnp.float32)
    low = (rest - mid).astype(jnp.bfloat16).astype(jnp.float32)
    return high, mid, low


def pack_kernel(
    frames_ref, vectors_in, degrees_ref, table_in,
    packed_ref, vectors_ref, root_ref, table_ref, degree_ref, sems,
):
    ncv = frames_ref.shape[0]
    copies = [
        pltpu.make_async_copy(vectors_in, vectors_ref, sems.at[0]),
        pltpu.make_async_copy(degrees_ref, degree_ref, sems.at[1]),
        pltpu.make_async_copy(frames_ref, packed_ref.at[pl.ds(0, ncv)], sems.at[2]),
        pltpu.make_async_copy(table_in, table_ref, sems.at[3]),
    ]
    for copy in copies:
        copy.start()
    copies[0].wait()
    copies[1].wait()
    root = lax.rsqrt(degree_ref[...])[None, :]
    root_ref[...] = root
    packed_ref[ncv:, :] = (vectors_ref[...].astype(jnp.float32) * root).astype(jnp.bfloat16)
    copies[2].wait()
    copies[3].wait()


def edge_rows(square, ones_first):
    high, mid, low = split3(square * unit)
    row = lax.broadcasted_iota(jnp.int32, (16, square.shape[1]), 0)
    base = 3 if ones_first else 0
    ones_at = 0 if ones_first else 3
    block = jnp.where((row >= ones_at) & (row < ones_at + 3), 1.0, 0.0)
    block = jnp.where(row == base, high, block)
    block = jnp.where(row == base + 1, mid, block)
    return jnp.where(row == base + 2, low, block)


def own_side(own):
    own = own.astype(jnp.float32)
    high, mid, low = split3(own * (-2.0 * unit))
    edge = edge_rows(jnp.sum(own * own, axis=0, keepdims=True), True)
    return jnp.concatenate([high, mid, low, edge], axis=0).T.astype(jnp.bfloat16)


def tile_image(left_ref, kern_ref, blocks):
    both = blocks[0] if len(blocks) == 1 else jnp.concatenate(blocks, axis=1)
    ncv = both.shape[0] // 2
    x, v = both[:ncv, :], both[ncv:, :]
    wide = x.astype(jnp.float32)
    edge = edge_rows(jnp.sum(wide * wide, axis=0, keepdims=True), False).astype(jnp.bfloat16)
    right = jnp.concatenate([x, x, x, edge], axis=0)
    chunk, total = 256, right.shape[1]
    for start in range(0, total, chunk):
        power = jnp.dot(
            left_ref[...], right[:, start : start + chunk], preferred_element_type=jnp.float32
        )
        kern_ref[:, start : start + chunk] = jnp.exp2(power).astype(jnp.bfloat16)
    return lax.dot_general(kern_ref[:, :total], v, NT, preferred_element_type=jnp.float32)


def own_kernel(packed_ref, left_ref, image_ref, kern_ref):
    left_ref[...] = own_side(packed_ref[: packed_ref.shape[0] // 2, :])
    image_ref[...] = tile_image(left_ref, kern_ref, [packed_ref[...]])


def add_blocks(places, sizes, table_ref, left_ref, blocks_ref, image_ref, list_ref, kern_ref):
    n_row, n_col = sizes
    my_row, my_col = lax.axis_index("row"), lax.axis_index("col")
    me = my_row * n_col + my_col
    first, second = table_ref[:, 0, :], table_ref[:, 1, :]
    other = jnp.where(first == me, second, jnp.where(second == me, first, -1))
    words = []
    for start in range(0, n_row * n_col, 16):
        bit = jnp.zeros(other.shape, jnp.float32)
        for b in range(16):
            bit = jnp.where(other == start + b, float(1 << b), bit)
        words.append(jnp.sum(bit).astype(jnp.int32))

    count = jnp.int32(0)
    for step, (row_bits, col_bits) in enumerate(places):
        block = (my_row ^ row_bits) * n_col + (my_col ^ col_bits)
        word = words[0]
        for w in range(1, len(words)):
            word = jnp.where(block // 16 == w, words[w], word)
        list_ref[count] = step
        count += (word >> (block % 16)) & 1

    def visit(pair, _):
        blocks = [blocks_ref[list_ref[2 * pair]], blocks_ref[list_ref[2 * pair + 1]]]
        image_ref[...] += tile_image(left_ref, kern_ref, blocks)
        return 0

    lax.fori_loop(0, count // 2, visit, 0)

    @pl.when(count % 2 == 1)
    def _():
        image_ref[...] += tile_image(left_ref, kern_ref, [blocks_ref[list_ref[count - 1]]])


def part_kernel(
    places, sizes, table_ref, left_ref, blocks_ref, before_ref, image_ref, list_ref, kern_ref
):
    image_ref[...] = before_ref[...]
    add_blocks(places, sizes, table_ref, left_ref, blocks_ref, image_ref, list_ref, kern_ref)


def last_kernel(
    places, sizes, table_ref, left_ref, blocks_ref, before_ref, vectors_ref, root_ref,
    applied_ref, gram_ref, image_ref, list_ref, kern_ref,
):
    image_ref[...] = before_ref[...]
    add_blocks(places, sizes, table_ref, left_ref, blocks_ref, image_ref, list_ref, kern_ref)
    n = vectors_ref.shape[0]
    applied = image_ref[...].T * root_ref[...]
    applied_ref[...] = applied
    both = jnp.concatenate([applied, vectors_ref[...].astype(jnp.float32)], axis=0)
    gram = lax.dot_general(
        both, both, NT, precision=lax.Precision.HIGHEST, preferred_element_type=jnp.float32
    )
    wide = jnp.concatenate(
        [gram[:n, :n], gram[n:, :], jnp.zeros((n, n), jnp.float32)], axis=1
    )
    tile = jnp.concatenate([wide[: n // 2, :], wide[n // 2 :, :]], axis=1)
    for device in range(gram_ref.shape[0]):
        gram_ref[device] = tile


def inverse_factors(grams):
    n = grams[0].shape[0]
    half = 64
    tiles = range(n // 8)
    shape = (8, 2 * half)
    row = lax.broadcasted_iota(jnp.int32, shape, 0)
    lane = lax.broadcasted_iota(jnp.int32, shape, 1)
    columns = [
        [
            jnp.where(
                lane < half,
                jnp.broadcast_to(grams[0][8 * t : 8 * t + 8, j : j + 1], shape),
                jnp.broadcast_to(grams[1][8 * t : 8 * t + 8, j : j + 1], shape),
            )
            for t in tiles
        ]
        for j in range(n)
    ]
    right = [jnp.where(lane % half == row + 8 * t, 1.0, 0.0) for t in tiles]
    pivots = [jnp.ones(shape, jnp.float32) for t in tiles]
    for k in range(n):
        top, at = k // 8, k % 8
        pivot = columns[k][top][at : at + 1, :]
        pivots[top] = jnp.where(row == at, pivot, pivots[top])
        if k == n - 1:
            break
        scale = 1.0 / pivot
        factor = {t: columns[k][t] * scale for t in tiles if t >= top}
        factor[top] = jnp.where(row > at, factor[top], 0.0)
        for column in columns[k + 1 :] + [right]:
            line = column[top][at : at + 1, :]
            for t in factor:
                column[t] = column[t] - factor[t] * line
    result = jnp.concatenate([r * lax.rsqrt(p) for r, p in zip(right, pivots)], axis=0)
    return result[:, :n], result[:, half : half + n]


def finish_kernel(total_frames, grams_ref, applied_ref, basis_ref, ritz_ref):
    tile = grams_ref[0]
    for device in range(1, grams_ref.shape[0]):
        tile += grams_ref[device]
    n = applied_ref.shape[0]
    gram = jnp.concatenate([tile[:, : 4 * n], tile[:, 4 * n :]], axis=0)
    exact = functools.partial(
        lax.dot_general, precision=lax.Precision.HIGHEST, preferred_element_type=jnp.float32
    )
    plain = (((1,), (0,)), ((), ()))
    image_inverse, vector_inverse = inverse_factors([gram[:, :n], gram[:, 2 * n : 3 * n]])
    basis_ref[...] = exact(image_inverse * math.sqrt(total_frames), applied_ref[...], plain)
    half = exact(vector_inverse, gram[:, n : 2 * n], plain)
    ritz_ref[...] = exact(half, vector_inverse, NT)


def sent(x, hop):
    n_row, n_col = lax.axis_size("row"), lax.axis_size("col")
    pairs = [
        (r * n_col + c, (r ^ hop[0]) * n_col + (c ^ hop[1]))
        for r in range(n_row)
        for c in range(n_col)
    ]
    return lax.ppermute(x, ("row", "col"), pairs)


def beyond(offsets, hop):
    return [(r ^ hop[0], c ^ hop[1]) for r, c in offsets]


def exchange_plan(n_row, n_col):
    if (n_row, n_col) == (4, 4):
        direct = [(0, 3), (2, 1), (1, 1)]
        return direct, [((0, 3), [(1, 1), (2, 1)]), ((3, 1), [(0, 3)]), ((1, 1), [(2, 1)])]
    lines = [(r, 1) for r in range(1, n_row)]
    chips = [(0, c) for c in range(3, n_col, 2)]
    return chips + lines, [(chip, lines) for chip in chips]


def per_device(frames, vectors, degrees, tile_table):
    ncv, rows = frames.shape
    nvec = vectors.shape[0]
    n_row, n_col = lax.axis_size("row"), lax.axis_size("col")
    devices = n_row * n_col
    sizes = (n_row, n_col)
    vmem = pl.BlockSpec(memory_space=pltpu.VMEM)

    def call(kernel, name, outs, *args, limit=16, where=vmem, **keywords):
        shapes = [jax.ShapeDtypeStruct(*out) for out in outs]
        return pl.pallas_call(
            kernel,
            out_shape=shapes,
            in_specs=[where] * len(args),
            out_specs=[vmem] * len(outs),
            compiler_params=pltpu.CompilerParams(vmem_limit_bytes=limit * MIB),
            name=name,
            **keywords,
        )(*args)

    image_type = ((rows, nvec), jnp.float32)
    kern_scratch = pltpu.VMEM((rows, 2 * rows), jnp.bfloat16)

    table = tile_table.transpose(1, 2, 0)
    packed, vectors, root, table = call(
        pack_kernel,
        "pack",
        [
            ((ncv + nvec, rows), jnp.bfloat16),
            (vectors.shape, vectors.dtype),
            ((1, rows), jnp.float32),
            (table.shape, table.dtype),
        ],
        *(
            pltpu.with_memory_space_constraint(x, pltpu.HBM)
            for x in (frames, vectors, degrees, table)
        ),
        where=pl.BlockSpec(memory_space=pltpu.HBM),
        scratch_shapes=[
            pltpu.VMEM(degrees.shape, degrees.dtype),
            pltpu.SemaphoreType.DMA((4,)),
        ],
    )
    core = (0, 1)
    direct, forwards = exchange_plan(n_row, n_col)
    held = {offset: sent(packed, offset) for offset in direct}
    left, image = call(
        own_kernel,
        "own",
        [((rows, 3 * ncv + 16), jnp.bfloat16), image_type],
        packed,
        scratch_shapes=[kern_scratch],
    )

    def add(name, places, blocks, image):
        (image,) = call(
            functools.partial(part_kernel, places, sizes),
            name,
            [image_type],
            table,
            left,
            blocks,
            image,
            input_output_aliases={3: 0},
            scratch_shapes=[pltpu.SMEM((len(places) + 1,), jnp.int32), kern_scratch],
        )
        return image

    early, others = direct[0], direct[1:]
    held[early], image = lax.optimization_barrier((held[early], image))
    image = add("add_first", [early], held[early][None], image)
    rest, image = lax.optimization_barrier(([held[offset] for offset in others], image))
    held.update(zip(others, rest))
    across_places = []
    across = []
    for hop, offsets in forwards:
        across.append(sent(jnp.stack([held[offset] for offset in offsets]), hop))
        across_places += beyond(offsets, hop)
    other_near = sent(jnp.stack([packed] + [held[offset] for offset in direct]), core)
    near = jnp.concatenate([jnp.stack([held[offset] for offset in others]), other_near])
    image = add("add_near", others + beyond([(0, 0)] + direct, core), near, image)
    across, image = lax.optimization_barrier((across, image))
    across = jnp.concatenate(across)
    far = sent(across, core)
    image = add("add_across", across_places, across, image)
    far_places = beyond(across_places, core)
    applied, gram = call(
        functools.partial(last_kernel, far_places, sizes),
        "add_far",
        [((nvec, rows), jnp.float32), ((devices, nvec // 2, 8 * nvec), jnp.float32)],
        table,
        left,
        far,
        image,
        vectors,
        root,
        scratch_shapes=[
            pltpu.VMEM(*image_type),
            pltpu.SMEM((len(far_places) + 1,), jnp.int32),
            kern_scratch,
        ],
    )
    grams = lax.all_to_all(gram, ("row", "col"), 0, 0)
    basis, ritz = call(
        functools.partial(finish_kernel, rows * devices),
        "finish",
        [((nvec, rows), jnp.float32), ((nvec, nvec), jnp.float32)],
        grams,
        applied,
    )
    return (basis, ritz)


def solution(mesh):
    split = P(None, ("grp", "row", "col"))
    return jax.shard_map(
        per_device,
        mesh=mesh,
        in_specs=(split, split, P(("grp", "row", "col")), P()),
        out_specs=(split, P("grp", None)),
        check_vma=False,
    )
```

```python
import functools
import math

import jax
import jax.numpy as jnp
from jax import lax
from jax.experimental import pallas as pl
from jax.experimental.pallas import tpu as pltpu
from jax.sharding import PartitionSpec as P

unit = -math.log2(math.e) / 4.0

NT = (((1,), (1,)), ((), ()))
MIB = 1024 * 1024


def split3(x):
    high = x.astype(jnp.bfloat16).astype(jnp.float32)
    rest = x - high
    mid = rest.astype(jnp.bfloat16).astype(jnp.float32)
    low = (rest - mid).astype(jnp.bfloat16).astype(jnp.float32)
    return high, mid, low


def pack_kernel(
    frames_ref, vectors_in, degrees_ref, table_in,
    packed_ref, vectors_ref, root_ref, table_ref, degree_ref, sems,
):
    ncv = frames_ref.shape[0]
    copies = [
        pltpu.make_async_copy(vectors_in, vectors_ref, sems.at[0]),
        pltpu.make_async_copy(degrees_ref, degree_ref, sems.at[1]),
        pltpu.make_async_copy(frames_ref, packed_ref.at[pl.ds(0, ncv)], sems.at[2]),
        pltpu.make_async_copy(table_in, table_ref, sems.at[3]),
    ]
    for copy in copies:
        copy.start()
    copies[0].wait()
    copies[1].wait()
    root = lax.rsqrt(degree_ref[...])[None, :]
    root_ref[...] = root
    packed_ref[ncv:, :] = (vectors_ref[...].astype(jnp.float32) * root).astype(jnp.bfloat16)
    copies[2].wait()
    copies[3].wait()


def edge_rows(square, ones_first):
    high, mid, low = split3(square * unit)
    row = lax.broadcasted_iota(jnp.int32, (16, square.shape[1]), 0)
    base = 3 if ones_first else 0
    ones_at = 0 if ones_first else 3
    block = jnp.where((row >= ones_at) & (row < ones_at + 3), 1.0, 0.0)
    block = jnp.where(row == base, high, block)
    block = jnp.where(row == base + 1, mid, block)
    return jnp.where(row == base + 2, low, block)


def own_side(own):
    own = own.astype(jnp.float32)
    high, mid, low = split3(own * (-2.0 * unit))
    edge = edge_rows(jnp.sum(own * own, axis=0, keepdims=True), True)
    return jnp.concatenate([high, mid, low, edge], axis=0).T.astype(jnp.bfloat16)


def tile_image(left_ref, blocks):
    both = blocks[0] if len(blocks) == 1 else jnp.concatenate(blocks, axis=1)
    ncv = both.shape[0] // 2
    x, v = both[:ncv, :], both[ncv:, :]
    wide = x.astype(jnp.float32)
    edge = edge_rows(jnp.sum(wide * wide, axis=0, keepdims=True), False).astype(jnp.bfloat16)
    right = jnp.concatenate([x, x, x, edge], axis=0)
    power = jnp.dot(left_ref[...], right, preferred_element_type=jnp.float32)
    kern = jnp.exp2(power).astype(jnp.bfloat16)
    return lax.dot_general(kern, v, NT, preferred_element_type=jnp.float32)


def own_kernel(packed_ref, left_ref, image_ref):
    left_ref[...] = own_side(packed_ref[: packed_ref.shape[0] // 2, :])
    image_ref[...] = tile_image(left_ref, [packed_ref[...]])


def add_blocks(places, sizes, table_ref, left_ref, blocks_ref, image_ref, list_ref):
    n_row, n_col = sizes
    my_row, my_col = lax.axis_index("row"), lax.axis_index("col")
    me = my_row * n_col + my_col
    first, second = table_ref[:, 0, :], table_ref[:, 1, :]
    other = jnp.where(first == me, second, jnp.where(second == me, first, -1))
    words = []
    for start in range(0, n_row * n_col, 16):
        bit = jnp.zeros(other.shape, jnp.float32)
        for b in range(16):
            bit = jnp.where(other == start + b, float(1 << b), bit)
        words.append(jnp.sum(bit).astype(jnp.int32))

    count = jnp.int32(0)
    for step, (row_bits, col_bits) in enumerate(places):
        block = (my_row ^ row_bits) * n_col + (my_col ^ col_bits)
        word = words[0]
        for w in range(1, len(words)):
            word = jnp.where(block // 16 == w, words[w], word)
        list_ref[count] = step
        count += (word >> (block % 16)) & 1

    def visit(pair, _):
        blocks = [blocks_ref[list_ref[2 * pair]], blocks_ref[list_ref[2 * pair + 1]]]
        image_ref[...] += tile_image(left_ref, blocks)
        return 0

    lax.fori_loop(0, count // 2, visit, 0)

    @pl.when(count % 2 == 1)
    def _():
        image_ref[...] += tile_image(left_ref, [blocks_ref[list_ref[count - 1]]])


def part_kernel(places, sizes, table_ref, left_ref, blocks_ref, before_ref, image_ref, list_ref):
    image_ref[...] = before_ref[...]
    add_blocks(places, sizes, table_ref, left_ref, blocks_ref, image_ref, list_ref)


def last_kernel(
    places, sizes, table_ref, left_ref, blocks_ref, before_ref, vectors_ref, root_ref,
    applied_ref, gram_ref, image_ref, list_ref,
):
    image_ref[...] = before_ref[...]
    add_blocks(places, sizes, table_ref, left_ref, blocks_ref, image_ref, list_ref)
    n = vectors_ref.shape[0]
    applied = image_ref[...].T * root_ref[...]
    applied_ref[...] = applied
    both = jnp.concatenate([applied, vectors_ref[...].astype(jnp.float32)], axis=0)
    gram = lax.dot_general(
        both, both, NT, precision=lax.Precision.HIGHEST, preferred_element_type=jnp.float32
    )
    wide = jnp.concatenate(
        [gram[:n, :n], gram[n:, :], jnp.zeros((n, n), jnp.float32)], axis=1
    )
    tile = jnp.concatenate([wide[: n // 2, :], wide[n // 2 :, :]], axis=1)
    for device in range(gram_ref.shape[0]):
        gram_ref[device] = tile


def inverse_factors(grams):
    n = grams[0].shape[0]
    half = 64
    tiles = range(n // 8)
    shape = (8, 2 * half)
    row = lax.broadcasted_iota(jnp.int32, shape, 0)
    lane = lax.broadcasted_iota(jnp.int32, shape, 1)
    columns = [
        [
            jnp.where(
                lane < half,
                jnp.broadcast_to(grams[0][8 * t : 8 * t + 8, j : j + 1], shape),
                jnp.broadcast_to(grams[1][8 * t : 8 * t + 8, j : j + 1], shape),
            )
            for t in tiles
        ]
        for j in range(n)
    ]
    right = [jnp.where(lane % half == row + 8 * t, 1.0, 0.0) for t in tiles]
    pivots = [jnp.ones(shape, jnp.float32) for t in tiles]
    for k in range(n):
        top, at = k // 8, k % 8
        pivot = columns[k][top][at : at + 1, :]
        pivots[top] = jnp.where(row == at, pivot, pivots[top])
        if k == n - 1:
            break
        scale = 1.0 / pivot
        factor = {t: columns[k][t] * scale for t in tiles if t >= top}
        factor[top] = jnp.where(row > at, factor[top], 0.0)
        for column in columns[k + 1 :] + [right]:
            line = column[top][at : at + 1, :]
            for t in factor:
                column[t] = column[t] - factor[t] * line
    result = jnp.concatenate([r * lax.rsqrt(p) for r, p in zip(right, pivots)], axis=0)
    return result[:, :n], result[:, half : half + n]


def finish_kernel(total_frames, grams_ref, applied_ref, basis_ref, ritz_ref):
    tile = grams_ref[0]
    for device in range(1, grams_ref.shape[0]):
        tile += grams_ref[device]
    n = applied_ref.shape[0]
    gram = jnp.concatenate([tile[:, : 4 * n], tile[:, 4 * n :]], axis=0)
    exact = functools.partial(
        lax.dot_general, precision=lax.Precision.HIGHEST, preferred_element_type=jnp.float32
    )
    plain = (((1,), (0,)), ((), ()))
    image_inverse, vector_inverse = inverse_factors([gram[:, :n], gram[:, 2 * n : 3 * n]])
    basis_ref[...] = exact(image_inverse * math.sqrt(total_frames), applied_ref[...], plain)
    half = exact(vector_inverse, gram[:, n : 2 * n], plain)
    ritz_ref[...] = exact(half, vector_inverse, NT)


def sent(x, hop):
    n_row, n_col = lax.axis_size("row"), lax.axis_size("col")
    pairs = [
        (r * n_col + c, (r ^ hop[0]) * n_col + (c ^ hop[1]))
        for r in range(n_row)
        for c in range(n_col)
    ]
    return lax.ppermute(x, ("row", "col"), pairs)


def beyond(offsets, hop):
    return [(r ^ hop[0], c ^ hop[1]) for r, c in offsets]


def exchange_plan(n_row, n_col):
    if (n_row, n_col) == (4, 4):
        direct = [(0, 3), (1, 1), (3, 1), (2, 1)]
        return direct, [((0, 3), [(2, 1), (3, 1)]), ((1, 1), [(0, 3)])]
    lines = [(r, 1) for r in range(1, n_row)]
    chips = [(0, c) for c in range(3, n_col, 2)]
    return chips + lines, [(chip, lines) for chip in chips]


def per_device(frames, vectors, degrees, tile_table):
    ncv, rows = frames.shape
    nvec = vectors.shape[0]
    n_row, n_col = lax.axis_size("row"), lax.axis_size("col")
    devices = n_row * n_col
    sizes = (n_row, n_col)
    vmem = pl.BlockSpec(memory_space=pltpu.VMEM)

    def call(kernel, name, outs, *args, limit=16, where=vmem, **keywords):
        shapes = [jax.ShapeDtypeStruct(*out) for out in outs]
        return pl.pallas_call(
            kernel,
            out_shape=shapes,
            in_specs=[where] * len(args),
            out_specs=[vmem] * len(outs),
            compiler_params=pltpu.CompilerParams(vmem_limit_bytes=limit * MIB),
            name=name,
            **keywords,
        )(*args)

    image_type = ((rows, nvec), jnp.float32)

    table = tile_table.transpose(1, 2, 0)
    packed, vectors, root, table = call(
        pack_kernel,
        "pack",
        [
            ((ncv + nvec, rows), jnp.bfloat16),
            (vectors.shape, vectors.dtype),
            ((1, rows), jnp.float32),
            (table.shape, table.dtype),
        ],
        *(
            pltpu.with_memory_space_constraint(x, pltpu.HBM)
            for x in (frames, vectors, degrees, table)
        ),
        where=pl.BlockSpec(memory_space=pltpu.HBM),
        scratch_shapes=[
            pltpu.VMEM(degrees.shape, degrees.dtype),
            pltpu.SemaphoreType.DMA((4,)),
        ],
    )
    core = (0, 1)
    direct, forwards = exchange_plan(n_row, n_col)
    held = {offset: sent(packed, offset) for offset in direct}
    left, image = call(
        own_kernel,
        "own",
        [((rows, 3 * ncv + 16), jnp.bfloat16), image_type],
        packed,
    )

    def add(name, places, blocks, image):
        (image,) = call(
            functools.partial(part_kernel, places, sizes),
            name,
            [image_type],
            table,
            left,
            blocks,
            image,
            input_output_aliases={3: 0},
            scratch_shapes=[pltpu.SMEM((len(places) + 1,), jnp.int32)],
        )
        return image

    early, others = direct[0], direct[1:]
    held[early], image = lax.optimization_barrier((held[early], image))
    image = add("add_first", [early], held[early][None], image)
    rest, image = lax.optimization_barrier(([held[offset] for offset in others], image))
    held.update(zip(others, rest))
    across_places = []
    across = []
    for hop, offsets in forwards:
        across.append(sent(jnp.stack([held[offset] for offset in offsets]), hop))
        across_places += beyond(offsets, hop)
    other_near = sent(jnp.stack([packed] + [held[offset] for offset in direct]), core)
    near = jnp.concatenate([jnp.stack([held[offset] for offset in others]), other_near])
    image = add("add_near", others + beyond([(0, 0)] + direct, core), near, image)
    across, image = lax.optimization_barrier((across, image))
    across = jnp.concatenate(across)
    far = sent(across, core)
    image = add("add_across", across_places, across, image)
    far_places = beyond(across_places, core)
    applied, gram = call(
        functools.partial(last_kernel, far_places, sizes),
        "add_far",
        [((nvec, rows), jnp.float32), ((devices, nvec // 2, 8 * nvec), jnp.float32)],
        table,
        left,
        far,
        image,
        vectors,
        root,
        scratch_shapes=[
            pltpu.VMEM(*image_type),
            pltpu.SMEM((len(far_places) + 1,), jnp.int32),
        ],
    )
    grams = lax.all_to_all(gram, ("row", "col"), 0, 0)
    basis, ritz = call(
        functools.partial(finish_kernel, rows * devices),
        "finish",
        [((nvec, rows), jnp.float32), ((nvec, nvec), jnp.float32)],
        grams,
        applied,
    )
    return (basis, ritz)


def solution(mesh):
    split = P(None, ("grp", "row", "col"))
    return jax.shard_map(
        per_device,
        mesh=mesh,
        in_specs=(split, split, P(("grp", "row", "col")), P()),
        out_specs=(split, P("grp", None)),
        check_vma=False,
    )
```

```python
import functools
import math

import jax
import jax.numpy as jnp
from jax import lax
from jax.experimental import pallas as pl
from jax.experimental.pallas import tpu as pltpu
from jax.sharding import PartitionSpec as P

unit = -math.log2(math.e) / 4.0

NT = (((1,), (1,)), ((), ()))
MIB = 1024 * 1024


def split3(x):
    high = x.astype(jnp.bfloat16).astype(jnp.float32)
    rest = x - high
    mid = rest.astype(jnp.bfloat16).astype(jnp.float32)
    low = (rest - mid).astype(jnp.bfloat16).astype(jnp.float32)
    return high, mid, low


def pack_kernel(
    frames_ref, vectors_in, degrees_ref, table_in,
    packed_ref, vectors_ref, root_ref, table_ref, degree_ref, sems,
):
    ncv = frames_ref.shape[0]
    copies = [
        pltpu.make_async_copy(vectors_in, vectors_ref, sems.at[0]),
        pltpu.make_async_copy(degrees_ref, degree_ref, sems.at[1]),
        pltpu.make_async_copy(frames_ref, packed_ref.at[pl.ds(0, ncv)], sems.at[2]),
        pltpu.make_async_copy(table_in, table_ref, sems.at[3]),
    ]
    for copy in copies:
        copy.start()
    copies[0].wait()
    copies[1].wait()
    root = lax.rsqrt(degree_ref[...])[None, :]
    root_ref[...] = root
    packed_ref[ncv:, :] = (vectors_ref[...].astype(jnp.float32) * root).astype(jnp.bfloat16)
    copies[2].wait()
    copies[3].wait()


def edge_rows(square, ones_first):
    high, mid, low = split3(square * unit)
    row = lax.broadcasted_iota(jnp.int32, (16, square.shape[1]), 0)
    base = 3 if ones_first else 0
    ones_at = 0 if ones_first else 3
    block = jnp.where((row >= ones_at) & (row < ones_at + 3), 1.0, 0.0)
    block = jnp.where(row == base, high, block)
    block = jnp.where(row == base + 1, mid, block)
    return jnp.where(row == base + 2, low, block)


def own_side(own):
    own = own.astype(jnp.float32)
    high, mid, low = split3(own * (-2.0 * unit))
    edge = edge_rows(jnp.sum(own * own, axis=0, keepdims=True), True)
    return jnp.concatenate([high, mid, low, edge], axis=0).T.astype(jnp.bfloat16)


def tile_image(left_ref, blocks):
    both = blocks[0] if len(blocks) == 1 else jnp.concatenate(blocks, axis=1)
    ncv = both.shape[0] // 2
    x, v = both[:ncv, :], both[ncv:, :]
    wide = x.astype(jnp.float32)
    edge = edge_rows(jnp.sum(wide * wide, axis=0, keepdims=True), False).astype(jnp.bfloat16)
    right = jnp.concatenate([x, x, x, edge], axis=0)
    power = jnp.dot(left_ref[...], right, preferred_element_type=jnp.float32)
    kern = jnp.exp2(power).astype(jnp.bfloat16)
    return lax.dot_general(kern, v, NT, preferred_element_type=jnp.float32)


def own_kernel(packed_ref, left_ref, image_ref):
    left_ref[...] = own_side(packed_ref[: packed_ref.shape[0] // 2, :])
    image_ref[...] = tile_image(left_ref, [packed_ref[...]])


def add_blocks(places, sizes, table_ref, left_ref, blocks_ref, image_ref, list_ref):
    n_row, n_col = sizes
    my_row, my_col = lax.axis_index("row"), lax.axis_index("col")
    me = my_row * n_col + my_col
    first, second = table_ref[:, 0, :], table_ref[:, 1, :]
    other = jnp.where(first == me, second, jnp.where(second == me, first, -1))
    words = []
    for start in range(0, n_row * n_col, 16):
        bit = jnp.zeros(other.shape, jnp.float32)
        for b in range(16):
            bit = jnp.where(other == start + b, float(1 << b), bit)
        words.append(jnp.sum(bit).astype(jnp.int32))

    count = jnp.int32(0)
    for step, (row_bits, col_bits) in enumerate(places):
        block = (my_row ^ row_bits) * n_col + (my_col ^ col_bits)
        word = words[0]
        for w in range(1, len(words)):
            word = jnp.where(block // 16 == w, words[w], word)
        list_ref[count] = step
        count += (word >> (block % 16)) & 1

    def visit(pair, _):
        blocks = [blocks_ref[list_ref[2 * pair]], blocks_ref[list_ref[2 * pair + 1]]]
        image_ref[...] += tile_image(left_ref, blocks)
        return 0

    lax.fori_loop(0, count // 2, visit, 0)

    @pl.when(count % 2 == 1)
    def _():
        image_ref[...] += tile_image(left_ref, [blocks_ref[list_ref[count - 1]]])


def part_kernel(places, sizes, table_ref, left_ref, blocks_ref, before_ref, image_ref, list_ref):
    image_ref[...] = before_ref[...]
    add_blocks(places, sizes, table_ref, left_ref, blocks_ref, image_ref, list_ref)


def last_kernel(
    places, sizes, table_ref, left_ref, blocks_ref, before_ref, vectors_ref, root_ref,
    applied_ref, gram_ref, image_ref, list_ref,
):
    image_ref[...] = before_ref[...]
    add_blocks(places, sizes, table_ref, left_ref, blocks_ref, image_ref, list_ref)
    n = vectors_ref.shape[0]
    applied = image_ref[...].T * root_ref[...]
    applied_ref[...] = applied
    both = jnp.concatenate([applied, vectors_ref[...].astype(jnp.float32)], axis=0)
    gram = lax.dot_general(
        both, both, NT, precision=lax.Precision.HIGHEST, preferred_element_type=jnp.float32
    )
    wide = jnp.concatenate(
        [gram[:n, :n], gram[n:, :], jnp.zeros((n, n), jnp.float32)], axis=1
    )
    tile = jnp.concatenate([wide[: n // 2, :], wide[n // 2 :, :]], axis=1)
    for device in range(gram_ref.shape[0]):
        gram_ref[device] = tile


def inverse_factors(grams):
    n = grams[0].shape[0]
    half = 64
    tiles = range(n // 8)
    shape = (8, 2 * half)
    row = lax.broadcasted_iota(jnp.int32, shape, 0)
    lane = lax.broadcasted_iota(jnp.int32, shape, 1)
    columns = [
        [
            jnp.where(
                lane < half,
                jnp.broadcast_to(grams[0][8 * t : 8 * t + 8, j : j + 1], shape),
                jnp.broadcast_to(grams[1][8 * t : 8 * t + 8, j : j + 1], shape),
            )
            for t in tiles
        ]
        for j in range(n)
    ]
    right = [jnp.where(lane % half == row + 8 * t, 1.0, 0.0) for t in tiles]
    pivots = [jnp.ones(shape, jnp.float32) for t in tiles]
    for k in range(n):
        top, at = k // 8, k % 8
        pivot = columns[k][top][at : at + 1, :]
        pivots[top] = jnp.where(row == at, pivot, pivots[top])
        if k == n - 1:
            break
        scale = 1.0 / pivot
        factor = {t: columns[k][t] * scale for t in tiles if t >= top}
        factor[top] = jnp.where(row > at, factor[top], 0.0)
        for column in columns[k + 1 :] + [right]:
            line = column[top][at : at + 1, :]
            for t in factor:
                column[t] = column[t] - factor[t] * line
    result = jnp.concatenate([r * lax.rsqrt(p) for r, p in zip(right, pivots)], axis=0)
    return result[:, :n], result[:, half : half + n]


def finish_kernel(total_frames, grams_ref, applied_ref, basis_ref, ritz_ref):
    tile = grams_ref[0]
    for device in range(1, grams_ref.shape[0]):
        tile += grams_ref[device]
    n = applied_ref.shape[0]
    gram = jnp.concatenate([tile[:, : 4 * n], tile[:, 4 * n :]], axis=0)
    exact = functools.partial(
        lax.dot_general, precision=lax.Precision.HIGHEST, preferred_element_type=jnp.float32
    )
    plain = (((1,), (0,)), ((), ()))
    image_inverse, vector_inverse = inverse_factors([gram[:, :n], gram[:, 2 * n : 3 * n]])
    basis_ref[...] = exact(image_inverse * math.sqrt(total_frames), applied_ref[...], plain)
    half = exact(vector_inverse, gram[:, n : 2 * n], plain)
    ritz_ref[...] = exact(half, vector_inverse, NT)


def sent(x, hop):
    n_row, n_col = lax.axis_size("row"), lax.axis_size("col")
    pairs = [
        (r * n_col + c, (r ^ hop[0]) * n_col + (c ^ hop[1]))
        for r in range(n_row)
        for c in range(n_col)
    ]
    return lax.ppermute(x, ("row", "col"), pairs)


def beyond(offsets, hop):
    return [(r ^ hop[0], c ^ hop[1]) for r, c in offsets]


def exchange_plan(n_row, n_col):
    if (n_row, n_col) == (4, 4):
        direct = [(0, 3), (3, 1), (1, 1), (2, 1)]
        return direct, [((0, 3), [(2, 1), (3, 1)]), ((1, 1), [(0, 3)])]
    lines = [(r, 1) for r in range(1, n_row)]
    chips = [(0, c) for c in range(3, n_col, 2)]
    return chips + lines, [(chip, lines) for chip in chips]


def per_device(frames, vectors, degrees, tile_table):
    ncv, rows = frames.shape
    nvec = vectors.shape[0]
    n_row, n_col = lax.axis_size("row"), lax.axis_size("col")
    devices = n_row * n_col
    sizes = (n_row, n_col)
    vmem = pl.BlockSpec(memory_space=pltpu.VMEM)

    def call(kernel, name, outs, *args, limit=16, where=vmem, **keywords):
        shapes = [jax.ShapeDtypeStruct(*out) for out in outs]
        return pl.pallas_call(
            kernel,
            out_shape=shapes,
            in_specs=[where] * len(args),
            out_specs=[vmem] * len(outs),
            compiler_params=pltpu.CompilerParams(vmem_limit_bytes=limit * MIB),
            name=name,
            **keywords,
        )(*args)

    image_type = ((rows, nvec), jnp.float32)

    table = tile_table.transpose(1, 2, 0)
    packed, vectors, root, table = call(
        pack_kernel,
        "pack",
        [
            ((ncv + nvec, rows), jnp.bfloat16),
            (vectors.shape, vectors.dtype),
            ((1, rows), jnp.float32),
            (table.shape, table.dtype),
        ],
        *(
            pltpu.with_memory_space_constraint(x, pltpu.HBM)
            for x in (frames, vectors, degrees, table)
        ),
        where=pl.BlockSpec(memory_space=pltpu.HBM),
        scratch_shapes=[
            pltpu.VMEM(degrees.shape, degrees.dtype),
            pltpu.SemaphoreType.DMA((4,)),
        ],
    )
    core = (0, 1)
    direct, forwards = exchange_plan(n_row, n_col)
    held = {offset: sent(packed, offset) for offset in direct}
    left, image = call(
        own_kernel,
        "own",
        [((rows, 3 * ncv + 16), jnp.bfloat16), image_type],
        packed,
    )

    def add(name, places, blocks, image):
        (image,) = call(
            functools.partial(part_kernel, places, sizes),
            name,
            [image_type],
            table,
            left,
            blocks,
            image,
            input_output_aliases={3: 0},
            scratch_shapes=[pltpu.SMEM((len(places) + 1,), jnp.int32)],
        )
        return image

    early, others = direct[0], direct[1:]
    held[early], image = lax.optimization_barrier((held[early], image))
    image = add("add_first", [early], held[early][None], image)
    rest, image = lax.optimization_barrier(([held[offset] for offset in others], image))
    held.update(zip(others, rest))
    across_places = []
    across = []
    for hop, offsets in forwards:
        across.append(sent(jnp.stack([held[offset] for offset in offsets]), hop))
        across_places += beyond(offsets, hop)
    other_near = sent(jnp.stack([packed] + [held[offset] for offset in direct]), core)
    near = jnp.concatenate([jnp.stack([held[offset] for offset in others]), other_near])
    image = add("add_near", others + beyond([(0, 0)] + direct, core), near, image)
    across, image = lax.optimization_barrier((across, image))
    across = jnp.concatenate(across)
    far = sent(across, core)
    image = add("add_across", across_places, across, image)
    far_places = beyond(across_places, core)
    applied, gram = call(
        functools.partial(last_kernel, far_places, sizes),
        "add_far",
        [((nvec, rows), jnp.float32), ((devices, nvec // 2, 8 * nvec), jnp.float32)],
        table,
        left,
        far,
        image,
        vectors,
        root,
        scratch_shapes=[
            pltpu.VMEM(*image_type),
            pltpu.SMEM((len(far_places) + 1,), jnp.int32),
        ],
    )
    grams = lax.all_to_all(gram, ("row", "col"), 0, 0)
    basis, ritz = call(
        functools.partial(finish_kernel, rows * devices),
        "finish",
        [((nvec, rows), jnp.float32), ((nvec, nvec), jnp.float32)],
        grams,
        applied,
    )
    return (basis, ritz)


def solution(mesh):
    split = P(None, ("grp", "row", "col"))
    return jax.shard_map(
        per_device,
        mesh=mesh,
        in_specs=(split, split, P(("grp", "row", "col")), P()),
        out_specs=(split, P("grp", None)),
        check_vma=False,
    )
```

```python
import functools
import math

import jax
import jax.numpy as jnp
from jax import lax
from jax.experimental import pallas as pl
from jax.experimental.pallas import tpu as pltpu
from jax.sharding import PartitionSpec as P

unit = -math.log2(math.e) / 4.0

NT = (((1,), (1,)), ((), ()))
MIB = 1024 * 1024


def split3(x):
    high = x.astype(jnp.bfloat16).astype(jnp.float32)
    rest = x - high
    mid = rest.astype(jnp.bfloat16).astype(jnp.float32)
    low = (rest - mid).astype(jnp.bfloat16).astype(jnp.float32)
    return high, mid, low


def pack_kernel(
    frames_ref, vectors_in, degrees_ref, table_in,
    packed_ref, vectors_ref, root_ref, table_ref, degree_ref, sems,
):
    ncv = frames_ref.shape[0]
    copies = [
        pltpu.make_async_copy(vectors_in, vectors_ref, sems.at[0]),
        pltpu.make_async_copy(degrees_ref, degree_ref, sems.at[1]),
        pltpu.make_async_copy(frames_ref, packed_ref.at[pl.ds(0, ncv)], sems.at[2]),
        pltpu.make_async_copy(table_in, table_ref, sems.at[3]),
    ]
    for copy in copies:
        copy.start()
    copies[0].wait()
    copies[1].wait()
    root = lax.rsqrt(degree_ref[...])[None, :]
    root_ref[...] = root
    packed_ref[ncv:, :] = (vectors_ref[...].astype(jnp.float32) * root).astype(jnp.bfloat16)
    copies[2].wait()
    copies[3].wait()


def edge_rows(square, ones_first):
    high, mid, low = split3(square * unit)
    row = lax.broadcasted_iota(jnp.int32, (16, square.shape[1]), 0)
    base = 3 if ones_first else 0
    ones_at = 0 if ones_first else 3
    block = jnp.where((row >= ones_at) & (row < ones_at + 3), 1.0, 0.0)
    block = jnp.where(row == base, high, block)
    block = jnp.where(row == base + 1, mid, block)
    return jnp.where(row == base + 2, low, block)


def own_side(own):
    own = own.astype(jnp.float32)
    high, mid, low = split3(own * (-2.0 * unit))
    edge = edge_rows(jnp.sum(own * own, axis=0, keepdims=True), True)
    return jnp.concatenate([high, mid, low, edge], axis=0).astype(jnp.bfloat16)


def tile_image(side_ref, blocks):
    both = blocks[0] if len(blocks) == 1 else jnp.concatenate(blocks, axis=1)
    ncv = both.shape[0] // 2
    x, v = both[:ncv, :], both[ncv:, :]
    wide = x.astype(jnp.float32)
    edge = edge_rows(jnp.sum(wide * wide, axis=0, keepdims=True), False).astype(jnp.bfloat16)
    other = jnp.concatenate([x, x, x, edge], axis=0).T
    power = jnp.dot(other, side_ref[...], preferred_element_type=jnp.float32)
    kern = jnp.exp2(power).astype(jnp.bfloat16)
    return jnp.dot(v, kern, preferred_element_type=jnp.float32)


def own_kernel(packed_ref, side_ref, image_ref):
    side_ref[...] = own_side(packed_ref[: packed_ref.shape[0] // 2, :])
    image_ref[...] = tile_image(side_ref, [packed_ref[...]])


def add_blocks(places, sizes, table_ref, side_ref, blocks_ref, image_ref, list_ref):
    n_row, n_col = sizes
    my_row, my_col = lax.axis_index("row"), lax.axis_index("col")
    me = my_row * n_col + my_col
    first, second = table_ref[:, 0, :], table_ref[:, 1, :]
    other = jnp.where(first == me, second, jnp.where(second == me, first, -1))
    words = []
    for start in range(0, n_row * n_col, 16):
        bit = jnp.zeros(other.shape, jnp.float32)
        for b in range(16):
            bit = jnp.where(other == start + b, float(1 << b), bit)
        words.append(jnp.sum(bit).astype(jnp.int32))

    count = jnp.int32(0)
    for step, (row_bits, col_bits) in enumerate(places):
        block = (my_row ^ row_bits) * n_col + (my_col ^ col_bits)
        word = words[0]
        for w in range(1, len(words)):
            word = jnp.where(block // 16 == w, words[w], word)
        list_ref[count] = step
        count += (word >> (block % 16)) & 1

    def visit(pair, _):
        blocks = [blocks_ref[list_ref[2 * pair]], blocks_ref[list_ref[2 * pair + 1]]]
        image_ref[...] += tile_image(side_ref, blocks)
        return 0

    lax.fori_loop(0, count // 2, visit, 0)

    @pl.when(count % 2 == 1)
    def _():
        image_ref[...] += tile_image(side_ref, [blocks_ref[list_ref[count - 1]]])


def part_kernel(places, sizes, table_ref, side_ref, blocks_ref, before_ref, image_ref, list_ref):
    image_ref[...] = before_ref[...]
    add_blocks(places, sizes, table_ref, side_ref, blocks_ref, image_ref, list_ref)


def last_kernel(
    places, sizes, table_ref, side_ref, blocks_ref, before_ref, vectors_ref, root_ref,
    applied_ref, gram_ref, image_ref, list_ref,
):
    image_ref[...] = before_ref[...]
    add_blocks(places, sizes, table_ref, side_ref, blocks_ref, image_ref, list_ref)
    n = vectors_ref.shape[0]
    applied = image_ref[...] * root_ref[...]
    applied_ref[...] = applied
    both = jnp.concatenate([applied, vectors_ref[...].astype(jnp.float32)], axis=0)
    gram = lax.dot_general(
        both, both, NT, precision=lax.Precision.HIGHEST, preferred_element_type=jnp.float32
    )
    wide = jnp.concatenate(
        [gram[:n, :n], gram[n:, :], jnp.zeros((n, n), jnp.float32)], axis=1
    )
    tile = jnp.concatenate([wide[: n // 2, :], wide[n // 2 :, :]], axis=1)
    for device in range(gram_ref.shape[0]):
        gram_ref[device] = tile


def inverse_factors(grams):
    n = grams[0].shape[0]
    half = 64
    tiles = range(n // 8)
    shape = (8, 2 * half)
    row = lax.broadcasted_iota(jnp.int32, shape, 0)
    lane = lax.broadcasted_iota(jnp.int32, shape, 1)
    columns = [
        [
            jnp.where(
                lane < half,
                jnp.broadcast_to(grams[0][8 * t : 8 * t + 8, j : j + 1], shape),
                jnp.broadcast_to(grams[1][8 * t : 8 * t + 8, j : j + 1], shape),
            )
            for t in tiles
        ]
        for j in range(n)
    ]
    right = [jnp.where(lane % half == row + 8 * t, 1.0, 0.0) for t in tiles]
    pivots = [jnp.ones(shape, jnp.float32) for t in tiles]
    for k in range(n):
        top, at = k // 8, k % 8
        pivot = columns[k][top][at : at + 1, :]
        pivots[top] = jnp.where(row == at, pivot, pivots[top])
        if k == n - 1:
            break
        scale = 1.0 / pivot
        factor = {t: columns[k][t] * scale for t in tiles if t >= top}
        factor[top] = jnp.where(row > at, factor[top], 0.0)
        for column in columns[k + 1 :] + [right]:
            line = column[top][at : at + 1, :]
            for t in factor:
                column[t] = column[t] - factor[t] * line
    result = jnp.concatenate([r * lax.rsqrt(p) for r, p in zip(right, pivots)], axis=0)
    return result[:, :n], result[:, half : half + n]


def finish_kernel(total_frames, grams_ref, applied_ref, basis_ref, ritz_ref):
    tile = grams_ref[0]
    for device in range(1, grams_ref.shape[0]):
        tile += grams_ref[device]
    n = applied_ref.shape[0]
    gram = jnp.concatenate([tile[:, : 4 * n], tile[:, 4 * n :]], axis=0)
    exact = functools.partial(
        lax.dot_general, precision=lax.Precision.HIGHEST, preferred_element_type=jnp.float32
    )
    plain = (((1,), (0,)), ((), ()))
    image_inverse, vector_inverse = inverse_factors([gram[:, :n], gram[:, 2 * n : 3 * n]])
    basis_ref[...] = exact(image_inverse * math.sqrt(total_frames), applied_ref[...], plain)
    half = exact(vector_inverse, gram[:, n : 2 * n], plain)
    ritz_ref[...] = exact(half, vector_inverse, NT)


def sent(x, hop):
    n_row, n_col = lax.axis_size("row"), lax.axis_size("col")
    pairs = [
        (r * n_col + c, (r ^ hop[0]) * n_col + (c ^ hop[1]))
        for r in range(n_row)
        for c in range(n_col)
    ]
    return lax.ppermute(x, ("row", "col"), pairs)


def beyond(offsets, hop):
    return [(r ^ hop[0], c ^ hop[1]) for r, c in offsets]


def exchange_plan(n_row, n_col):
    if (n_row, n_col) == (4, 4):
        direct = [(0, 3), (2, 1), (1, 1)]
        return direct, [((0, 3), [(1, 1), (2, 1)]), ((3, 1), [(0, 3)]), ((1, 1), [(2, 1)])]
    lines = [(r, 1) for r in range(1, n_row)]
    chips = [(0, c) for c in range(3, n_col, 2)]
    return chips + lines, [(chip, lines) for chip in chips]


def per_device(frames, vectors, degrees, tile_table):
    ncv, rows = frames.shape
    nvec = vectors.shape[0]
    n_row, n_col = lax.axis_size("row"), lax.axis_size("col")
    devices = n_row * n_col
    sizes = (n_row, n_col)
    vmem = pl.BlockSpec(memory_space=pltpu.VMEM)

    def call(kernel, name, outs, *args, limit=16, where=vmem, **keywords):
        shapes = [jax.ShapeDtypeStruct(*out) for out in outs]
        return pl.pallas_call(
            kernel,
            out_shape=shapes,
            in_specs=[where] * len(args),
            out_specs=[vmem] * len(outs),
            compiler_params=pltpu.CompilerParams(vmem_limit_bytes=limit * MIB),
            name=name,
            **keywords,
        )(*args)

    image_type = ((nvec, rows), jnp.float32)

    table = tile_table.transpose(1, 2, 0)
    packed, vectors, root, table = call(
        pack_kernel,
        "pack",
        [
            ((ncv + nvec, rows), jnp.bfloat16),
            (vectors.shape, vectors.dtype),
            ((1, rows), jnp.float32),
            (table.shape, table.dtype),
        ],
        *(
            pltpu.with_memory_space_constraint(x, pltpu.HBM)
            for x in (frames, vectors, degrees, table)
        ),
        where=pl.BlockSpec(memory_space=pltpu.HBM),
        scratch_shapes=[
            pltpu.VMEM(degrees.shape, degrees.dtype),
            pltpu.SemaphoreType.DMA((4,)),
        ],
    )
    core = (0, 1)
    direct, forwards = exchange_plan(n_row, n_col)
    held = {offset: sent(packed, offset) for offset in direct}
    side, image = call(
        own_kernel,
        "own",
        [((3 * ncv + 16, rows), jnp.bfloat16), image_type],
        packed,
    )

    def add(name, places, blocks, image):
        (image,) = call(
            functools.partial(part_kernel, places, sizes),
            name,
            [image_type],
            table,
            side,
            blocks,
            image,
            input_output_aliases={3: 0},
            scratch_shapes=[pltpu.SMEM((len(places) + 1,), jnp.int32)],
        )
        return image

    early, others = direct[0], direct[1:]
    held[early], image = lax.optimization_barrier((held[early], image))
    image = add("add_first", [early], held[early][None], image)
    rest, image = lax.optimization_barrier(([held[offset] for offset in others], image))
    held.update(zip(others, rest))
    across_places = []
    across = []
    for hop, offsets in forwards:
        across.append(sent(jnp.stack([held[offset] for offset in offsets]), hop))
        across_places += beyond(offsets, hop)
    other_near = sent(jnp.stack([packed] + [held[offset] for offset in direct]), core)
    near = jnp.concatenate([jnp.stack([held[offset] for offset in others]), other_near])
    image = add("add_near", others + beyond([(0, 0)] + direct, core), near, image)
    across, image = lax.optimization_barrier((across, image))
    across = jnp.concatenate(across)
    far = sent(across, core)
    image = add("add_across", across_places, across, image)
    far_places = beyond(across_places, core)
    applied, gram = call(
        functools.partial(last_kernel, far_places, sizes),
        "add_far",
        [((nvec, rows), jnp.float32), ((devices, nvec // 2, 8 * nvec), jnp.float32)],
        table,
        side,
        far,
        image,
        vectors,
        root,
        scratch_shapes=[
            pltpu.VMEM(*image_type),
            pltpu.SMEM((len(far_places) + 1,), jnp.int32),
        ],
    )
    grams = lax.all_to_all(gram, ("row", "col"), 0, 0)
    basis, ritz = call(
        functools.partial(finish_kernel, rows * devices),
        "finish",
        [((nvec, rows), jnp.float32), ((nvec, nvec), jnp.float32)],
        grams,
        applied,
    )
    return (basis, ritz)


def solution(mesh):
    split = P(None, ("grp", "row", "col"))
    return jax.shard_map(
        per_device,
        mesh=mesh,
        in_specs=(split, split, P(("grp", "row", "col")), P()),
        out_specs=(split, P("grp", None)),
        check_vma=False,
    )
```

```python
import functools
import math

import jax
import jax.numpy as jnp
from jax import lax
from jax.experimental import pallas as pl
from jax.experimental.pallas import tpu as pltpu
from jax.sharding import PartitionSpec as P

unit = -math.log2(math.e) / 4.0

NT = (((1,), (1,)), ((), ()))
MIB = 1024 * 1024


def split3(x):
    high = x.astype(jnp.bfloat16).astype(jnp.float32)
    rest = x - high
    mid = rest.astype(jnp.bfloat16).astype(jnp.float32)
    low = (rest - mid).astype(jnp.bfloat16).astype(jnp.float32)
    return high, mid, low


def pack_kernel(
    frames_ref, vectors_in, degrees_ref, table_in,
    packed_ref, vectors_ref, root_ref, table_ref, degree_ref, sems,
):
    ncv = frames_ref.shape[0]
    copies = [
        pltpu.make_async_copy(vectors_in, vectors_ref, sems.at[0]),
        pltpu.make_async_copy(degrees_ref, degree_ref, sems.at[1]),
        pltpu.make_async_copy(frames_ref, packed_ref.at[pl.ds(0, ncv)], sems.at[2]),
        pltpu.make_async_copy(table_in, table_ref, sems.at[3]),
    ]
    for copy in copies:
        copy.start()
    copies[0].wait()
    copies[1].wait()
    root = lax.rsqrt(degree_ref[...])[None, :]
    root_ref[...] = root
    packed_ref[ncv:, :] = (vectors_ref[...].astype(jnp.float32) * root).astype(jnp.bfloat16)
    copies[2].wait()
    copies[3].wait()


def edge_rows(square, ones_first):
    high, mid, low = split3(square * unit)
    row = lax.broadcasted_iota(jnp.int32, (16, square.shape[1]), 0)
    base = 3 if ones_first else 0
    ones_at = 0 if ones_first else 3
    block = jnp.where((row >= ones_at) & (row < ones_at + 3), 1.0, 0.0)
    block = jnp.where(row == base, high, block)
    block = jnp.where(row == base + 1, mid, block)
    return jnp.where(row == base + 2, low, block)


def own_side(own):
    own = own.astype(jnp.float32)
    high, mid, low = split3(own * (-2.0 * unit))
    edge = edge_rows(jnp.sum(own * own, axis=0, keepdims=True), True)
    return jnp.concatenate([high, mid, low, edge], axis=0).astype(jnp.bfloat16)


def tile_image(side_ref, blocks):
    both = blocks[0] if len(blocks) == 1 else jnp.concatenate(blocks, axis=1)
    ncv = both.shape[0] // 2
    x, v = both[:ncv, :], both[ncv:, :]
    wide = x.astype(jnp.float32)
    edge = edge_rows(jnp.sum(wide * wide, axis=0, keepdims=True), False).astype(jnp.bfloat16)
    other = jnp.concatenate([x, x, x, edge], axis=0).T
    power = jnp.dot(other, side_ref[...], preferred_element_type=jnp.float32)
    kern = jnp.exp2(power).astype(jnp.bfloat16)
    return jnp.dot(v, kern, preferred_element_type=jnp.float32)


def own_kernel(packed_ref, side_ref, image_ref):
    side_ref[...] = own_side(packed_ref[: packed_ref.shape[0] // 2, :])
    image_ref[...] = tile_image(side_ref, [packed_ref[...]])


def add_blocks(places, sizes, table_ref, side_ref, blocks_ref, image_ref, list_ref):
    n_row, n_col = sizes
    my_row, my_col = lax.axis_index("row"), lax.axis_index("col")
    me = my_row * n_col + my_col
    first, second = table_ref[:, 0, :], table_ref[:, 1, :]
    other = jnp.where(first == me, second, jnp.where(second == me, first, -1))
    words = []
    for start in range(0, n_row * n_col, 16):
        bit = jnp.zeros(other.shape, jnp.float32)
        for b in range(16):
            bit = jnp.where(other == start + b, float(1 << b), bit)
        words.append(jnp.sum(bit).astype(jnp.int32))

    count = jnp.int32(0)
    for step, (row_bits, col_bits) in enumerate(places):
        block = (my_row ^ row_bits) * n_col + (my_col ^ col_bits)
        word = words[0]
        for w in range(1, len(words)):
            word = jnp.where(block // 16 == w, words[w], word)
        list_ref[count] = step
        count += (word >> (block % 16)) & 1

    def add_group(start, size):
        blocks = [blocks_ref[list_ref[start + k]] for k in range(size)]
        image_ref[...] += tile_image(side_ref, blocks)

    def add_triple(group, _):
        add_group(3 * group, 3)
        return 0

    def add_pair(group, _):
        add_group(3 * triples + 2 * group, 2)
        return 0

    triples = jnp.maximum(count // 3 - (count % 3 == 1).astype(jnp.int32), 0)
    rest = count - 3 * triples
    lax.fori_loop(0, triples, add_triple, 0)
    lax.fori_loop(0, rest // 2, add_pair, 0)

    @pl.when(rest == 1)
    def _():
        add_group(0, 1)


def part_kernel(places, sizes, table_ref, side_ref, blocks_ref, before_ref, image_ref, list_ref):
    image_ref[...] = before_ref[...]
    add_blocks(places, sizes, table_ref, side_ref, blocks_ref, image_ref, list_ref)


def last_kernel(
    places, sizes, table_ref, side_ref, blocks_ref, before_ref, vectors_ref, root_ref,
    applied_ref, gram_ref, image_ref, list_ref,
):
    image_ref[...] = before_ref[...]
    add_blocks(places, sizes, table_ref, side_ref, blocks_ref, image_ref, list_ref)
    n = vectors_ref.shape[0]
    applied = image_ref[...] * root_ref[...]
    applied_ref[...] = applied
    both = jnp.concatenate([applied, vectors_ref[...].astype(jnp.float32)], axis=0)
    gram = lax.dot_general(
        both, both, NT, precision=lax.Precision.HIGHEST, preferred_element_type=jnp.float32
    )
    wide = jnp.concatenate(
        [gram[:n, :n], gram[n:, :], jnp.zeros((n, n), jnp.float32)], axis=1
    )
    tile = jnp.concatenate([wide[: n // 2, :], wide[n // 2 :, :]], axis=1)
    for device in range(gram_ref.shape[0]):
        gram_ref[device] = tile


def inverse_factors(grams):
    n = grams[0].shape[0]
    half = 64
    tiles = range(n // 8)
    shape = (8, 2 * half)
    row = lax.broadcasted_iota(jnp.int32, shape, 0)
    lane = lax.broadcasted_iota(jnp.int32, shape, 1)
    columns = [
        [
            jnp.where(
                lane < half,
                jnp.broadcast_to(grams[0][8 * t : 8 * t + 8, j : j + 1], shape),
                jnp.broadcast_to(grams[1][8 * t : 8 * t + 8, j : j + 1], shape),
            )
            for t in tiles
        ]
        for j in range(n)
    ]
    right = [jnp.where(lane % half == row + 8 * t, 1.0, 0.0) for t in tiles]
    pivots = [jnp.ones(shape, jnp.float32) for t in tiles]
    for k in range(n):
        top, at = k // 8, k % 8
        pivot = columns[k][top][at : at + 1, :]
        pivots[top] = jnp.where(row == at, pivot, pivots[top])
        if k == n - 1:
            break
        scale = 1.0 / pivot
        factor = {t: columns[k][t] * scale for t in tiles if t >= top}
        factor[top] = jnp.where(row > at, factor[top], 0.0)
        for column in columns[k + 1 :] + [right]:
            line = column[top][at : at + 1, :]
            for t in factor:
                column[t] = column[t] - factor[t] * line
    result = jnp.concatenate([r * lax.rsqrt(p) for r, p in zip(right, pivots)], axis=0)
    return result[:, :n], result[:, half : half + n]


def finish_kernel(total_frames, grams_ref, applied_ref, basis_ref, ritz_ref):
    tile = grams_ref[0]
    for device in range(1, grams_ref.shape[0]):
        tile += grams_ref[device]
    n = applied_ref.shape[0]
    gram = jnp.concatenate([tile[:, : 4 * n], tile[:, 4 * n :]], axis=0)
    exact = functools.partial(
        lax.dot_general, precision=lax.Precision.HIGHEST, preferred_element_type=jnp.float32
    )
    plain = (((1,), (0,)), ((), ()))
    image_inverse, vector_inverse = inverse_factors([gram[:, :n], gram[:, 2 * n : 3 * n]])
    basis_ref[...] = exact(image_inverse * math.sqrt(total_frames), applied_ref[...], plain)
    half = exact(vector_inverse, gram[:, n : 2 * n], plain)
    ritz_ref[...] = exact(half, vector_inverse, NT)


def sent(x, hop):
    n_row, n_col = lax.axis_size("row"), lax.axis_size("col")
    pairs = [
        (r * n_col + c, (r ^ hop[0]) * n_col + (c ^ hop[1]))
        for r in range(n_row)
        for c in range(n_col)
    ]
    return lax.ppermute(x, ("row", "col"), pairs)


def beyond(offsets, hop):
    return [(r ^ hop[0], c ^ hop[1]) for r, c in offsets]


def exchange_plan(n_row, n_col):
    if (n_row, n_col) == (4, 4):
        direct = [(0, 3), (2, 1), (1, 1)]
        return direct, [((0, 3), [(1, 1), (2, 1)]), ((3, 1), [(0, 3)]), ((1, 1), [(2, 1)])]
    lines = [(r, 1) for r in range(1, n_row)]
    chips = [(0, c) for c in range(3, n_col, 2)]
    return chips + lines, [(chip, lines) for chip in chips]


def per_device(frames, vectors, degrees, tile_table):
    ncv, rows = frames.shape
    nvec = vectors.shape[0]
    n_row, n_col = lax.axis_size("row"), lax.axis_size("col")
    devices = n_row * n_col
    sizes = (n_row, n_col)
    vmem = pl.BlockSpec(memory_space=pltpu.VMEM)

    def call(kernel, name, outs, *args, limit=24, where=vmem, **keywords):
        shapes = [jax.ShapeDtypeStruct(*out) for out in outs]
        return pl.pallas_call(
            kernel,
            out_shape=shapes,
            in_specs=[where] * len(args),
            out_specs=[vmem] * len(outs),
            compiler_params=pltpu.CompilerParams(vmem_limit_bytes=limit * MIB),
            name=name,
            **keywords,
        )(*args)

    image_type = ((nvec, rows), jnp.float32)

    table = tile_table.transpose(1, 2, 0)
    packed, vectors, root, table = call(
        pack_kernel,
        "pack",
        [
            ((ncv + nvec, rows), jnp.bfloat16),
            (vectors.shape, vectors.dtype),
            ((1, rows), jnp.float32),
            (table.shape, table.dtype),
        ],
        *(
            pltpu.with_memory_space_constraint(x, pltpu.HBM)
            for x in (frames, vectors, degrees, table)
        ),
        where=pl.BlockSpec(memory_space=pltpu.HBM),
        scratch_shapes=[
            pltpu.VMEM(degrees.shape, degrees.dtype),
            pltpu.SemaphoreType.DMA((4,)),
        ],
    )
    core = (0, 1)
    direct, forwards = exchange_plan(n_row, n_col)
    held = {offset: sent(packed, offset) for offset in direct}
    side, image = call(
        own_kernel,
        "own",
        [((3 * ncv + 16, rows), jnp.bfloat16), image_type],
        packed,
    )

    def add(name, places, blocks, image):
        (image,) = call(
            functools.partial(part_kernel, places, sizes),
            name,
            [image_type],
            table,
            side,
            blocks,
            image,
            input_output_aliases={3: 0},
            scratch_shapes=[pltpu.SMEM((len(places) + 1,), jnp.int32)],
        )
        return image

    early, others = direct[0], direct[1:]
    held[early], image = lax.optimization_barrier((held[early], image))
    image = add("add_first", [early], held[early][None], image)
    rest, image = lax.optimization_barrier(([held[offset] for offset in direct], image))
    held.update(zip(direct, rest))
    across_places = []
    across = []
    for hop, offsets in forwards:
        across.append(sent(jnp.stack([held[offset] for offset in offsets]), hop))
        across_places += beyond(offsets, hop)
    near = jnp.stack([held[offset] for offset in others + [early]] + [packed])
    other_near = sent(near, core)
    image = add("add_near", others, near, image)
    image = add("add_core", beyond(others + [early, (0, 0)], core), other_near, image)
    across, image = lax.optimization_barrier((across, image))
    across = jnp.concatenate(across)
    far = sent(across, core)
    image = add("add_across", across_places, across, image)
    far_places = beyond(across_places, core)
    applied, gram = call(
        functools.partial(last_kernel, far_places, sizes),
        "add_far",
        [((nvec, rows), jnp.float32), ((devices, nvec // 2, 8 * nvec), jnp.float32)],
        table,
        side,
        far,
        image,
        vectors,
        root,
        scratch_shapes=[
            pltpu.VMEM(*image_type),
            pltpu.SMEM((len(far_places) + 1,), jnp.int32),
        ],
    )
    grams = lax.all_to_all(gram, ("row", "col"), 0, 0)
    basis, ritz = call(
        functools.partial(finish_kernel, rows * devices),
        "finish",
        [((nvec, rows), jnp.float32), ((nvec, nvec), jnp.float32)],
        grams,
        applied,
    )
    return (basis, ritz)


def solution(mesh):
    split = P(None, ("grp", "row", "col"))
    return jax.shard_map(
        per_device,
        mesh=mesh,
        in_specs=(split, split, P(("grp", "row", "col")), P()),
        out_specs=(split, P("grp", None)),
        check_vma=False,
    )
```

```python
import functools
import math

import jax
import jax.numpy as jnp
from jax import lax
from jax.experimental import pallas as pl
from jax.experimental.pallas import tpu as pltpu
from jax.sharding import PartitionSpec as P

unit = -math.log2(math.e) / 4.0

NT = (((1,), (1,)), ((), ()))
MIB = 1024 * 1024


def split3(x):
    high = x.astype(jnp.bfloat16).astype(jnp.float32)
    rest = x - high
    mid = rest.astype(jnp.bfloat16).astype(jnp.float32)
    low = (rest - mid).astype(jnp.bfloat16).astype(jnp.float32)
    return high, mid, low


def pack_kernel(
    frames_ref, vectors_in, degrees_ref, table_in,
    packed_ref, vectors_ref, root_ref, table_ref, degree_ref, sems,
):
    ncv = frames_ref.shape[0]
    copies = [
        pltpu.make_async_copy(vectors_in, vectors_ref, sems.at[0]),
        pltpu.make_async_copy(degrees_ref, degree_ref, sems.at[1]),
        pltpu.make_async_copy(frames_ref, packed_ref.at[pl.ds(0, ncv)], sems.at[2]),
        pltpu.make_async_copy(table_in, table_ref, sems.at[3]),
    ]
    for copy in copies:
        copy.start()
    copies[0].wait()
    copies[1].wait()
    root = lax.rsqrt(degree_ref[...])[None, :]
    root_ref[...] = root
    packed_ref[ncv:, :] = (vectors_ref[...].astype(jnp.float32) * root).astype(jnp.bfloat16)
    copies[2].wait()
    copies[3].wait()


def edge_rows(square, ones_first):
    high, mid, low = split3(square * unit)
    row = lax.broadcasted_iota(jnp.int32, (16, square.shape[1]), 0)
    base = 3 if ones_first else 0
    ones_at = 0 if ones_first else 3
    block = jnp.where((row >= ones_at) & (row < ones_at + 3), 1.0, 0.0)
    block = jnp.where(row == base, high, block)
    block = jnp.where(row == base + 1, mid, block)
    return jnp.where(row == base + 2, low, block)


def own_side(own):
    own = own.astype(jnp.float32)
    high, mid, low = split3(own * (-2.0 * unit))
    edge = edge_rows(jnp.sum(own * own, axis=0, keepdims=True), True)
    return jnp.concatenate([high, mid, low, edge], axis=0).astype(jnp.bfloat16)


def tile_image(side_ref, blocks):
    both = blocks[0] if len(blocks) == 1 else jnp.concatenate(blocks, axis=1)
    ncv = both.shape[0] // 2
    x, v = both[:ncv, :], both[ncv:, :]
    wide = x.astype(jnp.float32)
    edge = edge_rows(jnp.sum(wide * wide, axis=0, keepdims=True), False).astype(jnp.bfloat16)
    other = jnp.concatenate([x, x, x, edge], axis=0).T
    power = jnp.dot(other, side_ref[...], preferred_element_type=jnp.float32)
    kern = jnp.exp2(power).astype(jnp.bfloat16)
    return jnp.dot(v, kern, preferred_element_type=jnp.float32)


def own_kernel(packed_ref, side_ref, image_ref):
    side_ref[...] = own_side(packed_ref[: packed_ref.shape[0] // 2, :])
    image_ref[...] = tile_image(side_ref, [packed_ref[...]])


def add_blocks(target, places, sizes, table_ref, side_ref, blocks_ref, image_ref, list_ref):
    n_row, n_col = sizes
    my_row, my_col = lax.axis_index("row"), lax.axis_index("col")

    def number(offset):
        return (my_row ^ offset[0]) * n_col + (my_col ^ offset[1])

    first, second = table_ref[:, 0, :], table_ref[:, 1, :]
    me = number(target)
    other = jnp.where(first == me, second, jnp.where(second == me, first, -1))
    words = []
    for start in range(0, n_row * n_col, 16):
        bit = jnp.zeros(other.shape, jnp.float32)
        for b in range(16):
            bit = jnp.where(other == start + b, float(1 << b), bit)
        words.append(jnp.sum(bit).astype(jnp.int32))

    count = jnp.int32(0)
    for step, place in enumerate(places):
        block = number(place)
        word = words[0]
        for w in range(1, len(words)):
            word = jnp.where(block // 16 == w, words[w], word)
        list_ref[count] = step
        count += (word >> (block % 16)) & 1

    def add_group(start, size):
        blocks = [blocks_ref[list_ref[start + k]] for k in range(size)]
        image_ref[...] += tile_image(side_ref, blocks)

    def add_triple(group, _):
        add_group(3 * group, 3)
        return 0

    def add_pair(group, _):
        add_group(3 * triples + 2 * group, 2)
        return 0

    triples = jnp.maximum(count // 3 - (count % 3 == 1).astype(jnp.int32), 0)
    rest = count - 3 * triples
    if len(places) >= 3:
        lax.fori_loop(0, triples, add_triple, 0)
    if len(places) >= 2:
        lax.fori_loop(0, rest // 2, add_pair, 0)

    @pl.when(rest == 1)
    def _():
        add_group(0, 1)


def meet_kernel(
    places, sizes, table_ref, side_ref, blocks_ref, before_ref, image_ref, partner_side_ref, list_ref
):
    partner_side_ref[...] = own_side(blocks_ref[0, : blocks_ref.shape[1] // 2, :])
    image_ref[...] = before_ref[...]
    add_blocks((0, 0), places, sizes, table_ref, side_ref, blocks_ref, image_ref, list_ref)


def first_kernel(target, places, sizes, table_ref, side_ref, blocks_ref, image_ref, list_ref):
    image_ref[...] = jnp.zeros_like(image_ref)
    add_blocks(target, places, sizes, table_ref, side_ref, blocks_ref, image_ref, list_ref)


def part_kernel(
    target, places, sizes, table_ref, side_ref, blocks_ref, before_ref, image_ref, list_ref
):
    image_ref[...] = before_ref[...]
    add_blocks(target, places, sizes, table_ref, side_ref, blocks_ref, image_ref, list_ref)


def last_kernel(vectors_ref, root_ref, *refs):
    *part_refs, applied_ref, gram_ref = refs
    image = sum(part_ref[...] for part_ref in part_refs)
    n = vectors_ref.shape[0]
    applied = image * root_ref[...]
    applied_ref[...] = applied
    both = jnp.concatenate([applied, vectors_ref[...].astype(jnp.float32)], axis=0)
    gram = lax.dot_general(
        both, both, NT, precision=lax.Precision.HIGHEST, preferred_element_type=jnp.float32
    )
    wide = jnp.concatenate(
        [gram[:n, :n], gram[n:, :], jnp.zeros((n, n), jnp.float32)], axis=1
    )
    tile = jnp.concatenate([wide[: n // 2, :], wide[n // 2 :, :]], axis=1)
    for device in range(gram_ref.shape[0]):
        gram_ref[device] = tile


def inverse_factors(grams):
    n = grams[0].shape[0]
    half = 64
    tiles = range(n // 8)
    shape = (8, 2 * half)
    row = lax.broadcasted_iota(jnp.int32, shape, 0)
    lane = lax.broadcasted_iota(jnp.int32, shape, 1)
    columns = [
        [
            jnp.where(
                lane < half,
                jnp.broadcast_to(grams[0][8 * t : 8 * t + 8, j : j + 1], shape),
                jnp.broadcast_to(grams[1][8 * t : 8 * t + 8, j : j + 1], shape),
            )
            for t in tiles
        ]
        for j in range(n)
    ]
    right = [jnp.where(lane % half == row + 8 * t, 1.0, 0.0) for t in tiles]
    pivots = [jnp.ones(shape, jnp.float32) for t in tiles]
    for k in range(n):
        top, at = k // 8, k % 8
        pivot = columns[k][top][at : at + 1, :]
        pivots[top] = jnp.where(row == at, pivot, pivots[top])
        if k == n - 1:
            break
        scale = 1.0 / pivot
        factor = {t: columns[k][t] * scale for t in tiles if t >= top}
        factor[top] = jnp.where(row > at, factor[top], 0.0)
        for column in columns[k + 1 :] + [right]:
            line = column[top][at : at + 1, :]
            for t in factor:
                column[t] = column[t] - factor[t] * line
    result = jnp.concatenate([r * lax.rsqrt(p) for r, p in zip(right, pivots)], axis=0)
    return result[:, :n], result[:, half : half + n]


def finish_kernel(total_frames, grams_ref, applied_ref, basis_ref, ritz_ref):
    tile = grams_ref[0]
    for device in range(1, grams_ref.shape[0]):
        tile += grams_ref[device]
    n = applied_ref.shape[0]
    gram = jnp.concatenate([tile[:, : 4 * n], tile[:, 4 * n :]], axis=0)
    exact = functools.partial(
        lax.dot_general, precision=lax.Precision.HIGHEST, preferred_element_type=jnp.float32
    )
    plain = (((1,), (0,)), ((), ()))
    image_inverse, vector_inverse = inverse_factors([gram[:, :n], gram[:, 2 * n : 3 * n]])
    basis_ref[...] = exact(image_inverse * math.sqrt(total_frames), applied_ref[...], plain)
    half = exact(vector_inverse, gram[:, n : 2 * n], plain)
    ritz_ref[...] = exact(half, vector_inverse, NT)


def sent(x, hop):
    n_row, n_col = lax.axis_size("row"), lax.axis_size("col")
    pairs = [
        (r * n_col + c, (r ^ hop[0]) * n_col + (c ^ hop[1]))
        for r in range(n_row)
        for c in range(n_col)
    ]
    return lax.ppermute(x, ("row", "col"), pairs)


def beyond(offsets, hop):
    return [(r ^ hop[0], c ^ hop[1]) for r, c in offsets]


def per_device(frames, vectors, degrees, tile_table):
    ncv, rows = frames.shape
    nvec = vectors.shape[0]
    n_row, n_col = lax.axis_size("row"), lax.axis_size("col")
    devices = n_row * n_col
    sizes = (n_row, n_col)
    vmem = pl.BlockSpec(memory_space=pltpu.VMEM)

    def call(kernel, name, outs, *args, limit=24, where=vmem, **keywords):
        shapes = [jax.ShapeDtypeStruct(*out) for out in outs]
        return pl.pallas_call(
            kernel,
            out_shape=shapes,
            in_specs=[where] * len(args),
            out_specs=[vmem] * len(outs),
            compiler_params=pltpu.CompilerParams(vmem_limit_bytes=limit * MIB),
            name=name,
            **keywords,
        )(*args)

    image_type = ((nvec, rows), jnp.float32)

    table = tile_table.transpose(1, 2, 0)
    packed, vectors, root, table = call(
        pack_kernel,
        "pack",
        [
            ((ncv + nvec, rows), jnp.bfloat16),
            (vectors.shape, vectors.dtype),
            ((1, rows), jnp.float32),
            (table.shape, table.dtype),
        ],
        *(
            pltpu.with_memory_space_constraint(x, pltpu.HBM)
            for x in (frames, vectors, degrees, table)
        ),
        where=pl.BlockSpec(memory_space=pltpu.HBM),
        scratch_shapes=[
            pltpu.VMEM(degrees.shape, degrees.dtype),
            pltpu.SemaphoreType.DMA((4,)),
        ],
    )
    core = (0, 1)
    lines = [(r, 1) for r in range(n_row - 1, 0, -1)]
    if n_row == 4:
        lines = [(3, 1), (1, 1), (2, 1)]
    partners = [(0, c) for c in range(3, n_col, 2)]
    met = [sent(packed, hop) for hop in partners]
    line = [sent(packed, hop) for hop in lines]

    def call_blocks(kernel, name, outs, places, *args, **keywords):
        return call(
            functools.partial(kernel, places, sizes),
            name,
            outs,
            table,
            *args,
            scratch_shapes=[pltpu.SMEM((len(places) + 1,), jnp.int32)],
            **keywords,
        )

    side_type = ((3 * ncv + 16, rows), jnp.bfloat16)
    side, image = call(own_kernel, "own", [side_type, image_type], packed)
    met, image = lax.optimization_barrier((met, image))
    sides = []
    for hop, block in zip(partners, met):
        image, partner_side = call_blocks(
            meet_kernel,
            "meet",
            [image_type, side_type],
            [hop],
            side,
            block[None],
            image,
            input_output_aliases={3: 0},
        )
        sides.append(partner_side)
    line, image = lax.optimization_barrier((line, image))
    near = jnp.stack(line)
    other = sent(jnp.stack(line + met + [packed]), core)
    other_lines = beyond(lines, core)
    parts = []
    for hop, partner_side in zip(partners, sides):
        (part,) = call_blocks(
            functools.partial(first_kernel, hop), "partner_near", [image_type], lines, partner_side, near
        )
        (part,) = call_blocks(
            functools.partial(part_kernel, hop),
            "partner_core",
            [image_type],
            other_lines,
            partner_side,
            other,
            part,
            input_output_aliases={3: 0},
        )
        parts.append(part)
    parts, image = lax.optimization_barrier((parts, image))
    received = [sent(part, hop) for hop, part in zip(partners, parts)]
    (image,) = call_blocks(
        functools.partial(part_kernel, (0, 0)),
        "add_own",
        [image_type],
        lines + beyond(lines + partners + [(0, 0)], core),
        side,
        jnp.concatenate([near, other]),
        image,
        input_output_aliases={3: 0},
    )
    applied, gram = call(
        last_kernel,
        "last",
        [((nvec, rows), jnp.float32), ((devices, nvec // 2, 8 * nvec), jnp.float32)],
        vectors,
        root,
        image,
        *received,
    )
    grams = lax.all_to_all(gram, ("row", "col"), 0, 0)
    basis, ritz = call(
        functools.partial(finish_kernel, rows * devices),
        "finish",
        [((nvec, rows), jnp.float32), ((nvec, nvec), jnp.float32)],
        grams,
        applied,
    )
    return (basis, ritz)


def solution(mesh):
    split = P(None, ("grp", "row", "col"))
    return jax.shard_map(
        per_device,
        mesh=mesh,
        in_specs=(split, split, P(("grp", "row", "col")), P()),
        out_specs=(split, P("grp", None)),
        check_vma=False,
    )
```

```python
import functools
import math

import jax
import jax.numpy as jnp
from jax import lax
from jax.experimental import pallas as pl
from jax.experimental.pallas import tpu as pltpu
from jax.sharding import PartitionSpec as P

unit = -math.log2(math.e) / 4.0

NT = (((1,), (1,)), ((), ()))
MIB = 1024 * 1024


def split3(x):
    high = x.astype(jnp.bfloat16).astype(jnp.float32)
    rest = x - high
    mid = rest.astype(jnp.bfloat16).astype(jnp.float32)
    low = (rest - mid).astype(jnp.bfloat16).astype(jnp.float32)
    return high, mid, low


def pack_kernel(
    frames_ref, vectors_in, degrees_ref, table_in,
    packed_ref, vectors_ref, root_ref, table_ref, degree_ref, sems,
):
    ncv = frames_ref.shape[0]
    copies = [
        pltpu.make_async_copy(vectors_in, vectors_ref, sems.at[0]),
        pltpu.make_async_copy(degrees_ref, degree_ref, sems.at[1]),
        pltpu.make_async_copy(frames_ref, packed_ref.at[pl.ds(0, ncv)], sems.at[2]),
        pltpu.make_async_copy(table_in, table_ref, sems.at[3]),
    ]
    for copy in copies:
        copy.start()
    copies[0].wait()
    copies[1].wait()
    root = lax.rsqrt(degree_ref[...])[None, :]
    root_ref[...] = root
    packed_ref[ncv:, :] = (vectors_ref[...].astype(jnp.float32) * root).astype(jnp.bfloat16)
    copies[2].wait()
    copies[3].wait()


def edge_rows(square, ones_first):
    high, mid, low = split3(square * unit)
    row = lax.broadcasted_iota(jnp.int32, (16, square.shape[1]), 0)
    base = 3 if ones_first else 0
    ones_at = 0 if ones_first else 3
    block = jnp.where((row >= ones_at) & (row < ones_at + 3), 1.0, 0.0)
    block = jnp.where(row == base, high, block)
    block = jnp.where(row == base + 1, mid, block)
    return jnp.where(row == base + 2, low, block)


def own_side(own):
    own = own.astype(jnp.float32)
    high, mid, low = split3(own * (-2.0 * unit))
    edge = edge_rows(jnp.sum(own * own, axis=0, keepdims=True), True)
    return jnp.concatenate([high, mid, low, edge], axis=0).astype(jnp.bfloat16)


def tile_image(side_ref, blocks):
    both = blocks[0] if len(blocks) == 1 else jnp.concatenate(blocks, axis=1)
    ncv = both.shape[0] // 2
    x, v = both[:ncv, :], both[ncv:, :]
    wide = x.astype(jnp.float32)
    edge = edge_rows(jnp.sum(wide * wide, axis=0, keepdims=True), False).astype(jnp.bfloat16)
    other = jnp.concatenate([x, x, x, edge], axis=0).T
    power = jnp.dot(other, side_ref[...], preferred_element_type=jnp.float32)
    kern = jnp.exp2(power).astype(jnp.bfloat16)
    return jnp.dot(v, kern, preferred_element_type=jnp.float32)


def own_kernel(packed_ref, side_ref, image_ref):
    side_ref[...] = own_side(packed_ref[: packed_ref.shape[0] // 2, :])
    image_ref[...] = tile_image(side_ref, [packed_ref[...]])


def add_blocks(target, places, sizes, table_ref, side_ref, blocks_ref, image_ref, list_ref):
    n_row, n_col = sizes
    my_row, my_col = lax.axis_index("row"), lax.axis_index("col")

    def number(offset):
        return (my_row ^ offset[0]) * n_col + (my_col ^ offset[1])

    first, second = table_ref[:, 0, :], table_ref[:, 1, :]
    me = number(target)
    other = jnp.where(first == me, second, jnp.where(second == me, first, -1))
    words = []
    for start in range(0, n_row * n_col, 16):
        bit = jnp.zeros(other.shape, jnp.float32)
        for b in range(16):
            bit = jnp.where(other == start + b, float(1 << b), bit)
        words.append(jnp.sum(bit).astype(jnp.int32))

    count = jnp.int32(0)
    for step, place in enumerate(places):
        block = number(place)
        word = words[0]
        for w in range(1, len(words)):
            word = jnp.where(block // 16 == w, words[w], word)
        list_ref[count] = step
        count += (word >> (block % 16)) & 1

    def add_group(start, size):
        blocks = [blocks_ref[list_ref[start + k]] for k in range(size)]
        image_ref[...] += tile_image(side_ref, blocks)

    def add_triple(group, _):
        add_group(3 * group, 3)
        return 0

    def add_pair(group, _):
        add_group(3 * triples + 2 * group, 2)
        return 0

    triples = jnp.maximum(count // 3 - (count % 3 == 1).astype(jnp.int32), 0)
    rest = count - 3 * triples
    if len(places) >= 3:
        lax.fori_loop(0, triples, add_triple, 0)
    if len(places) >= 2:
        lax.fori_loop(0, rest // 2, add_pair, 0)

    @pl.when(rest == 1)
    def _():
        add_group(0, 1)


def meet_kernel(
    places, sizes, table_ref, side_ref, blocks_ref, before_ref, image_ref, partner_side_ref, list_ref
):
    partner_side_ref[...] = own_side(blocks_ref[0, : blocks_ref.shape[1] // 2, :])
    image_ref[...] = before_ref[...]
    add_blocks((0, 0), places, sizes, table_ref, side_ref, blocks_ref, image_ref, list_ref)


def first_kernel(target, places, sizes, table_ref, side_ref, blocks_ref, image_ref, list_ref):
    image_ref[...] = jnp.zeros_like(image_ref)
    add_blocks(target, places, sizes, table_ref, side_ref, blocks_ref, image_ref, list_ref)


def part_kernel(
    target, places, sizes, table_ref, side_ref, blocks_ref, before_ref, image_ref, list_ref
):
    image_ref[...] = before_ref[...]
    add_blocks(target, places, sizes, table_ref, side_ref, blocks_ref, image_ref, list_ref)


def last_kernel(vectors_ref, root_ref, *refs):
    *part_refs, applied_ref, gram_ref = refs
    image = sum(part_ref[...] for part_ref in part_refs)
    n = vectors_ref.shape[0]
    applied = image * root_ref[...]
    applied_ref[...] = applied
    both = jnp.concatenate([applied, vectors_ref[...].astype(jnp.float32)], axis=0)
    gram = lax.dot_general(
        both, both, NT, precision=lax.Precision.HIGHEST, preferred_element_type=jnp.float32
    )
    wide = jnp.concatenate(
        [gram[:n, :n], gram[n:, :], jnp.zeros((n, n), jnp.float32)], axis=1
    )
    tile = jnp.concatenate([wide[: n // 2, :], wide[n // 2 :, :]], axis=1)
    for device in range(gram_ref.shape[0]):
        gram_ref[device] = tile


def inverse_factors(grams):
    n = grams[0].shape[0]
    half = 64
    tiles = range(n // 8)
    shape = (8, 2 * half)
    row = lax.broadcasted_iota(jnp.int32, shape, 0)
    lane = lax.broadcasted_iota(jnp.int32, shape, 1)
    columns = [
        [
            jnp.where(
                lane < half,
                jnp.broadcast_to(grams[0][8 * t : 8 * t + 8, j : j + 1], shape),
                jnp.broadcast_to(grams[1][8 * t : 8 * t + 8, j : j + 1], shape),
            )
            for t in tiles
        ]
        for j in range(n)
    ]
    right = [jnp.where(lane % half == row + 8 * t, 1.0, 0.0) for t in tiles]
    pivots = [jnp.ones(shape, jnp.float32) for t in tiles]
    for k in range(n):
        top, at = k // 8, k % 8
        pivot = columns[k][top][at : at + 1, :]
        pivots[top] = jnp.where(row == at, pivot, pivots[top])
        if k == n - 1:
            break
        scale = 1.0 / pivot
        factor = {t: columns[k][t] * scale for t in tiles if t >= top}
        factor[top] = jnp.where(row > at, factor[top], 0.0)
        for column in columns[k + 1 :] + [right]:
            line = column[top][at : at + 1, :]
            for t in factor:
                column[t] = column[t] - factor[t] * line
    result = jnp.concatenate([r * lax.rsqrt(p) for r, p in zip(right, pivots)], axis=0)
    return result[:, :n], result[:, half : half + n]


def finish_kernel(total_frames, grams_ref, applied_ref, basis_ref, ritz_ref):
    tile = grams_ref[0]
    for device in range(1, grams_ref.shape[0]):
        tile += grams_ref[device]
    n = applied_ref.shape[0]
    gram = jnp.concatenate([tile[:, : 4 * n], tile[:, 4 * n :]], axis=0)
    exact = functools.partial(
        lax.dot_general, precision=lax.Precision.HIGHEST, preferred_element_type=jnp.float32
    )
    plain = (((1,), (0,)), ((), ()))
    image_inverse, vector_inverse = inverse_factors([gram[:, :n], gram[:, 2 * n : 3 * n]])
    basis_ref[...] = exact(image_inverse * math.sqrt(total_frames), applied_ref[...], plain)
    half = exact(vector_inverse, gram[:, n : 2 * n], plain)
    ritz_ref[...] = exact(half, vector_inverse, NT)


def sent(x, hop):
    n_row, n_col = lax.axis_size("row"), lax.axis_size("col")
    pairs = [
        (r * n_col + c, (r ^ hop[0]) * n_col + (c ^ hop[1]))
        for r in range(n_row)
        for c in range(n_col)
    ]
    return lax.ppermute(x, ("row", "col"), pairs)


def beyond(offsets, hop):
    return [(r ^ hop[0], c ^ hop[1]) for r, c in offsets]


def per_device(frames, vectors, degrees, tile_table):
    ncv, rows = frames.shape
    nvec = vectors.shape[0]
    n_row, n_col = lax.axis_size("row"), lax.axis_size("col")
    devices = n_row * n_col
    sizes = (n_row, n_col)
    vmem = pl.BlockSpec(memory_space=pltpu.VMEM)

    def call(kernel, name, outs, *args, limit=24, where=vmem, **keywords):
        shapes = [jax.ShapeDtypeStruct(*out) for out in outs]
        return pl.pallas_call(
            kernel,
            out_shape=shapes,
            in_specs=[where] * len(args),
            out_specs=[vmem] * len(outs),
            compiler_params=pltpu.CompilerParams(vmem_limit_bytes=limit * MIB),
            name=name,
            **keywords,
        )(*args)

    image_type = ((nvec, rows), jnp.float32)

    table = tile_table.transpose(1, 2, 0)
    packed, vectors, root, table = call(
        pack_kernel,
        "pack",
        [
            ((ncv + nvec, rows), jnp.bfloat16),
            (vectors.shape, vectors.dtype),
            ((1, rows), jnp.float32),
            (table.shape, table.dtype),
        ],
        *(
            pltpu.with_memory_space_constraint(x, pltpu.HBM)
            for x in (frames, vectors, degrees, table)
        ),
        where=pl.BlockSpec(memory_space=pltpu.HBM),
        scratch_shapes=[
            pltpu.VMEM(degrees.shape, degrees.dtype),
            pltpu.SemaphoreType.DMA((4,)),
        ],
    )
    core = (0, 1)
    lines = [(r, 1) for r in range(n_row - 1, 0, -1)]
    if n_row == 4:
        lines = [(3, 1), (1, 1), (2, 1)]
    partners = [(0, c) for c in range(3, n_col, 2)]
    met = [sent(packed, hop) for hop in partners]
    line = [sent(packed, hop) for hop in lines]

    def call_blocks(kernel, name, outs, places, *args, **keywords):
        return call(
            functools.partial(kernel, places, sizes),
            name,
            outs,
            table,
            *args,
            scratch_shapes=[pltpu.SMEM((len(places) + 1,), jnp.int32)],
            **keywords,
        )

    def add_part(name, target, places, side, blocks, part):
        kernel = part_kernel if part is not None else first_kernel
        before = [] if part is None else [part]
        (part,) = call_blocks(
            functools.partial(kernel, target),
            name,
            [image_type],
            places,
            side,
            blocks,
            *before,
            input_output_aliases={3: 0} if before else {},
        )
        return part

    side_type = ((3 * ncv + 16, rows), jnp.bfloat16)
    side, image = call(own_kernel, "own", [side_type, image_type], packed)
    met, image = lax.optimization_barrier((met, image))
    sides = []
    for hop, block in zip(partners, met):
        image, partner_side = call_blocks(
            meet_kernel,
            "meet",
            [image_type, side_type],
            [hop],
            side,
            block[None],
            image,
            input_output_aliases={3: 0},
        )
        sides.append(partner_side)
    early, image = lax.optimization_barrier((line[1:], image))
    held, held_at = early + met + [packed], lines[1:] + partners + [(0, 0)]
    near = jnp.stack(held)
    other = sent(near, core)
    parts = [None for _ in partners]
    for blocks, offsets in ((near, lines[1:]), (other, beyond(lines[1:], core))):
        for k, hop in enumerate(partners):
            parts[k] = add_part("partner", hop, offsets, sides[k], blocks, parts[k])
    late, parts, image = lax.optimization_barrier((line[:1], parts, image))
    late = jnp.stack(late)
    other_late = sent(late, core)
    for blocks, offsets in ((late, lines[:1]), (other_late, beyond(lines[:1], core))):
        for k, hop in enumerate(partners):
            parts[k] = add_part("partner_late", hop, offsets, sides[k], blocks, parts[k])
    parts, image = lax.optimization_barrier((parts, image))
    received = [sent(part, hop) for hop, part in zip(partners, parts)]
    own_places = lines[1:] + beyond(held_at, core) + lines[:1] + beyond(lines[:1], core)
    blocks = jnp.concatenate([near[: n_row - 2], other, late, other_late])
    image = add_part("add_own", (0, 0), own_places, side, blocks, image)
    applied, gram = call(
        last_kernel,
        "last",
        [((nvec, rows), jnp.float32), ((devices, nvec // 2, 8 * nvec), jnp.float32)],
        vectors,
        root,
        image,
        *received,
    )
    grams = lax.all_to_all(gram, ("row", "col"), 0, 0)
    basis, ritz = call(
        functools.partial(finish_kernel, rows * devices),
        "finish",
        [((nvec, rows), jnp.float32), ((nvec, nvec), jnp.float32)],
        grams,
        applied,
    )
    return (basis, ritz)


def solution(mesh):
    split = P(None, ("grp", "row", "col"))
    return jax.shard_map(
        per_device,
        mesh=mesh,
        in_specs=(split, split, P(("grp", "row", "col")), P()),
        out_specs=(split, P("grp", None)),
        check_vma=False,
    )
```

```python
import functools
import math

import jax
import jax.numpy as jnp
from jax import lax
from jax.experimental import pallas as pl
from jax.experimental.pallas import tpu as pltpu
from jax.sharding import PartitionSpec as P

unit = -math.log2(math.e) / 4.0

NT = (((1,), (1,)), ((), ()))
MIB = 1024 * 1024


def split3(x):
    high = x.astype(jnp.bfloat16).astype(jnp.float32)
    rest = x - high
    mid = rest.astype(jnp.bfloat16).astype(jnp.float32)
    low = (rest - mid).astype(jnp.bfloat16).astype(jnp.float32)
    return high, mid, low


def pack_kernel(
    frames_ref, vectors_in, degrees_ref, table_in,
    packed_ref, vectors_ref, root_ref, table_ref, degree_ref, sems,
):
    ncv = frames_ref.shape[0]
    copies = [
        pltpu.make_async_copy(vectors_in, vectors_ref, sems.at[0]),
        pltpu.make_async_copy(degrees_ref, degree_ref, sems.at[1]),
        pltpu.make_async_copy(frames_ref, packed_ref.at[pl.ds(0, ncv)], sems.at[2]),
        pltpu.make_async_copy(table_in, table_ref, sems.at[3]),
    ]
    for copy in copies:
        copy.start()
    copies[0].wait()
    copies[1].wait()
    root = lax.rsqrt(degree_ref[...])[None, :]
    root_ref[...] = root
    packed_ref[ncv:, :] = (vectors_ref[...].astype(jnp.float32) * root).astype(jnp.bfloat16)
    copies[2].wait()
    copies[3].wait()


def edge_rows(square, ones_first):
    high, mid, low = split3(square * unit)
    row = lax.broadcasted_iota(jnp.int32, (16, square.shape[1]), 0)
    base = 3 if ones_first else 0
    ones_at = 0 if ones_first else 3
    block = jnp.where((row >= ones_at) & (row < ones_at + 3), 1.0, 0.0)
    block = jnp.where(row == base, high, block)
    block = jnp.where(row == base + 1, mid, block)
    return jnp.where(row == base + 2, low, block)


def own_side(own):
    own = own.astype(jnp.float32)
    high, mid, low = split3(own * (-2.0 * unit))
    edge = edge_rows(jnp.sum(own * own, axis=0, keepdims=True), True)
    return jnp.concatenate([high, mid, low, edge], axis=0).astype(jnp.bfloat16)


def tile_image(side_ref, blocks):
    both = blocks[0] if len(blocks) == 1 else jnp.concatenate(blocks, axis=1)
    ncv = both.shape[0] // 2
    x, v = both[:ncv, :], both[ncv:, :]
    wide = x.astype(jnp.float32)
    edge = edge_rows(jnp.sum(wide * wide, axis=0, keepdims=True), False).astype(jnp.bfloat16)
    other = jnp.concatenate([x, x, x, edge], axis=0).T
    power = jnp.dot(other, side_ref[...], preferred_element_type=jnp.float32)
    kern = jnp.exp2(power).astype(jnp.bfloat16)
    return jnp.dot(v, kern, preferred_element_type=jnp.float32)


def own_kernel(packed_ref, side_ref, image_ref):
    side_ref[...] = own_side(packed_ref[: packed_ref.shape[0] // 2, :])
    image_ref[...] = tile_image(side_ref, [packed_ref[...]])


def add_blocks(target, places, sizes, table_ref, side_ref, blocks_ref, image_ref, list_ref):
    n_row, n_col = sizes
    my_row, my_col = lax.axis_index("row"), lax.axis_index("col")

    def number(offset):
        return (my_row ^ offset[0]) * n_col + (my_col ^ offset[1])

    first, second = table_ref[:, 0, :], table_ref[:, 1, :]
    me = number(target)
    other = jnp.where(first == me, second, jnp.where(second == me, first, -1))
    words = []
    for start in range(0, n_row * n_col, 16):
        bit = jnp.zeros(other.shape, jnp.float32)
        for b in range(16):
            bit = jnp.where(other == start + b, float(1 << b), bit)
        words.append(jnp.sum(bit).astype(jnp.int32))

    count = jnp.int32(0)
    for step, place in enumerate(places):
        block = number(place)
        word = words[0]
        for w in range(1, len(words)):
            word = jnp.where(block // 16 == w, words[w], word)
        list_ref[count] = step
        count += (word >> (block % 16)) & 1

    def add_group(start, size):
        blocks = [blocks_ref[list_ref[start + k]] for k in range(size)]
        image_ref[...] += tile_image(side_ref, blocks)

    def add_triple(group, _):
        add_group(3 * group, 3)
        return 0

    def add_pair(group, _):
        add_group(3 * triples + 2 * group, 2)
        return 0

    triples = jnp.maximum(count // 3 - (count % 3 == 1).astype(jnp.int32), 0)
    rest = count - 3 * triples
    if len(places) >= 3:
        lax.fori_loop(0, triples, add_triple, 0)
    if len(places) >= 2:
        lax.fori_loop(0, rest // 2, add_pair, 0)

    @pl.when(rest == 1)
    def _():
        add_group(0, 1)


def side_kernel(block_ref, side_ref):
    side_ref[...] = own_side(block_ref[: block_ref.shape[0] // 2, :])


def first_kernel(target, places, sizes, table_ref, side_ref, blocks_ref, image_ref, list_ref):
    image_ref[...] = jnp.zeros_like(image_ref)
    add_blocks(target, places, sizes, table_ref, side_ref, blocks_ref, image_ref, list_ref)


def part_kernel(
    target, places, sizes, table_ref, side_ref, blocks_ref, before_ref, image_ref, list_ref
):
    image_ref[...] = before_ref[...]
    add_blocks(target, places, sizes, table_ref, side_ref, blocks_ref, image_ref, list_ref)


def last_kernel(vectors_ref, root_ref, *refs):
    *part_refs, applied_ref, gram_ref = refs
    image = sum(part_ref[...] for part_ref in part_refs)
    n = vectors_ref.shape[0]
    applied = image * root_ref[...]
    applied_ref[...] = applied
    both = jnp.concatenate([applied, vectors_ref[...].astype(jnp.float32)], axis=0)
    gram = lax.dot_general(
        both, both, NT, precision=lax.Precision.HIGHEST, preferred_element_type=jnp.float32
    )
    wide = jnp.concatenate(
        [gram[:n, :n], gram[n:, :], jnp.zeros((n, n), jnp.float32)], axis=1
    )
    tile = jnp.concatenate([wide[: n // 2, :], wide[n // 2 :, :]], axis=1)
    for device in range(gram_ref.shape[0]):
        gram_ref[device] = tile


def inverse_factors(grams):
    n = grams[0].shape[0]
    half = 64
    tiles = range(n // 8)
    shape = (8, 2 * half)
    row = lax.broadcasted_iota(jnp.int32, shape, 0)
    lane = lax.broadcasted_iota(jnp.int32, shape, 1)
    columns = [
        [
            jnp.where(
                lane < half,
                jnp.broadcast_to(grams[0][8 * t : 8 * t + 8, j : j + 1], shape),
                jnp.broadcast_to(grams[1][8 * t : 8 * t + 8, j : j + 1], shape),
            )
            for t in tiles
        ]
        for j in range(n)
    ]
    right = [jnp.where(lane % half == row + 8 * t, 1.0, 0.0) for t in tiles]
    pivots = [jnp.ones(shape, jnp.float32) for t in tiles]
    for k in range(n):
        top, at = k // 8, k % 8
        pivot = columns[k][top][at : at + 1, :]
        pivots[top] = jnp.where(row == at, pivot, pivots[top])
        if k == n - 1:
            break
        scale = 1.0 / pivot
        factor = {t: columns[k][t] * scale for t in tiles if t >= top}
        factor[top] = jnp.where(row > at, factor[top], 0.0)
        for column in columns[k + 1 :] + [right]:
            line = column[top][at : at + 1, :]
            for t in factor:
                column[t] = column[t] - factor[t] * line
    result = jnp.concatenate([r * lax.rsqrt(p) for r, p in zip(right, pivots)], axis=0)
    return result[:, :n], result[:, half : half + n]


def finish_kernel(total_frames, grams_ref, applied_ref, basis_ref, ritz_ref):
    tile = grams_ref[0]
    for device in range(1, grams_ref.shape[0]):
        tile += grams_ref[device]
    n = applied_ref.shape[0]
    gram = jnp.concatenate([tile[:, : 4 * n], tile[:, 4 * n :]], axis=0)
    exact = functools.partial(
        lax.dot_general, precision=lax.Precision.HIGHEST, preferred_element_type=jnp.float32
    )
    plain = (((1,), (0,)), ((), ()))
    image_inverse, vector_inverse = inverse_factors([gram[:, :n], gram[:, 2 * n : 3 * n]])
    basis_ref[...] = exact(image_inverse * math.sqrt(total_frames), applied_ref[...], plain)
    half = exact(vector_inverse, gram[:, n : 2 * n], plain)
    ritz_ref[...] = exact(half, vector_inverse, NT)


def sent(x, hop):
    n_row, n_col = lax.axis_size("row"), lax.axis_size("col")
    pairs = [
        (r * n_col + c, (r ^ hop[0]) * n_col + (c ^ hop[1]))
        for r in range(n_row)
        for c in range(n_col)
    ]
    return lax.ppermute(x, ("row", "col"), pairs)


def beyond(offsets, hop):
    return [(r ^ hop[0], c ^ hop[1]) for r, c in offsets]


def per_device(frames, vectors, degrees, tile_table):
    ncv, rows = frames.shape
    nvec = vectors.shape[0]
    n_row, n_col = lax.axis_size("row"), lax.axis_size("col")
    devices = n_row * n_col
    sizes = (n_row, n_col)
    vmem = pl.BlockSpec(memory_space=pltpu.VMEM)

    def call(kernel, name, outs, *args, limit=24, where=vmem, **keywords):
        shapes = [jax.ShapeDtypeStruct(*out) for out in outs]
        return pl.pallas_call(
            kernel,
            out_shape=shapes,
            in_specs=[where] * len(args),
            out_specs=[vmem] * len(outs),
            compiler_params=pltpu.CompilerParams(vmem_limit_bytes=limit * MIB),
            name=name,
            **keywords,
        )(*args)

    image_type = ((nvec, rows), jnp.float32)

    table = tile_table.transpose(1, 2, 0)
    packed, vectors, root, table = call(
        pack_kernel,
        "pack",
        [
            ((ncv + nvec, rows), jnp.bfloat16),
            (vectors.shape, vectors.dtype),
            ((1, rows), jnp.float32),
            (table.shape, table.dtype),
        ],
        *(
            pltpu.with_memory_space_constraint(x, pltpu.HBM)
            for x in (frames, vectors, degrees, table)
        ),
        where=pl.BlockSpec(memory_space=pltpu.HBM),
        scratch_shapes=[
            pltpu.VMEM(degrees.shape, degrees.dtype),
            pltpu.SemaphoreType.DMA((4,)),
        ],
    )
    core = (0, 1)
    lines = [(r, 1) for r in range(n_row - 1, 0, -1)]
    if n_row == 4:
        lines = [(3, 1), (1, 1), (2, 1)]
    partners = [(0, c) for c in range(3, n_col, 2)]
    met = [sent(packed, hop) for hop in partners]
    line = [sent(packed, hop) for hop in lines[1:]]

    def call_blocks(kernel, name, outs, places, *args, **keywords):
        return call(
            functools.partial(kernel, places, sizes),
            name,
            outs,
            table,
            *args,
            scratch_shapes=[pltpu.SMEM((len(places) + 1,), jnp.int32)],
            **keywords,
        )

    def add_part(name, target, places, side, blocks, part):
        kernel = part_kernel if part is not None else first_kernel
        before = [] if part is None else [part]
        (part,) = call_blocks(
            functools.partial(kernel, target),
            name,
            [image_type],
            places,
            side,
            blocks,
            *before,
            input_output_aliases={3: 0} if before else {},
        )
        return part

    side_type = ((3 * ncv + 16, rows), jnp.bfloat16)
    side, image = call(own_kernel, "own", [side_type, image_type], packed)
    ready, image = lax.optimization_barrier((packed, image))
    line = [sent(ready, hop) for hop in lines[:1]] + line
    met, image = lax.optimization_barrier((met, image))
    sides = [call(side_kernel, "side", [side_type], block)[0] for block in met]
    early, sides = lax.optimization_barrier((line[1:], sides))
    held, held_at = early + met + [packed], lines[1:] + partners + [(0, 0)]
    near = jnp.stack(held)
    other = sent(near, core)
    parts = [None for _ in partners]
    for blocks, offsets in ((near, lines[1:]), (other, beyond(lines[1:], core))):
        for k, hop in enumerate(partners):
            parts[k] = add_part("partner", hop, offsets, sides[k], blocks, parts[k])
    late, parts, image = lax.optimization_barrier((line[:1], parts, image))
    late = jnp.stack(late)
    other_late = sent(late, core)
    for blocks, offsets in ((late, lines[:1]), (other_late, beyond(lines[:1], core))):
        for k, hop in enumerate(partners):
            parts[k] = add_part("partner_late", hop, offsets, sides[k], blocks, parts[k])
    parts, image = lax.optimization_barrier((parts, image))
    received = [sent(part, hop) for hop, part in zip(partners, parts)]
    own_places = held_at[:-1] + beyond(held_at, core) + lines[:1] + beyond(lines[:1], core)
    blocks = jnp.concatenate([near[:-1], other, late, other_late])
    image = add_part("add_own", (0, 0), own_places, side, blocks, image)
    applied, gram = call(
        last_kernel,
        "last",
        [((nvec, rows), jnp.float32), ((devices, nvec // 2, 8 * nvec), jnp.float32)],
        vectors,
        root,
        image,
        *received,
    )
    grams = lax.all_to_all(gram, ("row", "col"), 0, 0)
    basis, ritz = call(
        functools.partial(finish_kernel, rows * devices),
        "finish",
        [((nvec, rows), jnp.float32), ((nvec, nvec), jnp.float32)],
        grams,
        applied,
    )
    return (basis, ritz)


def solution(mesh):
    split = P(None, ("grp", "row", "col"))
    return jax.shard_map(
        per_device,
        mesh=mesh,
        in_specs=(split, split, P(("grp", "row", "col")), P()),
        out_specs=(split, P("grp", None)),
        check_vma=False,
    )
```

```python
import functools
import math

import jax
import jax.numpy as jnp
from jax import lax
from jax.experimental import pallas as pl
from jax.experimental.pallas import tpu as pltpu
from jax.sharding import PartitionSpec as P

unit = -math.log2(math.e) / 4.0

NT = (((1,), (1,)), ((), ()))
MIB = 1024 * 1024


def split3(x):
    high = x.astype(jnp.bfloat16).astype(jnp.float32)
    rest = x - high
    mid = rest.astype(jnp.bfloat16).astype(jnp.float32)
    low = (rest - mid).astype(jnp.bfloat16).astype(jnp.float32)
    return high, mid, low


def pack_kernel(
    frames_ref, vectors_in, degrees_ref, table_in,
    packed_ref, vectors_ref, root_ref, table_ref, degree_ref, sems,
):
    ncv = frames_ref.shape[0]
    copies = [
        pltpu.make_async_copy(vectors_in, vectors_ref, sems.at[0]),
        pltpu.make_async_copy(degrees_ref, degree_ref, sems.at[1]),
        pltpu.make_async_copy(frames_ref, packed_ref.at[pl.ds(0, ncv)], sems.at[2]),
        pltpu.make_async_copy(table_in, table_ref, sems.at[3]),
    ]
    for copy in copies:
        copy.start()
    copies[0].wait()
    copies[1].wait()
    root = lax.rsqrt(degree_ref[...])[None, :]
    root_ref[...] = root
    packed_ref[ncv:, :] = (vectors_ref[...].astype(jnp.float32) * root).astype(jnp.bfloat16)
    copies[2].wait()
    copies[3].wait()


def edge_rows(square, ones_first):
    high, mid, low = split3(square * unit)
    row = lax.broadcasted_iota(jnp.int32, (16, square.shape[1]), 0)
    base = 3 if ones_first else 0
    ones_at = 0 if ones_first else 3
    block = jnp.where((row >= ones_at) & (row < ones_at + 3), 1.0, 0.0)
    block = jnp.where(row == base, high, block)
    block = jnp.where(row == base + 1, mid, block)
    return jnp.where(row == base + 2, low, block)


def own_side(own):
    own = own.astype(jnp.float32)
    high, mid, low = split3(own * (-2.0 * unit))
    edge = edge_rows(jnp.sum(own * own, axis=0, keepdims=True), True)
    return jnp.concatenate([high, mid, low, edge], axis=0).astype(jnp.bfloat16)


def tile_image(side_ref, blocks):
    both = blocks[0] if len(blocks) == 1 else jnp.concatenate(blocks, axis=1)
    ncv = both.shape[0] // 2
    x, v = both[:ncv, :], both[ncv:, :]
    wide = x.astype(jnp.float32)
    edge = edge_rows(jnp.sum(wide * wide, axis=0, keepdims=True), False).astype(jnp.bfloat16)
    other = jnp.concatenate([x, x, x, edge], axis=0).T
    power = jnp.dot(other, side_ref[...], preferred_element_type=jnp.float32)
    kern = jnp.exp2(power).astype(jnp.bfloat16)
    return jnp.dot(v, kern, preferred_element_type=jnp.float32)


def own_kernel(packed_ref, side_ref, image_ref):
    side_ref[...] = own_side(packed_ref[: packed_ref.shape[0] // 2, :])
    image_ref[...] = tile_image(side_ref, [packed_ref[...]])


def add_blocks(target, places, sizes, table_ref, side_ref, blocks_ref, image_ref, list_ref):
    n_row, n_col = sizes
    my_row, my_col = lax.axis_index("row"), lax.axis_index("col")

    def number(offset):
        return (my_row ^ offset[0]) * n_col + (my_col ^ offset[1])

    first, second = table_ref[:, 0, :], table_ref[:, 1, :]
    me = number(target)
    other = jnp.where(first == me, second, jnp.where(second == me, first, -1))
    words = []
    for start in range(0, n_row * n_col, 16):
        bit = jnp.zeros(other.shape, jnp.float32)
        for b in range(16):
            bit = jnp.where(other == start + b, float(1 << b), bit)
        words.append(jnp.sum(bit).astype(jnp.int32))

    count = jnp.int32(0)
    for step, place in enumerate(places):
        block = number(place)
        word = words[0]
        for w in range(1, len(words)):
            word = jnp.where(block // 16 == w, words[w], word)
        list_ref[count] = step
        count += (word >> (block % 16)) & 1

    def add_group(start, size):
        blocks = [blocks_ref[list_ref[start + k]] for k in range(size)]
        image_ref[...] += tile_image(side_ref, blocks)

    def add_triple(group, _):
        add_group(3 * group, 3)
        return 0

    def add_pair(group, _):
        add_group(3 * triples + 2 * group, 2)
        return 0

    triples = jnp.maximum(count // 3 - (count % 3 == 1).astype(jnp.int32), 0)
    rest = count - 3 * triples
    if len(places) >= 3:
        lax.fori_loop(0, triples, add_triple, 0)
    if len(places) >= 2:
        lax.fori_loop(0, rest // 2, add_pair, 0)

    @pl.when(rest == 1)
    def _():
        add_group(0, 1)


def side_kernel(block_ref, side_ref):
    side_ref[...] = own_side(block_ref[: block_ref.shape[0] // 2, :])


def first_kernel(target, places, sizes, table_ref, side_ref, blocks_ref, image_ref, list_ref):
    image_ref[...] = jnp.zeros_like(image_ref)
    add_blocks(target, places, sizes, table_ref, side_ref, blocks_ref, image_ref, list_ref)


def part_kernel(
    target, places, sizes, table_ref, side_ref, blocks_ref, before_ref, image_ref, list_ref
):
    image_ref[...] = before_ref[...]
    add_blocks(target, places, sizes, table_ref, side_ref, blocks_ref, image_ref, list_ref)


def last_kernel(vectors_ref, root_ref, *refs):
    *part_refs, applied_ref, gram_ref = refs
    image = sum(part_ref[...] for part_ref in part_refs)
    n = vectors_ref.shape[0]
    applied = image * root_ref[...]
    applied_ref[...] = applied
    both = jnp.concatenate([applied, vectors_ref[...].astype(jnp.float32)], axis=0)
    gram = lax.dot_general(
        both, both, NT, precision=lax.Precision.HIGHEST, preferred_element_type=jnp.float32
    )
    wide = jnp.concatenate(
        [gram[:n, :n], gram[n:, :], jnp.zeros((n, n), jnp.float32)], axis=1
    )
    tile = jnp.concatenate([wide[: n // 2, :], wide[n // 2 :, :]], axis=1)
    for device in range(gram_ref.shape[0]):
        gram_ref[device] = tile


def inverse_factors(grams):
    n = grams[0].shape[0]
    half = 64
    tiles = range(n // 8)
    shape = (8, 2 * half)
    row = lax.broadcasted_iota(jnp.int32, shape, 0)
    lane = lax.broadcasted_iota(jnp.int32, shape, 1)
    columns = [
        [
            jnp.where(
                lane < half,
                jnp.broadcast_to(grams[0][8 * t : 8 * t + 8, j : j + 1], shape),
                jnp.broadcast_to(grams[1][8 * t : 8 * t + 8, j : j + 1], shape),
            )
            for t in tiles
        ]
        for j in range(n)
    ]
    right = [jnp.where(lane % half == row + 8 * t, 1.0, 0.0) for t in tiles]
    pivots = [jnp.ones(shape, jnp.float32) for t in tiles]
    for k in range(n):
        top, at = k // 8, k % 8
        pivot = columns[k][top][at : at + 1, :]
        pivots[top] = jnp.where(row == at, pivot, pivots[top])
        if k == n - 1:
            break
        scale = 1.0 / pivot
        factor = {t: columns[k][t] * scale for t in tiles if t >= top}
        factor[top] = jnp.where(row > at, factor[top], 0.0)
        for column in columns[k + 1 :] + [right]:
            line = column[top][at : at + 1, :]
            for t in factor:
                column[t] = column[t] - factor[t] * line
    result = jnp.concatenate([r * lax.rsqrt(p) for r, p in zip(right, pivots)], axis=0)
    return result[:, :n], result[:, half : half + n]


def finish_kernel(total_frames, grams_ref, applied_ref, basis_ref, ritz_ref):
    tile = grams_ref[0]
    for device in range(1, grams_ref.shape[0]):
        tile += grams_ref[device]
    n = applied_ref.shape[0]
    gram = jnp.concatenate([tile[:, : 4 * n], tile[:, 4 * n :]], axis=0)
    exact = functools.partial(
        lax.dot_general, precision=lax.Precision.HIGHEST, preferred_element_type=jnp.float32
    )
    plain = (((1,), (0,)), ((), ()))
    image_inverse, vector_inverse = inverse_factors([gram[:, :n], gram[:, 2 * n : 3 * n]])
    basis_ref[...] = exact(image_inverse * math.sqrt(total_frames), applied_ref[...], plain)
    half = exact(vector_inverse, gram[:, n : 2 * n], plain)
    ritz_ref[...] = exact(half, vector_inverse, NT)


def sent(x, hop):
    n_row, n_col = lax.axis_size("row"), lax.axis_size("col")
    pairs = [
        (r * n_col + c, (r ^ hop[0]) * n_col + (c ^ hop[1]))
        for r in range(n_row)
        for c in range(n_col)
    ]
    return lax.ppermute(x, ("row", "col"), pairs)


def beyond(offsets, hop):
    return [(r ^ hop[0], c ^ hop[1]) for r, c in offsets]


def per_device(frames, vectors, degrees, tile_table):
    ncv, rows = frames.shape
    nvec = vectors.shape[0]
    n_row, n_col = lax.axis_size("row"), lax.axis_size("col")
    devices = n_row * n_col
    sizes = (n_row, n_col)
    vmem = pl.BlockSpec(memory_space=pltpu.VMEM)

    def call(kernel, name, outs, *args, limit=24, where=vmem, **keywords):
        shapes = [jax.ShapeDtypeStruct(*out) for out in outs]
        return pl.pallas_call(
            kernel,
            out_shape=shapes,
            in_specs=[where] * len(args),
            out_specs=[vmem] * len(outs),
            compiler_params=pltpu.CompilerParams(vmem_limit_bytes=limit * MIB),
            name=name,
            **keywords,
        )(*args)

    image_type = ((nvec, rows), jnp.float32)

    table = tile_table.transpose(1, 2, 0)
    packed, vectors, root, table = call(
        pack_kernel,
        "pack",
        [
            ((ncv + nvec, rows), jnp.bfloat16),
            (vectors.shape, vectors.dtype),
            ((1, rows), jnp.float32),
            (table.shape, table.dtype),
        ],
        *(
            pltpu.with_memory_space_constraint(x, pltpu.HBM)
            for x in (frames, vectors, degrees, table)
        ),
        where=pl.BlockSpec(memory_space=pltpu.HBM),
        scratch_shapes=[
            pltpu.VMEM(degrees.shape, degrees.dtype),
            pltpu.SemaphoreType.DMA((4,)),
        ],
    )
    core = (0, 1)
    lines = [(r, 1) for r in range(n_row - 1, 0, -1)]
    if n_row == 4:
        lines = [(3, 1), (1, 1), (2, 1)]
    partners = [(0, c) for c in range(3, n_col, 2)]
    met = [sent(packed, hop) for hop in partners]
    line = [sent(packed, hop) for hop in lines]

    def call_blocks(kernel, name, outs, places, *args, **keywords):
        return call(
            functools.partial(kernel, places, sizes),
            name,
            outs,
            table,
            *args,
            scratch_shapes=[pltpu.SMEM((len(places) + 1,), jnp.int32)],
            **keywords,
        )

    def add_part(name, target, places, side, blocks, part):
        kernel = part_kernel if part is not None else first_kernel
        before = [] if part is None else [part]
        (part,) = call_blocks(
            functools.partial(kernel, target),
            name,
            [image_type],
            places,
            side,
            blocks,
            *before,
            input_output_aliases={3: 0} if before else {},
        )
        return part

    side_type = ((3 * ncv + 16, rows), jnp.bfloat16)
    side, image = call(own_kernel, "own", [side_type, image_type], packed)
    met, early, image = lax.optimization_barrier((met, line[1:], image))
    sides = [call(side_kernel, "side", [side_type], block)[0] for block in met]
    held, held_at = early + met + [packed], lines[1:] + partners + [(0, 0)]
    near = jnp.stack(held)
    other = sent(near, core)
    parts = [None for _ in partners]
    for blocks, offsets in ((near, lines[1:]), (other, beyond(lines[1:], core))):
        for k, hop in enumerate(partners):
            parts[k] = add_part("partner", hop, offsets, sides[k], blocks, parts[k])
    late, parts, image = lax.optimization_barrier((line[:1], parts, image))
    late = jnp.stack(late)
    other_late = sent(late, core)
    for blocks, offsets in ((late, lines[:1]), (other_late, beyond(lines[:1], core))):
        for k, hop in enumerate(partners):
            parts[k] = add_part("partner_late", hop, offsets, sides[k], blocks, parts[k])
    parts, image = lax.optimization_barrier((parts, image))
    received = [sent(part, hop) for hop, part in zip(partners, parts)]
    own_places = held_at[:-1] + beyond(held_at, core) + lines[:1] + beyond(lines[:1], core)
    blocks = jnp.concatenate([near[:-1], other, late, other_late])
    image = add_part("add_own", (0, 0), own_places, side, blocks, image)
    applied, gram = call(
        last_kernel,
        "last",
        [((nvec, rows), jnp.float32), ((devices, nvec // 2, 8 * nvec), jnp.float32)],
        vectors,
        root,
        image,
        *received,
    )
    grams = lax.all_to_all(gram, ("row", "col"), 0, 0)
    basis, ritz = call(
        functools.partial(finish_kernel, rows * devices),
        "finish",
        [((nvec, rows), jnp.float32), ((nvec, nvec), jnp.float32)],
        grams,
        applied,
    )
    return (basis, ritz)


def solution(mesh):
    split = P(None, ("grp", "row", "col"))
    return jax.shard_map(
        per_device,
        mesh=mesh,
        in_specs=(split, split, P(("grp", "row", "col")), P()),
        out_specs=(split, P("grp", None)),
        check_vma=False,
    )
```

```python
import functools
import math

import jax
import jax.numpy as jnp
from jax import lax
from jax.experimental import pallas as pl
from jax.experimental.pallas import tpu as pltpu
from jax.sharding import PartitionSpec as P

unit = -math.log2(math.e) / 4.0

NT = (((1,), (1,)), ((), ()))
MIB = 1024 * 1024


def split3(x):
    high = x.astype(jnp.bfloat16).astype(jnp.float32)
    rest = x - high
    mid = rest.astype(jnp.bfloat16).astype(jnp.float32)
    low = (rest - mid).astype(jnp.bfloat16).astype(jnp.float32)
    return high, mid, low


def pack_kernel(
    frames_ref, vectors_in, degrees_ref, table_in,
    packed_ref, vectors_ref, root_ref, table_ref, degree_ref, sems,
):
    ncv = frames_ref.shape[0]
    copies = [
        pltpu.make_async_copy(vectors_in, vectors_ref, sems.at[0]),
        pltpu.make_async_copy(degrees_ref, degree_ref, sems.at[1]),
        pltpu.make_async_copy(frames_ref, packed_ref.at[pl.ds(0, ncv)], sems.at[2]),
        pltpu.make_async_copy(table_in, table_ref, sems.at[3]),
    ]
    for copy in copies:
        copy.start()
    copies[0].wait()
    copies[1].wait()
    root = lax.rsqrt(degree_ref[...])[None, :]
    root_ref[...] = root
    packed_ref[ncv:, :] = (vectors_ref[...].astype(jnp.float32) * root).astype(jnp.bfloat16)
    copies[2].wait()
    copies[3].wait()


def edge_rows(square, ones_first):
    high, mid, low = split3(square * unit)
    row = lax.broadcasted_iota(jnp.int32, (16, square.shape[1]), 0)
    base = 3 if ones_first else 0
    ones_at = 0 if ones_first else 3
    block = jnp.where((row >= ones_at) & (row < ones_at + 3), 1.0, 0.0)
    block = jnp.where(row == base, high, block)
    block = jnp.where(row == base + 1, mid, block)
    return jnp.where(row == base + 2, low, block)


def own_side(own):
    own = own.astype(jnp.float32)
    high, mid, low = split3(own * (-2.0 * unit))
    edge = edge_rows(jnp.sum(own * own, axis=0, keepdims=True), True)
    return jnp.concatenate([high, mid, low, edge], axis=0).astype(jnp.bfloat16)


def tile_image(side_ref, blocks):
    both = blocks[0] if len(blocks) == 1 else jnp.concatenate(blocks, axis=1)
    ncv = both.shape[0] // 2
    x, v = both[:ncv, :], both[ncv:, :]
    wide = x.astype(jnp.float32)
    edge = edge_rows(jnp.sum(wide * wide, axis=0, keepdims=True), False).astype(jnp.bfloat16)
    other = jnp.concatenate([x, x, x, edge], axis=0).T
    power = jnp.dot(other, side_ref[...], preferred_element_type=jnp.float32)
    kern = jnp.exp2(power).astype(jnp.bfloat16)
    return jnp.dot(v, kern, preferred_element_type=jnp.float32)


def own_kernel(packed_ref, side_ref, image_ref):
    side_ref[...] = own_side(packed_ref[: packed_ref.shape[0] // 2, :])
    image_ref[...] = tile_image(side_ref, [packed_ref[...]])


def add_blocks(target, places, sizes, table_ref, side_ref, blocks_ref, image_ref, list_ref):
    n_row, n_col = sizes
    my_row, my_col = lax.axis_index("row"), lax.axis_index("col")

    def number(offset):
        return (my_row ^ offset[0]) * n_col + (my_col ^ offset[1])

    first, second = table_ref[:, 0, :], table_ref[:, 1, :]
    me = number(target)
    other = jnp.where(first == me, second, jnp.where(second == me, first, -1))
    words = []
    for start in range(0, n_row * n_col, 16):
        bit = jnp.zeros(other.shape, jnp.float32)
        for b in range(16):
            bit = jnp.where(other == start + b, float(1 << b), bit)
        words.append(jnp.sum(bit).astype(jnp.int32))

    count = jnp.int32(0)
    for step, place in enumerate(places):
        block = number(place)
        word = words[0]
        for w in range(1, len(words)):
            word = jnp.where(block // 16 == w, words[w], word)
        list_ref[count] = step
        count += (word >> (block % 16)) & 1

    def add_group(start, size):
        blocks = [blocks_ref[list_ref[start + k]] for k in range(size)]
        image_ref[...] += tile_image(side_ref, blocks)

    def add_triple(group, _):
        add_group(3 * group, 3)
        return 0

    def add_pair(group, _):
        add_group(3 * triples + 2 * group, 2)
        return 0

    triples = jnp.maximum(count // 3 - (count % 3 == 1).astype(jnp.int32), 0)
    rest = count - 3 * triples
    if len(places) >= 3:
        lax.fori_loop(0, triples, add_triple, 0)
    if len(places) >= 2:
        lax.fori_loop(0, rest // 2, add_pair, 0)

    @pl.when(rest == 1)
    def _():
        add_group(0, 1)


def side_kernel(block_ref, side_ref):
    side_ref[...] = own_side(block_ref[: block_ref.shape[0] // 2, :])


def first_kernel(target, places, sizes, table_ref, side_ref, blocks_ref, image_ref, list_ref):
    image_ref[...] = jnp.zeros_like(image_ref)
    add_blocks(target, places, sizes, table_ref, side_ref, blocks_ref, image_ref, list_ref)


def part_kernel(
    target, places, sizes, table_ref, side_ref, blocks_ref, before_ref, image_ref, list_ref
):
    image_ref[...] = before_ref[...]
    add_blocks(target, places, sizes, table_ref, side_ref, blocks_ref, image_ref, list_ref)


def last_kernel(vectors_ref, root_ref, *refs):
    *part_refs, applied_ref, gram_ref = refs
    image = sum(part_ref[...] for part_ref in part_refs)
    n = vectors_ref.shape[0]
    applied = image * root_ref[...]
    applied_ref[...] = applied
    both = jnp.concatenate([applied, vectors_ref[...].astype(jnp.float32)], axis=0)
    gram = lax.dot_general(
        both, both, NT, precision=lax.Precision.HIGHEST, preferred_element_type=jnp.float32
    )
    wide = jnp.concatenate(
        [gram[:n, :n], gram[n:, :], jnp.zeros((n, n), jnp.float32)], axis=1
    )
    tile = jnp.concatenate([wide[: n // 2, :], wide[n // 2 :, :]], axis=1)
    for device in range(gram_ref.shape[0]):
        gram_ref[device] = tile


def inverse_factors(grams):
    n = grams[0].shape[0]
    half = 64
    tiles = range(n // 8)
    shape = (8, 2 * half)
    row = lax.broadcasted_iota(jnp.int32, shape, 0)
    lane = lax.broadcasted_iota(jnp.int32, shape, 1)
    columns = [
        [
            jnp.where(
                lane < half,
                jnp.broadcast_to(grams[0][8 * t : 8 * t + 8, j : j + 1], shape),
                jnp.broadcast_to(grams[1][8 * t : 8 * t + 8, j : j + 1], shape),
            )
            for t in tiles
        ]
        for j in range(n)
    ]
    right = [jnp.where(lane % half == row + 8 * t, 1.0, 0.0) for t in tiles]
    pivots = [jnp.ones(shape, jnp.float32) for t in tiles]
    for k in range(n):
        top, at = k // 8, k % 8
        pivot = columns[k][top][at : at + 1, :]
        pivots[top] = jnp.where(row == at, pivot, pivots[top])
        if k == n - 1:
            break
        scale = 1.0 / pivot
        factor = {t: columns[k][t] * scale for t in tiles if t >= top}
        factor[top] = jnp.where(row > at, factor[top], 0.0)
        for column in columns[k + 1 :] + [right]:
            line = column[top][at : at + 1, :]
            for t in factor:
                column[t] = column[t] - factor[t] * line
    result = jnp.concatenate([r * lax.rsqrt(p) for r, p in zip(right, pivots)], axis=0)
    return result[:, :n], result[:, half : half + n]


def finish_kernel(total_frames, grams_ref, applied_ref, basis_out, ritz_out, basis_ref, ritz_ref, sems):
    tile = grams_ref[0]
    for device in range(1, grams_ref.shape[0]):
        tile += grams_ref[device]
    n = applied_ref.shape[0]
    gram = jnp.concatenate([tile[:, : 4 * n], tile[:, 4 * n :]], axis=0)
    exact = functools.partial(
        lax.dot_general, precision=lax.Precision.HIGHEST, preferred_element_type=jnp.float32
    )
    plain = (((1,), (0,)), ((), ()))
    image_inverse, vector_inverse = inverse_factors([gram[:, :n], gram[:, 2 * n : 3 * n]])
    basis_ref[...] = exact(image_inverse * math.sqrt(total_frames), applied_ref[...], plain)
    copies = [
        pltpu.make_async_copy(basis_ref, basis_out, sems.at[0]),
        pltpu.make_async_copy(ritz_ref, ritz_out, sems.at[1]),
    ]
    copies[0].start()
    half = exact(vector_inverse, gram[:, n : 2 * n], plain)
    ritz_ref[...] = exact(half, vector_inverse, NT)
    copies[1].start()
    for copy in copies:
        copy.wait()


def sent(x, hop):
    n_row, n_col = lax.axis_size("row"), lax.axis_size("col")
    pairs = [
        (r * n_col + c, (r ^ hop[0]) * n_col + (c ^ hop[1]))
        for r in range(n_row)
        for c in range(n_col)
    ]
    return lax.ppermute(x, ("row", "col"), pairs)


def beyond(offsets, hop):
    return [(r ^ hop[0], c ^ hop[1]) for r, c in offsets]


def per_device(frames, vectors, degrees, tile_table):
    ncv, rows = frames.shape
    nvec = vectors.shape[0]
    n_row, n_col = lax.axis_size("row"), lax.axis_size("col")
    devices = n_row * n_col
    sizes = (n_row, n_col)
    vmem = pl.BlockSpec(memory_space=pltpu.VMEM)

    def call(kernel, name, outs, *args, limit=24, where=vmem, to=vmem, **keywords):
        shapes = [jax.ShapeDtypeStruct(*out) for out in outs]
        return pl.pallas_call(
            kernel,
            out_shape=shapes,
            in_specs=[where] * len(args),
            out_specs=[to] * len(outs),
            compiler_params=pltpu.CompilerParams(vmem_limit_bytes=limit * MIB),
            name=name,
            **keywords,
        )(*args)

    image_type = ((nvec, rows), jnp.float32)

    table = tile_table.transpose(1, 2, 0)
    packed, vectors, root, table = call(
        pack_kernel,
        "pack",
        [
            ((ncv + nvec, rows), jnp.bfloat16),
            (vectors.shape, vectors.dtype),
            ((1, rows), jnp.float32),
            (table.shape, table.dtype),
        ],
        *(
            pltpu.with_memory_space_constraint(x, pltpu.HBM)
            for x in (frames, vectors, degrees, table)
        ),
        where=pl.BlockSpec(memory_space=pltpu.HBM),
        scratch_shapes=[
            pltpu.VMEM(degrees.shape, degrees.dtype),
            pltpu.SemaphoreType.DMA((4,)),
        ],
    )
    core = (0, 1)
    lines = [(r, 1) for r in range(n_row - 1, 0, -1)]
    if n_row == 4:
        lines = [(3, 1), (1, 1), (2, 1)]
    partners = [(0, c) for c in range(3, n_col, 2)]
    met = [sent(packed, hop) for hop in partners]
    line = [sent(packed, hop) for hop in lines]

    def call_blocks(kernel, name, outs, places, *args, **keywords):
        return call(
            functools.partial(kernel, places, sizes),
            name,
            outs,
            table,
            *args,
            scratch_shapes=[pltpu.SMEM((len(places) + 1,), jnp.int32)],
            **keywords,
        )

    def add_part(name, target, places, side, blocks, part):
        kernel = part_kernel if part is not None else first_kernel
        before = [] if part is None else [part]
        (part,) = call_blocks(
            functools.partial(kernel, target),
            name,
            [image_type],
            places,
            side,
            blocks,
            *before,
            input_output_aliases={3: 0} if before else {},
        )
        return part

    side_type = ((3 * ncv + 16, rows), jnp.bfloat16)
    side, image = call(own_kernel, "own", [side_type, image_type], packed)
    met, image = lax.optimization_barrier((met, image))
    sides = [call(side_kernel, "side", [side_type], block)[0] for block in met]
    early, sides = lax.optimization_barrier((line[1:], sides))
    held, held_at = early + met + [packed], lines[1:] + partners + [(0, 0)]
    near = jnp.stack(held)
    other = sent(near, core)
    parts = [None for _ in partners]
    for blocks, offsets in ((near, lines[1:]), (other, beyond(lines[1:], core))):
        for k, hop in enumerate(partners):
            parts[k] = add_part("partner", hop, offsets, sides[k], blocks, parts[k])
    late, parts, image = lax.optimization_barrier((line[:1], parts, image))
    late = jnp.stack(late)
    other_late = sent(late, core)
    for k, hop in enumerate(partners):
        parts[k] = add_part("partner_late", hop, lines[:1], sides[k], late, parts[k])
    parts, image = lax.optimization_barrier((parts, image))
    image = add_part("add_met", (0, 0), partners, side, jnp.stack(met), image)
    other_late, parts, image = lax.optimization_barrier((other_late, parts, image))
    for k, hop in enumerate(partners):
        parts[k] = add_part(
            "partner_late", hop, beyond(lines[:1], core), sides[k], other_late, parts[k]
        )
    parts, image = lax.optimization_barrier((parts, image))
    received = [sent(part, hop) for hop, part in zip(partners, parts)]
    own_places = lines[1:] + beyond(held_at, core) + lines[:1] + beyond(lines[:1], core)
    blocks = jnp.concatenate([near[: n_row - 2], other, late, other_late])
    image = add_part("add_own", (0, 0), own_places, side, blocks, image)
    applied, gram = call(
        last_kernel,
        "last",
        [((nvec, rows), jnp.float32), ((devices, nvec // 2, 8 * nvec), jnp.float32)],
        vectors,
        root,
        image,
        *received,
    )
    grams = lax.all_to_all(gram, ("row", "col"), 0, 0)
    basis, ritz = call(
        functools.partial(finish_kernel, rows * devices),
        "finish",
        [((nvec, rows), jnp.float32), ((nvec, nvec), jnp.float32)],
        grams,
        applied,
        to=pl.BlockSpec(memory_space=pltpu.HBM),
        scratch_shapes=[
            pltpu.VMEM((nvec, rows), jnp.float32),
            pltpu.VMEM((nvec, nvec), jnp.float32),
            pltpu.SemaphoreType.DMA((2,)),
        ],
    )
    return (basis, ritz)


def solution(mesh):
    split = P(None, ("grp", "row", "col"))
    return jax.shard_map(
        per_device,
        mesh=mesh,
        in_specs=(split, split, P(("grp", "row", "col")), P()),
        out_specs=(split, P("grp", None)),
        check_vma=False,
    )
```

```python
import functools
import math

import jax
import jax.numpy as jnp
from jax import lax
from jax.experimental import pallas as pl
from jax.experimental.pallas import tpu as pltpu
from jax.sharding import PartitionSpec as P

unit = -math.log2(math.e) / 4.0

NT = (((1,), (1,)), ((), ()))
MIB = 1024 * 1024


def split3(x):
    high = x.astype(jnp.bfloat16).astype(jnp.float32)
    rest = x - high
    mid = rest.astype(jnp.bfloat16).astype(jnp.float32)
    low = (rest - mid).astype(jnp.bfloat16).astype(jnp.float32)
    return high, mid, low


def pack_kernel(
    frames_ref, vectors_in, degrees_ref, table_in,
    packed_ref, vectors_ref, root_ref, table_ref, degree_ref, sems,
):
    ncv = frames_ref.shape[0]
    copies = [
        pltpu.make_async_copy(vectors_in, vectors_ref, sems.at[0]),
        pltpu.make_async_copy(degrees_ref, degree_ref, sems.at[1]),
        pltpu.make_async_copy(frames_ref, packed_ref.at[pl.ds(0, ncv)], sems.at[2]),
        pltpu.make_async_copy(table_in, table_ref, sems.at[3]),
    ]
    for copy in copies:
        copy.start()
    copies[0].wait()
    copies[1].wait()
    root = lax.rsqrt(degree_ref[...])[None, :]
    root_ref[...] = root
    packed_ref[ncv:, :] = (vectors_ref[...].astype(jnp.float32) * root).astype(jnp.bfloat16)
    copies[2].wait()
    copies[3].wait()


def edge_rows(square, ones_first):
    high, mid, low = split3(square * unit)
    row = lax.broadcasted_iota(jnp.int32, (16, square.shape[1]), 0)
    base = 3 if ones_first else 0
    ones_at = 0 if ones_first else 3
    block = jnp.where((row >= ones_at) & (row < ones_at + 3), 1.0, 0.0)
    block = jnp.where(row == base, high, block)
    block = jnp.where(row == base + 1, mid, block)
    return jnp.where(row == base + 2, low, block)


def own_side(own):
    own = own.astype(jnp.float32)
    high, mid, low = split3(own * (-2.0 * unit))
    edge = edge_rows(jnp.sum(own * own, axis=0, keepdims=True), True)
    return jnp.concatenate([high, mid, low, edge], axis=0).astype(jnp.bfloat16)


def tile_image(side_ref, blocks):
    both = blocks[0] if len(blocks) == 1 else jnp.concatenate(blocks, axis=1)
    ncv = both.shape[0] // 2
    x, v = both[:ncv, :], both[ncv:, :]
    wide = x.astype(jnp.float32)
    edge = edge_rows(jnp.sum(wide * wide, axis=0, keepdims=True), False).astype(jnp.bfloat16)
    other = jnp.concatenate([x, x, x, edge], axis=0).T
    power = jnp.dot(other, side_ref[...], preferred_element_type=jnp.float32)
    kern = jnp.exp2(power).astype(jnp.bfloat16)
    return jnp.dot(v, kern, preferred_element_type=jnp.float32)


def own_kernel(packed_ref, side_ref, image_ref):
    side_ref[...] = own_side(packed_ref[: packed_ref.shape[0] // 2, :])
    image_ref[...] = tile_image(side_ref, [packed_ref[...]])


def add_blocks(target, places, sizes, table_ref, side_ref, blocks_ref, image_ref, list_ref):
    n_row, n_col = sizes
    my_row, my_col = lax.axis_index("row"), lax.axis_index("col")

    def number(offset):
        return (my_row ^ offset[0]) * n_col + (my_col ^ offset[1])

    first, second = table_ref[:, 0, :], table_ref[:, 1, :]
    me = number(target)
    other = jnp.where(first == me, second, jnp.where(second == me, first, -1))
    words = []
    for start in range(0, n_row * n_col, 16):
        bit = jnp.zeros(other.shape, jnp.float32)
        for b in range(16):
            bit = jnp.where(other == start + b, float(1 << b), bit)
        words.append(jnp.sum(bit).astype(jnp.int32))

    count = jnp.int32(0)
    for step, place in enumerate(places):
        block = number(place)
        word = words[0]
        for w in range(1, len(words)):
            word = jnp.where(block // 16 == w, words[w], word)
        list_ref[count] = step
        count += (word >> (block % 16)) & 1

    def add_group(start, size):
        blocks = [blocks_ref[list_ref[start + k]] for k in range(size)]
        image_ref[...] += tile_image(side_ref, blocks)

    def add_triple(group, _):
        add_group(3 * group, 3)
        return 0

    def add_pair(group, _):
        add_group(3 * triples + 2 * group, 2)
        return 0

    triples = jnp.maximum(count // 3 - (count % 3 == 1).astype(jnp.int32), 0)
    rest = count - 3 * triples
    if len(places) >= 3:
        lax.fori_loop(0, triples, add_triple, 0)
    if len(places) >= 2:
        lax.fori_loop(0, rest // 2, add_pair, 0)

    @pl.when(rest == 1)
    def _():
        add_group(0, 1)


def side_kernel(block_ref, side_ref):
    side_ref[...] = own_side(block_ref[: block_ref.shape[0] // 2, :])


def first_kernel(target, places, sizes, table_ref, side_ref, blocks_ref, image_ref, list_ref):
    image_ref[...] = jnp.zeros_like(image_ref)
    add_blocks(target, places, sizes, table_ref, side_ref, blocks_ref, image_ref, list_ref)


def part_kernel(
    target, places, sizes, table_ref, side_ref, blocks_ref, before_ref, image_ref, list_ref
):
    image_ref[...] = before_ref[...]
    add_blocks(target, places, sizes, table_ref, side_ref, blocks_ref, image_ref, list_ref)


def last_kernel(vectors_ref, root_ref, *refs):
    *part_refs, applied_ref, gram_ref = refs
    image = sum(part_ref[...] for part_ref in part_refs)
    n = vectors_ref.shape[0]
    applied = image * root_ref[...]
    applied_ref[...] = applied
    both = jnp.concatenate([applied, vectors_ref[...].astype(jnp.float32)], axis=0)
    gram = lax.dot_general(
        both, both, NT, precision=lax.Precision.HIGHEST, preferred_element_type=jnp.float32
    )
    wide = jnp.concatenate(
        [gram[:n, :n], gram[n:, :], jnp.zeros((n, n), jnp.float32)], axis=1
    )
    tile = jnp.concatenate([wide[: n // 2, :], wide[n // 2 :, :]], axis=1)
    for device in range(gram_ref.shape[0]):
        gram_ref[device] = tile


def inverse_factors(grams):
    n = grams[0].shape[0]
    half = 64
    tiles = range(n // 8)
    shape = (8, 2 * half)
    row = lax.broadcasted_iota(jnp.int32, shape, 0)
    lane = lax.broadcasted_iota(jnp.int32, shape, 1)
    columns = [
        [
            jnp.where(
                lane < half,
                jnp.broadcast_to(grams[0][8 * t : 8 * t + 8, j : j + 1], shape),
                jnp.broadcast_to(grams[1][8 * t : 8 * t + 8, j : j + 1], shape),
            )
            for t in tiles
        ]
        for j in range(n)
    ]
    right = [jnp.where(lane % half == row + 8 * t, 1.0, 0.0) for t in tiles]
    pivots = [jnp.ones(shape, jnp.float32) for t in tiles]
    for k in range(n):
        top, at = k // 8, k % 8
        pivot = columns[k][top][at : at + 1, :]
        pivots[top] = jnp.where(row == at, pivot, pivots[top])
        if k == n - 1:
            break
        scale = 1.0 / pivot
        factor = {t: columns[k][t] * scale for t in tiles if t >= top}
        factor[top] = jnp.where(row > at, factor[top], 0.0)
        for column in columns[k + 1 :] + [right]:
            line = column[top][at : at + 1, :]
            for t in factor:
                column[t] = column[t] - factor[t] * line
    result = jnp.concatenate([r * lax.rsqrt(p) for r, p in zip(right, pivots)], axis=0)
    return result[:, :n], result[:, half : half + n]


def finish_kernel(total_frames, grams_ref, applied_ref, basis_out, ritz_out, basis_ref, ritz_ref, sems):
    tile = grams_ref[0]
    for device in range(1, grams_ref.shape[0]):
        tile += grams_ref[device]
    n = applied_ref.shape[0]
    gram = jnp.concatenate([tile[:, : 4 * n], tile[:, 4 * n :]], axis=0)
    exact = functools.partial(
        lax.dot_general, precision=lax.Precision.HIGHEST, preferred_element_type=jnp.float32
    )
    plain = (((1,), (0,)), ((), ()))
    image_inverse, vector_inverse = inverse_factors([gram[:, :n], gram[:, 2 * n : 3 * n]])
    basis_ref[...] = exact(image_inverse * math.sqrt(total_frames), applied_ref[...], plain)
    copies = [
        pltpu.make_async_copy(basis_ref, basis_out, sems.at[0]),
        pltpu.make_async_copy(ritz_ref, ritz_out, sems.at[1]),
    ]
    copies[0].start()
    half = exact(vector_inverse, gram[:, n : 2 * n], plain)
    ritz_ref[...] = exact(half, vector_inverse, NT)
    copies[1].start()
    for copy in copies:
        copy.wait()


def sent(x, hop):
    n_row, n_col = lax.axis_size("row"), lax.axis_size("col")
    pairs = [
        (r * n_col + c, (r ^ hop[0]) * n_col + (c ^ hop[1]))
        for r in range(n_row)
        for c in range(n_col)
    ]
    return lax.ppermute(x, ("row", "col"), pairs)


def beyond(offsets, hop):
    return [(r ^ hop[0], c ^ hop[1]) for r, c in offsets]


def per_device(frames, vectors, degrees, tile_table):
    ncv, rows = frames.shape
    nvec = vectors.shape[0]
    n_row, n_col = lax.axis_size("row"), lax.axis_size("col")
    devices = n_row * n_col
    sizes = (n_row, n_col)
    vmem = pl.BlockSpec(memory_space=pltpu.VMEM)

    def call(kernel, name, outs, *args, limit=24, where=vmem, to=vmem, **keywords):
        shapes = [jax.ShapeDtypeStruct(*out) for out in outs]
        return pl.pallas_call(
            kernel,
            out_shape=shapes,
            in_specs=[where] * len(args),
            out_specs=[to] * len(outs),
            compiler_params=pltpu.CompilerParams(vmem_limit_bytes=limit * MIB),
            name=name,
            **keywords,
        )(*args)

    image_type = ((nvec, rows), jnp.float32)

    table = tile_table.transpose(1, 2, 0)
    packed, vectors, root, table = call(
        pack_kernel,
        "pack",
        [
            ((ncv + nvec, rows), jnp.bfloat16),
            (vectors.shape, vectors.dtype),
            ((1, rows), jnp.float32),
            (table.shape, table.dtype),
        ],
        *(
            pltpu.with_memory_space_constraint(x, pltpu.HBM)
            for x in (frames, vectors, degrees, table)
        ),
        where=pl.BlockSpec(memory_space=pltpu.HBM),
        scratch_shapes=[
            pltpu.VMEM(degrees.shape, degrees.dtype),
            pltpu.SemaphoreType.DMA((4,)),
        ],
    )
    core = (0, 1)
    lines = [(r, 1) for r in range(n_row - 1, 0, -1)]
    if n_row == 4:
        lines = [(1, 1), (2, 1), (3, 1)]
    partners = [(0, c) for c in range(3, n_col, 2)]
    met = [sent(packed, hop) for hop in partners]
    line = [sent(packed, hop) for hop in lines]

    def call_blocks(kernel, name, outs, places, *args, **keywords):
        return call(
            functools.partial(kernel, places, sizes),
            name,
            outs,
            table,
            *args,
            scratch_shapes=[pltpu.SMEM((len(places) + 1,), jnp.int32)],
            **keywords,
        )

    def add_part(name, target, places, side, blocks, part):
        kernel = part_kernel if part is not None else first_kernel
        before = [] if part is None else [part]
        (part,) = call_blocks(
            functools.partial(kernel, target),
            name,
            [image_type],
            places,
            side,
            blocks,
            *before,
            input_output_aliases={3: 0} if before else {},
        )
        return part

    side_type = ((3 * ncv + 16, rows), jnp.bfloat16)
    side, image = call(own_kernel, "own", [side_type, image_type], packed)
    met, image = lax.optimization_barrier((met, image))
    sides = [call(side_kernel, "side", [side_type], block)[0] for block in met]
    early, sides = lax.optimization_barrier((line[1:], sides))
    held, held_at = early + met + [packed], lines[1:] + partners + [(0, 0)]
    near = jnp.stack(held)
    other = sent(near, core)
    parts = [None for _ in partners]
    for blocks, offsets in ((near, lines[1:]), (other, beyond(lines[1:], core))):
        for k, hop in enumerate(partners):
            parts[k] = add_part("partner", hop, offsets, sides[k], blocks, parts[k])
    late, parts, image = lax.optimization_barrier((line[:1], parts, image))
    late = jnp.stack(late)
    other_late = sent(late, core)
    for k, hop in enumerate(partners):
        parts[k] = add_part("partner_late", hop, lines[:1], sides[k], late, parts[k])
    parts, image = lax.optimization_barrier((parts, image))
    image = add_part("add_met", (0, 0), partners, side, jnp.stack(met), image)
    other_late, parts, image = lax.optimization_barrier((other_late, parts, image))
    for k, hop in enumerate(partners):
        parts[k] = add_part(
            "partner_late", hop, beyond(lines[:1], core), sides[k], other_late, parts[k]
        )
    parts, image = lax.optimization_barrier((parts, image))
    received = [sent(part, hop) for hop, part in zip(partners, parts)]
    own_places = lines[1:] + beyond(held_at, core) + lines[:1] + beyond(lines[:1], core)
    blocks = jnp.concatenate([near[: n_row - 2], other, late, other_late])
    image = add_part("add_own", (0, 0), own_places, side, blocks, image)
    applied, gram = call(
        last_kernel,
        "last",
        [((nvec, rows), jnp.float32), ((devices, nvec // 2, 8 * nvec), jnp.float32)],
        vectors,
        root,
        image,
        *received,
    )
    grams = lax.all_to_all(gram, ("row", "col"), 0, 0)
    basis, ritz = call(
        functools.partial(finish_kernel, rows * devices),
        "finish",
        [((nvec, rows), jnp.float32), ((nvec, nvec), jnp.float32)],
        grams,
        applied,
        to=pl.BlockSpec(memory_space=pltpu.HBM),
        scratch_shapes=[
            pltpu.VMEM((nvec, rows), jnp.float32),
            pltpu.VMEM((nvec, nvec), jnp.float32),
            pltpu.SemaphoreType.DMA((2,)),
        ],
    )
    return (basis, ritz)


def solution(mesh):
    split = P(None, ("grp", "row", "col"))
    return jax.shard_map(
        per_device,
        mesh=mesh,
        in_specs=(split, split, P(("grp", "row", "col")), P()),
        out_specs=(split, P("grp", None)),
        check_vma=False,
    )
```

```python
import functools
import math

import jax
import jax.numpy as jnp
from jax import lax
from jax.experimental import pallas as pl
from jax.experimental.pallas import tpu as pltpu
from jax.sharding import PartitionSpec as P

unit = -math.log2(math.e) / 4.0

NT = (((1,), (1,)), ((), ()))
MIB = 1024 * 1024


def split3(x):
    high = x.astype(jnp.bfloat16).astype(jnp.float32)
    rest = x - high
    mid = rest.astype(jnp.bfloat16).astype(jnp.float32)
    low = (rest - mid).astype(jnp.bfloat16).astype(jnp.float32)
    return high, mid, low


def pack_kernel(
    frames_ref, vectors_in, degrees_ref, table_in,
    packed_ref, vectors_ref, root_ref, table_ref, degree_ref, sems,
):
    ncv = frames_ref.shape[0]
    copies = [
        pltpu.make_async_copy(vectors_in, vectors_ref, sems.at[0]),
        pltpu.make_async_copy(degrees_ref, degree_ref, sems.at[1]),
        pltpu.make_async_copy(frames_ref, packed_ref.at[pl.ds(0, ncv)], sems.at[2]),
        pltpu.make_async_copy(table_in, table_ref, sems.at[3]),
    ]
    for copy in copies:
        copy.start()
    copies[0].wait()
    copies[1].wait()
    root = lax.rsqrt(degree_ref[...])[None, :]
    root_ref[...] = root
    packed_ref[ncv:, :] = (vectors_ref[...].astype(jnp.float32) * root).astype(jnp.bfloat16)
    copies[2].wait()
    copies[3].wait()


def edge_rows(square, ones_first):
    high, mid, low = split3(square * unit)
    row = lax.broadcasted_iota(jnp.int32, (16, square.shape[1]), 0)
    base = 3 if ones_first else 0
    ones_at = 0 if ones_first else 3
    block = jnp.where((row >= ones_at) & (row < ones_at + 3), 1.0, 0.0)
    block = jnp.where(row == base, high, block)
    block = jnp.where(row == base + 1, mid, block)
    return jnp.where(row == base + 2, low, block)


def own_side(own):
    own = own.astype(jnp.float32)
    high, mid, low = split3(own * (-2.0 * unit))
    edge = edge_rows(jnp.sum(own * own, axis=0, keepdims=True), True)
    return jnp.concatenate([high, mid, low, edge], axis=0).astype(jnp.bfloat16)


def tile_image(side_ref, blocks):
    both = blocks[0] if len(blocks) == 1 else jnp.concatenate(blocks, axis=1)
    ncv = both.shape[0] // 2
    x, v = both[:ncv, :], both[ncv:, :]
    wide = x.astype(jnp.float32)
    edge = edge_rows(jnp.sum(wide * wide, axis=0, keepdims=True), False).astype(jnp.bfloat16)
    other = jnp.concatenate([x, x, x, edge], axis=0).T
    power = jnp.dot(other, side_ref[...], preferred_element_type=jnp.float32)
    kern = jnp.exp2(power).astype(jnp.bfloat16)
    return jnp.dot(v, kern, preferred_element_type=jnp.float32)


def own_kernel(packed_ref, side_ref, image_ref):
    side_ref[...] = own_side(packed_ref[: packed_ref.shape[0] // 2, :])
    image_ref[...] = tile_image(side_ref, [packed_ref[...]])


def add_blocks(target, places, sizes, table_ref, side_ref, blocks_ref, image_ref, list_ref):
    n_row, n_col = sizes
    my_row, my_col = lax.axis_index("row"), lax.axis_index("col")

    def number(offset):
        return (my_row ^ offset[0]) * n_col + (my_col ^ offset[1])

    first, second = table_ref[:, 0, :], table_ref[:, 1, :]
    me = number(target)
    other = jnp.where(first == me, second, jnp.where(second == me, first, -1))
    words = []
    for start in range(0, n_row * n_col, 16):
        bit = jnp.zeros(other.shape, jnp.float32)
        for b in range(16):
            bit = jnp.where(other == start + b, float(1 << b), bit)
        words.append(jnp.sum(bit).astype(jnp.int32))

    count = jnp.int32(0)
    for step, place in enumerate(places):
        block = number(place)
        word = words[0]
        for w in range(1, len(words)):
            word = jnp.where(block // 16 == w, words[w], word)
        list_ref[count] = step
        count += (word >> (block % 16)) & 1

    def add_group(start, size):
        blocks = [blocks_ref[list_ref[start + k]] for k in range(size)]
        image_ref[...] += tile_image(side_ref, blocks)

    def add_triple(group, _):
        add_group(3 * group, 3)
        return 0

    def add_pair(group, _):
        add_group(3 * triples + 2 * group, 2)
        return 0

    triples = jnp.maximum(count // 3 - (count % 3 == 1).astype(jnp.int32), 0)
    rest = count - 3 * triples
    if len(places) >= 3:
        lax.fori_loop(0, triples, add_triple, 0)
    if len(places) >= 2:
        lax.fori_loop(0, rest // 2, add_pair, 0)

    @pl.when(rest == 1)
    def _():
        add_group(0, 1)


def meet_kernel(
    places, sizes, table_ref, side_ref, blocks_ref, before_ref, image_ref, partner_side_ref, list_ref
):
    partner_side_ref[...] = own_side(blocks_ref[0, : blocks_ref.shape[1] // 2, :])
    image_ref[...] = before_ref[...]
    add_blocks((0, 0), places, sizes, table_ref, side_ref, blocks_ref, image_ref, list_ref)


def first_kernel(target, places, sizes, table_ref, side_ref, blocks_ref, image_ref, list_ref):
    image_ref[...] = jnp.zeros_like(image_ref)
    add_blocks(target, places, sizes, table_ref, side_ref, blocks_ref, image_ref, list_ref)


def part_kernel(
    target, places, sizes, table_ref, side_ref, blocks_ref, before_ref, image_ref, list_ref
):
    image_ref[...] = before_ref[...]
    add_blocks(target, places, sizes, table_ref, side_ref, blocks_ref, image_ref, list_ref)


def last_kernel(vectors_ref, root_ref, *refs):
    *part_refs, applied_ref, gram_ref = refs
    image = sum(part_ref[...] for part_ref in part_refs)
    n = vectors_ref.shape[0]
    applied = image * root_ref[...]
    applied_ref[...] = applied
    both = jnp.concatenate([applied, vectors_ref[...].astype(jnp.float32)], axis=0)
    gram = lax.dot_general(
        both, both, NT, precision=lax.Precision.HIGHEST, preferred_element_type=jnp.float32
    )
    wide = jnp.concatenate(
        [gram[:n, :n], gram[n:, :], jnp.zeros((n, n), jnp.float32)], axis=1
    )
    tile = jnp.concatenate([wide[: n // 2, :], wide[n // 2 :, :]], axis=1)
    for device in range(gram_ref.shape[0]):
        gram_ref[device] = tile


def inverse_factors(grams):
    n = grams[0].shape[0]
    half = 64
    tiles = range(n // 8)
    shape = (8, 2 * half)
    row = lax.broadcasted_iota(jnp.int32, shape, 0)
    lane = lax.broadcasted_iota(jnp.int32, shape, 1)
    columns = [
        [
            jnp.where(
                lane < half,
                jnp.broadcast_to(grams[0][8 * t : 8 * t + 8, j : j + 1], shape),
                jnp.broadcast_to(grams[1][8 * t : 8 * t + 8, j : j + 1], shape),
            )
            for t in tiles
        ]
        for j in range(n)
    ]
    right = [jnp.where(lane % half == row + 8 * t, 1.0, 0.0) for t in tiles]
    pivots = [jnp.ones(shape, jnp.float32) for t in tiles]
    for k in range(n):
        top, at = k // 8, k % 8
        pivot = columns[k][top][at : at + 1, :]
        pivots[top] = jnp.where(row == at, pivot, pivots[top])
        if k == n - 1:
            break
        scale = 1.0 / pivot
        factor = {t: columns[k][t] * scale for t in tiles if t >= top}
        factor[top] = jnp.where(row > at, factor[top], 0.0)
        for column in columns[k + 1 :] + [right]:
            line = column[top][at : at + 1, :]
            for t in factor:
                column[t] = column[t] - factor[t] * line
    result = jnp.concatenate([r * lax.rsqrt(p) for r, p in zip(right, pivots)], axis=0)
    return result[:, :n], result[:, half : half + n]


def finish_kernel(total_frames, grams_ref, applied_ref, basis_ref, ritz_ref):
    tile = grams_ref[0]
    for device in range(1, grams_ref.shape[0]):
        tile += grams_ref[device]
    n = applied_ref.shape[0]
    gram = jnp.concatenate([tile[:, : 4 * n], tile[:, 4 * n :]], axis=0)
    exact = functools.partial(
        lax.dot_general, precision=lax.Precision.HIGHEST, preferred_element_type=jnp.float32
    )
    plain = (((1,), (0,)), ((), ()))
    image_inverse, vector_inverse = inverse_factors([gram[:, :n], gram[:, 2 * n : 3 * n]])
    basis_ref[...] = exact(image_inverse * math.sqrt(total_frames), applied_ref[...], plain)
    half = exact(vector_inverse, gram[:, n : 2 * n], plain)
    ritz_ref[...] = exact(half, vector_inverse, NT)


def sent(x, hop):
    n_row, n_col = lax.axis_size("row"), lax.axis_size("col")
    pairs = [
        (r * n_col + c, (r ^ hop[0]) * n_col + (c ^ hop[1]))
        for r in range(n_row)
        for c in range(n_col)
    ]
    return lax.ppermute(x, ("row", "col"), pairs)


def beyond(offsets, hop):
    return [(r ^ hop[0], c ^ hop[1]) for r, c in offsets]


def per_device(frames, vectors, degrees, tile_table):
    ncv, rows = frames.shape
    nvec = vectors.shape[0]
    n_row, n_col = lax.axis_size("row"), lax.axis_size("col")
    devices = n_row * n_col
    sizes = (n_row, n_col)
    vmem = pl.BlockSpec(memory_space=pltpu.VMEM)

    def call(kernel, name, outs, *args, limit=24, where=vmem, **keywords):
        shapes = [jax.ShapeDtypeStruct(*out) for out in outs]
        return pl.pallas_call(
            kernel,
            out_shape=shapes,
            in_specs=[where] * len(args),
            out_specs=[vmem] * len(outs),
            compiler_params=pltpu.CompilerParams(vmem_limit_bytes=limit * MIB),
            name=name,
            **keywords,
        )(*args)

    image_type = ((nvec, rows), jnp.float32)

    table = tile_table.transpose(1, 2, 0)
    packed, vectors, root, table = call(
        pack_kernel,
        "pack",
        [
            ((ncv + nvec, rows), jnp.bfloat16),
            (vectors.shape, vectors.dtype),
            ((1, rows), jnp.float32),
            (table.shape, table.dtype),
        ],
        *(
            pltpu.with_memory_space_constraint(x, pltpu.HBM)
            for x in (frames, vectors, degrees, table)
        ),
        where=pl.BlockSpec(memory_space=pltpu.HBM),
        scratch_shapes=[
            pltpu.VMEM(degrees.shape, degrees.dtype),
            pltpu.SemaphoreType.DMA((4,)),
        ],
    )
    core = (0, 1)
    lines = [(r, 1) for r in range(n_row - 1, 0, -1)]
    if n_row == 4:
        lines = [(3, 1), (1, 1), (2, 1)]
    partners = [(0, c) for c in range(3, n_col, 2)]
    met = [sent(packed, hop) for hop in partners]
    line = [sent(packed, hop) for hop in lines]

    def call_blocks(kernel, name, outs, places, *args, **keywords):
        return call(
            functools.partial(kernel, places, sizes),
            name,
            outs,
            table,
            *args,
            scratch_shapes=[pltpu.SMEM((len(places) + 1,), jnp.int32)],
            **keywords,
        )

    def add_part(name, target, places, side, blocks, part):
        kernel = part_kernel if part is not None else first_kernel
        before = [] if part is None else [part]
        (part,) = call_blocks(
            functools.partial(kernel, target),
            name,
            [image_type],
            places,
            side,
            blocks,
            *before,
            input_output_aliases={3: 0} if before else {},
        )
        return part

    side_type = ((3 * ncv + 16, rows), jnp.bfloat16)
    side, image = call(own_kernel, "own", [side_type, image_type], packed)
    met, image = lax.optimization_barrier((met, image))
    sides = []
    for hop, block in zip(partners, met):
        image, partner_side = call_blocks(
            meet_kernel,
            "meet",
            [image_type, side_type],
            [hop],
            side,
            block[None],
            image,
            input_output_aliases={3: 0},
        )
        sides.append(partner_side)
    early, image = lax.optimization_barrier((line[1:], image))
    held, held_at = early + met + [packed], lines[1:] + partners + [(0, 0)]
    near = jnp.stack(held)
    other = sent(near, core)
    parts = [None] * len(partners)
    for k, hop in enumerate(partners):
        parts[k] = add_part("partner", hop, lines[1:], sides[k], near, None)
    late, parts, image = lax.optimization_barrier((line[:1], parts, image))
    late = jnp.stack(late)
    other_late = sent(late, core)
    middle = jnp.concatenate([other[: n_row - 2], late])
    for k, hop in enumerate(partners):
        places = beyond(lines[1:], core) + lines[:1]
        parts[k] = add_part("partner_middle", hop, places, sides[k], middle, parts[k])
    other_late, parts = lax.optimization_barrier((other_late, parts))
    for k, hop in enumerate(partners):
        parts[k] = add_part(
            "partner_late", hop, beyond(lines[:1], core), sides[k], other_late, parts[k]
        )
    parts, image = lax.optimization_barrier((parts, image))
    received = [sent(part, hop) for hop, part in zip(partners, parts)]
    own_places = lines[1:] + beyond(held_at, core) + lines[:1] + beyond(lines[:1], core)
    blocks = jnp.concatenate([near[: n_row - 2], other, late, other_late])
    image = add_part("add_own", (0, 0), own_places, side, blocks, image)
    applied, gram = call(
        last_kernel,
        "last",
        [((nvec, rows), jnp.float32), ((devices, nvec // 2, 8 * nvec), jnp.float32)],
        vectors,
        root,
        image,
        *received,
    )
    grams = lax.all_to_all(gram, ("row", "col"), 0, 0)
    basis, ritz = call(
        functools.partial(finish_kernel, rows * devices),
        "finish",
        [((nvec, rows), jnp.float32), ((nvec, nvec), jnp.float32)],
        grams,
        applied,
    )
    return (basis, ritz)


def solution(mesh):
    split = P(None, ("grp", "row", "col"))
    return jax.shard_map(
        per_device,
        mesh=mesh,
        in_specs=(split, split, P(("grp", "row", "col")), P()),
        out_specs=(split, P("grp", None)),
        check_vma=False,
    )
```

```python
import functools
import math

import jax
import jax.numpy as jnp
from jax import lax
from jax.experimental import pallas as pl
from jax.experimental.pallas import tpu as pltpu
from jax.sharding import PartitionSpec as P

unit = -math.log2(math.e) / 4.0

NT = (((1,), (1,)), ((), ()))
MIB = 1024 * 1024


def split3(x):
    high = x.astype(jnp.bfloat16).astype(jnp.float32)
    rest = x - high
    mid = rest.astype(jnp.bfloat16).astype(jnp.float32)
    low = (rest - mid).astype(jnp.bfloat16).astype(jnp.float32)
    return high, mid, low


def pack_kernel(
    frames_ref, vectors_in, degrees_ref, table_in,
    packed_ref, vectors_ref, root_ref, table_ref, degree_ref, sems,
):
    ncv = frames_ref.shape[0]
    copies = [
        pltpu.make_async_copy(vectors_in, vectors_ref, sems.at[0]),
        pltpu.make_async_copy(degrees_ref, degree_ref, sems.at[1]),
        pltpu.make_async_copy(frames_ref, packed_ref.at[pl.ds(0, ncv)], sems.at[2]),
        pltpu.make_async_copy(table_in, table_ref, sems.at[3]),
    ]
    for copy in copies:
        copy.start()
    copies[0].wait()
    copies[1].wait()
    root = lax.rsqrt(degree_ref[...])[None, :]
    root_ref[...] = root
    packed_ref[ncv:, :] = (vectors_ref[...].astype(jnp.float32) * root).astype(jnp.bfloat16)
    copies[2].wait()
    copies[3].wait()


def edge_rows(square, ones_first):
    high, mid, low = split3(square * unit)
    row = lax.broadcasted_iota(jnp.int32, (16, square.shape[1]), 0)
    base = 3 if ones_first else 0
    ones_at = 0 if ones_first else 3
    block = jnp.where((row >= ones_at) & (row < ones_at + 3), 1.0, 0.0)
    block = jnp.where(row == base, high, block)
    block = jnp.where(row == base + 1, mid, block)
    return jnp.where(row == base + 2, low, block)


def own_side(own):
    own = own.astype(jnp.float32)
    high, mid, low = split3(own * (-2.0 * unit))
    edge = edge_rows(jnp.sum(own * own, axis=0, keepdims=True), True)
    return jnp.concatenate([high, mid, low, edge], axis=0).astype(jnp.bfloat16)


def tile_image(side_ref, blocks):
    both = blocks[0] if len(blocks) == 1 else jnp.concatenate(blocks, axis=1)
    ncv = both.shape[0] // 2
    x, v = both[:ncv, :], both[ncv:, :]
    wide = x.astype(jnp.float32)
    edge = edge_rows(jnp.sum(wide * wide, axis=0, keepdims=True), False).astype(jnp.bfloat16)
    other = jnp.concatenate([x, x, x, edge], axis=0).T
    power = jnp.dot(other, side_ref[...], preferred_element_type=jnp.float32)
    kern = jnp.exp2(power).astype(jnp.bfloat16)
    return jnp.dot(v, kern, preferred_element_type=jnp.float32)


def own_kernel(targets, sizes, table_ref, packed_ref, side_ref, image_ref, masks_ref):
    n_row, n_col = sizes
    my_row, my_col = lax.axis_index("row"), lax.axis_index("col")
    first, second = table_ref[:, 0, :], table_ref[:, 1, :]
    for t, target in enumerate(targets):
        block = (my_row ^ target[0]) * n_col + (my_col ^ target[1])
        other = jnp.where(first == block, second, jnp.where(second == block, first, -1))
        for word in range(n_row * n_col // 16):
            bit = jnp.zeros(other.shape, jnp.float32)
            for b in range(16):
                bit = jnp.where(other == 16 * word + b, float(1 << b), bit)
            masks_ref[t, word] = jnp.sum(bit).astype(jnp.int32)
    side_ref[...] = own_side(packed_ref[: packed_ref.shape[0] // 2, :])
    image_ref[...] = tile_image(side_ref, [packed_ref[...]])


def add_blocks(target, places, sizes, masks_ref, side_ref, blocks_ref, image_ref, list_ref):
    my_row, my_col = lax.axis_index("row"), lax.axis_index("col")

    count = jnp.int32(0)
    for step, place in enumerate(places):
        block = (my_row ^ place[0]) * sizes[1] + (my_col ^ place[1])
        list_ref[count] = step
        count += (masks_ref[target, block // 16] >> (block % 16)) & 1

    def add_group(start, size):
        blocks = [blocks_ref[list_ref[start + k]] for k in range(size)]
        image_ref[...] += tile_image(side_ref, blocks)

    def add_triple(group, _):
        add_group(3 * group, 3)
        return 0

    def add_pair(group, _):
        add_group(3 * triples + 2 * group, 2)
        return 0

    triples = jnp.maximum(count // 3 - (count % 3 == 1).astype(jnp.int32), 0)
    rest = count - 3 * triples
    if len(places) >= 3:
        lax.fori_loop(0, triples, add_triple, 0)
    if len(places) >= 2:
        lax.fori_loop(0, rest // 2, add_pair, 0)

    @pl.when(rest == 1)
    def _():
        add_group(0, 1)


def meet_kernel(
    places, sizes, masks_ref, side_ref, blocks_ref, before_ref, image_ref, partner_side_ref, list_ref
):
    partner_side_ref[...] = own_side(blocks_ref[0, : blocks_ref.shape[1] // 2, :])
    image_ref[...] = before_ref[...]
    add_blocks(0, places, sizes, masks_ref, side_ref, blocks_ref, image_ref, list_ref)


def first_kernel(target, places, sizes, masks_ref, side_ref, blocks_ref, image_ref, list_ref):
    image_ref[...] = jnp.zeros_like(image_ref)
    add_blocks(target, places, sizes, masks_ref, side_ref, blocks_ref, image_ref, list_ref)


def part_kernel(
    target, places, sizes, masks_ref, side_ref, blocks_ref, before_ref, image_ref, list_ref
):
    image_ref[...] = before_ref[...]
    add_blocks(target, places, sizes, masks_ref, side_ref, blocks_ref, image_ref, list_ref)


def last_kernel(vectors_ref, root_ref, *refs):
    *part_refs, applied_ref, gram_ref = refs
    image = sum(part_ref[...] for part_ref in part_refs)
    n = vectors_ref.shape[0]
    applied = image * root_ref[...]
    applied_ref[...] = applied
    both = jnp.concatenate([applied, vectors_ref[...].astype(jnp.float32)], axis=0)
    gram = lax.dot_general(
        both, both, NT, precision=lax.Precision.HIGHEST, preferred_element_type=jnp.float32
    )
    wide = jnp.concatenate(
        [gram[:n, :n], gram[n:, :], jnp.zeros((n, n), jnp.float32)], axis=1
    )
    tile = jnp.concatenate([wide[: n // 2, :], wide[n // 2 :, :]], axis=1)
    for device in range(gram_ref.shape[0]):
        gram_ref[device] = tile


def inverse_factors(grams):
    n = grams[0].shape[0]
    half = 64
    tiles = range(n // 8)
    shape = (8, 2 * half)
    row = lax.broadcasted_iota(jnp.int32, shape, 0)
    lane = lax.broadcasted_iota(jnp.int32, shape, 1)
    columns = [
        [
            jnp.where(
                lane < half,
                jnp.broadcast_to(grams[0][8 * t : 8 * t + 8, j : j + 1], shape),
                jnp.broadcast_to(grams[1][8 * t : 8 * t + 8, j : j + 1], shape),
            )
            for t in tiles
        ]
        for j in range(n)
    ]
    right = [jnp.where(lane % half == row + 8 * t, 1.0, 0.0) for t in tiles]
    pivots = [jnp.ones(shape, jnp.float32) for t in tiles]
    for k in range(n):
        top, at = k // 8, k % 8
        pivot = columns[k][top][at : at + 1, :]
        pivots[top] = jnp.where(row == at, pivot, pivots[top])
        if k == n - 1:
            break
        scale = 1.0 / pivot
        factor = {t: columns[k][t] * scale for t in tiles if t >= top}
        factor[top] = jnp.where(row > at, factor[top], 0.0)
        for column in columns[k + 1 :] + [right]:
            line = column[top][at : at + 1, :]
            for t in factor:
                column[t] = column[t] - factor[t] * line
    result = jnp.concatenate([r * lax.rsqrt(p) for r, p in zip(right, pivots)], axis=0)
    return result[:, :n], result[:, half : half + n]


def finish_kernel(total_frames, grams_ref, applied_ref, basis_ref, ritz_ref):
    tile = grams_ref[0]
    for device in range(1, grams_ref.shape[0]):
        tile += grams_ref[device]
    n = applied_ref.shape[0]
    gram = jnp.concatenate([tile[:, : 4 * n], tile[:, 4 * n :]], axis=0)
    exact = functools.partial(
        lax.dot_general, precision=lax.Precision.HIGHEST, preferred_element_type=jnp.float32
    )
    plain = (((1,), (0,)), ((), ()))
    image_inverse, vector_inverse = inverse_factors([gram[:, :n], gram[:, 2 * n : 3 * n]])
    basis_ref[...] = exact(image_inverse * math.sqrt(total_frames), applied_ref[...], plain)
    half = exact(vector_inverse, gram[:, n : 2 * n], plain)
    ritz_ref[...] = exact(half, vector_inverse, NT)


def sent(x, hop):
    n_row, n_col = lax.axis_size("row"), lax.axis_size("col")
    pairs = [
        (r * n_col + c, (r ^ hop[0]) * n_col + (c ^ hop[1]))
        for r in range(n_row)
        for c in range(n_col)
    ]
    return lax.ppermute(x, ("row", "col"), pairs)


def beyond(offsets, hop):
    return [(r ^ hop[0], c ^ hop[1]) for r, c in offsets]


def per_device(frames, vectors, degrees, tile_table):
    ncv, rows = frames.shape
    nvec = vectors.shape[0]
    n_row, n_col = lax.axis_size("row"), lax.axis_size("col")
    devices = n_row * n_col
    sizes = (n_row, n_col)
    vmem = pl.BlockSpec(memory_space=pltpu.VMEM)
    smem = pl.BlockSpec(memory_space=pltpu.SMEM)

    def call(kernel, name, outs, *args, limit=24, where=vmem, to=vmem, **keywords):
        shapes = [jax.ShapeDtypeStruct(*out) if isinstance(out, tuple) else out for out in outs]
        where = where if isinstance(where, list) else [where] * len(args)
        to = to if isinstance(to, list) else [to] * len(outs)
        return pl.pallas_call(
            kernel,
            out_shape=shapes,
            in_specs=where,
            out_specs=to,
            compiler_params=pltpu.CompilerParams(vmem_limit_bytes=limit * MIB),
            name=name,
            **keywords,
        )(*args)

    image_type = ((nvec, rows), jnp.float32)

    table = tile_table.transpose(1, 2, 0)
    packed, vectors, root, table = call(
        pack_kernel,
        "pack",
        [
            ((ncv + nvec, rows), jnp.bfloat16),
            (vectors.shape, vectors.dtype),
            ((1, rows), jnp.float32),
            (table.shape, table.dtype),
        ],
        *(
            pltpu.with_memory_space_constraint(x, pltpu.HBM)
            for x in (frames, vectors, degrees, table)
        ),
        where=pl.BlockSpec(memory_space=pltpu.HBM),
        scratch_shapes=[
            pltpu.VMEM(degrees.shape, degrees.dtype),
            pltpu.SemaphoreType.DMA((4,)),
        ],
    )
    core = (0, 1)
    lines = [(r, 1) for r in range(n_row - 1, 0, -1)]
    if n_row == 4:
        lines = [(3, 1), (1, 1), (2, 1)]
    partners = [(0, c) for c in range(3, n_col, 2)]
    met = [sent(packed, hop) for hop in partners]
    line = [sent(packed, hop) for hop in lines]

    def call_blocks(kernel, name, outs, places, *args, **keywords):
        return call(
            functools.partial(kernel, places, sizes),
            name,
            outs,
            masks,
            *args,
            where=[smem] + [vmem] * len(args),
            scratch_shapes=[pltpu.SMEM((len(places) + 1,), jnp.int32)],
            **keywords,
        )

    def add_part(name, target, places, side, blocks, part):
        kernel = part_kernel if part is not None else first_kernel
        before = [] if part is None else [part]
        (part,) = call_blocks(
            functools.partial(kernel, targets.index(target)),
            name,
            [image_type],
            places,
            side,
            blocks,
            *before,
            input_output_aliases={3: 0} if before else {},
        )
        return part

    side_type = ((3 * ncv + 16, rows), jnp.bfloat16)
    targets = [(0, 0)] + partners
    side, image, masks = call(
        functools.partial(own_kernel, targets, sizes),
        "own",
        [side_type, image_type, pltpu.SMEM((len(targets), devices // 16), jnp.int32)],
        table,
        packed,
        to=[vmem, vmem, smem],
    )
    met, image = lax.optimization_barrier((met, image))
    sides = []
    for hop, block in zip(partners, met):
        image, partner_side = call_blocks(
            meet_kernel,
            "meet",
            [image_type, side_type],
            [hop],
            side,
            block[None],
            image,
            input_output_aliases={3: 0},
        )
        sides.append(partner_side)
    early, image = lax.optimization_barrier((line[1:], image))
    held, held_at = early + met + [packed], lines[1:] + partners + [(0, 0)]
    near = jnp.stack(held)
    other = sent(near, core)
    parts = [None] * len(partners)
    for k, hop in enumerate(partners):
        parts[k] = add_part("partner", hop, lines[1:], sides[k], near, None)
    late, parts, image = lax.optimization_barrier((line[:1], parts, image))
    late = jnp.stack(late)
    other_late = sent(late, core)
    middle = jnp.concatenate([other[: n_row - 2], late])
    for k, hop in enumerate(partners):
        places = beyond(lines[1:], core) + lines[:1]
        parts[k] = add_part("partner_middle", hop, places, sides[k], middle, parts[k])
    other_late, parts = lax.optimization_barrier((other_late, parts))
    for k, hop in enumerate(partners):
        parts[k] = add_part(
            "partner_late", hop, beyond(lines[:1], core), sides[k], other_late, parts[k]
        )
    parts, image = lax.optimization_barrier((parts, image))
    received = [sent(part, hop) for hop, part in zip(partners, parts)]
    own_places = lines[1:] + beyond(held_at, core) + lines[:1] + beyond(lines[:1], core)
    blocks = jnp.concatenate([near[: n_row - 2], other, late, other_late])
    image = add_part("add_own", (0, 0), own_places, side, blocks, image)
    applied, gram = call(
        last_kernel,
        "last",
        [((nvec, rows), jnp.float32), ((devices, nvec // 2, 8 * nvec), jnp.float32)],
        vectors,
        root,
        image,
        *received,
    )
    grams = lax.all_to_all(gram, ("row", "col"), 0, 0)
    basis, ritz = call(
        functools.partial(finish_kernel, rows * devices),
        "finish",
        [((nvec, rows), jnp.float32), ((nvec, nvec), jnp.float32)],
        grams,
        applied,
    )
    return (basis, ritz)


def solution(mesh):
    split = P(None, ("grp", "row", "col"))
    return jax.shard_map(
        per_device,
        mesh=mesh,
        in_specs=(split, split, P(("grp", "row", "col")), P()),
        out_specs=(split, P("grp", None)),
        check_vma=False,
    )
```

```python
import functools
import math

import jax
import jax.numpy as jnp
from jax import lax
from jax.experimental import pallas as pl
from jax.experimental.pallas import tpu as pltpu
from jax.sharding import PartitionSpec as P

unit = -math.log2(math.e) / 4.0

NT = (((1,), (1,)), ((), ()))
MIB = 1024 * 1024


def split3(x):
    high = x.astype(jnp.bfloat16).astype(jnp.float32)
    rest = x - high
    mid = rest.astype(jnp.bfloat16).astype(jnp.float32)
    low = (rest - mid).astype(jnp.bfloat16).astype(jnp.float32)
    return high, mid, low


def pack_kernel(
    frames_ref, vectors_in, degrees_ref, table_in,
    packed_ref, vectors_ref, root_ref, table_ref, degree_ref, sems,
):
    ncv = frames_ref.shape[0]
    copies = [
        pltpu.make_async_copy(vectors_in, vectors_ref, sems.at[0]),
        pltpu.make_async_copy(degrees_ref, degree_ref, sems.at[1]),
        pltpu.make_async_copy(frames_ref, packed_ref.at[pl.ds(0, ncv)], sems.at[2]),
        pltpu.make_async_copy(table_in, table_ref, sems.at[3]),
    ]
    for copy in copies:
        copy.start()
    copies[0].wait()
    copies[1].wait()
    root = lax.rsqrt(degree_ref[...])[None, :]
    root_ref[...] = root
    packed_ref[ncv:, :] = (vectors_ref[...].astype(jnp.float32) * root).astype(jnp.bfloat16)
    copies[2].wait()
    copies[3].wait()


def edge_rows(square, ones_first):
    high, mid, low = split3(square * unit)
    row = lax.broadcasted_iota(jnp.int32, (16, square.shape[1]), 0)
    base = 3 if ones_first else 0
    ones_at = 0 if ones_first else 3
    block = jnp.where((row >= ones_at) & (row < ones_at + 3), 1.0, 0.0)
    block = jnp.where(row == base, high, block)
    block = jnp.where(row == base + 1, mid, block)
    return jnp.where(row == base + 2, low, block)


def own_side(own):
    own = own.astype(jnp.float32)
    high, mid, low = split3(own * (-2.0 * unit))
    edge = edge_rows(jnp.sum(own * own, axis=0, keepdims=True), True)
    return jnp.concatenate([high, mid, low, edge], axis=0).astype(jnp.bfloat16)


def tile_image(side_ref, blocks):
    both = blocks[0] if len(blocks) == 1 else jnp.concatenate(blocks, axis=1)
    ncv = both.shape[0] // 2
    x, v = both[:ncv, :], both[ncv:, :]
    wide = x.astype(jnp.float32)
    edge = edge_rows(jnp.sum(wide * wide, axis=0, keepdims=True), False).astype(jnp.bfloat16)
    other = jnp.concatenate([x, x, x, edge], axis=0).T
    power = jnp.dot(other, side_ref[...], preferred_element_type=jnp.float32)
    kern = jnp.exp2(power).astype(jnp.bfloat16)
    return jnp.dot(v, kern, preferred_element_type=jnp.float32)


def own_kernel(targets, sizes, table_ref, packed_ref, side_ref, image_ref, masks_ref):
    n_row, n_col = sizes
    my_row, my_col = lax.axis_index("row"), lax.axis_index("col")
    first, second = table_ref[:, 0, :], table_ref[:, 1, :]
    for t, target in enumerate(targets):
        block = (my_row ^ target[0]) * n_col + (my_col ^ target[1])
        other = jnp.where(first == block, second, jnp.where(second == block, first, -1))
        for word in range(n_row * n_col // 16):
            bit = jnp.zeros(other.shape, jnp.float32)
            for b in range(16):
                bit = jnp.where(other == 16 * word + b, float(1 << b), bit)
            masks_ref[t, word] = jnp.sum(bit).astype(jnp.int32)
    side_ref[...] = own_side(packed_ref[: packed_ref.shape[0] // 2, :])
    image_ref[...] = tile_image(side_ref, [packed_ref[...]])


def add_blocks(target, places, sizes, masks_ref, side_ref, blocks_ref, image_ref, list_ref):
    my_row, my_col = lax.axis_index("row"), lax.axis_index("col")

    count = jnp.int32(0)
    for step, place in enumerate(places):
        block = (my_row ^ place[0]) * sizes[1] + (my_col ^ place[1])
        list_ref[count] = step
        count += (masks_ref[target, block // 16] >> (block % 16)) & 1

    def add_group(start, size):
        blocks = [blocks_ref[list_ref[start + k]] for k in range(size)]
        image_ref[...] += tile_image(side_ref, blocks)

    def add_triple(group, _):
        add_group(3 * group, 3)
        return 0

    def add_pair(group, _):
        add_group(3 * triples + 2 * group, 2)
        return 0

    triples = jnp.maximum(count // 3 - (count % 3 == 1).astype(jnp.int32), 0)
    rest = count - 3 * triples
    if len(places) >= 3:
        lax.fori_loop(0, triples, add_triple, 0)
    if len(places) >= 2:
        lax.fori_loop(0, rest // 2, add_pair, 0)

    @pl.when(rest == 1)
    def _():
        add_group(0, 1)


def meet_kernel(
    places, sizes, masks_ref, side_ref, blocks_ref, before_ref, image_ref, partner_side_ref, list_ref
):
    partner_side_ref[...] = own_side(blocks_ref[0, : blocks_ref.shape[1] // 2, :])
    image_ref[...] = before_ref[...]
    add_blocks(0, places, sizes, masks_ref, side_ref, blocks_ref, image_ref, list_ref)


def first_kernel(target, places, sizes, masks_ref, side_ref, blocks_ref, image_ref, list_ref):
    image_ref[...] = jnp.zeros_like(image_ref)
    add_blocks(target, places, sizes, masks_ref, side_ref, blocks_ref, image_ref, list_ref)


def part_kernel(
    target, places, sizes, masks_ref, side_ref, blocks_ref, before_ref, image_ref, list_ref
):
    image_ref[...] = before_ref[...]
    add_blocks(target, places, sizes, masks_ref, side_ref, blocks_ref, image_ref, list_ref)


def last_kernel(vectors_ref, root_ref, *refs):
    *part_refs, applied_ref, gram_ref = refs
    image = sum(part_ref[...] for part_ref in part_refs)
    n = vectors_ref.shape[0]
    applied = image * root_ref[...]
    applied_ref[...] = applied
    high, mid, low = split3(applied)
    pieces = jnp.concatenate(
        [high, mid, low, vectors_ref[...].astype(jnp.float32)], axis=0
    ).astype(jnp.bfloat16)
    product = lax.dot_general(pieces, pieces, NT, preferred_element_type=jnp.float32)
    rows = jnp.concatenate([product[:n] + product[n : 2 * n] + product[2 * n : 3 * n], product[3 * n :]], axis=0)
    gram = rows[:, :n] + rows[:, n : 2 * n] + rows[:, 2 * n : 3 * n]
    wide = jnp.concatenate(
        [gram[:n, :], gram[n:, :], rows[n:, 3 * n :], jnp.zeros((n, n), jnp.float32)], axis=1
    )
    tile = jnp.concatenate([wide[: n // 2, :], wide[n // 2 :, :]], axis=1)
    for device in range(gram_ref.shape[0]):
        gram_ref[device] = tile


def inverse_factors(grams):
    n = grams[0].shape[0]
    half = 64
    tiles = range(n // 8)
    shape = (8, 2 * half)
    row = lax.broadcasted_iota(jnp.int32, shape, 0)
    lane = lax.broadcasted_iota(jnp.int32, shape, 1)
    columns = [
        [
            jnp.where(
                lane < half,
                jnp.broadcast_to(grams[0][8 * t : 8 * t + 8, j : j + 1], shape),
                jnp.broadcast_to(grams[1][8 * t : 8 * t + 8, j : j + 1], shape),
            )
            for t in tiles
        ]
        for j in range(n)
    ]
    right = [jnp.where(lane % half == row + 8 * t, 1.0, 0.0) for t in tiles]
    done = [jnp.zeros(shape, jnp.float32) for t in tiles]
    for k in range(0, n, 2):
        top, at = k // 8, k % 8
        left, next_left = columns[k], columns[k + 1]
        a, b = left[top][at : at + 1, :], left[top][at + 1 : at + 2, :]
        d = next_left[top][at + 1 : at + 2, :]
        det = a * d - b * b
        root = lax.rsqrt(a)
        line, next_line = right[top][at : at + 1, :], right[top][at + 1 : at + 2, :]
        lower = (next_line - line * (b * root * root)) * (lax.rsqrt(det) * a * root)
        done[top] = jnp.where(row == at, line * root, jnp.where(row == at + 1, lower, done[top]))
        if k + 2 == n:
            break
        scale = 1.0 / det
        p, q, s = d * scale, b * scale, a * scale
        factor = {t: left[t] * p - next_left[t] * q for t in tiles if t >= top}
        next_factor = {t: next_left[t] * s - left[t] * q for t in tiles if t >= top}
        factor[top] = jnp.where(row > at + 1, factor[top], 0.0)
        next_factor[top] = jnp.where(row > at + 1, next_factor[top], 0.0)
        for column in columns[k + 2 :] + [right]:
            line, next_line = column[top][at : at + 1, :], column[top][at + 1 : at + 2, :]
            for t in factor:
                column[t] = column[t] - (factor[t] * line + next_factor[t] * next_line)
    result = jnp.concatenate(done, axis=0)
    return result[:, :n], result[:, half : half + n]


def finish_kernel(total_frames, grams_ref, applied_ref, basis_ref, ritz_ref):
    tile = grams_ref[0]
    for device in range(1, grams_ref.shape[0]):
        tile += grams_ref[device]
    n = applied_ref.shape[0]
    gram = jnp.concatenate([tile[:, : 4 * n], tile[:, 4 * n :]], axis=0)
    exact = functools.partial(
        lax.dot_general, precision=lax.Precision.HIGHEST, preferred_element_type=jnp.float32
    )
    plain = (((1,), (0,)), ((), ()))
    image_inverse, vector_inverse = inverse_factors([gram[:, :n], gram[:, 2 * n : 3 * n]])
    basis_ref[...] = exact(image_inverse * math.sqrt(total_frames), applied_ref[...], plain)
    half = exact(vector_inverse, gram[:, n : 2 * n], plain)
    ritz_ref[...] = exact(half, vector_inverse, NT)


def sent(x, hop):
    n_row, n_col = lax.axis_size("row"), lax.axis_size("col")
    pairs = [
        (r * n_col + c, (r ^ hop[0]) * n_col + (c ^ hop[1]))
        for r in range(n_row)
        for c in range(n_col)
    ]
    return lax.ppermute(x, ("row", "col"), pairs)


def beyond(offsets, hop):
    return [(r ^ hop[0], c ^ hop[1]) for r, c in offsets]


def per_device(frames, vectors, degrees, tile_table):
    ncv, rows = frames.shape
    nvec = vectors.shape[0]
    n_row, n_col = lax.axis_size("row"), lax.axis_size("col")
    devices = n_row * n_col
    sizes = (n_row, n_col)
    vmem = pl.BlockSpec(memory_space=pltpu.VMEM)
    smem = pl.BlockSpec(memory_space=pltpu.SMEM)

    def call(kernel, name, outs, *args, limit=24, where=vmem, to=vmem, **keywords):
        shapes = [jax.ShapeDtypeStruct(*out) if isinstance(out, tuple) else out for out in outs]
        where = where if isinstance(where, list) else [where] * len(args)
        to = to if isinstance(to, list) else [to] * len(outs)
        return pl.pallas_call(
            kernel,
            out_shape=shapes,
            in_specs=where,
            out_specs=to,
            compiler_params=pltpu.CompilerParams(vmem_limit_bytes=limit * MIB),
            name=name,
            **keywords,
        )(*args)

    image_type = ((nvec, rows), jnp.float32)

    table = tile_table.transpose(1, 2, 0)
    packed, vectors, root, table = call(
        pack_kernel,
        "pack",
        [
            ((ncv + nvec, rows), jnp.bfloat16),
            (vectors.shape, vectors.dtype),
            ((1, rows), jnp.float32),
            (table.shape, table.dtype),
        ],
        *(
            pltpu.with_memory_space_constraint(x, pltpu.HBM)
            for x in (frames, vectors, degrees, table)
        ),
        where=pl.BlockSpec(memory_space=pltpu.HBM),
        scratch_shapes=[
            pltpu.VMEM(degrees.shape, degrees.dtype),
            pltpu.SemaphoreType.DMA((4,)),
        ],
    )
    core = (0, 1)
    lines = [(r, 1) for r in range(n_row - 1, 0, -1)]
    if n_row == 4:
        lines = [(3, 1), (1, 1), (2, 1)]
    partners = [(0, c) for c in range(3, n_col, 2)]
    met = [sent(packed, hop) for hop in partners]
    line = [sent(packed, hop) for hop in lines]

    def call_blocks(kernel, name, outs, places, *args, **keywords):
        return call(
            functools.partial(kernel, places, sizes),
            name,
            outs,
            masks,
            *args,
            where=[smem] + [vmem] * len(args),
            scratch_shapes=[pltpu.SMEM((len(places) + 1,), jnp.int32)],
            **keywords,
        )

    def add_part(name, target, places, side, blocks, part):
        kernel = part_kernel if part is not None else first_kernel
        before = [] if part is None else [part]
        (part,) = call_blocks(
            functools.partial(kernel, targets.index(target)),
            name,
            [image_type],
            places,
            side,
            blocks,
            *before,
            input_output_aliases={3: 0} if before else {},
        )
        return part

    side_type = ((3 * ncv + 16, rows), jnp.bfloat16)
    targets = [(0, 0)] + partners
    side, image, masks = call(
        functools.partial(own_kernel, targets, sizes),
        "own",
        [side_type, image_type, pltpu.SMEM((len(targets), devices // 16), jnp.int32)],
        table,
        packed,
        to=[vmem, vmem, smem],
    )
    met, image = lax.optimization_barrier((met, image))
    sides = []
    for hop, block in zip(partners, met):
        image, partner_side = call_blocks(
            meet_kernel,
            "meet",
            [image_type, side_type],
            [hop],
            side,
            block[None],
            image,
            input_output_aliases={3: 0},
        )
        sides.append(partner_side)
    early, image = lax.optimization_barrier((line[1:], image))
    held, held_at = early + met + [packed], lines[1:] + partners + [(0, 0)]
    near = jnp.stack(held)
    other = sent(near, core)
    parts = [None] * len(partners)
    for k, hop in enumerate(partners):
        parts[k] = add_part("partner", hop, lines[1:], sides[k], near, None)
    late, parts, image = lax.optimization_barrier((line[:1], parts, image))
    late = jnp.stack(late)
    other_late = sent(late, core)
    middle = jnp.concatenate([other[: n_row - 2], late])
    for k, hop in enumerate(partners):
        places = beyond(lines[1:], core) + lines[:1]
        parts[k] = add_part("partner_middle", hop, places, sides[k], middle, parts[k])
    other_late, parts = lax.optimization_barrier((other_late, parts))
    for k, hop in enumerate(partners):
        parts[k] = add_part(
            "partner_late", hop, beyond(lines[:1], core), sides[k], other_late, parts[k]
        )
    parts, image = lax.optimization_barrier((parts, image))
    received = [sent(part, hop) for hop, part in zip(partners, parts)]
    own_places = lines[1:] + beyond(held_at, core) + lines[:1] + beyond(lines[:1], core)
    blocks = jnp.concatenate([near[: n_row - 2], other, late, other_late])
    image = add_part("add_own", (0, 0), own_places, side, blocks, image)
    applied, gram = call(
        last_kernel,
        "last",
        [((nvec, rows), jnp.float32), ((devices, nvec // 2, 8 * nvec), jnp.float32)],
        vectors,
        root,
        image,
        *received,
    )
    grams = lax.all_to_all(gram, ("row", "col"), 0, 0)
    basis, ritz = call(
        functools.partial(finish_kernel, rows * devices),
        "finish",
        [((nvec, rows), jnp.float32), ((nvec, nvec), jnp.float32)],
        grams,
        applied,
    )
    return (basis, ritz)


def solution(mesh):
    split = P(None, ("grp", "row", "col"))
    return jax.shard_map(
        per_device,
        mesh=mesh,
        in_specs=(split, split, P(("grp", "row", "col")), P()),
        out_specs=(split, P("grp", None)),
        check_vma=False,
    )
```

```python
import functools
import math

import jax
import jax.numpy as jnp
from jax import lax
from jax.experimental import pallas as pl
from jax.experimental.pallas import tpu as pltpu
from jax.sharding import PartitionSpec as P

unit = -math.log2(math.e) / 4.0

NT = (((1,), (1,)), ((), ()))
MIB = 1024 * 1024


def split3(x):
    high = x.astype(jnp.bfloat16).astype(jnp.float32)
    rest = x - high
    mid = rest.astype(jnp.bfloat16).astype(jnp.float32)
    low = (rest - mid).astype(jnp.bfloat16).astype(jnp.float32)
    return high, mid, low


def pack_kernel(
    frames_ref, vectors_in, degrees_ref, table_in,
    packed_ref, vectors_ref, root_ref, table_ref, degree_ref, sems,
):
    ncv = frames_ref.shape[0]
    copies = [
        pltpu.make_async_copy(vectors_in, vectors_ref, sems.at[0]),
        pltpu.make_async_copy(degrees_ref, degree_ref, sems.at[1]),
        pltpu.make_async_copy(frames_ref, packed_ref.at[pl.ds(0, ncv)], sems.at[2]),
        pltpu.make_async_copy(table_in, table_ref, sems.at[3]),
    ]
    for copy in copies:
        copy.start()
    copies[0].wait()
    copies[1].wait()
    root = lax.rsqrt(degree_ref[...])[None, :]
    root_ref[...] = root
    packed_ref[ncv:, :] = (vectors_ref[...].astype(jnp.float32) * root).astype(jnp.bfloat16)
    copies[2].wait()
    copies[3].wait()


def edge_rows(square, ones_first):
    high, mid, low = split3(square * unit)
    row = lax.broadcasted_iota(jnp.int32, (16, square.shape[1]), 0)
    base = 3 if ones_first else 0
    ones_at = 0 if ones_first else 3
    block = jnp.where((row >= ones_at) & (row < ones_at + 3), 1.0, 0.0)
    block = jnp.where(row == base, high, block)
    block = jnp.where(row == base + 1, mid, block)
    return jnp.where(row == base + 2, low, block)


def own_side(own):
    own = own.astype(jnp.float32)
    high, mid, low = split3(own * (-2.0 * unit))
    edge = edge_rows(jnp.sum(own * own, axis=0, keepdims=True), True)
    return jnp.concatenate([high, mid, low, edge], axis=0).astype(jnp.bfloat16)


def tile_image(side_ref, blocks):
    both = blocks[0] if len(blocks) == 1 else jnp.concatenate(blocks, axis=1)
    ncv = both.shape[0] // 2
    x, v = both[:ncv, :], both[ncv:, :]
    wide = x.astype(jnp.float32)
    edge = edge_rows(jnp.sum(wide * wide, axis=0, keepdims=True), False).astype(jnp.bfloat16)
    other = jnp.concatenate([x, x, x, edge], axis=0).T
    power = jnp.dot(other, side_ref[...], preferred_element_type=jnp.float32)
    kern = jnp.exp2(power).astype(jnp.bfloat16)
    return jnp.dot(v, kern, preferred_element_type=jnp.float32)


def own_kernel(targets, sizes, table_ref, packed_ref, side_ref, image_ref, masks_ref):
    n_row, n_col = sizes
    my_row, my_col = lax.axis_index("row"), lax.axis_index("col")
    first, second = table_ref[:, 0, :], table_ref[:, 1, :]
    for t, target in enumerate(targets):
        block = (my_row ^ target[0]) * n_col + (my_col ^ target[1])
        other = jnp.where(first == block, second, jnp.where(second == block, first, -1))
        for word in range(n_row * n_col // 16):
            bit = jnp.zeros(other.shape, jnp.float32)
            for b in range(16):
                bit = jnp.where(other == 16 * word + b, float(1 << b), bit)
            masks_ref[t, word] = jnp.sum(bit).astype(jnp.int32)
    side_ref[...] = own_side(packed_ref[: packed_ref.shape[0] // 2, :])
    image_ref[...] = tile_image(side_ref, [packed_ref[...]])


def add_blocks(target, places, sizes, masks_ref, side_ref, blocks_ref, image_ref, list_ref):
    my_row, my_col = lax.axis_index("row"), lax.axis_index("col")

    count = jnp.int32(0)
    for step, place in enumerate(places):
        block = (my_row ^ place[0]) * sizes[1] + (my_col ^ place[1])
        list_ref[count] = step
        count += (masks_ref[target, block // 16] >> (block % 16)) & 1

    def add_group(start, size):
        blocks = [blocks_ref[list_ref[start + k]] for k in range(size)]
        image_ref[...] += tile_image(side_ref, blocks)

    fours = jnp.maximum(count // 4 - (count % 4 == 1).astype(jnp.int32), 0)
    rest = count - 4 * fours

    def add_four(group, _):
        add_group(4 * group, 4)
        return 0

    if len(places) >= 4:
        lax.fori_loop(0, fours, add_four, 0)
    if len(places) >= 3:
        pl.when(rest >= 3)(lambda: add_group(4 * fours, 3))
    if len(places) >= 2:
        pl.when(rest % 3 == 2)(lambda: add_group(count - 2, 2))
    pl.when(rest == 1)(lambda: add_group(count - 1, 1))


def meet_kernel(
    places, sizes, masks_ref, side_ref, blocks_ref, before_ref, image_ref, partner_side_ref, list_ref
):
    partner_side_ref[...] = own_side(blocks_ref[0, : blocks_ref.shape[1] // 2, :])
    image_ref[...] = before_ref[...]
    add_blocks(0, places, sizes, masks_ref, side_ref, blocks_ref, image_ref, list_ref)


def first_kernel(target, places, sizes, masks_ref, side_ref, blocks_ref, image_ref, list_ref):
    image_ref[...] = jnp.zeros_like(image_ref)
    add_blocks(target, places, sizes, masks_ref, side_ref, blocks_ref, image_ref, list_ref)


def part_kernel(
    target, places, sizes, masks_ref, side_ref, blocks_ref, before_ref, image_ref, list_ref
):
    image_ref[...] = before_ref[...]
    add_blocks(target, places, sizes, masks_ref, side_ref, blocks_ref, image_ref, list_ref)


def last_kernel(vectors_ref, root_ref, *refs):
    *part_refs, applied_ref, gram_ref = refs
    image = sum(part_ref[...] for part_ref in part_refs)
    n = vectors_ref.shape[0]
    applied = image * root_ref[...]
    applied_ref[...] = applied
    both = jnp.concatenate([applied, vectors_ref[...].astype(jnp.float32)], axis=0)
    gram = lax.dot_general(
        both, both, NT, precision=lax.Precision.HIGHEST, preferred_element_type=jnp.float32
    )
    wide = jnp.concatenate(
        [gram[:n, :n], gram[n:, :], jnp.zeros((n, n), jnp.float32)], axis=1
    )
    tile = jnp.concatenate([wide[: n // 2, :], wide[n // 2 :, :]], axis=1)
    for device in range(gram_ref.shape[0]):
        gram_ref[device] = tile


def inverse_factors(grams):
    n = grams[0].shape[0]
    half = 64
    tiles = range(n // 8)
    shape = (8, 2 * half)
    row = lax.broadcasted_iota(jnp.int32, shape, 0)
    lane = lax.broadcasted_iota(jnp.int32, shape, 1)
    columns = [
        [
            jnp.where(
                lane < half,
                jnp.broadcast_to(grams[0][8 * t : 8 * t + 8, j : j + 1], shape),
                jnp.broadcast_to(grams[1][8 * t : 8 * t + 8, j : j + 1], shape),
            )
            for t in tiles
        ]
        for j in range(n)
    ]
    right = [jnp.where(lane % half == row + 8 * t, 1.0, 0.0) for t in tiles]
    pivots = [jnp.ones(shape, jnp.float32) for t in tiles]
    for k in range(n):
        top, at = k // 8, k % 8
        pivot = columns[k][top][at : at + 1, :]
        pivots[top] = jnp.where(row == at, pivot, pivots[top])
        if k == n - 1:
            break
        scale = 1.0 / pivot
        factor = {t: columns[k][t] * scale for t in tiles if t >= top}
        factor[top] = jnp.where(row > at, factor[top], 0.0)
        for column in columns[k + 1 :] + [right]:
            line = column[top][at : at + 1, :]
            for t in factor:
                column[t] = column[t] - factor[t] * line
    result = jnp.concatenate([r * lax.rsqrt(p) for r, p in zip(right, pivots)], axis=0)
    return result[:, :n], result[:, half : half + n]


def finish_kernel(total_frames, grams_ref, applied_ref, basis_ref, ritz_ref):
    tile = grams_ref[0]
    for device in range(1, grams_ref.shape[0]):
        tile += grams_ref[device]
    n = applied_ref.shape[0]
    gram = jnp.concatenate([tile[:, : 4 * n], tile[:, 4 * n :]], axis=0)
    exact = functools.partial(
        lax.dot_general, precision=lax.Precision.HIGHEST, preferred_element_type=jnp.float32
    )
    plain = (((1,), (0,)), ((), ()))
    image_inverse, vector_inverse = inverse_factors([gram[:, :n], gram[:, 2 * n : 3 * n]])
    basis_ref[...] = exact(image_inverse * math.sqrt(total_frames), applied_ref[...], plain)
    half = exact(vector_inverse, gram[:, n : 2 * n], plain)
    ritz_ref[...] = exact(half, vector_inverse, NT)


def sent(x, hop):
    n_row, n_col = lax.axis_size("row"), lax.axis_size("col")
    pairs = [
        (r * n_col + c, (r ^ hop[0]) * n_col + (c ^ hop[1]))
        for r in range(n_row)
        for c in range(n_col)
    ]
    return lax.ppermute(x, ("row", "col"), pairs)


def beyond(offsets, hop):
    return [(r ^ hop[0], c ^ hop[1]) for r, c in offsets]


def per_device(frames, vectors, degrees, tile_table):
    ncv, rows = frames.shape
    nvec = vectors.shape[0]
    n_row, n_col = lax.axis_size("row"), lax.axis_size("col")
    devices = n_row * n_col
    sizes = (n_row, n_col)
    vmem = pl.BlockSpec(memory_space=pltpu.VMEM)
    smem = pl.BlockSpec(memory_space=pltpu.SMEM)

    def call(kernel, name, outs, *args, limit=24, where=vmem, to=vmem, **keywords):
        shapes = [jax.ShapeDtypeStruct(*out) if isinstance(out, tuple) else out for out in outs]
        where = where if isinstance(where, list) else [where] * len(args)
        to = to if isinstance(to, list) else [to] * len(outs)
        return pl.pallas_call(
            kernel,
            out_shape=shapes,
            in_specs=where,
            out_specs=to,
            compiler_params=pltpu.CompilerParams(vmem_limit_bytes=limit * MIB),
            name=name,
            **keywords,
        )(*args)

    image_type = ((nvec, rows), jnp.float32)

    table = tile_table.transpose(1, 2, 0)
    packed, vectors, root, table = call(
        pack_kernel,
        "pack",
        [
            ((ncv + nvec, rows), jnp.bfloat16),
            (vectors.shape, vectors.dtype),
            ((1, rows), jnp.float32),
            (table.shape, table.dtype),
        ],
        *(
            pltpu.with_memory_space_constraint(x, pltpu.HBM)
            for x in (frames, vectors, degrees, table)
        ),
        where=pl.BlockSpec(memory_space=pltpu.HBM),
        scratch_shapes=[
            pltpu.VMEM(degrees.shape, degrees.dtype),
            pltpu.SemaphoreType.DMA((4,)),
        ],
    )
    core = (0, 1)
    lines = [(r, 1) for r in range(n_row - 1, 0, -1)]
    if n_row == 4:
        lines = [(3, 1), (1, 1), (2, 1)]
    partners = [(0, c) for c in range(3, n_col, 2)]
    met = [sent(packed, hop) for hop in partners]
    line = [sent(packed, hop) for hop in lines]

    def call_blocks(kernel, name, outs, places, *args, **keywords):
        return call(
            functools.partial(kernel, places, sizes),
            name,
            outs,
            masks,
            *args,
            where=[smem] + [vmem] * len(args),
            scratch_shapes=[pltpu.SMEM((len(places) + 1,), jnp.int32)],
            **keywords,
        )

    def add_part(name, target, places, side, blocks, part):
        kernel = part_kernel if part is not None else first_kernel
        before = [] if part is None else [part]
        (part,) = call_blocks(
            functools.partial(kernel, targets.index(target)),
            name,
            [image_type],
            places,
            side,
            blocks,
            *before,
            input_output_aliases={3: 0} if before else {},
        )
        return part

    side_type = ((3 * ncv + 16, rows), jnp.bfloat16)
    targets = [(0, 0)] + partners
    side, image, masks = call(
        functools.partial(own_kernel, targets, sizes),
        "own",
        [side_type, image_type, pltpu.SMEM((len(targets), devices // 16), jnp.int32)],
        table,
        packed,
        to=[vmem, vmem, smem],
    )
    met, image = lax.optimization_barrier((met, image))
    sides = []
    for hop, block in zip(partners, met):
        image, partner_side = call_blocks(
            meet_kernel,
            "meet",
            [image_type, side_type],
            [hop],
            side,
            block[None],
            image,
            input_output_aliases={3: 0},
        )
        sides.append(partner_side)
    early, image = lax.optimization_barrier((line[1:], image))
    held, held_at = early + met + [packed], lines[1:] + partners + [(0, 0)]
    near = jnp.stack(held)
    other = sent(near, core)
    parts = [None] * len(partners)
    for k, hop in enumerate(partners):
        parts[k] = add_part("partner", hop, lines[1:], sides[k], near, None)
    late, parts, image = lax.optimization_barrier((line[:1], parts, image))
    late = jnp.stack(late)
    other_late = sent(late, core)
    middle = jnp.concatenate([other[: n_row - 2], late])
    for k, hop in enumerate(partners):
        places = beyond(lines[1:], core) + lines[:1]
        parts[k] = add_part("partner_middle", hop, places, sides[k], middle, parts[k])
    other_late, parts = lax.optimization_barrier((other_late, parts))
    for k, hop in enumerate(partners):
        parts[k] = add_part(
            "partner_late", hop, beyond(lines[:1], core), sides[k], other_late, parts[k]
        )
    parts, image = lax.optimization_barrier((parts, image))
    received = [sent(part, hop) for hop, part in zip(partners, parts)]
    own_places = lines[1:] + beyond(held_at, core) + lines[:1] + beyond(lines[:1], core)
    blocks = jnp.concatenate([near[: n_row - 2], other, late, other_late])
    image = add_part("add_own", (0, 0), own_places, side, blocks, image)
    applied, gram = call(
        last_kernel,
        "last",
        [((nvec, rows), jnp.float32), ((devices, nvec // 2, 8 * nvec), jnp.float32)],
        vectors,
        root,
        image,
        *received,
    )
    grams = lax.all_to_all(gram, ("row", "col"), 0, 0)
    basis, ritz = call(
        functools.partial(finish_kernel, rows * devices),
        "finish",
        [((nvec, rows), jnp.float32), ((nvec, nvec), jnp.float32)],
        grams,
        applied,
    )
    return (basis, ritz)


def solution(mesh):
    split = P(None, ("grp", "row", "col"))
    return jax.shard_map(
        per_device,
        mesh=mesh,
        in_specs=(split, split, P(("grp", "row", "col")), P()),
        out_specs=(split, P("grp", None)),
        check_vma=False,
    )
```

```python
import functools
import math

import jax
import jax.numpy as jnp
from jax import lax
from jax.experimental import pallas as pl
from jax.experimental.pallas import tpu as pltpu
from jax.sharding import PartitionSpec as P

unit = -math.log2(math.e) / 4.0

NT = (((1,), (1,)), ((), ()))
MIB = 1024 * 1024


def split3(x):
    high = x.astype(jnp.bfloat16).astype(jnp.float32)
    rest = x - high
    mid = rest.astype(jnp.bfloat16).astype(jnp.float32)
    low = (rest - mid).astype(jnp.bfloat16).astype(jnp.float32)
    return high, mid, low


def pack_kernel(
    frames_ref, vectors_in, degrees_ref, table_in,
    packed_ref, vectors_ref, root_ref, table_ref, degree_ref, sems,
):
    ncv = frames_ref.shape[0]
    copies = [
        pltpu.make_async_copy(vectors_in, vectors_ref, sems.at[0]),
        pltpu.make_async_copy(degrees_ref, degree_ref, sems.at[1]),
        pltpu.make_async_copy(frames_ref, packed_ref.at[pl.ds(0, ncv)], sems.at[2]),
        pltpu.make_async_copy(table_in, table_ref, sems.at[3]),
    ]
    for copy in copies:
        copy.start()
    copies[0].wait()
    copies[1].wait()
    root = lax.rsqrt(degree_ref[...])[None, :]
    root_ref[...] = root
    packed_ref[ncv:, :] = (vectors_ref[...].astype(jnp.float32) * root).astype(jnp.bfloat16)
    copies[2].wait()
    copies[3].wait()


def edge_rows(square, ones_first):
    high, mid, low = split3(square * unit)
    row = lax.broadcasted_iota(jnp.int32, (16, square.shape[1]), 0)
    base = 3 if ones_first else 0
    ones_at = 0 if ones_first else 3
    block = jnp.where((row >= ones_at) & (row < ones_at + 3), 1.0, 0.0)
    block = jnp.where(row == base, high, block)
    block = jnp.where(row == base + 1, mid, block)
    return jnp.where(row == base + 2, low, block)


def own_side(own):
    own = own.astype(jnp.float32)
    high, mid, low = split3(own * (-2.0 * unit))
    edge = edge_rows(jnp.sum(own * own, axis=0, keepdims=True), True)
    return jnp.concatenate([high, mid, low, edge], axis=0).astype(jnp.bfloat16)


def tile_image(side_ref, blocks):
    both = blocks[0] if len(blocks) == 1 else jnp.concatenate(blocks, axis=1)
    ncv = both.shape[0] // 2
    x, v = both[:ncv, :], both[ncv:, :]
    wide = x.astype(jnp.float32)
    edge = edge_rows(jnp.sum(wide * wide, axis=0, keepdims=True), False).astype(jnp.bfloat16)
    other = jnp.concatenate([x, x, x, edge], axis=0).T
    power = jnp.dot(other, side_ref[...], preferred_element_type=jnp.float32)
    kern = jnp.exp2(power).astype(jnp.bfloat16)
    return jnp.dot(v, kern, preferred_element_type=jnp.float32)


def own_kernel(targets, sizes, table_ref, packed_ref, side_ref, image_ref, masks_ref):
    n_row, n_col = sizes
    my_row, my_col = lax.axis_index("row"), lax.axis_index("col")
    first, second = table_ref[:, 0, :], table_ref[:, 1, :]
    for t, target in enumerate(targets):
        block = (my_row ^ target[0]) * n_col + (my_col ^ target[1])
        other = jnp.where(first == block, second, jnp.where(second == block, first, -1))
        for word in range(n_row * n_col // 16):
            bit = jnp.zeros(other.shape, jnp.float32)
            for b in range(16):
                bit = jnp.where(other == 16 * word + b, float(1 << b), bit)
            masks_ref[t, word] = jnp.sum(bit).astype(jnp.int32)
    side_ref[...] = own_side(packed_ref[: packed_ref.shape[0] // 2, :])
    image_ref[...] = tile_image(side_ref, [packed_ref[...]])


def add_blocks(target, places, sizes, masks_ref, side_ref, blocks_ref, image_ref, list_ref):
    my_row, my_col = lax.axis_index("row"), lax.axis_index("col")

    count = jnp.int32(0)
    for step, place in enumerate(places):
        block = (my_row ^ place[0]) * sizes[1] + (my_col ^ place[1])
        list_ref[count] = step
        count += (masks_ref[target, block // 16] >> (block % 16)) & 1

    def add_group(start, size):
        blocks = [blocks_ref[list_ref[start + k]] for k in range(size)]
        image_ref[...] += tile_image(side_ref, blocks)

    fours = jnp.maximum(count // 4 - (count % 4 == 1).astype(jnp.int32), 0)
    rest = count - 4 * fours

    def add_four(group, _):
        add_group(4 * group, 4)
        return 0

    if len(places) >= 4:
        lax.fori_loop(0, fours, add_four, 0)
    if len(places) >= 3:
        pl.when(rest >= 3)(lambda: add_group(4 * fours, 3))
    if len(places) >= 2:
        pl.when(rest % 3 == 2)(lambda: add_group(count - 2, 2))
    pl.when(rest == 1)(lambda: add_group(count - 1, 1))


def side_kernel(block_ref, side_ref):
    side_ref[...] = own_side(block_ref[: block_ref.shape[0] // 2, :])


def first_kernel(target, places, sizes, masks_ref, side_ref, blocks_ref, image_ref, list_ref):
    image_ref[...] = jnp.zeros_like(image_ref)
    add_blocks(target, places, sizes, masks_ref, side_ref, blocks_ref, image_ref, list_ref)


def part_kernel(
    target, places, sizes, masks_ref, side_ref, blocks_ref, before_ref, image_ref, list_ref
):
    image_ref[...] = before_ref[...]
    add_blocks(target, places, sizes, masks_ref, side_ref, blocks_ref, image_ref, list_ref)


def last_kernel(vectors_ref, root_ref, *refs):
    *part_refs, applied_ref, gram_ref = refs
    image = sum(part_ref[...] for part_ref in part_refs)
    n = vectors_ref.shape[0]
    applied = image * root_ref[...]
    applied_ref[...] = applied
    both = jnp.concatenate([applied, vectors_ref[...].astype(jnp.float32)], axis=0)
    gram = lax.dot_general(
        both, both, NT, precision=lax.Precision.HIGHEST, preferred_element_type=jnp.float32
    )
    wide = jnp.concatenate(
        [gram[:n, :n], gram[n:, :], jnp.zeros((n, n), jnp.float32)], axis=1
    )
    tile = jnp.concatenate([wide[: n // 2, :], wide[n // 2 :, :]], axis=1)
    for device in range(gram_ref.shape[0]):
        gram_ref[device] = tile


def inverse_factors(grams):
    n = grams[0].shape[0]
    half = 64
    tiles = range(n // 8)
    shape = (8, 2 * half)
    row = lax.broadcasted_iota(jnp.int32, shape, 0)
    lane = lax.broadcasted_iota(jnp.int32, shape, 1)
    columns = [
        [
            jnp.where(
                lane < half,
                jnp.broadcast_to(grams[0][8 * t : 8 * t + 8, j : j + 1], shape),
                jnp.broadcast_to(grams[1][8 * t : 8 * t + 8, j : j + 1], shape),
            )
            for t in tiles
        ]
        for j in range(n)
    ]
    right = [jnp.where(lane % half == row + 8 * t, 1.0, 0.0) for t in tiles]
    pivots = [jnp.ones(shape, jnp.float32) for t in tiles]
    for k in range(n):
        top, at = k // 8, k % 8
        pivot = columns[k][top][at : at + 1, :]
        pivots[top] = jnp.where(row == at, pivot, pivots[top])
        if k == n - 1:
            break
        scale = 1.0 / pivot
        factor = {t: columns[k][t] * scale for t in tiles if t >= top}
        factor[top] = jnp.where(row > at, factor[top], 0.0)
        for column in columns[k + 1 :] + [right]:
            line = column[top][at : at + 1, :]
            for t in factor:
                column[t] = column[t] - factor[t] * line
    result = jnp.concatenate([r * lax.rsqrt(p) for r, p in zip(right, pivots)], axis=0)
    return result[:, :n], result[:, half : half + n]


def finish_kernel(total_frames, grams_ref, applied_ref, basis_ref, ritz_ref):
    tile = grams_ref[0]
    for device in range(1, grams_ref.shape[0]):
        tile += grams_ref[device]
    n = applied_ref.shape[0]
    gram = jnp.concatenate([tile[:, : 4 * n], tile[:, 4 * n :]], axis=0)
    exact = functools.partial(
        lax.dot_general, precision=lax.Precision.HIGHEST, preferred_element_type=jnp.float32
    )
    plain = (((1,), (0,)), ((), ()))
    image_inverse, vector_inverse = inverse_factors([gram[:, :n], gram[:, 2 * n : 3 * n]])
    basis_ref[...] = exact(image_inverse * math.sqrt(total_frames), applied_ref[...], plain)
    half = exact(vector_inverse, gram[:, n : 2 * n], plain)
    ritz_ref[...] = exact(half, vector_inverse, NT)


def sent(x, hop):
    n_row, n_col = lax.axis_size("row"), lax.axis_size("col")
    pairs = [
        (r * n_col + c, (r ^ hop[0]) * n_col + (c ^ hop[1]))
        for r in range(n_row)
        for c in range(n_col)
    ]
    return lax.ppermute(x, ("row", "col"), pairs)


def beyond(offsets, hop):
    return [(r ^ hop[0], c ^ hop[1]) for r, c in offsets]


def per_device(frames, vectors, degrees, tile_table):
    ncv, rows = frames.shape
    nvec = vectors.shape[0]
    n_row, n_col = lax.axis_size("row"), lax.axis_size("col")
    devices = n_row * n_col
    sizes = (n_row, n_col)
    vmem = pl.BlockSpec(memory_space=pltpu.VMEM)
    smem = pl.BlockSpec(memory_space=pltpu.SMEM)

    def call(kernel, name, outs, *args, limit=24, where=vmem, to=vmem, **keywords):
        shapes = [jax.ShapeDtypeStruct(*out) if isinstance(out, tuple) else out for out in outs]
        where = where if isinstance(where, list) else [where] * len(args)
        to = to if isinstance(to, list) else [to] * len(outs)
        return pl.pallas_call(
            kernel,
            out_shape=shapes,
            in_specs=where,
            out_specs=to,
            compiler_params=pltpu.CompilerParams(vmem_limit_bytes=limit * MIB),
            name=name,
            **keywords,
        )(*args)

    image_type = ((nvec, rows), jnp.float32)

    table = tile_table.transpose(1, 2, 0)
    packed, vectors, root, table = call(
        pack_kernel,
        "pack",
        [
            ((ncv + nvec, rows), jnp.bfloat16),
            (vectors.shape, vectors.dtype),
            ((1, rows), jnp.float32),
            (table.shape, table.dtype),
        ],
        *(
            pltpu.with_memory_space_constraint(x, pltpu.HBM)
            for x in (frames, vectors, degrees, table)
        ),
        where=pl.BlockSpec(memory_space=pltpu.HBM),
        scratch_shapes=[
            pltpu.VMEM(degrees.shape, degrees.dtype),
            pltpu.SemaphoreType.DMA((4,)),
        ],
    )
    core = (0, 1)
    lines = [(r, 1) for r in range(n_row - 1, 0, -1)]
    if n_row == 4:
        lines = [(3, 1), (1, 1), (2, 1)]
    partners = [(0, c) for c in range(3, n_col, 2)]
    met = [sent(packed, hop) for hop in partners]
    line = [sent(packed, hop) for hop in lines]

    def call_blocks(kernel, name, outs, places, *args, **keywords):
        return call(
            functools.partial(kernel, places, sizes),
            name,
            outs,
            masks,
            *args,
            where=[smem] + [vmem] * len(args),
            scratch_shapes=[pltpu.SMEM((len(places) + 1,), jnp.int32)],
            **keywords,
        )

    def add_part(name, target, places, side, blocks, part):
        kernel = part_kernel if part is not None else first_kernel
        before = [] if part is None else [part]
        (part,) = call_blocks(
            functools.partial(kernel, targets.index(target)),
            name,
            [image_type],
            places,
            side,
            blocks,
            *before,
            input_output_aliases={3: 0} if before else {},
        )
        return part

    side_type = ((3 * ncv + 16, rows), jnp.bfloat16)
    targets = [(0, 0)] + partners
    side, image, masks = call(
        functools.partial(own_kernel, targets, sizes),
        "own",
        [side_type, image_type, pltpu.SMEM((len(targets), devices // 16), jnp.int32)],
        table,
        packed,
        to=[vmem, vmem, smem],
    )
    met, image = lax.optimization_barrier((met, image))
    sides = [call(side_kernel, "side", [side_type], block)[0] for block in met]
    early, sides = lax.optimization_barrier((line[1:], sides))
    held, held_at = early + met + [packed], lines[1:] + partners + [(0, 0)]
    near = jnp.stack(held)
    other = sent(near, core)
    parts = [None] * len(partners)
    for k, hop in enumerate(partners):
        parts[k] = add_part("partner", hop, lines[1:], sides[k], near, None)
    late, parts, image = lax.optimization_barrier((line[:1], parts, image))
    late = jnp.stack(late)
    other_late = sent(late, core)
    middle = jnp.concatenate([other[: n_row - 2], late])
    for k, hop in enumerate(partners):
        places = beyond(lines[1:], core) + lines[:1]
        parts[k] = add_part("partner_middle", hop, places, sides[k], middle, parts[k])
    other_late, parts = lax.optimization_barrier((other_late, parts))
    for k, hop in enumerate(partners):
        parts[k] = add_part(
            "partner_late", hop, beyond(lines[:1], core), sides[k], other_late, parts[k]
        )
    parts, image = lax.optimization_barrier((parts, image))
    received = [sent(part, hop) for hop, part in zip(partners, parts)]
    own_places = held_at[:-1] + beyond(held_at, core) + lines[:1] + beyond(lines[:1], core)
    blocks = jnp.concatenate([near[:-1], other, late, other_late])
    image = add_part("add_own", (0, 0), own_places, side, blocks, image)
    applied, gram = call(
        last_kernel,
        "last",
        [((nvec, rows), jnp.float32), ((devices, nvec // 2, 8 * nvec), jnp.float32)],
        vectors,
        root,
        image,
        *received,
    )
    grams = lax.all_to_all(gram, ("row", "col"), 0, 0)
    basis, ritz = call(
        functools.partial(finish_kernel, rows * devices),
        "finish",
        [((nvec, rows), jnp.float32), ((nvec, nvec), jnp.float32)],
        grams,
        applied,
    )
    return (basis, ritz)


def solution(mesh):
    split = P(None, ("grp", "row", "col"))
    return jax.shard_map(
        per_device,
        mesh=mesh,
        in_specs=(split, split, P(("grp", "row", "col")), P()),
        out_specs=(split, P("grp", None)),
        check_vma=False,
    )
```

```python
import functools
import math

import jax
import jax.numpy as jnp
from jax import lax
from jax.experimental import pallas as pl
from jax.experimental.pallas import tpu as pltpu
from jax.sharding import PartitionSpec as P

unit = -math.log2(math.e) / 4.0

NT = (((1,), (1,)), ((), ()))
MIB = 1024 * 1024


def split3(x):
    high = x.astype(jnp.bfloat16).astype(jnp.float32)
    rest = x - high
    mid = rest.astype(jnp.bfloat16).astype(jnp.float32)
    low = (rest - mid).astype(jnp.bfloat16).astype(jnp.float32)
    return high, mid, low


def pack_kernel(
    frames_ref, vectors_in, degrees_ref, table_in,
    packed_ref, vectors_ref, root_ref, table_ref, degree_ref, sems,
):
    ncv = frames_ref.shape[0]
    copies = [
        pltpu.make_async_copy(vectors_in, vectors_ref, sems.at[0]),
        pltpu.make_async_copy(degrees_ref, degree_ref, sems.at[1]),
        pltpu.make_async_copy(frames_ref, packed_ref.at[pl.ds(0, ncv)], sems.at[2]),
        pltpu.make_async_copy(table_in, table_ref, sems.at[3]),
    ]
    for copy in copies:
        copy.start()
    copies[0].wait()
    copies[1].wait()
    root = lax.rsqrt(degree_ref[...])[None, :]
    root_ref[...] = root
    packed_ref[ncv:, :] = (vectors_ref[...].astype(jnp.float32) * root).astype(jnp.bfloat16)
    copies[2].wait()
    copies[3].wait()


def edge_rows(square, ones_first):
    high, mid, low = split3(square * unit)
    row = lax.broadcasted_iota(jnp.int32, (16, square.shape[1]), 0)
    base = 3 if ones_first else 0
    ones_at = 0 if ones_first else 3
    block = jnp.where((row >= ones_at) & (row < ones_at + 3), 1.0, 0.0)
    block = jnp.where(row == base, high, block)
    block = jnp.where(row == base + 1, mid, block)
    return jnp.where(row == base + 2, low, block)


def own_side(own):
    own = own.astype(jnp.float32)
    high, mid, low = split3(own * (-2.0 * unit))
    edge = edge_rows(jnp.sum(own * own, axis=0, keepdims=True), True)
    return jnp.concatenate([high, mid, low, edge], axis=0).astype(jnp.bfloat16)


def tile_image(side_ref, blocks):
    both = blocks[0] if len(blocks) == 1 else jnp.concatenate(blocks, axis=1)
    ncv = both.shape[0] // 2
    x, v = both[:ncv, :], both[ncv:, :]
    wide = x.astype(jnp.float32)
    edge = edge_rows(jnp.sum(wide * wide, axis=0, keepdims=True), False).astype(jnp.bfloat16)
    other = jnp.concatenate([x, x, x, edge], axis=0).T
    power = jnp.dot(other, side_ref[...], preferred_element_type=jnp.float32)
    kern = jnp.exp2(power).astype(jnp.bfloat16)
    return jnp.dot(v, kern, preferred_element_type=jnp.float32)


def own_kernel(targets, sizes, table_ref, packed_ref, side_ref, image_ref, masks_ref):
    n_row, n_col = sizes
    my_row, my_col = lax.axis_index("row"), lax.axis_index("col")
    first, second = table_ref[:, 0, :], table_ref[:, 1, :]
    for t, target in enumerate(targets):
        block = (my_row ^ target[0]) * n_col + (my_col ^ target[1])
        other = jnp.where(first == block, second, jnp.where(second == block, first, -1))
        for word in range(n_row * n_col // 16):
            bit = jnp.zeros(other.shape, jnp.float32)
            for b in range(16):
                bit = jnp.where(other == 16 * word + b, float(1 << b), bit)
            masks_ref[t, word] = jnp.sum(bit).astype(jnp.int32)
    side_ref[...] = own_side(packed_ref[: packed_ref.shape[0] // 2, :])
    image_ref[...] = tile_image(side_ref, [packed_ref[...]])


def add_blocks(target, places, sizes, masks_ref, side_ref, blocks_ref, image_ref, list_ref):
    my_row, my_col = lax.axis_index("row"), lax.axis_index("col")

    count = jnp.int32(0)
    for step, place in enumerate(places):
        block = (my_row ^ place[0]) * sizes[1] + (my_col ^ place[1])
        list_ref[count] = step
        count += (masks_ref[target, block // 16] >> (block % 16)) & 1

    def add_group(start, size):
        blocks = [blocks_ref[list_ref[start + k]] for k in range(size)]
        image_ref[...] += tile_image(side_ref, blocks)

    fours = jnp.maximum(count // 4 - (count % 4 == 1).astype(jnp.int32), 0)
    rest = count - 4 * fours

    def add_four(group, _):
        add_group(4 * group, 4)
        return 0

    if len(places) >= 4:
        lax.fori_loop(0, fours, add_four, 0)
    if len(places) >= 3:
        pl.when(rest >= 3)(lambda: add_group(4 * fours, 3))
    if len(places) >= 2:
        pl.when(rest % 3 == 2)(lambda: add_group(count - 2, 2))
    pl.when(rest == 1)(lambda: add_group(count - 1, 1))


def meet_kernel(
    places, sizes, masks_ref, side_ref, blocks_ref, before_ref, image_ref, partner_side_ref, list_ref
):
    partner_side_ref[...] = own_side(blocks_ref[0, : blocks_ref.shape[1] // 2, :])
    image_ref[...] = before_ref[...]
    add_blocks(0, places, sizes, masks_ref, side_ref, blocks_ref, image_ref, list_ref)


def first_kernel(target, places, sizes, masks_ref, side_ref, blocks_ref, image_ref, list_ref):
    image_ref[...] = jnp.zeros_like(image_ref)
    add_blocks(target, places, sizes, masks_ref, side_ref, blocks_ref, image_ref, list_ref)


def part_kernel(
    target, places, sizes, masks_ref, side_ref, blocks_ref, before_ref, image_ref, list_ref
):
    image_ref[...] = before_ref[...]
    add_blocks(target, places, sizes, masks_ref, side_ref, blocks_ref, image_ref, list_ref)


def last_kernel(vectors_ref, root_ref, *refs):
    *part_refs, applied_ref, gram_ref = refs
    image = sum(part_ref[...] for part_ref in part_refs)
    n = vectors_ref.shape[0]
    applied = image * root_ref[...]
    applied_ref[...] = applied
    both = jnp.concatenate([applied, vectors_ref[...].astype(jnp.float32)], axis=0)
    gram = lax.dot_general(
        both, both, NT, precision=lax.Precision.HIGHEST, preferred_element_type=jnp.float32
    )
    wide = jnp.concatenate(
        [gram[:n, :n], gram[n:, :], jnp.zeros((n, n), jnp.float32)], axis=1
    )
    tile = jnp.concatenate([wide[: n // 2, :], wide[n // 2 :, :]], axis=1)
    for device in range(gram_ref.shape[0]):
        gram_ref[device] = tile


def inverse_factors(grams):
    n = grams[0].shape[0]
    half = 64
    tiles = range(n // 8)
    shape = (8, 2 * half)
    row = lax.broadcasted_iota(jnp.int32, shape, 0)
    lane = lax.broadcasted_iota(jnp.int32, shape, 1)
    columns = [
        [
            jnp.where(
                lane < half,
                jnp.broadcast_to(grams[0][8 * t : 8 * t + 8, j : j + 1], shape),
                jnp.broadcast_to(grams[1][8 * t : 8 * t + 8, j : j + 1], shape),
            )
            for t in tiles
        ]
        for j in range(n)
    ]
    right = [jnp.where(lane % half == row + 8 * t, 1.0, 0.0) for t in tiles]
    pivots = [jnp.ones(shape, jnp.float32) for t in tiles]
    for k in range(n):
        top, at = k // 8, k % 8
        pivot = columns[k][top][at : at + 1, :]
        pivots[top] = jnp.where(row == at, pivot, pivots[top])
        if k == n - 1:
            break
        scale = 1.0 / pivot
        factor = {t: columns[k][t] * scale for t in tiles if t >= top}
        factor[top] = jnp.where(row > at, factor[top], 0.0)
        for column in columns[k + 1 :] + [right]:
            line = column[top][at : at + 1, :]
            for t in factor:
                column[t] = column[t] - factor[t] * line
    result = jnp.concatenate([r * lax.rsqrt(p) for r, p in zip(right, pivots)], axis=0)
    return result[:, :n], result[:, half : half + n]


def finish_kernel(total_frames, grams_ref, applied_ref, basis_ref, ritz_ref):
    tile = grams_ref[0]
    for device in range(1, grams_ref.shape[0]):
        tile += grams_ref[device]
    n = applied_ref.shape[0]
    gram = jnp.concatenate([tile[:, : 4 * n], tile[:, 4 * n :]], axis=0)
    exact = functools.partial(
        lax.dot_general, precision=lax.Precision.HIGHEST, preferred_element_type=jnp.float32
    )
    plain = (((1,), (0,)), ((), ()))
    image_inverse, vector_inverse = inverse_factors([gram[:, :n], gram[:, 2 * n : 3 * n]])
    basis_ref[...] = exact(image_inverse * math.sqrt(total_frames), applied_ref[...], plain)
    half = exact(vector_inverse, gram[:, n : 2 * n], plain)
    ritz_ref[...] = exact(half, vector_inverse, NT)


def sent(x, hop):
    n_row, n_col = lax.axis_size("row"), lax.axis_size("col")
    pairs = [
        (r * n_col + c, (r ^ hop[0]) * n_col + (c ^ hop[1]))
        for r in range(n_row)
        for c in range(n_col)
    ]
    return lax.ppermute(x, ("row", "col"), pairs)


def beyond(offsets, hop):
    return [(r ^ hop[0], c ^ hop[1]) for r, c in offsets]


def per_device(frames, vectors, degrees, tile_table):
    ncv, rows = frames.shape
    nvec = vectors.shape[0]
    n_row, n_col = lax.axis_size("row"), lax.axis_size("col")
    devices = n_row * n_col
    sizes = (n_row, n_col)
    vmem = pl.BlockSpec(memory_space=pltpu.VMEM)
    smem = pl.BlockSpec(memory_space=pltpu.SMEM)

    def call(kernel, name, outs, *args, limit=24, where=vmem, to=vmem, **keywords):
        shapes = [jax.ShapeDtypeStruct(*out) if isinstance(out, tuple) else out for out in outs]
        where = where if isinstance(where, list) else [where] * len(args)
        to = to if isinstance(to, list) else [to] * len(outs)
        return pl.pallas_call(
            kernel,
            out_shape=shapes,
            in_specs=where,
            out_specs=to,
            compiler_params=pltpu.CompilerParams(vmem_limit_bytes=limit * MIB),
            name=name,
            **keywords,
        )(*args)

    image_type = ((nvec, rows), jnp.float32)

    table = tile_table.transpose(1, 2, 0)
    packed, vectors, root, table = call(
        pack_kernel,
        "pack",
        [
            ((ncv + nvec, rows), jnp.bfloat16),
            (vectors.shape, vectors.dtype),
            ((1, rows), jnp.float32),
            (table.shape, table.dtype),
        ],
        *(
            pltpu.with_memory_space_constraint(x, pltpu.HBM)
            for x in (frames, vectors, degrees, table)
        ),
        where=pl.BlockSpec(memory_space=pltpu.HBM),
        scratch_shapes=[
            pltpu.VMEM(degrees.shape, degrees.dtype),
            pltpu.SemaphoreType.DMA((4,)),
        ],
    )
    core = (0, 1)
    lines = [(r, 1) for r in range(n_row - 1, 0, -1)]
    if n_row == 4:
        lines = [(3, 1), (1, 1), (2, 1)]
    partners = [(0, c) for c in range(3, n_col, 2)]
    met = [sent(packed, hop) for hop in partners]
    line = [sent(packed, hop) for hop in lines]

    def call_blocks(kernel, name, outs, places, *args, **keywords):
        return call(
            functools.partial(kernel, places, sizes),
            name,
            outs,
            masks,
            *args,
            where=[smem] + [vmem] * len(args),
            scratch_shapes=[pltpu.SMEM((len(places) + 1,), jnp.int32)],
            **keywords,
        )

    def add_part(name, target, places, side, blocks, part):
        kernel = part_kernel if part is not None else first_kernel
        before = [] if part is None else [part]
        (part,) = call_blocks(
            functools.partial(kernel, targets.index(target)),
            name,
            [image_type],
            places,
            side,
            blocks,
            *before,
            input_output_aliases={3: 0} if before else {},
        )
        return part

    side_type = ((3 * ncv + 16, rows), jnp.bfloat16)
    targets = [(0, 0)] + partners
    side, image, masks = call(
        functools.partial(own_kernel, targets, sizes),
        "own",
        [side_type, image_type, pltpu.SMEM((len(targets), devices // 16), jnp.int32)],
        table,
        packed,
        to=[vmem, vmem, smem],
    )
    met, image = lax.optimization_barrier((met, image))
    sides = []
    for hop, block in zip(partners, met):
        image, partner_side = call_blocks(
            meet_kernel,
            "meet",
            [image_type, side_type],
            [hop],
            side,
            block[None],
            image,
            input_output_aliases={3: 0},
        )
        sides.append(partner_side)
    early, image = lax.optimization_barrier((line[1:], image))
    held, held_at = early + met + [packed], lines[1:] + partners + [(0, 0)]
    near = jnp.stack(held)
    other = sent(near, core)
    parts = [None] * len(partners)
    for k, hop in enumerate(partners):
        parts[k] = add_part("partner", hop, lines[1:], sides[k], near, None)
    image = add_part("add_early", (0, 0), lines[1:], side, near, image)
    late, parts, image = lax.optimization_barrier((line[:1], parts, image))
    late = jnp.stack(late)
    other_late = sent(late, core)
    middle = jnp.concatenate([other[: n_row - 2], late])
    for k, hop in enumerate(partners):
        places = beyond(lines[1:], core) + lines[:1]
        parts[k] = add_part("partner_middle", hop, places, sides[k], middle, parts[k])
    other_late, parts = lax.optimization_barrier((other_late, parts))
    for k, hop in enumerate(partners):
        parts[k] = add_part(
            "partner_late", hop, beyond(lines[:1], core), sides[k], other_late, parts[k]
        )
    parts, image = lax.optimization_barrier((parts, image))
    received = [sent(part, hop) for hop, part in zip(partners, parts)]
    own_places = beyond(held_at, core) + lines[:1] + beyond(lines[:1], core)
    blocks = jnp.concatenate([other, late, other_late])
    image = add_part("add_own", (0, 0), own_places, side, blocks, image)
    applied, gram = call(
        last_kernel,
        "last",
        [((nvec, rows), jnp.float32), ((devices, nvec // 2, 8 * nvec), jnp.float32)],
        vectors,
        root,
        image,
        *received,
    )
    grams = lax.all_to_all(gram, ("row", "col"), 0, 0)
    basis, ritz = call(
        functools.partial(finish_kernel, rows * devices),
        "finish",
        [((nvec, rows), jnp.float32), ((nvec, nvec), jnp.float32)],
        grams,
        applied,
    )
    return (basis, ritz)


def solution(mesh):
    split = P(None, ("grp", "row", "col"))
    return jax.shard_map(
        per_device,
        mesh=mesh,
        in_specs=(split, split, P(("grp", "row", "col")), P()),
        out_specs=(split, P("grp", None)),
        check_vma=False,
    )
```

```python
import functools
import math

import jax
import jax.numpy as jnp
from jax import lax
from jax.experimental import pallas as pl
from jax.experimental.pallas import tpu as pltpu
from jax.sharding import PartitionSpec as P

unit = -math.log2(math.e) / 4.0

NT = (((1,), (1,)), ((), ()))
MIB = 1024 * 1024


def split3(x):
    high = x.astype(jnp.bfloat16).astype(jnp.float32)
    rest = x - high
    mid = rest.astype(jnp.bfloat16).astype(jnp.float32)
    low = (rest - mid).astype(jnp.bfloat16).astype(jnp.float32)
    return high, mid, low


def pack_kernel(
    frames_ref, vectors_in, degrees_ref, table_in,
    packed_ref, vectors_ref, root_ref, table_ref, degree_ref, sems,
):
    ncv = frames_ref.shape[0]
    copies = [
        pltpu.make_async_copy(vectors_in, vectors_ref, sems.at[0]),
        pltpu.make_async_copy(degrees_ref, degree_ref, sems.at[1]),
        pltpu.make_async_copy(frames_ref, packed_ref.at[pl.ds(0, ncv)], sems.at[2]),
        pltpu.make_async_copy(table_in, table_ref, sems.at[3]),
    ]
    for copy in copies:
        copy.start()
    copies[0].wait()
    copies[1].wait()
    root = lax.rsqrt(degree_ref[...])[None, :]
    root_ref[...] = root
    packed_ref[ncv:, :] = (vectors_ref[...].astype(jnp.float32) * root).astype(jnp.bfloat16)
    copies[2].wait()
    copies[3].wait()


def edge_rows(square, ones_first):
    high, mid, low = split3(square * unit)
    row = lax.broadcasted_iota(jnp.int32, (16, square.shape[1]), 0)
    base = 3 if ones_first else 0
    ones_at = 0 if ones_first else 3
    block = jnp.where((row >= ones_at) & (row < ones_at + 3), 1.0, 0.0)
    block = jnp.where(row == base, high, block)
    block = jnp.where(row == base + 1, mid, block)
    return jnp.where(row == base + 2, low, block)


def own_side(own):
    own = own.astype(jnp.float32)
    high, mid, low = split3(own * (-2.0 * unit))
    edge = edge_rows(jnp.sum(own * own, axis=0, keepdims=True), True)
    return jnp.concatenate([high, mid, low, edge], axis=0).astype(jnp.bfloat16)


def tile_image(side_ref, blocks):
    both = blocks[0] if len(blocks) == 1 else jnp.concatenate(blocks, axis=1)
    ncv = both.shape[0] // 2
    x, v = both[:ncv, :], both[ncv:, :]
    wide = x.astype(jnp.float32)
    edge = edge_rows(jnp.sum(wide * wide, axis=0, keepdims=True), False).astype(jnp.bfloat16)
    other = jnp.concatenate([x, x, x, edge], axis=0).T
    power = jnp.dot(other, side_ref[...], preferred_element_type=jnp.float32)
    kern = jnp.exp2(power).astype(jnp.bfloat16)
    return jnp.dot(v, kern, preferred_element_type=jnp.float32)


def own_kernel(targets, sizes, table_ref, packed_ref, side_ref, image_ref, masks_ref):
    n_row, n_col = sizes
    my_row, my_col = lax.axis_index("row"), lax.axis_index("col")
    first, second = table_ref[:, 0, :], table_ref[:, 1, :]
    for t, target in enumerate(targets):
        block = (my_row ^ target[0]) * n_col + (my_col ^ target[1])
        other = jnp.where(first == block, second, jnp.where(second == block, first, -1))
        for word in range(n_row * n_col // 16):
            bit = jnp.zeros(other.shape, jnp.float32)
            for b in range(16):
                bit = jnp.where(other == 16 * word + b, float(1 << b), bit)
            masks_ref[t, word] = jnp.sum(bit).astype(jnp.int32)
    side_ref[...] = own_side(packed_ref[: packed_ref.shape[0] // 2, :])
    image_ref[...] = tile_image(side_ref, [packed_ref[...]])


def add_blocks(target, places, sizes, masks_ref, side_ref, blocks_ref, image_ref, list_ref):
    my_row, my_col = lax.axis_index("row"), lax.axis_index("col")

    count = jnp.int32(0)
    for step, place in enumerate(places):
        block = (my_row ^ place[0]) * sizes[1] + (my_col ^ place[1])
        list_ref[count] = step
        count += (masks_ref[target, block // 16] >> (block % 16)) & 1

    def add_group(start, size):
        blocks = [blocks_ref[list_ref[start + k]] for k in range(size)]
        image_ref[...] += tile_image(side_ref, blocks)

    fours = jnp.maximum(count // 4 - (count % 4 == 1).astype(jnp.int32), 0)
    rest = count - 4 * fours

    def add_four(group, _):
        add_group(4 * group, 4)
        return 0

    if len(places) >= 5:
        pl.when(count == 5)(lambda: add_group(0, 5))
        rest = jnp.where(count == 5, 0, rest)
    if len(places) >= 4:
        lax.fori_loop(0, fours, add_four, 0)
    if len(places) >= 3:
        pl.when(rest >= 3)(lambda: add_group(4 * fours, 3))
    if len(places) >= 2:
        pl.when(rest % 3 == 2)(lambda: add_group(count - 2, 2))
    pl.when(rest == 1)(lambda: add_group(count - 1, 1))


def meet_kernel(
    places, sizes, masks_ref, side_ref, blocks_ref, before_ref, image_ref, partner_side_ref, list_ref
):
    partner_side_ref[...] = own_side(blocks_ref[0, : blocks_ref.shape[1] // 2, :])
    image_ref[...] = before_ref[...]
    add_blocks(0, places, sizes, masks_ref, side_ref, blocks_ref, image_ref, list_ref)


def first_kernel(target, places, sizes, masks_ref, side_ref, blocks_ref, image_ref, list_ref):
    image_ref[...] = jnp.zeros_like(image_ref)
    add_blocks(target, places, sizes, masks_ref, side_ref, blocks_ref, image_ref, list_ref)


def part_kernel(
    target, places, sizes, masks_ref, side_ref, blocks_ref, before_ref, image_ref, list_ref
):
    image_ref[...] = before_ref[...]
    add_blocks(target, places, sizes, masks_ref, side_ref, blocks_ref, image_ref, list_ref)


def last_kernel(vectors_ref, root_ref, *refs):
    *part_refs, applied_ref, gram_ref = refs
    image = sum(part_ref[...] for part_ref in part_refs)
    n = vectors_ref.shape[0]
    applied = image * root_ref[...]
    applied_ref[...] = applied
    both = jnp.concatenate([applied, vectors_ref[...].astype(jnp.float32)], axis=0)
    gram = lax.dot_general(
        both, both, NT, precision=lax.Precision.HIGHEST, preferred_element_type=jnp.float32
    )
    wide = jnp.concatenate(
        [gram[:n, :n], gram[n:, :], jnp.zeros((n, n), jnp.float32)], axis=1
    )
    tile = jnp.concatenate([wide[: n // 2, :], wide[n // 2 :, :]], axis=1)
    for device in range(gram_ref.shape[0]):
        gram_ref[device] = tile


def inverse_factors(grams):
    n = grams[0].shape[0]
    half = 64
    tiles = range(n // 8)
    shape = (8, 2 * half)
    row = lax.broadcasted_iota(jnp.int32, shape, 0)
    lane = lax.broadcasted_iota(jnp.int32, shape, 1)
    columns = [
        [
            jnp.where(
                lane < half,
                jnp.broadcast_to(grams[0][8 * t : 8 * t + 8, j : j + 1], shape),
                jnp.broadcast_to(grams[1][8 * t : 8 * t + 8, j : j + 1], shape),
            )
            for t in tiles
        ]
        for j in range(n)
    ]
    right = [jnp.where(lane % half == row + 8 * t, 1.0, 0.0) for t in tiles]
    pivots = [jnp.ones(shape, jnp.float32) for t in tiles]
    for k in range(n):
        top, at = k // 8, k % 8
        pivot = columns[k][top][at : at + 1, :]
        pivots[top] = jnp.where(row == at, pivot, pivots[top])
        if k == n - 1:
            break
        scale = 1.0 / pivot
        factor = {t: columns[k][t] * scale for t in tiles if t >= top}
        factor[top] = jnp.where(row > at, factor[top], 0.0)
        for column in columns[k + 1 :] + [right]:
            line = column[top][at : at + 1, :]
            for t in factor:
                column[t] = column[t] - factor[t] * line
    result = jnp.concatenate([r * lax.rsqrt(p) for r, p in zip(right, pivots)], axis=0)
    return result[:, :n], result[:, half : half + n]


def finish_kernel(total_frames, grams_ref, applied_ref, basis_ref, ritz_ref):
    tile = grams_ref[0]
    for device in range(1, grams_ref.shape[0]):
        tile += grams_ref[device]
    n = applied_ref.shape[0]
    gram = jnp.concatenate([tile[:, : 4 * n], tile[:, 4 * n :]], axis=0)
    exact = functools.partial(
        lax.dot_general, precision=lax.Precision.HIGHEST, preferred_element_type=jnp.float32
    )
    plain = (((1,), (0,)), ((), ()))
    image_inverse, vector_inverse = inverse_factors([gram[:, :n], gram[:, 2 * n : 3 * n]])
    basis_ref[...] = exact(image_inverse * math.sqrt(total_frames), applied_ref[...], plain)
    half = exact(vector_inverse, gram[:, n : 2 * n], plain)
    ritz_ref[...] = exact(half, vector_inverse, NT)


def sent(x, hop):
    n_row, n_col = lax.axis_size("row"), lax.axis_size("col")
    pairs = [
        (r * n_col + c, (r ^ hop[0]) * n_col + (c ^ hop[1]))
        for r in range(n_row)
        for c in range(n_col)
    ]
    return lax.ppermute(x, ("row", "col"), pairs)


def beyond(offsets, hop):
    return [(r ^ hop[0], c ^ hop[1]) for r, c in offsets]


def per_device(frames, vectors, degrees, tile_table):
    ncv, rows = frames.shape
    nvec = vectors.shape[0]
    n_row, n_col = lax.axis_size("row"), lax.axis_size("col")
    devices = n_row * n_col
    sizes = (n_row, n_col)
    vmem = pl.BlockSpec(memory_space=pltpu.VMEM)
    smem = pl.BlockSpec(memory_space=pltpu.SMEM)

    def call(kernel, name, outs, *args, limit=24, where=vmem, to=vmem, **keywords):
        shapes = [jax.ShapeDtypeStruct(*out) if isinstance(out, tuple) else out for out in outs]
        where = where if isinstance(where, list) else [where] * len(args)
        to = to if isinstance(to, list) else [to] * len(outs)
        return pl.pallas_call(
            kernel,
            out_shape=shapes,
            in_specs=where,
            out_specs=to,
            compiler_params=pltpu.CompilerParams(vmem_limit_bytes=limit * MIB),
            name=name,
            **keywords,
        )(*args)

    image_type = ((nvec, rows), jnp.float32)

    table = tile_table.transpose(1, 2, 0)
    packed, vectors, root, table = call(
        pack_kernel,
        "pack",
        [
            ((ncv + nvec, rows), jnp.bfloat16),
            (vectors.shape, vectors.dtype),
            ((1, rows), jnp.float32),
            (table.shape, table.dtype),
        ],
        *(
            pltpu.with_memory_space_constraint(x, pltpu.HBM)
            for x in (frames, vectors, degrees, table)
        ),
        where=pl.BlockSpec(memory_space=pltpu.HBM),
        scratch_shapes=[
            pltpu.VMEM(degrees.shape, degrees.dtype),
            pltpu.SemaphoreType.DMA((4,)),
        ],
    )
    core = (0, 1)
    lines = [(r, 1) for r in range(n_row - 1, 0, -1)]
    if n_row == 4:
        lines = [(3, 1), (1, 1), (2, 1)]
    partners = [(0, c) for c in range(3, n_col, 2)]
    met = [sent(packed, hop) for hop in partners]
    line = [sent(packed, hop) for hop in lines]

    def call_blocks(kernel, name, outs, places, *args, **keywords):
        return call(
            functools.partial(kernel, places, sizes),
            name,
            outs,
            masks,
            *args,
            where=[smem] + [vmem] * len(args),
            scratch_shapes=[pltpu.SMEM((len(places) + 1,), jnp.int32)],
            **keywords,
        )

    def add_part(name, target, places, side, blocks, part):
        kernel = part_kernel if part is not None else first_kernel
        before = [] if part is None else [part]
        (part,) = call_blocks(
            functools.partial(kernel, targets.index(target)),
            name,
            [image_type],
            places,
            side,
            blocks,
            *before,
            input_output_aliases={3: 0} if before else {},
        )
        return part

    side_type = ((3 * ncv + 16, rows), jnp.bfloat16)
    targets = [(0, 0)] + partners
    side, image, masks = call(
        functools.partial(own_kernel, targets, sizes),
        "own",
        [side_type, image_type, pltpu.SMEM((len(targets), devices // 16), jnp.int32)],
        table,
        packed,
        to=[vmem, vmem, smem],
    )
    met, image = lax.optimization_barrier((met, image))
    sides = []
    for hop, block in zip(partners, met):
        image, partner_side = call_blocks(
            meet_kernel,
            "meet",
            [image_type, side_type],
            [hop],
            side,
            block[None],
            image,
            input_output_aliases={3: 0},
        )
        sides.append(partner_side)
    early, image = lax.optimization_barrier((line[1:], image))
    held, held_at = early + met + [packed], lines[1:] + partners + [(0, 0)]
    near = jnp.stack(held)
    other = sent(near, core)
    parts = [None] * len(partners)
    for k, hop in enumerate(partners):
        parts[k] = add_part("partner", hop, lines[1:], sides[k], near, None)
    late, parts, image = lax.optimization_barrier((line[:1], parts, image))
    late = jnp.stack(late)
    other_late = sent(late, core)
    middle = jnp.concatenate([other[: n_row - 2], late])
    for k, hop in enumerate(partners):
        places = beyond(lines[1:], core) + lines[:1]
        parts[k] = add_part("partner_middle", hop, places, sides[k], middle, parts[k])
    other_late, parts = lax.optimization_barrier((other_late, parts))
    for k, hop in enumerate(partners):
        parts[k] = add_part(
            "partner_late", hop, beyond(lines[:1], core), sides[k], other_late, parts[k]
        )
    parts, image = lax.optimization_barrier((parts, image))
    received = [sent(part, hop) for hop, part in zip(partners, parts)]
    own_places = lines[1:] + beyond(held_at, core) + lines[:1] + beyond(lines[:1], core)
    blocks = jnp.concatenate([near[: n_row - 2], other, late, other_late])
    image = add_part("add_own", (0, 0), own_places, side, blocks, image)
    applied, gram = call(
        last_kernel,
        "last",
        [((nvec, rows), jnp.float32), ((devices, nvec // 2, 8 * nvec), jnp.float32)],
        vectors,
        root,
        image,
        *received,
    )
    grams = lax.all_to_all(gram, ("row", "col"), 0, 0)
    basis, ritz = call(
        functools.partial(finish_kernel, rows * devices),
        "finish",
        [((nvec, rows), jnp.float32), ((nvec, nvec), jnp.float32)],
        grams,
        applied,
    )
    return (basis, ritz)


def solution(mesh):
    split = P(None, ("grp", "row", "col"))
    return jax.shard_map(
        per_device,
        mesh=mesh,
        in_specs=(split, split, P(("grp", "row", "col")), P()),
        out_specs=(split, P("grp", None)),
        check_vma=False,
    )
```

```python
import functools
import math

import jax
import jax.numpy as jnp
from jax import lax
from jax.experimental import pallas as pl
from jax.experimental.pallas import tpu as pltpu
from jax.sharding import PartitionSpec as P

unit = -math.log2(math.e) / 4.0

NT = (((1,), (1,)), ((), ()))
MIB = 1024 * 1024


def split3(x):
    high = x.astype(jnp.bfloat16).astype(jnp.float32)
    rest = x - high
    mid = rest.astype(jnp.bfloat16).astype(jnp.float32)
    low = (rest - mid).astype(jnp.bfloat16).astype(jnp.float32)
    return high, mid, low


def pack_kernel(
    frames_ref, vectors_in, degrees_ref, table_in,
    packed_ref, vectors_ref, root_ref, table_ref, degree_ref, sems,
):
    ncv = frames_ref.shape[0]
    copies = [
        pltpu.make_async_copy(degrees_ref, degree_ref, sems.at[0]),
        pltpu.make_async_copy(vectors_in, vectors_ref, sems.at[1]),
        pltpu.make_async_copy(frames_ref, packed_ref.at[pl.ds(0, ncv)], sems.at[2]),
        pltpu.make_async_copy(table_in, table_ref, sems.at[3]),
    ]
    for copy in copies:
        copy.start()
    copies[0].wait()
    root = lax.rsqrt(degree_ref[...])[None, :]
    root_ref[...] = root
    copies[1].wait()
    packed_ref[ncv:, :] = (vectors_ref[...].astype(jnp.float32) * root).astype(jnp.bfloat16)
    copies[2].wait()
    copies[3].wait()


def edge_rows(square, ones_first):
    high, mid, low = split3(square * unit)
    row = lax.broadcasted_iota(jnp.int32, (16, square.shape[1]), 0)
    base = 3 if ones_first else 0
    ones_at = 0 if ones_first else 3
    block = jnp.where((row >= ones_at) & (row < ones_at + 3), 1.0, 0.0)
    block = jnp.where(row == base, high, block)
    block = jnp.where(row == base + 1, mid, block)
    return jnp.where(row == base + 2, low, block)


def own_side(own):
    own = own.astype(jnp.float32)
    high, mid, low = split3(own * (-2.0 * unit))
    edge = edge_rows(jnp.sum(own * own, axis=0, keepdims=True), True)
    return jnp.concatenate([high, mid, low, edge], axis=0).astype(jnp.bfloat16)


def tile_image(side_ref, blocks):
    both = blocks[0] if len(blocks) == 1 else jnp.concatenate(blocks, axis=1)
    ncv = both.shape[0] // 2
    x, v = both[:ncv, :], both[ncv:, :]
    wide = x.astype(jnp.float32)
    edge = edge_rows(jnp.sum(wide * wide, axis=0, keepdims=True), False).astype(jnp.bfloat16)
    other = jnp.concatenate([x, x, x, edge], axis=0).T
    power = jnp.dot(other, side_ref[...], preferred_element_type=jnp.float32)
    kern = jnp.exp2(power).astype(jnp.bfloat16)
    return jnp.dot(v, kern, preferred_element_type=jnp.float32)


def own_kernel(targets, sizes, table_ref, packed_ref, side_ref, image_ref, masks_ref):
    n_row, n_col = sizes
    my_row, my_col = lax.axis_index("row"), lax.axis_index("col")
    first, second = table_ref[:, 0, :], table_ref[:, 1, :]
    for t, target in enumerate(targets):
        block = (my_row ^ target[0]) * n_col + (my_col ^ target[1])
        other = jnp.where(first == block, second, jnp.where(second == block, first, -1))
        for word in range(n_row * n_col // 16):
            bit = jnp.zeros(other.shape, jnp.float32)
            for b in range(16):
                bit = jnp.where(other == 16 * word + b, float(1 << b), bit)
            masks_ref[t, word] = jnp.sum(bit).astype(jnp.int32)
    side_ref[...] = own_side(packed_ref[: packed_ref.shape[0] // 2, :])
    image_ref[...] = tile_image(side_ref, [packed_ref[...]])


def add_blocks(target, places, sizes, masks_ref, side_ref, blocks_ref, image_ref, list_ref):
    my_row, my_col = lax.axis_index("row"), lax.axis_index("col")

    count = jnp.int32(0)
    for step, place in enumerate(places):
        block = (my_row ^ place[0]) * sizes[1] + (my_col ^ place[1])
        list_ref[count] = step
        count += (masks_ref[target, block // 16] >> (block % 16)) & 1

    def add_group(start, size):
        blocks = [blocks_ref[list_ref[start + k]] for k in range(size)]
        image_ref[...] += tile_image(side_ref, blocks)

    fours = jnp.maximum(count // 4 - (count % 4 == 1).astype(jnp.int32), 0)
    rest = count - 4 * fours

    def add_four(group, _):
        add_group(4 * group, 4)
        return 0

    if len(places) >= 4:
        lax.fori_loop(0, fours, add_four, 0)
    if len(places) >= 3:
        pl.when(rest >= 3)(lambda: add_group(4 * fours, 3))
    if len(places) >= 2:
        pl.when(rest % 3 == 2)(lambda: add_group(count - 2, 2))
    pl.when(rest == 1)(lambda: add_group(count - 1, 1))


def meet_kernel(
    places, sizes, masks_ref, side_ref, blocks_ref, before_ref, image_ref, partner_side_ref, list_ref
):
    partner_side_ref[...] = own_side(blocks_ref[0, : blocks_ref.shape[1] // 2, :])
    image_ref[...] = before_ref[...]
    add_blocks(0, places, sizes, masks_ref, side_ref, blocks_ref, image_ref, list_ref)


def first_kernel(target, places, sizes, masks_ref, side_ref, blocks_ref, image_ref, list_ref):
    image_ref[...] = jnp.zeros_like(image_ref)
    add_blocks(target, places, sizes, masks_ref, side_ref, blocks_ref, image_ref, list_ref)


def part_kernel(
    target, places, sizes, masks_ref, side_ref, blocks_ref, before_ref, image_ref, list_ref
):
    image_ref[...] = before_ref[...]
    add_blocks(target, places, sizes, masks_ref, side_ref, blocks_ref, image_ref, list_ref)


def last_kernel(vectors_ref, root_ref, *refs):
    *part_refs, applied_ref, gram_ref = refs
    image = sum(part_ref[...] for part_ref in part_refs)
    n = vectors_ref.shape[0]
    applied = image * root_ref[...]
    applied_ref[...] = applied
    both = jnp.concatenate([applied, vectors_ref[...].astype(jnp.float32)], axis=0)
    gram = lax.dot_general(
        both, both, NT, precision=lax.Precision.HIGHEST, preferred_element_type=jnp.float32
    )
    wide = jnp.concatenate(
        [gram[:n, :n], gram[n:, :], jnp.zeros((n, n), jnp.float32)], axis=1
    )
    tile = jnp.concatenate([wide[: n // 2, :], wide[n // 2 :, :]], axis=1)
    for device in range(gram_ref.shape[0]):
        gram_ref[device] = tile


def inverse_factors(grams):
    n = grams[0].shape[0]
    half = 64
    tiles = range(n // 8)
    shape = (8, 2 * half)
    row = lax.broadcasted_iota(jnp.int32, shape, 0)
    lane = lax.broadcasted_iota(jnp.int32, shape, 1)
    columns = [
        [
            jnp.where(
                lane < half,
                jnp.broadcast_to(grams[0][8 * t : 8 * t + 8, j : j + 1], shape),
                jnp.broadcast_to(grams[1][8 * t : 8 * t + 8, j : j + 1], shape),
            )
            for t in tiles
        ]
        for j in range(n)
    ]
    right = [jnp.where(lane % half == row + 8 * t, 1.0, 0.0) for t in tiles]
    pivots = [jnp.ones(shape, jnp.float32) for t in tiles]
    for k in range(n):
        top, at = k // 8, k % 8
        pivot = columns[k][top][at : at + 1, :]
        pivots[top] = jnp.where(row == at, pivot, pivots[top])
        if k == n - 1:
            break
        scale = 1.0 / pivot
        factor = {t: columns[k][t] * scale for t in tiles if t >= top}
        factor[top] = jnp.where(row > at, factor[top], 0.0)
        for column in columns[k + 1 :] + [right]:
            line = column[top][at : at + 1, :]
            for t in factor:
                column[t] = column[t] - factor[t] * line
    result = jnp.concatenate([r * lax.rsqrt(p) for r, p in zip(right, pivots)], axis=0)
    return result[:, :n], result[:, half : half + n]


def finish_kernel(total_frames, grams_ref, applied_ref, basis_ref, ritz_ref):
    tile = grams_ref[0]
    for device in range(1, grams_ref.shape[0]):
        tile += grams_ref[device]
    n = applied_ref.shape[0]
    gram = jnp.concatenate([tile[:, : 4 * n], tile[:, 4 * n :]], axis=0)
    exact = functools.partial(
        lax.dot_general, precision=lax.Precision.HIGHEST, preferred_element_type=jnp.float32
    )
    plain = (((1,), (0,)), ((), ()))
    image_inverse, vector_inverse = inverse_factors([gram[:, :n], gram[:, 2 * n : 3 * n]])
    basis_ref[...] = exact(image_inverse * math.sqrt(total_frames), applied_ref[...], plain)
    half = exact(vector_inverse, gram[:, n : 2 * n], plain)
    ritz_ref[...] = exact(half, vector_inverse, NT)


def sent(x, hop):
    n_row, n_col = lax.axis_size("row"), lax.axis_size("col")
    pairs = [
        (r * n_col + c, (r ^ hop[0]) * n_col + (c ^ hop[1]))
        for r in range(n_row)
        for c in range(n_col)
    ]
    return lax.ppermute(x, ("row", "col"), pairs)


def beyond(offsets, hop):
    return [(r ^ hop[0], c ^ hop[1]) for r, c in offsets]


def per_device(frames, vectors, degrees, tile_table):
    ncv, rows = frames.shape
    nvec = vectors.shape[0]
    n_row, n_col = lax.axis_size("row"), lax.axis_size("col")
    devices = n_row * n_col
    sizes = (n_row, n_col)
    vmem = pl.BlockSpec(memory_space=pltpu.VMEM)
    smem = pl.BlockSpec(memory_space=pltpu.SMEM)

    def call(kernel, name, outs, *args, limit=24, where=vmem, to=vmem, **keywords):
        shapes = [jax.ShapeDtypeStruct(*out) if isinstance(out, tuple) else out for out in outs]
        where = where if isinstance(where, list) else [where] * len(args)
        to = to if isinstance(to, list) else [to] * len(outs)
        return pl.pallas_call(
            kernel,
            out_shape=shapes,
            in_specs=where,
            out_specs=to,
            compiler_params=pltpu.CompilerParams(vmem_limit_bytes=limit * MIB),
            name=name,
            **keywords,
        )(*args)

    image_type = ((nvec, rows), jnp.float32)

    table = tile_table.transpose(1, 2, 0)
    packed, vectors, root, table = call(
        pack_kernel,
        "pack",
        [
            ((ncv + nvec, rows), jnp.bfloat16),
            (vectors.shape, vectors.dtype),
            ((1, rows), jnp.float32),
            (table.shape, table.dtype),
        ],
        *(
            pltpu.with_memory_space_constraint(x, pltpu.HBM)
            for x in (frames, vectors, degrees, table)
        ),
        where=pl.BlockSpec(memory_space=pltpu.HBM),
        scratch_shapes=[
            pltpu.VMEM(degrees.shape, degrees.dtype),
            pltpu.SemaphoreType.DMA((4,)),
        ],
    )
    core = (0, 1)
    lines = [(r, 1) for r in range(n_row - 1, 0, -1)]
    if n_row == 4:
        lines = [(3, 1), (1, 1), (2, 1)]
    partners = [(0, c) for c in range(3, n_col, 2)]
    met = [sent(packed, hop) for hop in partners]
    line = [sent(packed, hop) for hop in lines]

    def call_blocks(kernel, name, outs, places, *args, **keywords):
        return call(
            functools.partial(kernel, places, sizes),
            name,
            outs,
            masks,
            *args,
            where=[smem] + [vmem] * len(args),
            scratch_shapes=[pltpu.SMEM((len(places) + 1,), jnp.int32)],
            **keywords,
        )

    def add_part(name, target, places, side, blocks, part):
        kernel = part_kernel if part is not None else first_kernel
        before = [] if part is None else [part]
        (part,) = call_blocks(
            functools.partial(kernel, targets.index(target)),
            name,
            [image_type],
            places,
            side,
            blocks,
            *before,
            input_output_aliases={3: 0} if before else {},
        )
        return part

    side_type = ((3 * ncv + 16, rows), jnp.bfloat16)
    targets = [(0, 0)] + partners
    side, image, masks = call(
        functools.partial(own_kernel, targets, sizes),
        "own",
        [side_type, image_type, pltpu.SMEM((len(targets), devices // 16), jnp.int32)],
        table,
        packed,
        to=[vmem, vmem, smem],
    )
    met, image = lax.optimization_barrier((met, image))
    sides = []
    for hop, block in zip(partners, met):
        image, partner_side = call_blocks(
            meet_kernel,
            "meet",
            [image_type, side_type],
            [hop],
            side,
            block[None],
            image,
            input_output_aliases={3: 0},
        )
        sides.append(partner_side)
    early, image = lax.optimization_barrier((line[1:], image))
    held, held_at = early + met + [packed], lines[1:] + partners + [(0, 0)]
    near = jnp.stack(held)
    other = sent(near, core)
    parts = [None] * len(partners)
    for k, hop in enumerate(partners):
        parts[k] = add_part("partner", hop, lines[1:], sides[k], near, None)
    late, parts, image = lax.optimization_barrier((line[:1], parts, image))
    late = jnp.stack(late)
    other_late = sent(late, core)
    middle = jnp.concatenate([other[: n_row - 2], late])
    for k, hop in enumerate(partners):
        places = beyond(lines[1:], core) + lines[:1]
        parts[k] = add_part("partner_middle", hop, places, sides[k], middle, parts[k])
    other_late, parts = lax.optimization_barrier((other_late, parts))
    for k, hop in enumerate(partners):
        parts[k] = add_part(
            "partner_late", hop, beyond(lines[:1], core), sides[k], other_late, parts[k]
        )
    parts, image = lax.optimization_barrier((parts, image))
    received = [sent(part, hop) for hop, part in zip(partners, parts)]
    own_places = lines[1:] + beyond(held_at, core) + lines[:1] + beyond(lines[:1], core)
    blocks = jnp.concatenate([near[: n_row - 2], other, late, other_late])
    image = add_part("add_own", (0, 0), own_places, side, blocks, image)
    applied, gram = call(
        last_kernel,
        "last",
        [((nvec, rows), jnp.float32), ((devices, nvec // 2, 8 * nvec), jnp.float32)],
        vectors,
        root,
        image,
        *received,
    )
    grams = lax.all_to_all(gram, ("row", "col"), 0, 0)
    basis, ritz = call(
        functools.partial(finish_kernel, rows * devices),
        "finish",
        [((nvec, rows), jnp.float32), ((nvec, nvec), jnp.float32)],
        grams,
        applied,
    )
    return (basis, ritz)


def solution(mesh):
    split = P(None, ("grp", "row", "col"))
    return jax.shard_map(
        per_device,
        mesh=mesh,
        in_specs=(split, split, P(("grp", "row", "col")), P()),
        out_specs=(split, P("grp", None)),
        check_vma=False,
    )
```
